32 devices in a mesh: row: 16 (over z, x, core), col: 2 (over y).
Axes of the slice: x: 2, y: 2, z: 4, core: 2. Of those that a mesh axis runs over, the one named last changes fastest.
Arguments:
- pair: bfloat16 [512, 512, 128], P('row', 'col'), may hold values from -6 to 6
- cotangent: bfloat16 [64, 512, 512], P(None, 'row', 'col'), may hold values from -0.59765625 to 0.59765625
- w_left: bfloat16 [128, 64], replicated, may hold values from -0.5 to 0.5
- w_left_gate: bfloat16 [128, 64], replicated, may hold values from -0.5 to 0.5
- w_right: bfloat16 [128, 64], replicated, may hold values from -0.5 to 0.5
- w_right_gate: bfloat16 [128, 64], replicated, may hold values from -0.5 to 0.5
Outputs:
- pair_gradient: bfloat16 [512, 512, 128], P('row', 'col')
- grad_left: float32 [128, 64], replicated
- grad_left_gate: float32 [128, 64], replicated
- grad_right: float32 [128, 64], replicated
- grad_right_gate: float32 [128, 64], replicated
The draws below stay inside these ranges and needn't reach their ends.
All inputs are finite; a program needn't handle non-finite values.
Results may differ from the reference program's by a relative error of at most 0.0082.
Values may be sent and summed in bfloat16 or wider, within the bound.
No kernel may reach another device: no remote copies, remote signals or barrier semaphores. Data moves between devices by JAX's collectives and lax.ppermute only.
A program may use at most 128 MiB of HBM per device.

```python
import jax
import jax.numpy as jnp
from jax import lax

N = 512
C = 128
H = 64


def block_scale(key, shape, cuts, smallest, high):
    gain, own = 1.0, jax.random.fold_in(key, 6)
    for position, blocks in cuts:
        draws = jnp.exp(jax.random.uniform(jax.random.fold_in(own, position), (blocks,), jnp.float32, smallest / len(cuts), high / len(cuts)))
        gain = gain * jnp.repeat(draws, shape[position] // blocks).reshape([-1 if axis == position else 1 for axis in range(len(shape))])
    return gain


def bell_draw(own_key, extent, scale, reach, cuts=(), dtype=jnp.bfloat16):
    result = jax.random.normal(own_key, extent, jnp.float32) * scale
    if len(cuts) > 0:
        result = block_scale(own_key, extent, cuts, -0.22, 0.18) * result
    return jnp.clip(result, min=-reach, max=reach).astype(dtype)


def setup_inputs(seed: int = 0) -> dict:
    seeds = jax.random.split(jax.random.key(seed), 7)
    return {
        "pair": bell_draw(seeds[0], (N, N, C), 1.0, 6.0, ((0, 16), (1, 2))),
        "cotangent": bell_draw(seeds[1], (H, N, N), 0.1, 0.59765625, ((1, 16), (2, 2))),
        "w_left": bell_draw(seeds[2], (C, H), C ** -0.5, 0.5),
        "w_left_gate": bell_draw(seeds[3], (C, H), C ** -0.5, 0.5),
        "w_right": bell_draw(seeds[4], (C, H), C ** -0.5, 0.5),
        "w_right_gate": bell_draw(seeds[5], (C, H), C ** -0.5, 0.5),
    }


def reference(pair, cotangent, w_left, w_left_gate, w_right, w_right_gate):
    pair_f = pair.astype(jnp.float32)
    average = lax.optimization_barrier(jnp.mean(pair_f, axis=-1, keepdims=True))
    centered_input = pair_f - average
    variance = lax.optimization_barrier(jnp.mean(centered_input * centered_input, axis=-1, keepdims=True))
    inverse_scale = 1.0 / jnp.sqrt(variance + 1e-05)
    standardized_input = centered_input * inverse_scale
    normalized_input = standardized_input.astype(jnp.bfloat16)
    stacked = jnp.concatenate([w_left, w_left_gate, w_right, w_right_gate], axis=1)
    projected = jnp.einsum('ijd,dh->hij', normalized_input.astype(jnp.float32), stacked.astype(jnp.float32))
    q_left, p_left, q_right, p_right = jnp.split(projected, 4, axis=0)
    s_left = jax.nn.sigmoid(p_left)
    s_right = jax.nn.sigmoid(p_right)
    left = (s_left * q_left).astype(jnp.bfloat16)
    right = (s_right * q_right).astype(jnp.bfloat16)

    def per_channel(items):
        g_one, l_one, r_one = items
        d_l = jnp.dot(g_one, r_one, preferred_element_type=jnp.float32)
        d_r = jnp.dot(g_one.T, l_one, preferred_element_type=jnp.float32)
        return (d_l.astype(jnp.bfloat16), d_r.astype(jnp.bfloat16))
    d_left, d_right = lax.map(per_channel, (cotangent, left, right))
    grad_l = d_left.astype(jnp.float32)
    grad_r = d_right.astype(jnp.float32)
    e_left = grad_l * s_left
    f_left = grad_l * q_left * s_left * (1.0 - s_left)
    e_right = grad_r * s_right
    f_right = grad_r * q_right * s_right * (1.0 - s_right)
    grads = jnp.concatenate([e_left, f_left, e_right, f_right], axis=0).astype(jnp.bfloat16)
    weight_grads = jnp.einsum('ijd,hij->dh', normalized_input.astype(jnp.float32), grads.astype(jnp.float32)) / N
    normalized_gradient = jnp.einsum('hij,dh->ijd', grads.astype(jnp.float32), stacked.astype(jnp.float32))
    gradient_mean = lax.optimization_barrier(jnp.mean(normalized_gradient, axis=-1, keepdims=True))
    gradient_input_mean = lax.optimization_barrier(jnp.mean(normalized_gradient * standardized_input, axis=-1, keepdims=True))
    pair_gradient = ((normalized_gradient - gradient_mean - standardized_input * gradient_input_mean) * inverse_scale).astype(jnp.bfloat16)
    parts = jnp.split(weight_grads, 4, axis=1)
    return (pair_gradient, parts[0], parts[1], parts[2], parts[3])
```

```python
import jax
import jax.numpy as jnp
from jax import lax
from jax.sharding import PartitionSpec as P


def gathered_shards(pair, cotangent, w_left, w_left_gate, w_right, w_right_gate):
    pair_f = pair.astype(jnp.float32)
    average = jnp.mean(pair_f, axis=-1, keepdims=True)
    centered_input = pair_f - average
    variance = jnp.mean(centered_input * centered_input, axis=-1, keepdims=True)
    inverse_scale = 1.0 / jnp.sqrt(variance + 1e-05)
    standardized_input = centered_input * inverse_scale
    normalized_input = standardized_input.astype(jnp.bfloat16)
    stacked = jnp.concatenate([w_left, w_left_gate, w_right, w_right_gate], axis=1)
    projected = jnp.einsum(
        "rcd,dh->hrc", normalized_input, stacked, preferred_element_type=jnp.float32
    )
    q_left, p_left, q_right, p_right = jnp.split(projected, 4, axis=0)
    s_left = jax.nn.sigmoid(p_left)
    s_right = jax.nn.sigmoid(p_right)
    left = (s_left * q_left).astype(jnp.bfloat16)
    right = (s_right * q_right).astype(jnp.bfloat16)
    g_chan, left_chan, right_chan = (
        lax.all_to_all(cotangent, "col", split_axis=0, concat_axis=2, tiled=True),
        lax.all_to_all(left, "col", split_axis=0, concat_axis=2, tiled=True),
        lax.all_to_all(right, "col", split_axis=0, concat_axis=2, tiled=True),
    )
    residues = g_chan.shape[2]
    g_columns = lax.all_to_all(g_chan, "row", split_axis=2, concat_axis=1, tiled=True)
    d_left = jnp.einsum(
        "hij,hjk->hik",
        g_chan,
        lax.all_gather(right_chan, "row", axis=1, tiled=True),
        preferred_element_type=jnp.float32,
    )
    d_right = jnp.einsum(
        "hij,hik->hjk",
        g_columns,
        lax.all_gather(left_chan, "row", axis=1, tiled=True),
        preferred_element_type=jnp.float32,
    )
    d_left_tile, d_right_tile = (
        lax.all_to_all(d_left.astype(jnp.bfloat16), "col", split_axis=2, concat_axis=0, tiled=True),
        lax.all_to_all(
            d_right.astype(jnp.bfloat16), "col", split_axis=2, concat_axis=0, tiled=True
        ),
    )
    grad_l = d_left_tile.astype(jnp.float32)
    grad_r = d_right_tile.astype(jnp.float32)
    e_left = grad_l * s_left
    f_left = grad_l * q_left * s_left * (1.0 - s_left)
    e_right = grad_r * s_right
    f_right = grad_r * q_right * s_right * (1.0 - s_right)
    grads = jnp.concatenate([e_left, f_left, e_right, f_right], axis=0).astype(jnp.bfloat16)
    local_weights = jnp.einsum(
        "rcd,hrc->dh", normalized_input, grads, preferred_element_type=jnp.float32
    )
    total_weights = lax.psum(local_weights, ("row", "col")) / residues
    normalized_gradient = jnp.einsum(
        "hrc,dh->rcd", grads, stacked, preferred_element_type=jnp.float32
    )
    gradient_mean = jnp.mean(normalized_gradient, axis=-1, keepdims=True)
    gradient_input_mean = jnp.mean(normalized_gradient * standardized_input, axis=-1, keepdims=True)
    pair_gradient = (
        (normalized_gradient - gradient_mean - standardized_input * gradient_input_mean)
        * inverse_scale
    ).astype(jnp.bfloat16)
    pieces_w = jnp.split(total_weights, 4, axis=1)
    return (pair_gradient, pieces_w[0], pieces_w[1], pieces_w[2], pieces_w[3])


def axis_sum(value, axis, size):
    if size & (size - 1):
        return lax.psum(value, axis)
    step = 1
    while step < size:
        pairs = [(i, i ^ step) for i in range(size)]
        value = value + lax.ppermute(value, axis, pairs)
        step *= 2
    return value


def channel_shards(sizes, pair, cotangent, w_left, w_left_gate, w_right, w_right_gate):
    rows, cols = sizes
    devices = rows * cols
    hidden, r, c = cotangent.shape
    own = hidden // devices
    pair_f = pair.astype(jnp.float32)
    average = jnp.mean(pair_f, axis=-1, keepdims=True)
    centered_input = pair_f - average
    variance = jnp.mean(centered_input * centered_input, axis=-1, keepdims=True)
    inverse_scale = 1.0 / jnp.sqrt(variance + 1e-05)
    standardized_input = centered_input * inverse_scale
    normalized_input = standardized_input.astype(jnp.bfloat16)
    stacked = jnp.concatenate([w_left, w_left_gate, w_right, w_right_gate], axis=1)
    projected = jnp.einsum(
        "rcd,dh->hrc", normalized_input, stacked, preferred_element_type=jnp.float32
    )
    q_left, p_left, q_right, p_right = jnp.split(projected, 4, axis=0)
    s_left = jax.nn.sigmoid(p_left)
    s_right = jax.nn.sigmoid(p_right)
    left = (s_left * q_left).astype(jnp.bfloat16)
    right = (s_right * q_right).astype(jnp.bfloat16)

    def out_of(parts):
        parts = [p.reshape(devices, own, r, c) for p in parts]
        sent = jnp.concatenate(parts, axis=1)
        got = lax.all_to_all(sent, ("row", "col"), split_axis=0, concat_axis=0, tiled=True)
        got = got.reshape(rows, cols, len(parts), own, r, c)
        whole = got.transpose(2, 3, 0, 4, 1, 5)
        return whole.reshape(len(parts), own, rows * r, cols * c)

    def back(parts):
        whole = jnp.stack(parts, axis=0).reshape(len(parts), own, rows, r, cols, c)
        sent = whole.transpose(2, 4, 0, 1, 3, 5).reshape(devices, len(parts) * own, r, c)
        got = lax.all_to_all(sent, ("row", "col"), split_axis=0, concat_axis=0, tiled=True)
        got = got.reshape(devices, len(parts), own, r, c)
        return [got[:, i].reshape(hidden, r, c) for i in range(len(parts))]

    g_all, left_all, right_all = out_of([cotangent, left, right])
    d_left = jnp.einsum("hij,hjk->hik", g_all, right_all, preferred_element_type=jnp.float32)
    d_right = jnp.einsum("hij,hik->hjk", g_all, left_all, preferred_element_type=jnp.float32)
    d_left_tile, d_right_tile = back([d_left.astype(jnp.bfloat16), d_right.astype(jnp.bfloat16)])
    grad_l = d_left_tile.astype(jnp.float32)
    grad_r = d_right_tile.astype(jnp.float32)
    e_left = grad_l * s_left
    f_left = grad_l * q_left * s_left * (1.0 - s_left)
    e_right = grad_r * s_right
    f_right = grad_r * q_right * s_right * (1.0 - s_right)
    grads = jnp.concatenate([e_left, f_left, e_right, f_right], axis=0).astype(jnp.bfloat16)
    local_weights = jnp.einsum(
        "rcd,hrc->dh", normalized_input, grads, preferred_element_type=jnp.float32
    )
    total_weights = axis_sum(axis_sum(local_weights, "col", cols), "row", rows) / (rows * r)
    normalized_gradient = jnp.einsum(
        "hrc,dh->rcd", grads, stacked, preferred_element_type=jnp.float32
    )
    gradient_mean = jnp.mean(normalized_gradient, axis=-1, keepdims=True)
    gradient_input_mean = jnp.mean(normalized_gradient * standardized_input, axis=-1, keepdims=True)
    pair_gradient = (
        (normalized_gradient - gradient_mean - standardized_input * gradient_input_mean)
        * inverse_scale
    ).astype(jnp.bfloat16)
    pieces_w = jnp.split(total_weights, 4, axis=1)
    return (pair_gradient, pieces_w[0], pieces_w[1], pieces_w[2], pieces_w[3])


def solution(mesh):
    in_specs = (P("row", "col", None), P(None, "row", "col"), P(), P(), P(), P())
    out_specs = (P("row", "col", None), P(), P(), P(), P())
    sizes = (mesh.shape["row"], mesh.shape["col"])

    def shards(pair, cotangent, *weights):
        if cotangent.shape[0] % (sizes[0] * sizes[1]) == 0:
            return channel_shards(sizes, pair, cotangent, *weights)
        return gathered_shards(pair, cotangent, *weights)

    return jax.shard_map(shards, mesh=mesh, in_specs=in_specs, out_specs=out_specs, check_vma=False)
```

```python
import functools

import jax
import jax.numpy as jnp
from jax import lax
from jax.experimental import pallas as pl
from jax.experimental.pallas import tpu as pltpu
from jax.sharding import PartitionSpec as P

BF16, F32 = jnp.bfloat16, jnp.float32


def gathered_shards(pair, cotangent, w_left, w_left_gate, w_right, w_right_gate):
    pair_f = pair.astype(jnp.float32)
    average = jnp.mean(pair_f, axis=-1, keepdims=True)
    centered_input = pair_f - average
    variance = jnp.mean(centered_input * centered_input, axis=-1, keepdims=True)
    inverse_scale = 1.0 / jnp.sqrt(variance + 1e-05)
    standardized_input = centered_input * inverse_scale
    normalized_input = standardized_input.astype(jnp.bfloat16)
    stacked = jnp.concatenate([w_left, w_left_gate, w_right, w_right_gate], axis=1)
    projected = jnp.einsum(
        "rcd,dh->hrc", normalized_input, stacked, preferred_element_type=jnp.float32
    )
    q_left, p_left, q_right, p_right = jnp.split(projected, 4, axis=0)
    s_left = jax.nn.sigmoid(p_left)
    s_right = jax.nn.sigmoid(p_right)
    left = (s_left * q_left).astype(jnp.bfloat16)
    right = (s_right * q_right).astype(jnp.bfloat16)
    g_chan, left_chan, right_chan = (
        lax.all_to_all(cotangent, "col", split_axis=0, concat_axis=2, tiled=True),
        lax.all_to_all(left, "col", split_axis=0, concat_axis=2, tiled=True),
        lax.all_to_all(right, "col", split_axis=0, concat_axis=2, tiled=True),
    )
    residues = g_chan.shape[2]
    g_columns = lax.all_to_all(g_chan, "row", split_axis=2, concat_axis=1, tiled=True)
    d_left = jnp.einsum(
        "hij,hjk->hik",
        g_chan,
        lax.all_gather(right_chan, "row", axis=1, tiled=True),
        preferred_element_type=jnp.float32,
    )
    d_right = jnp.einsum(
        "hij,hik->hjk",
        g_columns,
        lax.all_gather(left_chan, "row", axis=1, tiled=True),
        preferred_element_type=jnp.float32,
    )
    d_left_tile, d_right_tile = (
        lax.all_to_all(d_left.astype(jnp.bfloat16), "col", split_axis=2, concat_axis=0, tiled=True),
        lax.all_to_all(
            d_right.astype(jnp.bfloat16), "col", split_axis=2, concat_axis=0, tiled=True
        ),
    )
    grad_l = d_left_tile.astype(jnp.float32)
    grad_r = d_right_tile.astype(jnp.float32)
    e_left = grad_l * s_left
    f_left = grad_l * q_left * s_left * (1.0 - s_left)
    e_right = grad_r * s_right
    f_right = grad_r * q_right * s_right * (1.0 - s_right)
    grads = jnp.concatenate([e_left, f_left, e_right, f_right], axis=0).astype(jnp.bfloat16)
    local_weights = jnp.einsum(
        "rcd,hrc->dh", normalized_input, grads, preferred_element_type=jnp.float32
    )
    total_weights = lax.psum(local_weights, ("row", "col")) / residues
    normalized_gradient = jnp.einsum(
        "hrc,dh->rcd", grads, stacked, preferred_element_type=jnp.float32
    )
    gradient_mean = jnp.mean(normalized_gradient, axis=-1, keepdims=True)
    gradient_input_mean = jnp.mean(normalized_gradient * standardized_input, axis=-1, keepdims=True)
    pair_gradient = (
        (normalized_gradient - gradient_mean - standardized_input * gradient_input_mean)
        * inverse_scale
    ).astype(jnp.bfloat16)
    pieces_w = jnp.split(total_weights, 4, axis=1)
    return (pair_gradient, pieces_w[0], pieces_w[1], pieces_w[2], pieces_w[3])


NT = (((1,), (1,)), ((), ()))
TN = (((0,), (0,)), ((), ()))
NN = (((1,), (0,)), ((), ()))


def stack_weights(w_refs, wt_ref):
    h = w_refs[0].shape[1]
    for i, w_ref in enumerate(w_refs):
        wt_ref[pl.ds(i * h, h), :] = w_ref[...].astype(F32).T.astype(BF16)


def layer_norm(x):
    x = x.astype(F32)
    centered = x - jnp.mean(x, axis=-1, keepdims=True)
    variance = jnp.mean(centered * centered, axis=-1, keepdims=True)
    inverse_scale = lax.rsqrt(variance + 1e-05)
    return centered * inverse_scale, inverse_scale


def project(wt_ref, normed):
    projected = lax.dot_general(wt_ref[...], normed, NT, preferred_element_type=F32)
    h = projected.shape[0] // 4
    q_left, p_left, q_right, p_right = (projected[i * h : (i + 1) * h] for i in range(4))
    return q_left, jax.nn.sigmoid(p_left), q_right, jax.nn.sigmoid(p_right)


def put_lanes(ref, at, value):
    lanes = ref.shape[2]
    for i in range(ref.shape[0]):
        ref[i, at, :] = value[:, i * lanes : (i + 1) * lanes]


def get_lanes(ref, at):
    return jnp.concatenate([ref[i, at, :] for i in range(ref.shape[0])], axis=1)


def before_kernel(own, pair_ref, cot_ref, wl, wlg, wr, wrg, out_ref, wt_ref, rows_ref):
    stack_weights((wl, wlg, wr, wrg), wt_ref)
    h = wl.shape[1]
    rows = pair_ref.shape[0]

    def one_row(r, carry):
        normed, _ = layer_norm(pair_ref[r])
        q_left, s_left, q_right, s_right = project(wt_ref, normed.astype(BF16))
        start = pl.multiple_of(r * 2 * h, 2 * h)
        put_lanes(rows_ref, pl.ds(start, h), s_left * q_left)
        put_lanes(rows_ref, pl.ds(start + h, h), s_right * q_right)
        return carry

    lax.fori_loop(0, rows, one_row, 0, unroll=2)
    for channel in range(h):
        to, slot = channel // own, (channel % own) * 3
        out_ref[to, slot] = cot_ref[channel]
        for side in range(2):
            line = get_lanes(rows_ref, pl.ds(side * h + channel, rows, stride=2 * h))
            out_ref[to, slot + 1 + side] = line.astype(BF16)


def triangle_kernel(rows, cols, in_ref, out_ref, g_ref, l_ref, r_ref):
    r, c = in_ref.shape[2:]
    for a in range(rows):
        for b in range(cols):
            for i, ref in enumerate((g_ref, l_ref, r_ref)):
                ref[pl.ds(a * r, r), pl.ds(b * c, c)] = in_ref[a * cols + b, i]
    for i, (dims, ref) in enumerate(((NN, r_ref), (TN, l_ref))):
        d = lax.dot_general(g_ref[...], ref[...], dims, preferred_element_type=F32).astype(BF16)
        for a in range(rows):
            for b in range(cols):
                out_ref[a * cols + b, i] = d[a * r : (a + 1) * r, b * c : (b + 1) * c]


def after_kernel(own, pair_ref, d_ref, wl, wlg, wr, wrg, out_ref, grad_ref, wt_ref, rows_ref):
    stack_weights((wl, wlg, wr, wrg), wt_ref)
    h = wl.shape[1]
    rows = pair_ref.shape[0]

    @pl.when(pl.program_id(0) == 0)
    def _():
        grad_ref[...] = jnp.zeros_like(grad_ref)

    for channel in range(h):
        to, slot = channel // own, (channel % own) * 2
        for side in range(2):
            line = d_ref[to, slot + side].astype(F32)
            put_lanes(rows_ref, pl.ds(side * h + channel, rows, stride=2 * h), line)

    def one_row(r, carry):
        standardized, inverse_scale = layer_norm(pair_ref[r])
        normed = standardized.astype(BF16)
        q_left, s_left, q_right, s_right = project(wt_ref, normed)
        start = pl.multiple_of(r * 2 * h, 2 * h)
        e_left = get_lanes(rows_ref, pl.ds(start, h)) * s_left
        e_right = get_lanes(rows_ref, pl.ds(start + h, h)) * s_right
        f_left = e_left * q_left * (1.0 - s_left)
        f_right = e_right * q_right * (1.0 - s_right)
        grads = jnp.concatenate([e_left, f_left, e_right, f_right], axis=0).astype(BF16)
        grad_ref[...] += lax.dot_general(grads, normed, NN, preferred_element_type=F32)
        d_normed = lax.dot_general(grads, wt_ref[...], TN, preferred_element_type=F32)
        mean = jnp.mean(d_normed, axis=-1, keepdims=True)
        input_mean = jnp.mean(d_normed * standardized, axis=-1, keepdims=True)
        out_ref[r] = ((d_normed - mean - standardized * input_mean) * inverse_scale).astype(BF16)
        return carry

    lax.fori_loop(0, rows, one_row, 0, unroll=2)


def share_kernel(scale, in_ref, out_ref):
    total = jnp.sum(in_ref[...], axis=0, keepdims=True) * scale
    out_ref[...] = jnp.broadcast_to(total, out_ref.shape)


def weights_kernel(in_ref, *out_refs):
    total = in_ref[...].T
    h = total.shape[1] // 4
    for i, out_ref in enumerate(out_refs):
        out_ref[...] = total[:, i * h : (i + 1) * h]


def channel_shards(sizes, pair, cotangent, *weights):
    rows, cols = sizes
    devices = rows * cols
    hidden, r, c = cotangent.shape
    dim = pair.shape[2]
    own = hidden // devices
    block = 16 if r % 16 == 0 else r
    grid = (r // block,)
    params = pltpu.CompilerParams(vmem_limit_bytes=48 * 2**20)
    whole = pl.BlockSpec(weights[0].shape, lambda i: (0, 0))
    tile = pl.BlockSpec((block, c, dim), lambda i: (i, 0, 0))
    exchange = functools.partial(
        lax.all_to_all, axis_name=("row", "col"), split_axis=0, concat_axis=0, tiled=True
    )
    lanes = min(c, 128)
    scratch = [
        pltpu.VMEM((4 * hidden, dim), BF16),
        pltpu.VMEM((c // lanes, 2 * hidden * block, lanes), F32),
    ]

    sent = pl.pallas_call(
        functools.partial(before_kernel, own),
        grid=grid,
        in_specs=[tile, pl.BlockSpec((hidden, block, c), lambda i: (0, i, 0))] + [whole] * 4,
        out_specs=pl.BlockSpec((devices, 3 * own, block, c), lambda i: (0, 0, i, 0)),
        out_shape=jax.ShapeDtypeStruct((devices, 3 * own, r, c), BF16),
        scratch_shapes=scratch,
        compiler_params=params,
        name="before",
    )(pair, cotangent, *weights)

    n_i, n_k = rows * r, cols * c
    sent = pl.pallas_call(
        functools.partial(triangle_kernel, rows, cols),
        grid=(own,),
        in_specs=[pl.BlockSpec((devices, 3, r, c), lambda i: (0, i, 0, 0))],
        out_specs=pl.BlockSpec((devices, 2, r, c), lambda i: (0, i, 0, 0)),
        out_shape=jax.ShapeDtypeStruct((devices, 2 * own, r, c), BF16),
        scratch_shapes=[pltpu.VMEM((n_i, n_k), BF16)] * 3,
        compiler_params=params,
        name="triangle",
    )(exchange(sent))

    pair_gradient, local_weights = pl.pallas_call(
        functools.partial(after_kernel, own),
        grid=grid,
        in_specs=[tile, pl.BlockSpec((devices, 2 * own, block, c), lambda i: (0, 0, i, 0))]
        + [whole] * 4,
        out_specs=[tile, pl.BlockSpec((4 * hidden, dim), lambda i: (0, 0))],
        out_shape=[
            jax.ShapeDtypeStruct(pair.shape, BF16),
            jax.ShapeDtypeStruct((4 * hidden, dim), F32),
        ],
        scratch_shapes=scratch,
        compiler_params=params,
        name="after",
    )(pair, exchange(sent), *weights)

    blocks = exchange(local_weights.reshape(devices, 4 * own, dim))
    shared = pl.pallas_call(
        functools.partial(share_kernel, 1.0 / n_i),
        out_shape=jax.ShapeDtypeStruct(blocks.shape, F32),
        name="share",
    )(blocks)
    grads = pl.pallas_call(
        weights_kernel,
        out_shape=[jax.ShapeDtypeStruct((dim, hidden), F32)] * 4,
        name="weights",
    )(exchange(shared).reshape(4 * hidden, dim))
    return (pair_gradient, *grads)


def solution(mesh):
    in_specs = (P("row", "col", None), P(None, "row", "col"), P(), P(), P(), P())
    out_specs = (P("row", "col", None), P(), P(), P(), P())
    sizes = (mesh.shape["row"], mesh.shape["col"])

    def shards(pair, cotangent, *weights):
        if cotangent.shape[0] % (sizes[0] * sizes[1]) == 0:
            return channel_shards(sizes, pair, cotangent, *weights)
        return gathered_shards(pair, cotangent, *weights)

    return jax.shard_map(shards, mesh=mesh, in_specs=in_specs, out_specs=out_specs, check_vma=False)
```

```python
import functools

import jax
import jax.numpy as jnp
from jax import lax
from jax.experimental import pallas as pl
from jax.experimental.pallas import tpu as pltpu
from jax.sharding import PartitionSpec as P

BF16, F32 = jnp.bfloat16, jnp.float32


def gathered_shards(pair, cotangent, w_left, w_left_gate, w_right, w_right_gate):
    pair_f = pair.astype(jnp.float32)
    average = jnp.mean(pair_f, axis=-1, keepdims=True)
    centered_input = pair_f - average
    variance = jnp.mean(centered_input * centered_input, axis=-1, keepdims=True)
    inverse_scale = 1.0 / jnp.sqrt(variance + 1e-05)
    standardized_input = centered_input * inverse_scale
    normalized_input = standardized_input.astype(jnp.bfloat16)
    stacked = jnp.concatenate([w_left, w_left_gate, w_right, w_right_gate], axis=1)
    projected = jnp.einsum(
        "rcd,dh->hrc", normalized_input, stacked, preferred_element_type=jnp.float32
    )
    q_left, p_left, q_right, p_right = jnp.split(projected, 4, axis=0)
    s_left = jax.nn.sigmoid(p_left)
    s_right = jax.nn.sigmoid(p_right)
    left = (s_left * q_left).astype(jnp.bfloat16)
    right = (s_right * q_right).astype(jnp.bfloat16)
    g_chan, left_chan, right_chan = (
        lax.all_to_all(cotangent, "col", split_axis=0, concat_axis=2, tiled=True),
        lax.all_to_all(left, "col", split_axis=0, concat_axis=2, tiled=True),
        lax.all_to_all(right, "col", split_axis=0, concat_axis=2, tiled=True),
    )
    residues = g_chan.shape[2]
    g_columns = lax.all_to_all(g_chan, "row", split_axis=2, concat_axis=1, tiled=True)
    d_left = jnp.einsum(
        "hij,hjk->hik",
        g_chan,
        lax.all_gather(right_chan, "row", axis=1, tiled=True),
        preferred_element_type=jnp.float32,
    )
    d_right = jnp.einsum(
        "hij,hik->hjk",
        g_columns,
        lax.all_gather(left_chan, "row", axis=1, tiled=True),
        preferred_element_type=jnp.float32,
    )
    d_left_tile, d_right_tile = (
        lax.all_to_all(d_left.astype(jnp.bfloat16), "col", split_axis=2, concat_axis=0, tiled=True),
        lax.all_to_all(
            d_right.astype(jnp.bfloat16), "col", split_axis=2, concat_axis=0, tiled=True
        ),
    )
    grad_l = d_left_tile.astype(jnp.float32)
    grad_r = d_right_tile.astype(jnp.float32)
    e_left = grad_l * s_left
    f_left = grad_l * q_left * s_left * (1.0 - s_left)
    e_right = grad_r * s_right
    f_right = grad_r * q_right * s_right * (1.0 - s_right)
    grads = jnp.concatenate([e_left, f_left, e_right, f_right], axis=0).astype(jnp.bfloat16)
    local_weights = jnp.einsum(
        "rcd,hrc->dh", normalized_input, grads, preferred_element_type=jnp.float32
    )
    total_weights = lax.psum(local_weights, ("row", "col")) / residues
    normalized_gradient = jnp.einsum(
        "hrc,dh->rcd", grads, stacked, preferred_element_type=jnp.float32
    )
    gradient_mean = jnp.mean(normalized_gradient, axis=-1, keepdims=True)
    gradient_input_mean = jnp.mean(normalized_gradient * standardized_input, axis=-1, keepdims=True)
    pair_gradient = (
        (normalized_gradient - gradient_mean - standardized_input * gradient_input_mean)
        * inverse_scale
    ).astype(jnp.bfloat16)
    pieces_w = jnp.split(total_weights, 4, axis=1)
    return (pair_gradient, pieces_w[0], pieces_w[1], pieces_w[2], pieces_w[3])


NT = (((1,), (1,)), ((), ()))
TN = (((0,), (0,)), ((), ()))
NN = (((1,), (0,)), ((), ()))


def dot(a, b, dims=NN):
    return lax.dot_general(a, b, dims, preferred_element_type=F32)


def stack_weights(w_refs, w_ref):
    h = w_refs[0].shape[0]
    for i, ref in enumerate(w_refs):
        w_ref[pl.ds(i * h, h), :] = ref[...]


def layer_norm(x):
    x = x.T.astype(F32)
    centered = x - jnp.mean(x, axis=0, keepdims=True)
    variance = jnp.mean(centered * centered, axis=0, keepdims=True)
    inverse_scale = lax.rsqrt(variance + 1e-05)
    return centered * inverse_scale, inverse_scale


def project(w_ref, normed):
    projected = dot(w_ref[...], normed)
    h = projected.shape[0] // 4
    q_left, p_left, q_right, p_right = (projected[i * h : (i + 1) * h] for i in range(4))
    return q_left, jax.nn.sigmoid(p_left), q_right, jax.nn.sigmoid(p_right)


def put_lanes(ref, at, value):
    lanes = ref.shape[2]
    for i in range(ref.shape[0]):
        ref[i, at, :] = value[:, i * lanes : (i + 1) * lanes]


def get_lanes(ref, at):
    return jnp.concatenate([ref[i, at, :] for i in range(ref.shape[0])], axis=1)


def before_kernel(own, pair_ref, cot_ref, wl, wlg, wr, wrg, out_ref, w_ref, rows_ref):
    stack_weights((wl, wlg, wr, wrg), w_ref)
    h = wl.shape[0]
    rows = pair_ref.shape[0]

    def one_row(r, carry):
        normed, _ = layer_norm(pair_ref[r])
        q_left, s_left, q_right, s_right = project(w_ref, normed.astype(BF16))
        start = pl.multiple_of(r * 2 * h, 2 * h)
        put_lanes(rows_ref, pl.ds(start, h), s_left * q_left)
        put_lanes(rows_ref, pl.ds(start + h, h), s_right * q_right)
        return carry

    lax.fori_loop(0, rows, one_row, 0, unroll=4)
    for channel in range(h):
        to, slot = channel // own, (channel % own) * 3
        out_ref[to, slot] = cot_ref[channel]
        for side in range(2):
            line = get_lanes(rows_ref, pl.ds(side * h + channel, rows, stride=2 * h))
            out_ref[to, slot + 1 + side] = line.astype(BF16)


def triangle_kernel(rows, cols, in_ref, out_ref, g_ref, l_ref, r_ref):
    r, c = in_ref.shape[2:]
    for a in range(rows):
        for b in range(cols):
            for i, ref in enumerate((g_ref, l_ref, r_ref)):
                ref[pl.ds(a * r, r), pl.ds(b * c, c)] = in_ref[a * cols + b, i]
    for i, (dims, ref) in enumerate(((NN, r_ref), (TN, l_ref))):
        d = dot(g_ref[...], ref[...], dims).astype(BF16)
        for a in range(rows):
            for b in range(cols):
                out_ref[a * cols + b, i] = d[a * r : (a + 1) * r, b * c : (b + 1) * c]


def after_kernel(own, pair_ref, d_ref, wl, wlg, wr, wrg, out_ref, grad_ref, w_ref, back_ref, rows_ref):
    stack_weights((wl, wlg, wr, wrg), w_ref)
    back_ref[...] = w_ref[...].T
    h = wl.shape[0]
    rows = pair_ref.shape[0]

    @pl.when(pl.program_id(0) == 0)
    def _():
        grad_ref[...] = jnp.zeros_like(grad_ref)

    for channel in range(h):
        to, slot = channel // own, (channel % own) * 2
        for side in range(2):
            line = d_ref[to, slot + side].astype(F32)
            put_lanes(rows_ref, pl.ds(side * h + channel, rows, stride=2 * h), line)

    def one_row(r, carry):
        standardized, inverse_scale = layer_norm(pair_ref[r])
        normed = standardized.astype(BF16)
        q_left, s_left, q_right, s_right = project(w_ref, normed)
        start = pl.multiple_of(r * 2 * h, 2 * h)
        e_left = get_lanes(rows_ref, pl.ds(start, h)) * s_left
        e_right = get_lanes(rows_ref, pl.ds(start + h, h)) * s_right
        f_left = e_left * q_left * (1.0 - s_left)
        f_right = e_right * q_right * (1.0 - s_right)
        grads = jnp.concatenate([e_left, f_left, e_right, f_right], axis=0).astype(BF16)
        grad_ref[...] += dot(grads, normed, NT)
        d_normed = dot(back_ref[...], grads)
        mean = jnp.mean(d_normed, axis=0, keepdims=True)
        input_mean = jnp.mean(d_normed * standardized, axis=0, keepdims=True)
        moved = (d_normed - mean - standardized * input_mean) * inverse_scale
        out_ref[r] = moved.astype(BF16).T
        return carry

    lax.fori_loop(0, rows, one_row, 0, unroll=4)


def share_kernel(scale, in_ref, out_ref):
    total = jnp.sum(in_ref[...], axis=0, keepdims=True) * scale
    out_ref[...] = jnp.broadcast_to(total, out_ref.shape)


def weights_kernel(in_ref, *out_refs):
    h = out_refs[0].shape[0]
    for i, out_ref in enumerate(out_refs):
        out_ref[...] = in_ref[pl.ds(i * h, h), :]


def channel_shards(sizes, pair, cotangent, *weights):
    rows, cols = sizes
    devices = rows * cols
    hidden, r, c = cotangent.shape
    dim = pair.shape[2]
    own = hidden // devices
    block = 16 if r % 16 == 0 else r
    grid = (r // block,)
    params = pltpu.CompilerParams(vmem_limit_bytes=48 * 2**20)
    weights = [w.T for w in weights]
    whole = pl.BlockSpec((hidden, dim), lambda i: (0, 0))
    tile = pl.BlockSpec((block, c, dim), lambda i: (i, 0, 0))
    exchange = functools.partial(
        lax.all_to_all, axis_name=("row", "col"), split_axis=0, concat_axis=0, tiled=True
    )
    lanes = min(c, 128)
    stacked = pltpu.VMEM((4 * hidden, dim), BF16)
    rows_scratch = pltpu.VMEM((c // lanes, 2 * hidden * block, lanes), F32)

    sent = pl.pallas_call(
        functools.partial(before_kernel, own),
        grid=grid,
        in_specs=[tile, pl.BlockSpec((hidden, block, c), lambda i: (0, i, 0))] + [whole] * 4,
        out_specs=pl.BlockSpec((devices, 3 * own, block, c), lambda i: (0, 0, i, 0)),
        out_shape=jax.ShapeDtypeStruct((devices, 3 * own, r, c), BF16),
        scratch_shapes=[stacked, rows_scratch],
        compiler_params=params,
        name="before",
    )(pair, cotangent, *weights)

    n_i, n_k = rows * r, cols * c
    sent = pl.pallas_call(
        functools.partial(triangle_kernel, rows, cols),
        grid=(own,),
        in_specs=[pl.BlockSpec((devices, 3, r, c), lambda i: (0, i, 0, 0))],
        out_specs=pl.BlockSpec((devices, 2, r, c), lambda i: (0, i, 0, 0)),
        out_shape=jax.ShapeDtypeStruct((devices, 2 * own, r, c), BF16),
        scratch_shapes=[pltpu.VMEM((n_i, n_k), BF16)] * 3,
        compiler_params=params,
        name="triangle",
    )(exchange(sent))

    pair_gradient, local_weights = pl.pallas_call(
        functools.partial(after_kernel, own),
        grid=grid,
        in_specs=[tile, pl.BlockSpec((devices, 2 * own, block, c), lambda i: (0, 0, i, 0))]
        + [whole] * 4,
        out_specs=[tile, pl.BlockSpec((4 * hidden, dim), lambda i: (0, 0))],
        out_shape=[
            jax.ShapeDtypeStruct(pair.shape, BF16),
            jax.ShapeDtypeStruct((4 * hidden, dim), F32),
        ],
        scratch_shapes=[stacked, pltpu.VMEM((dim, 4 * hidden), BF16), rows_scratch],
        compiler_params=params,
        name="after",
    )(pair, exchange(sent), *weights)

    blocks = exchange(local_weights.reshape(devices, 4 * own, dim))
    shared = pl.pallas_call(
        functools.partial(share_kernel, 1.0 / n_i),
        out_shape=jax.ShapeDtypeStruct(blocks.shape, F32),
        name="share",
    )(blocks)
    grads = pl.pallas_call(
        weights_kernel,
        out_shape=[jax.ShapeDtypeStruct((hidden, dim), F32)] * 4,
        name="weights",
    )(exchange(shared).reshape(4 * hidden, dim))
    return (pair_gradient, *(g.T for g in grads))


def solution(mesh):
    in_specs = (P("row", "col", None), P(None, "row", "col"), P(), P(), P(), P())
    out_specs = (P("row", "col", None), P(), P(), P(), P())
    sizes = (mesh.shape["row"], mesh.shape["col"])

    def shards(pair, cotangent, *weights):
        if cotangent.shape[0] % (sizes[0] * sizes[1]) == 0:
            return channel_shards(sizes, pair, cotangent, *weights)
        return gathered_shards(pair, cotangent, *weights)

    return jax.shard_map(shards, mesh=mesh, in_specs=in_specs, out_specs=out_specs, check_vma=False)
```

```python
import functools

import jax
import jax.numpy as jnp
from jax import lax
from jax.experimental import pallas as pl
from jax.experimental.pallas import tpu as pltpu
from jax.sharding import PartitionSpec as P

BF16, F32 = jnp.bfloat16, jnp.float32


def gathered_shards(pair, cotangent, w_left, w_left_gate, w_right, w_right_gate):
    pair_f = pair.astype(jnp.float32)
    average = jnp.mean(pair_f, axis=-1, keepdims=True)
    centered_input = pair_f - average
    variance = jnp.mean(centered_input * centered_input, axis=-1, keepdims=True)
    inverse_scale = 1.0 / jnp.sqrt(variance + 1e-05)
    standardized_input = centered_input * inverse_scale
    normalized_input = standardized_input.astype(jnp.bfloat16)
    stacked = jnp.concatenate([w_left, w_left_gate, w_right, w_right_gate], axis=1)
    projected = jnp.einsum(
        "rcd,dh->hrc", normalized_input, stacked, preferred_element_type=jnp.float32
    )
    q_left, p_left, q_right, p_right = jnp.split(projected, 4, axis=0)
    s_left = jax.nn.sigmoid(p_left)
    s_right = jax.nn.sigmoid(p_right)
    left = (s_left * q_left).astype(jnp.bfloat16)
    right = (s_right * q_right).astype(jnp.bfloat16)
    g_chan, left_chan, right_chan = (
        lax.all_to_all(cotangent, "col", split_axis=0, concat_axis=2, tiled=True),
        lax.all_to_all(left, "col", split_axis=0, concat_axis=2, tiled=True),
        lax.all_to_all(right, "col", split_axis=0, concat_axis=2, tiled=True),
    )
    residues = g_chan.shape[2]
    g_columns = lax.all_to_all(g_chan, "row", split_axis=2, concat_axis=1, tiled=True)
    d_left = jnp.einsum(
        "hij,hjk->hik",
        g_chan,
        lax.all_gather(right_chan, "row", axis=1, tiled=True),
        preferred_element_type=jnp.float32,
    )
    d_right = jnp.einsum(
        "hij,hik->hjk",
        g_columns,
        lax.all_gather(left_chan, "row", axis=1, tiled=True),
        preferred_element_type=jnp.float32,
    )
    d_left_tile, d_right_tile = (
        lax.all_to_all(d_left.astype(jnp.bfloat16), "col", split_axis=2, concat_axis=0, tiled=True),
        lax.all_to_all(
            d_right.astype(jnp.bfloat16), "col", split_axis=2, concat_axis=0, tiled=True
        ),
    )
    grad_l = d_left_tile.astype(jnp.float32)
    grad_r = d_right_tile.astype(jnp.float32)
    e_left = grad_l * s_left
    f_left = grad_l * q_left * s_left * (1.0 - s_left)
    e_right = grad_r * s_right
    f_right = grad_r * q_right * s_right * (1.0 - s_right)
    grads = jnp.concatenate([e_left, f_left, e_right, f_right], axis=0).astype(jnp.bfloat16)
    local_weights = jnp.einsum(
        "rcd,hrc->dh", normalized_input, grads, preferred_element_type=jnp.float32
    )
    total_weights = lax.psum(local_weights, ("row", "col")) / residues
    normalized_gradient = jnp.einsum(
        "hrc,dh->rcd", grads, stacked, preferred_element_type=jnp.float32
    )
    gradient_mean = jnp.mean(normalized_gradient, axis=-1, keepdims=True)
    gradient_input_mean = jnp.mean(normalized_gradient * standardized_input, axis=-1, keepdims=True)
    pair_gradient = (
        (normalized_gradient - gradient_mean - standardized_input * gradient_input_mean)
        * inverse_scale
    ).astype(jnp.bfloat16)
    pieces_w = jnp.split(total_weights, 4, axis=1)
    return (pair_gradient, pieces_w[0], pieces_w[1], pieces_w[2], pieces_w[3])


NT = (((1,), (1,)), ((), ()))
TN = (((0,), (0,)), ((), ()))
NN = (((1,), (0,)), ((), ()))


def dot(a, b, dims=NN):
    return lax.dot_general(a, b, dims, preferred_element_type=F32)


def stack_weights(w_refs, w_ref):
    h = w_refs[0].shape[0]
    for i, ref in enumerate(w_refs):
        w_ref[pl.ds(i * h, h), :] = ref[...]


def layer_norm(x):
    x = x.T.astype(F32)
    centered = x - jnp.mean(x, axis=0, keepdims=True)
    variance = jnp.mean(centered * centered, axis=0, keepdims=True)
    inverse_scale = lax.rsqrt(variance + 1e-05)
    return centered * inverse_scale, inverse_scale


def project(w_ref, normed):
    projected = dot(w_ref[...], normed)
    h = projected.shape[0] // 4
    q_left, p_left, q_right, p_right = (projected[i * h : (i + 1) * h] for i in range(4))
    return q_left, jax.nn.sigmoid(p_left), q_right, jax.nn.sigmoid(p_right)


def put_lanes(ref, at, value):
    lanes = ref.shape[2]
    for i in range(ref.shape[0]):
        ref[i, at, :] = value[:, i * lanes : (i + 1) * lanes]


def get_lanes(ref, at):
    return jnp.concatenate([ref[i, at, :] for i in range(ref.shape[0])], axis=1)


def before_kernel(own, pair_ref, wl, wlg, wr, wrg, out_ref, w_ref, rows_ref):
    stack_weights((wl, wlg, wr, wrg), w_ref)
    h = wl.shape[0]
    rows = pair_ref.shape[0]

    def one_row(r, carry):
        normed, _ = layer_norm(pair_ref[r])
        q_left, s_left, q_right, s_right = project(w_ref, normed.astype(BF16))
        start = pl.multiple_of(r * 2 * h, 2 * h)
        put_lanes(rows_ref, pl.ds(start, h), s_left * q_left)
        put_lanes(rows_ref, pl.ds(start + h, h), s_right * q_right)
        return carry

    lax.fori_loop(0, rows, one_row, 0, unroll=4)
    for channel in range(h):
        to, slot = channel // own, (channel % own) * 2
        for side in range(2):
            line = get_lanes(rows_ref, pl.ds(side * h + channel, rows, stride=2 * h))
            out_ref[to, slot + side] = line.astype(BF16)


def triangle_kernel(rows, cols, cot_ref, in_ref, out_ref, g_ref, l_ref, r_ref):
    r, c = in_ref.shape[2:]
    for a in range(rows):
        for b in range(cols):
            at = (pl.ds(a * r, r), pl.ds(b * c, c))
            g_ref[at] = cot_ref[a * cols + b, 0]
            l_ref[at] = in_ref[a * cols + b, 0]
            r_ref[at] = in_ref[a * cols + b, 1]
    for i, (dims, ref) in enumerate(((NN, r_ref), (TN, l_ref))):
        d = dot(g_ref[...], ref[...], dims).astype(BF16)
        for a in range(rows):
            for b in range(cols):
                out_ref[a * cols + b, i] = d[a * r : (a + 1) * r, b * c : (b + 1) * c]


def gates_kernel(own, pair_ref, d_ref, wl, wlg, wr, wrg, grads_ref, sums_ref, w_ref, rows_ref):
    stack_weights((wl, wlg, wr, wrg), w_ref)
    h = wl.shape[0]
    rows = pair_ref.shape[0]

    @pl.when(pl.program_id(0) == 0)
    def _():
        sums_ref[...] = jnp.zeros_like(sums_ref)

    for channel in range(h):
        to, slot = channel // own, (channel % own) * 2
        for side in range(2):
            line = d_ref[to, slot + side].astype(F32)
            put_lanes(rows_ref, pl.ds(side * h + channel, rows, stride=2 * h), line)

    def one_row(r, carry):
        standardized, _ = layer_norm(pair_ref[r])
        normed = standardized.astype(BF16)
        q_left, s_left, q_right, s_right = project(w_ref, normed)
        start = pl.multiple_of(r * 2 * h, 2 * h)
        e_left = get_lanes(rows_ref, pl.ds(start, h)) * s_left
        e_right = get_lanes(rows_ref, pl.ds(start + h, h)) * s_right
        f_left = e_left * q_left * (1.0 - s_left)
        f_right = e_right * q_right * (1.0 - s_right)
        grads = jnp.concatenate([e_left, f_left, e_right, f_right], axis=0).astype(BF16)
        grads_ref[r] = grads
        sums_ref[...] += dot(grads, normed, NT)
        return carry

    lax.fori_loop(0, rows, one_row, 0, unroll=4)


def input_kernel(pair_ref, grads_ref, wl, wlg, wr, wrg, *refs):
    out_ref, back_ref = refs[-2:]
    h = wl.shape[0]
    for i, ref in enumerate((wl, wlg, wr, wrg)):
        back_ref[:, pl.ds(i * h, h)] = ref[...].T

    def one_row(r, carry):
        standardized, inverse_scale = layer_norm(pair_ref[r])
        d_normed = dot(back_ref[...], grads_ref[r])
        mean = jnp.mean(d_normed, axis=0, keepdims=True)
        input_mean = jnp.mean(d_normed * standardized, axis=0, keepdims=True)
        moved = (d_normed - mean - standardized * input_mean) * inverse_scale
        out_ref[r] = moved.astype(BF16).T
        return carry

    lax.fori_loop(0, pair_ref.shape[0], one_row, 0, unroll=4)


def finish_kernel(scale, a_ref, b_ref, *out_refs):
    h = out_refs[0].shape[0]
    for i, out_ref in enumerate(out_refs):
        at = pl.ds(i * h, h)
        out_ref[...] = (a_ref[at, :] + b_ref[at, :]) * scale


def channel_shards(sizes, pair, cotangent, *weights):
    rows, cols = sizes
    devices = rows * cols
    hidden, r, c = cotangent.shape
    dim = pair.shape[2]
    own = hidden // devices
    block = 16 if r % 16 == 0 else r
    pieces = 4 if r % 4 == 0 else 1
    weights = [w.T for w in weights]
    whole = pl.BlockSpec((hidden, dim), lambda i: (0, 0))
    tile = pl.BlockSpec((block, c, dim), lambda i: (i, 0, 0))
    exchange = functools.partial(
        lax.all_to_all, axis_name=("row", "col"), split_axis=0, concat_axis=0, tiled=True
    )
    stacked = pltpu.VMEM((4 * hidden, dim), BF16)
    lanes = min(c, 128)
    rows_scratch = pltpu.VMEM((c // lanes, 2 * hidden * block, lanes), F32)

    def cost(flops, *arrays):
        moved = sum(a.size * a.dtype.itemsize for a in arrays)
        return pl.CostEstimate(flops=flops, bytes_accessed=moved, transcendentals=0)

    def memory(mib):
        return pltpu.CompilerParams(vmem_limit_bytes=mib * 2**20)

    columns = r * c
    lr_shape = jax.ShapeDtypeStruct((devices, 2 * own, r, c), BF16)
    g_all = exchange(cotangent.reshape(devices, own, r, c))
    sent = pl.pallas_call(
        functools.partial(before_kernel, own),
        grid=(r // block,),
        in_specs=[tile] + [whole] * 4,
        out_specs=pl.BlockSpec((devices, 2 * own, block, c), lambda i: (0, 0, i, 0)),
        out_shape=lr_shape,
        scratch_shapes=[stacked, rows_scratch],
        compiler_params=memory(60),
        cost_estimate=cost(8 * hidden * dim * columns, pair, lr_shape),
        name="before",
    )(pair, *weights)

    n_i, n_k = rows * r, cols * c
    sent = pl.pallas_call(
        functools.partial(triangle_kernel, rows, cols),
        grid=(own,),
        in_specs=[
            pl.BlockSpec((devices, 1, r, c), lambda i: (0, i, 0, 0)),
            pl.BlockSpec((devices, 2, r, c), lambda i: (0, i, 0, 0)),
        ],
        out_specs=pl.BlockSpec((devices, 2, r, c), lambda i: (0, i, 0, 0)),
        out_shape=lr_shape,
        scratch_shapes=[pltpu.VMEM((n_i, n_k), BF16)] * 3,
        compiler_params=memory(32),
        name="triangle",
    )(g_all, exchange(sent))

    grads_shape = jax.ShapeDtypeStruct((r, 4 * hidden, c), BF16)
    sums_shape = jax.ShapeDtypeStruct((4 * hidden, dim), F32)
    grads, sums = pl.pallas_call(
        functools.partial(gates_kernel, own),
        grid=(r // block,),
        in_specs=[tile, pl.BlockSpec((devices, 2 * own, block, c), lambda i: (0, 0, i, 0))]
        + [whole] * 4,
        out_specs=[
            pl.BlockSpec((block, 4 * hidden, c), lambda i: (i, 0, 0)),
            pl.BlockSpec((4 * hidden, dim), lambda i: (0, 0)),
        ],
        out_shape=[grads_shape, sums_shape],
        scratch_shapes=[stacked, rows_scratch],
        compiler_params=memory(32),
        name="gates",
    )(pair, exchange(sent), *weights)

    def input_piece(piece, pair_gradient):
        held = [] if pair_gradient is None else [pair_gradient]
        at = pl.BlockSpec((r // pieces, c, dim), lambda i: (piece, 0, 0))
        return pl.pallas_call(
            input_kernel,
            grid=(1,),
            in_specs=[at, pl.BlockSpec((r // pieces, 4 * hidden, c), lambda i: (piece, 0, 0))]
            + [whole] * 4
            + [pl.BlockSpec(memory_space=pl.ANY)] * len(held),
            out_specs=at,
            out_shape=jax.ShapeDtypeStruct(pair.shape, BF16),
            scratch_shapes=[pltpu.VMEM((dim, 4 * hidden), BF16)],
            input_output_aliases={6: 0} if held else {},
            compiler_params=memory(32),
            cost_estimate=cost(8 * hidden * dim * columns // pieces, pair),
            name="input",
        )(pair, grads, *weights, *held)

    steps = []
    for axis, size in (("row", rows), ("col", cols)):
        if size & (size - 1):
            sums = lax.psum(sums, axis)
        else:
            steps += [(axis, size, 1 << i) for i in range(size.bit_length() - 1)]
    pair_gradient, other, piece = None, jnp.zeros_like(sums), 0
    for n, (axis, size, step) in enumerate(steps):
        if n > 0:
            sums = sums + other
        other = lax.ppermute(sums, axis, [(i, i ^ step) for i in range(size)])
        last = pieces if n == len(steps) - 1 else min(piece + 1, pieces)
        for piece in range(piece, last):
            pair_gradient = input_piece(piece, pair_gradient)
        piece = last
        other, pair_gradient = lax.optimization_barrier((other, pair_gradient))
    for piece in range(piece, pieces):
        pair_gradient = input_piece(piece, pair_gradient)

    weight_grads = pl.pallas_call(
        functools.partial(finish_kernel, 1.0 / n_i),
        out_shape=[jax.ShapeDtypeStruct((hidden, dim), F32)] * 4,
        name="finish",
    )(sums, other)
    return (pair_gradient, *(g.T for g in weight_grads))


def solution(mesh):
    in_specs = (P("row", "col", None), P(None, "row", "col"), P(), P(), P(), P())
    out_specs = (P("row", "col", None), P(), P(), P(), P())
    sizes = (mesh.shape["row"], mesh.shape["col"])

    def shards(pair, cotangent, *weights):
        if cotangent.shape[0] % (sizes[0] * sizes[1]) == 0:
            return channel_shards(sizes, pair, cotangent, *weights)
        return gathered_shards(pair, cotangent, *weights)

    return jax.shard_map(shards, mesh=mesh, in_specs=in_specs, out_specs=out_specs, check_vma=False)
```

```python
import functools

import jax
import jax.numpy as jnp
from jax import lax
from jax.experimental import pallas as pl
from jax.experimental.pallas import tpu as pltpu
from jax.sharding import PartitionSpec as P

BF16, F32 = jnp.bfloat16, jnp.float32


def gathered_shards(pair, cotangent, w_left, w_left_gate, w_right, w_right_gate):
    pair_f = pair.astype(jnp.float32)
    average = jnp.mean(pair_f, axis=-1, keepdims=True)
    centered_input = pair_f - average
    variance = jnp.mean(centered_input * centered_input, axis=-1, keepdims=True)
    inverse_scale = 1.0 / jnp.sqrt(variance + 1e-05)
    standardized_input = centered_input * inverse_scale
    normalized_input = standardized_input.astype(jnp.bfloat16)
    stacked = jnp.concatenate([w_left, w_left_gate, w_right, w_right_gate], axis=1)
    projected = jnp.einsum(
        "rcd,dh->hrc", normalized_input, stacked, preferred_element_type=jnp.float32
    )
    q_left, p_left, q_right, p_right = jnp.split(projected, 4, axis=0)
    s_left = jax.nn.sigmoid(p_left)
    s_right = jax.nn.sigmoid(p_right)
    left = (s_left * q_left).astype(jnp.bfloat16)
    right = (s_right * q_right).astype(jnp.bfloat16)
    g_chan, left_chan, right_chan = (
        lax.all_to_all(cotangent, "col", split_axis=0, concat_axis=2, tiled=True),
        lax.all_to_all(left, "col", split_axis=0, concat_axis=2, tiled=True),
        lax.all_to_all(right, "col", split_axis=0, concat_axis=2, tiled=True),
    )
    residues = g_chan.shape[2]
    g_columns = lax.all_to_all(g_chan, "row", split_axis=2, concat_axis=1, tiled=True)
    d_left = jnp.einsum(
        "hij,hjk->hik",
        g_chan,
        lax.all_gather(right_chan, "row", axis=1, tiled=True),
        preferred_element_type=jnp.float32,
    )
    d_right = jnp.einsum(
        "hij,hik->hjk",
        g_columns,
        lax.all_gather(left_chan, "row", axis=1, tiled=True),
        preferred_element_type=jnp.float32,
    )
    d_left_tile, d_right_tile = (
        lax.all_to_all(d_left.astype(jnp.bfloat16), "col", split_axis=2, concat_axis=0, tiled=True),
        lax.all_to_all(
            d_right.astype(jnp.bfloat16), "col", split_axis=2, concat_axis=0, tiled=True
        ),
    )
    grad_l = d_left_tile.astype(jnp.float32)
    grad_r = d_right_tile.astype(jnp.float32)
    e_left = grad_l * s_left
    f_left = grad_l * q_left * s_left * (1.0 - s_left)
    e_right = grad_r * s_right
    f_right = grad_r * q_right * s_right * (1.0 - s_right)
    grads = jnp.concatenate([e_left, f_left, e_right, f_right], axis=0).astype(jnp.bfloat16)
    local_weights = jnp.einsum(
        "rcd,hrc->dh", normalized_input, grads, preferred_element_type=jnp.float32
    )
    total_weights = lax.psum(local_weights, ("row", "col")) / residues
    normalized_gradient = jnp.einsum(
        "hrc,dh->rcd", grads, stacked, preferred_element_type=jnp.float32
    )
    gradient_mean = jnp.mean(normalized_gradient, axis=-1, keepdims=True)
    gradient_input_mean = jnp.mean(normalized_gradient * standardized_input, axis=-1, keepdims=True)
    pair_gradient = (
        (normalized_gradient - gradient_mean - standardized_input * gradient_input_mean)
        * inverse_scale
    ).astype(jnp.bfloat16)
    pieces_w = jnp.split(total_weights, 4, axis=1)
    return (pair_gradient, pieces_w[0], pieces_w[1], pieces_w[2], pieces_w[3])


NT = (((1,), (1,)), ((), ()))
TN = (((0,), (0,)), ((), ()))
NN = (((1,), (0,)), ((), ()))


def dot(a, b, dims=NN):
    return lax.dot_general(a, b, dims, preferred_element_type=F32)


def stack_weights(w_refs, w_ref):
    h = w_refs[0].shape[0]
    for i, ref in enumerate(w_refs):
        w_ref[pl.ds(i * h, h), :] = ref[...]


def layer_norm(x):
    x = x.T.astype(F32)
    centered = x - jnp.mean(x, axis=0, keepdims=True)
    variance = jnp.mean(centered * centered, axis=0, keepdims=True)
    inverse_scale = lax.rsqrt(variance + 1e-05)
    return centered * inverse_scale, inverse_scale


def project(w_ref, normed):
    projected = dot(w_ref[...], normed)
    h = projected.shape[0] // 4
    q_left, p_left, q_right, p_right = (projected[i * h : (i + 1) * h] for i in range(4))
    return q_left, jax.nn.sigmoid(p_left), q_right, jax.nn.sigmoid(p_right)


def put_lanes(ref, at, value):
    lanes = ref.shape[2]
    for i in range(ref.shape[0]):
        ref[i, at, :] = value[:, i * lanes : (i + 1) * lanes]


def get_lanes(ref, at):
    return jnp.concatenate([ref[i, at, :] for i in range(ref.shape[0])], axis=1)


def before_kernel(own, pair_ref, wl, wlg, wr, wrg, left_ref, right_ref, w_ref, rows_ref):
    stack_weights((wl, wlg, wr, wrg), w_ref)
    h = wl.shape[0]
    rows = pair_ref.shape[0]

    def one_row(r, carry):
        normed, _ = layer_norm(pair_ref[r])
        q_left, s_left, q_right, s_right = project(w_ref, normed.astype(BF16))
        start = pl.multiple_of(r * 2 * h, 2 * h)
        put_lanes(rows_ref, pl.ds(start, h), s_left * q_left)
        put_lanes(rows_ref, pl.ds(start + h, h), s_right * q_right)
        return carry

    lax.fori_loop(0, rows, one_row, 0, unroll=4)
    for channel in range(h):
        for side, out_ref in enumerate((left_ref, right_ref)):
            line = get_lanes(rows_ref, pl.ds(side * h + channel, rows, stride=2 * h))
            out_ref[channel // own, channel % own] = line.astype(BF16)


def triangle_kernel(rows, cols, dims, cot_ref, in_ref, out_ref, g_ref, x_ref):
    r, c = in_ref.shape[2:]
    for a in range(rows):
        for b in range(cols):
            at = (pl.ds(a * r, r), pl.ds(b * c, c))
            g_ref[at] = cot_ref[a * cols + b, 0]
            x_ref[at] = in_ref[a * cols + b, 0]
    d = dot(g_ref[...], x_ref[...], dims).astype(BF16)
    for a in range(rows):
        for b in range(cols):
            out_ref[a * cols + b, 0] = d[a * r : (a + 1) * r, b * c : (b + 1) * c]


def gates_kernel(own, pair_ref, d_ref, wq, wg, *refs):
    grads_ref, sums_ref, w_ref, rows_ref = refs[-4:]
    stack_weights((wq, wg), w_ref)
    h = wq.shape[0]
    rows = pair_ref.shape[0]
    mine = pl.ds(sums_ref.shape[0] - 2 * h, 2 * h)

    @pl.when(pl.program_id(0) == 0)
    def _():
        sums_ref[mine, :] = jnp.zeros((2 * h, sums_ref.shape[1]), F32)
        if len(refs) > 4:
            sums_ref[pl.ds(0, 2 * h), :] = refs[0][...]

    for channel in range(h):
        line = d_ref[channel // own, channel % own].astype(F32)
        put_lanes(rows_ref, pl.ds(channel, rows, stride=h), line)

    def one_row(r, carry):
        normed = layer_norm(pair_ref[r])[0].astype(BF16)
        projected = dot(w_ref[...], normed)
        q, s = projected[:h], jax.nn.sigmoid(projected[h:])
        e = get_lanes(rows_ref, pl.ds(pl.multiple_of(r * h, h), h)) * s
        f = e * q * (1.0 - s)
        grads = jnp.concatenate([e, f], axis=0).astype(BF16)
        grads_ref[r] = grads
        sums_ref[mine, :] += dot(grads, normed, NT)
        return carry

    lax.fori_loop(0, rows, one_row, 0, unroll=4)


def input_kernel(pair_ref, left_ref, right_ref, wl, wlg, wr, wrg, *refs):
    out_ref, back_ref = refs[-2:]
    h = wl.shape[0]
    for i, ref in enumerate((wl, wlg, wr, wrg)):
        back_ref[:, pl.ds(i * h, h)] = ref[...].T

    def one_row(r, carry):
        standardized, inverse_scale = layer_norm(pair_ref[r])
        grads = jnp.concatenate([left_ref[r], right_ref[r]], axis=0)
        d_normed = dot(back_ref[...], grads)
        mean = jnp.mean(d_normed, axis=0, keepdims=True)
        input_mean = jnp.mean(d_normed * standardized, axis=0, keepdims=True)
        moved = (d_normed - mean - standardized * input_mean) * inverse_scale
        out_ref[r] = moved.astype(BF16).T
        return carry

    lax.fori_loop(0, pair_ref.shape[0], one_row, 0, unroll=4)


def finish_kernel(scale, a_ref, b_ref, *out_refs):
    h = out_refs[0].shape[0]
    for i, out_ref in enumerate(out_refs):
        at = pl.ds(i * h, h)
        out_ref[...] = (a_ref[at, :] + b_ref[at, :]) * scale


def channel_shards(sizes, pair, cotangent, *weights):
    rows, cols = sizes
    devices = rows * cols
    hidden, r, c = cotangent.shape
    dim = pair.shape[2]
    own = hidden // devices
    block = 16 if r % 16 == 0 else r
    pieces = 4 if r % 4 == 0 else 1
    weights = [w.T for w in weights]
    whole = pl.BlockSpec((hidden, dim), lambda i: (0, 0))
    tile = pl.BlockSpec((block, c, dim), lambda i: (i, 0, 0))
    exchange = functools.partial(
        lax.all_to_all, axis_name=("row", "col"), split_axis=0, concat_axis=0, tiled=True
    )
    lanes = min(c, 128)

    def cost(flops, *arrays):
        moved = sum(a.size * a.dtype.itemsize for a in arrays)
        return pl.CostEstimate(flops=flops, bytes_accessed=moved, transcendentals=0)

    def memory(mib):
        return pltpu.CompilerParams(vmem_limit_bytes=mib * 2**20)

    columns = r * c
    n_i, n_k = rows * r, cols * c
    blocks_shape = jax.ShapeDtypeStruct((devices, own, r, c), BF16)
    by_rows = pl.BlockSpec((devices, own, block, c), lambda i: (0, 0, i, 0))
    by_channel = pl.BlockSpec((devices, 1, r, c), lambda i: (0, i, 0, 0))

    g_all = exchange(cotangent.reshape(blocks_shape.shape))
    left, right = pl.pallas_call(
        functools.partial(before_kernel, own),
        grid=(r // block,),
        in_specs=[tile] + [whole] * 4,
        out_specs=[by_rows] * 2,
        out_shape=[blocks_shape] * 2,
        scratch_shapes=[
            pltpu.VMEM((4 * hidden, dim), BF16),
            pltpu.VMEM((c // lanes, 2 * hidden * block, lanes), F32),
        ],
        compiler_params=memory(60),
        cost_estimate=cost(8 * hidden * dim * columns, pair, pair),
        name="before",
    )(pair, *weights)
    right_all = exchange(right)
    left_all = exchange(left)

    def triangle(dims, x_all):
        return pl.pallas_call(
            functools.partial(triangle_kernel, rows, cols, dims),
            grid=(own,),
            in_specs=[by_channel] * 2,
            out_specs=by_channel,
            out_shape=blocks_shape,
            scratch_shapes=[pltpu.VMEM((n_i, n_k), BF16)] * 2,
            compiler_params=memory(32),
            cost_estimate=cost(2 * own * n_i * n_i * n_k, pair, cotangent),
            name="triangle",
        )(g_all, x_all)

    def gates(d, w, *sums):
        return pl.pallas_call(
            functools.partial(gates_kernel, own),
            grid=(r // block,),
            in_specs=[tile, by_rows, whole, whole]
            + [pl.BlockSpec((2 * hidden, dim), lambda i: (0, 0))] * len(sums),
            out_specs=[
                pl.BlockSpec((block, 2 * hidden, c), lambda i: (i, 0, 0)),
                pl.BlockSpec((2 * hidden * (1 + len(sums)), dim), lambda i: (0, 0)),
            ],
            out_shape=[
                jax.ShapeDtypeStruct((r, 2 * hidden, c), BF16),
                jax.ShapeDtypeStruct((2 * hidden * (1 + len(sums)), dim), F32),
            ],
            scratch_shapes=[
                pltpu.VMEM((2 * hidden, dim), BF16),
                pltpu.VMEM((c // lanes, hidden * block, lanes), F32),
            ],
            compiler_params=memory(32),
            cost_estimate=cost(8 * hidden * dim * columns, pair, pair, pair),
            name="gates",
        )(pair, d, *w, *sums)

    d_left = exchange(triangle(NN, right_all))
    d_right = exchange(triangle(TN, left_all))
    grads_left, sums = gates(d_left, weights[:2])
    grads_right, sums = gates(d_right, weights[2:], sums)

    def input_piece(piece, pair_gradient):
        held = [] if pair_gradient is None else [pair_gradient]
        at = pl.BlockSpec((r // pieces, c, dim), lambda i: (piece, 0, 0))
        return pl.pallas_call(
            input_kernel,
            grid=(1,),
            in_specs=[at]
            + [pl.BlockSpec((r // pieces, 2 * hidden, c), lambda i: (piece, 0, 0))] * 2
            + [whole] * 4
            + [pl.BlockSpec(memory_space=pl.ANY)] * len(held),
            out_specs=at,
            out_shape=jax.ShapeDtypeStruct(pair.shape, BF16),
            scratch_shapes=[pltpu.VMEM((dim, 4 * hidden), BF16)],
            input_output_aliases={7: 0} if held else {},
            compiler_params=memory(32),
            cost_estimate=cost(8 * hidden * dim * columns // pieces, pair),
            name="input",
        )(pair, grads_left, grads_right, *weights, *held)

    steps = []
    for axis, size in (("row", rows), ("col", cols)):
        if size & (size - 1):
            sums = lax.psum(sums, axis)
        else:
            steps += [(axis, size, 1 << i) for i in range(size.bit_length() - 1)]
    pair_gradient, other, piece = None, jnp.zeros_like(sums), 0
    for n, (axis, size, step) in enumerate(steps):
        if n > 0:
            sums = sums + other
        other = lax.ppermute(sums, axis, [(i, i ^ step) for i in range(size)])
        last = pieces if n == len(steps) - 1 else min(piece + 1, pieces)
        for piece in range(piece, last):
            pair_gradient = input_piece(piece, pair_gradient)
        piece = last
        other, pair_gradient = lax.optimization_barrier((other, pair_gradient))
    for piece in range(piece, pieces):
        pair_gradient = input_piece(piece, pair_gradient)

    weight_grads = pl.pallas_call(
        functools.partial(finish_kernel, 1.0 / n_i),
        out_shape=[jax.ShapeDtypeStruct((hidden, dim), F32)] * 4,
        name="finish",
    )(sums, other)
    return (pair_gradient, *(g.T for g in weight_grads))


def solution(mesh):
    in_specs = (P("row", "col", None), P(None, "row", "col"), P(), P(), P(), P())
    out_specs = (P("row", "col", None), P(), P(), P(), P())
    sizes = (mesh.shape["row"], mesh.shape["col"])

    def shards(pair, cotangent, *weights):
        if cotangent.shape[0] % (sizes[0] * sizes[1]) == 0:
            return channel_shards(sizes, pair, cotangent, *weights)
        return gathered_shards(pair, cotangent, *weights)

    return jax.shard_map(shards, mesh=mesh, in_specs=in_specs, out_specs=out_specs, check_vma=False)
```

```python
import functools

import jax
import jax.numpy as jnp
from jax import lax
from jax.experimental import pallas as pl
from jax.experimental.pallas import tpu as pltpu
from jax.sharding import PartitionSpec as P

BF16, F32 = jnp.bfloat16, jnp.float32


def gathered_shards(pair, cotangent, w_left, w_left_gate, w_right, w_right_gate):
    pair_f = pair.astype(jnp.float32)
    average = jnp.mean(pair_f, axis=-1, keepdims=True)
    centered_input = pair_f - average
    variance = jnp.mean(centered_input * centered_input, axis=-1, keepdims=True)
    inverse_scale = 1.0 / jnp.sqrt(variance + 1e-05)
    standardized_input = centered_input * inverse_scale
    normalized_input = standardized_input.astype(jnp.bfloat16)
    stacked = jnp.concatenate([w_left, w_left_gate, w_right, w_right_gate], axis=1)
    projected = jnp.einsum(
        "rcd,dh->hrc", normalized_input, stacked, preferred_element_type=jnp.float32
    )
    q_left, p_left, q_right, p_right = jnp.split(projected, 4, axis=0)
    s_left = jax.nn.sigmoid(p_left)
    s_right = jax.nn.sigmoid(p_right)
    left = (s_left * q_left).astype(jnp.bfloat16)
    right = (s_right * q_right).astype(jnp.bfloat16)
    g_chan, left_chan, right_chan = (
        lax.all_to_all(cotangent, "col", split_axis=0, concat_axis=2, tiled=True),
        lax.all_to_all(left, "col", split_axis=0, concat_axis=2, tiled=True),
        lax.all_to_all(right, "col", split_axis=0, concat_axis=2, tiled=True),
    )
    residues = g_chan.shape[2]
    g_columns = lax.all_to_all(g_chan, "row", split_axis=2, concat_axis=1, tiled=True)
    d_left = jnp.einsum(
        "hij,hjk->hik",
        g_chan,
        lax.all_gather(right_chan, "row", axis=1, tiled=True),
        preferred_element_type=jnp.float32,
    )
    d_right = jnp.einsum(
        "hij,hik->hjk",
        g_columns,
        lax.all_gather(left_chan, "row", axis=1, tiled=True),
        preferred_element_type=jnp.float32,
    )
    d_left_tile, d_right_tile = (
        lax.all_to_all(d_left.astype(jnp.bfloat16), "col", split_axis=2, concat_axis=0, tiled=True),
        lax.all_to_all(
            d_right.astype(jnp.bfloat16), "col", split_axis=2, concat_axis=0, tiled=True
        ),
    )
    grad_l = d_left_tile.astype(jnp.float32)
    grad_r = d_right_tile.astype(jnp.float32)
    e_left = grad_l * s_left
    f_left = grad_l * q_left * s_left * (1.0 - s_left)
    e_right = grad_r * s_right
    f_right = grad_r * q_right * s_right * (1.0 - s_right)
    grads = jnp.concatenate([e_left, f_left, e_right, f_right], axis=0).astype(jnp.bfloat16)
    local_weights = jnp.einsum(
        "rcd,hrc->dh", normalized_input, grads, preferred_element_type=jnp.float32
    )
    total_weights = lax.psum(local_weights, ("row", "col")) / residues
    normalized_gradient = jnp.einsum(
        "hrc,dh->rcd", grads, stacked, preferred_element_type=jnp.float32
    )
    gradient_mean = jnp.mean(normalized_gradient, axis=-1, keepdims=True)
    gradient_input_mean = jnp.mean(normalized_gradient * standardized_input, axis=-1, keepdims=True)
    pair_gradient = (
        (normalized_gradient - gradient_mean - standardized_input * gradient_input_mean)
        * inverse_scale
    ).astype(jnp.bfloat16)
    pieces_w = jnp.split(total_weights, 4, axis=1)
    return (pair_gradient, pieces_w[0], pieces_w[1], pieces_w[2], pieces_w[3])


NT = (((1,), (1,)), ((), ()))
TN = (((0,), (0,)), ((), ()))
NN = (((1,), (0,)), ((), ()))


def dot(a, b, dims=NN):
    return lax.dot_general(a, b, dims, preferred_element_type=F32)


def stack_weights(w_refs, w_ref):
    h = w_refs[0].shape[0]
    for i, ref in enumerate(w_refs):
        w_ref[pl.ds(i * h, h), :] = ref[...]


def layer_norm(x):
    x = x.T.astype(F32)
    centered = x - jnp.mean(x, axis=0, keepdims=True)
    variance = jnp.mean(centered * centered, axis=0, keepdims=True)
    inverse_scale = lax.rsqrt(variance + 1e-05)
    return centered * inverse_scale, inverse_scale


def project(w_ref, normed):
    projected = dot(w_ref[...], normed)
    h = projected.shape[0] // 4
    q_left, p_left, q_right, p_right = (projected[i * h : (i + 1) * h] for i in range(4))
    return q_left, jax.nn.sigmoid(p_left), q_right, jax.nn.sigmoid(p_right)


def put_lanes(ref, at, value):
    lanes = ref.shape[2]
    for i in range(ref.shape[0]):
        ref[i, at, :] = value[:, i * lanes : (i + 1) * lanes]


def get_lanes(ref, at):
    return jnp.concatenate([ref[i, at, :] for i in range(ref.shape[0])], axis=1)


def before_kernel(own, pair_ref, wl, wlg, wr, wrg, out_ref, gates_ref, normed_ref, w_ref, rows_ref):
    stack_weights((wl, wlg, wr, wrg), w_ref)
    h = wl.shape[0]
    rows = pair_ref.shape[0]

    def one_row(r, carry):
        normed = layer_norm(pair_ref[r])[0].astype(BF16)
        normed_ref[r] = normed
        projected = dot(w_ref[...], normed)
        for side in range(2):
            q = projected[2 * side * h : (2 * side + 1) * h]
            s = jax.nn.sigmoid(projected[(2 * side + 1) * h : (2 * side + 2) * h])
            value = s * q
            start = pl.multiple_of(r * 2 * h + side * h, h)
            put_lanes(rows_ref, pl.ds(start, h), value)
            gates_ref[r, pl.ds(2 * side * h, h), :] = s
            gates_ref[r, pl.ds((2 * side + 1) * h, h), :] = value * (1.0 - s)
        return carry

    lax.fori_loop(0, rows, one_row, 0, unroll=4)
    for channel in range(h):
        to, slot = channel // own, (channel % own) * 2
        for side in range(2):
            line = get_lanes(rows_ref, pl.ds(side * h + channel, rows, stride=2 * h))
            out_ref[to, slot + side] = line.astype(BF16)


def triangle_kernel(rows, cols, cot_ref, in_ref, out_ref, g_ref, l_ref, r_ref):
    r, c = in_ref.shape[2:]
    for a in range(rows):
        for b in range(cols):
            at = (pl.ds(a * r, r), pl.ds(b * c, c))
            g_ref[at] = cot_ref[a * cols + b, 0]
            l_ref[at] = in_ref[a * cols + b, 0]
            r_ref[at] = in_ref[a * cols + b, 1]
    for i, (dims, ref) in enumerate(((NN, r_ref), (TN, l_ref))):
        d = dot(g_ref[...], ref[...], dims).astype(BF16)
        for a in range(rows):
            for b in range(cols):
                out_ref[a * cols + b, i] = d[a * r : (a + 1) * r, b * c : (b + 1) * c]


def gates_kernel(own, bit_ref, d_ref, gates_ref, normed_ref, grads_ref, kept_ref, sent_ref, sums_ref, rows_ref):
    rows, h = gates_ref.shape[0], gates_ref.shape[1] // 4

    @pl.when(pl.program_id(0) == 0)
    def _():
        sums_ref[...] = jnp.zeros_like(sums_ref)

    for channel in range(h):
        to, slot = channel // own, (channel % own) * 2
        for side in range(2):
            line = d_ref[to, slot + side].astype(F32)
            put_lanes(rows_ref, pl.ds(side * h + channel, rows, stride=2 * h), line)

    def one_row(r, carry):
        parts = []
        for side in range(2):
            d = get_lanes(rows_ref, pl.ds(pl.multiple_of(r * 2 * h + side * h, h), h))
            parts.append(d * gates_ref[r, pl.ds(2 * side * h, h), :])
            parts.append(d * gates_ref[r, pl.ds((2 * side + 1) * h, h), :])
        grads = jnp.concatenate(parts, axis=0).astype(BF16)
        grads_ref[r] = grads
        sums_ref[...] += dot(grads, normed_ref[r], NT)
        return carry

    lax.fori_loop(0, rows, one_row, 0, unroll=4)

    @pl.when(pl.program_id(0) == pl.num_programs(0) - 1)
    def _():
        bit = bit_ref[0]
        kept_ref[...] = sums_ref[pl.ds(pl.multiple_of(bit * 2 * h, 2 * h), 2 * h), :]
        sent_ref[...] = sums_ref[pl.ds(pl.multiple_of((1 - bit) * 2 * h, 2 * h), 2 * h), :]


def input_kernel(pair_ref, grads_ref, wl, wlg, wr, wrg, *refs):
    out_ref, back_ref = refs[-2:]
    h = wl.shape[0]
    for i, ref in enumerate((wl, wlg, wr, wrg)):
        back_ref[:, pl.ds(i * h, h)] = ref[...].T

    def one_row(r, carry):
        standardized, inverse_scale = layer_norm(pair_ref[r])
        d_normed = dot(back_ref[...], grads_ref[r])
        mean = jnp.mean(d_normed, axis=0, keepdims=True)
        input_mean = jnp.mean(d_normed * standardized, axis=0, keepdims=True)
        moved = (d_normed - mean - standardized * input_mean) * inverse_scale
        out_ref[r] = moved.astype(BF16).T
        return carry

    lax.fori_loop(0, pair_ref.shape[0], one_row, 0, unroll=4)


def finish_kernel(scale, bit_ref, mine_ref, other_ref, *out_refs):
    h = out_refs[0].shape[0]
    for i, out_ref in enumerate(out_refs):
        at = pl.ds(i % 2 * h, h)
        mine = bit_ref[0] == i // 2
        out_ref[...] = jnp.where(mine, mine_ref[at, :], other_ref[at, :]) * scale


def channel_shards(sizes, pair, cotangent, *weights):
    rows, cols = sizes
    devices = rows * cols
    hidden, r, c = cotangent.shape
    dim = pair.shape[2]
    own = hidden // devices
    block = 16 if r % 16 == 0 else r
    pieces = 4 if r % 4 == 0 else 1
    weights = [w.T for w in weights]
    whole = pl.BlockSpec((hidden, dim), lambda i: (0, 0))
    tile = pl.BlockSpec((block, c, dim), lambda i: (i, 0, 0))
    exchange = functools.partial(
        lax.all_to_all, axis_name=("row", "col"), split_axis=0, concat_axis=0, tiled=True
    )
    stacked = pltpu.VMEM((4 * hidden, dim), BF16)
    lanes = min(c, 128)
    rows_scratch = pltpu.VMEM((c // lanes, 2 * hidden * block, lanes), F32)

    def cost(flops, *arrays):
        moved = sum(a.size * a.dtype.itemsize for a in arrays)
        return pl.CostEstimate(flops=flops, bytes_accessed=moved, transcendentals=0)

    def memory(mib):
        return pltpu.CompilerParams(vmem_limit_bytes=mib * 2**20)

    columns = r * c
    lr_shape = jax.ShapeDtypeStruct((devices, 2 * own, r, c), BF16)
    gates_shape = jax.ShapeDtypeStruct((r, 4 * hidden, c), F32)
    normed_shape = jax.ShapeDtypeStruct((r, dim, c), BF16)
    by_hidden = pl.BlockSpec((block, 4 * hidden, c), lambda i: (i, 0, 0))
    by_dim = pl.BlockSpec((block, dim, c), lambda i: (i, 0, 0))
    g_all = exchange(cotangent.reshape(devices, own, r, c))
    sent, gates, normed = pl.pallas_call(
        functools.partial(before_kernel, own),
        grid=(r // block,),
        in_specs=[tile] + [whole] * 4,
        out_specs=[
            pl.BlockSpec((devices, 2 * own, block, c), lambda i: (0, 0, i, 0)),
            by_hidden,
            by_dim,
        ],
        out_shape=[lr_shape, gates_shape, normed_shape],
        scratch_shapes=[stacked, rows_scratch],
        compiler_params=memory(60),
        cost_estimate=cost(8 * hidden * dim * columns, pair, lr_shape, gates_shape),
        name="before",
    )(pair, *weights)

    n_i, n_k = rows * r, cols * c
    sent = pl.pallas_call(
        functools.partial(triangle_kernel, rows, cols),
        grid=(own,),
        in_specs=[
            pl.BlockSpec((devices, 1, r, c), lambda i: (0, i, 0, 0)),
            pl.BlockSpec((devices, 2, r, c), lambda i: (0, i, 0, 0)),
        ],
        out_specs=pl.BlockSpec((devices, 2, r, c), lambda i: (0, i, 0, 0)),
        out_shape=lr_shape,
        scratch_shapes=[pltpu.VMEM((n_i, n_k), BF16)] * 3,
        compiler_params=memory(32),
        name="triangle",
    )(g_all, exchange(sent))

    bit = (lax.axis_index("row") % 2).astype(jnp.int32).reshape(1)
    smem = pl.BlockSpec(memory_space=pltpu.SMEM)
    half_shape = jax.ShapeDtypeStruct((2 * hidden, dim), F32)
    half = pl.BlockSpec(half_shape.shape, lambda i: (0, 0))
    grads, kept, given = pl.pallas_call(
        functools.partial(gates_kernel, own),
        grid=(r // block,),
        in_specs=[
            smem,
            pl.BlockSpec((devices, 2 * own, block, c), lambda i: (0, 0, i, 0)),
            by_hidden,
            by_dim,
        ],
        out_specs=[by_hidden, half, half],
        out_shape=[jax.ShapeDtypeStruct((r, 4 * hidden, c), BF16), half_shape, half_shape],
        scratch_shapes=[pltpu.VMEM((4 * hidden, dim), F32), rows_scratch],
        compiler_params=memory(28),
        name="gates",
    )(bit, exchange(sent), gates, normed)

    def input_piece(piece, pair_gradient):
        held = [] if pair_gradient is None else [pair_gradient]
        at = pl.BlockSpec((r // pieces, c, dim), lambda i: (piece, 0, 0))
        return pl.pallas_call(
            input_kernel,
            grid=(1,),
            in_specs=[at, pl.BlockSpec((r // pieces, 4 * hidden, c), lambda i: (piece, 0, 0))]
            + [whole] * 4
            + [pl.BlockSpec(memory_space=pl.ANY)] * len(held),
            out_specs=at,
            out_shape=jax.ShapeDtypeStruct(pair.shape, BF16),
            scratch_shapes=[pltpu.VMEM((dim, 4 * hidden), BF16)],
            input_output_aliases={6: 0} if held else {},
            compiler_params=memory(16),
            cost_estimate=cost(8 * hidden * dim * columns // pieces, pair),
            name="input",
        )(pair, grads, *weights, *held)

    steps = [("row", rows, 1 << i) for i in range(1, rows.bit_length() - 1)][::-1]
    steps += [("col", cols, 1 << i) for i in range(cols.bit_length() - 1)]
    neighbours = [(i, i ^ 1) for i in range(rows)]
    pair_gradient = None
    mine = kept + lax.ppermute(given, "row", neighbours)
    for n, (axis, size, step) in enumerate(steps):
        other = lax.ppermute(mine, axis, [(i, i ^ step) for i in range(size)])
        for piece in range(n * pieces // len(steps), (n + 1) * pieces // len(steps)):
            pair_gradient = input_piece(piece, pair_gradient)
        if pair_gradient is not None:
            other, pair_gradient = lax.optimization_barrier((other, pair_gradient))
        mine = mine + other
    weight_grads = pl.pallas_call(
        functools.partial(finish_kernel, 1.0 / n_i),
        in_specs=[smem, pl.BlockSpec(memory_space=pltpu.VMEM), pl.BlockSpec(memory_space=pltpu.VMEM)],
        out_shape=[jax.ShapeDtypeStruct((hidden, dim), F32)] * 4,
        name="finish",
    )(bit, mine, lax.ppermute(mine, "row", neighbours))
    return (pair_gradient, *(g.T for g in weight_grads))


def solution(mesh):
    in_specs = (P("row", "col", None), P(None, "row", "col"), P(), P(), P(), P())
    out_specs = (P("row", "col", None), P(), P(), P(), P())
    sizes = (mesh.shape["row"], mesh.shape["col"])

    def shards(pair, cotangent, *weights):
        plain = all(size > 1 and size & (size - 1) == 0 for size in sizes)
        if plain and cotangent.shape[0] % (sizes[0] * sizes[1]) == 0:
            return channel_shards(sizes, pair, cotangent, *weights)
        return gathered_shards(pair, cotangent, *weights)

    return jax.shard_map(shards, mesh=mesh, in_specs=in_specs, out_specs=out_specs, check_vma=False)
```

```python
import functools

import jax
import jax.numpy as jnp
from jax import lax
from jax.experimental import pallas as pl
from jax.experimental.pallas import tpu as pltpu
from jax.sharding import PartitionSpec as P

BF16, F32 = jnp.bfloat16, jnp.float32


def gathered_shards(pair, cotangent, w_left, w_left_gate, w_right, w_right_gate):
    pair_f = pair.astype(jnp.float32)
    average = jnp.mean(pair_f, axis=-1, keepdims=True)
    centered_input = pair_f - average
    variance = jnp.mean(centered_input * centered_input, axis=-1, keepdims=True)
    inverse_scale = 1.0 / jnp.sqrt(variance + 1e-05)
    standardized_input = centered_input * inverse_scale
    normalized_input = standardized_input.astype(jnp.bfloat16)
    stacked = jnp.concatenate([w_left, w_left_gate, w_right, w_right_gate], axis=1)
    projected = jnp.einsum(
        "rcd,dh->hrc", normalized_input, stacked, preferred_element_type=jnp.float32
    )
    q_left, p_left, q_right, p_right = jnp.split(projected, 4, axis=0)
    s_left = jax.nn.sigmoid(p_left)
    s_right = jax.nn.sigmoid(p_right)
    left = (s_left * q_left).astype(jnp.bfloat16)
    right = (s_right * q_right).astype(jnp.bfloat16)
    g_chan, left_chan, right_chan = (
        lax.all_to_all(cotangent, "col", split_axis=0, concat_axis=2, tiled=True),
        lax.all_to_all(left, "col", split_axis=0, concat_axis=2, tiled=True),
        lax.all_to_all(right, "col", split_axis=0, concat_axis=2, tiled=True),
    )
    residues = g_chan.shape[2]
    g_columns = lax.all_to_all(g_chan, "row", split_axis=2, concat_axis=1, tiled=True)
    d_left = jnp.einsum(
        "hij,hjk->hik",
        g_chan,
        lax.all_gather(right_chan, "row", axis=1, tiled=True),
        preferred_element_type=jnp.float32,
    )
    d_right = jnp.einsum(
        "hij,hik->hjk",
        g_columns,
        lax.all_gather(left_chan, "row", axis=1, tiled=True),
        preferred_element_type=jnp.float32,
    )
    d_left_tile, d_right_tile = (
        lax.all_to_all(d_left.astype(jnp.bfloat16), "col", split_axis=2, concat_axis=0, tiled=True),
        lax.all_to_all(
            d_right.astype(jnp.bfloat16), "col", split_axis=2, concat_axis=0, tiled=True
        ),
    )
    grad_l = d_left_tile.astype(jnp.float32)
    grad_r = d_right_tile.astype(jnp.float32)
    e_left = grad_l * s_left
    f_left = grad_l * q_left * s_left * (1.0 - s_left)
    e_right = grad_r * s_right
    f_right = grad_r * q_right * s_right * (1.0 - s_right)
    grads = jnp.concatenate([e_left, f_left, e_right, f_right], axis=0).astype(jnp.bfloat16)
    local_weights = jnp.einsum(
        "rcd,hrc->dh", normalized_input, grads, preferred_element_type=jnp.float32
    )
    total_weights = lax.psum(local_weights, ("row", "col")) / residues
    normalized_gradient = jnp.einsum(
        "hrc,dh->rcd", grads, stacked, preferred_element_type=jnp.float32
    )
    gradient_mean = jnp.mean(normalized_gradient, axis=-1, keepdims=True)
    gradient_input_mean = jnp.mean(normalized_gradient * standardized_input, axis=-1, keepdims=True)
    pair_gradient = (
        (normalized_gradient - gradient_mean - standardized_input * gradient_input_mean)
        * inverse_scale
    ).astype(jnp.bfloat16)
    pieces_w = jnp.split(total_weights, 4, axis=1)
    return (pair_gradient, pieces_w[0], pieces_w[1], pieces_w[2], pieces_w[3])


NT = (((1,), (1,)), ((), ()))
TN = (((0,), (0,)), ((), ()))
NN = (((1,), (0,)), ((), ()))


def dot(a, b, dims=NN):
    return lax.dot_general(a, b, dims, preferred_element_type=F32)


def stack_weights(w_refs, w_ref):
    h = w_refs[0].shape[0]
    for i, ref in enumerate(w_refs):
        w_ref[pl.ds(i * h, h), :] = ref[...]


def layer_norm(x):
    x = x.T.astype(F32)
    centered = x - jnp.mean(x, axis=0, keepdims=True)
    variance = jnp.mean(centered * centered, axis=0, keepdims=True)
    inverse_scale = lax.rsqrt(variance + 1e-05)
    return centered * inverse_scale, inverse_scale


def project(w_ref, normed):
    projected = dot(w_ref[...], normed)
    h = projected.shape[0] // 4
    q_left, p_left, q_right, p_right = (projected[i * h : (i + 1) * h] for i in range(4))
    return q_left, jax.nn.sigmoid(p_left), q_right, jax.nn.sigmoid(p_right)


def put_lanes(ref, at, value):
    lanes = ref.shape[2]
    for i in range(ref.shape[0]):
        ref[i, at, :] = value[:, i * lanes : (i + 1) * lanes]


def get_lanes(ref, at):
    return jnp.concatenate([ref[i, at, :] for i in range(ref.shape[0])], axis=1)


def before_kernel(own, pair_ref, wl, wlg, wr, wrg, out_ref, gates_ref, normed_ref, w_ref, rows_ref):
    stack_weights((wl, wlg, wr, wrg), w_ref)
    h = wl.shape[0]
    rows = pair_ref.shape[0]

    def one_row(r, carry):
        normed = layer_norm(pair_ref[r])[0].astype(BF16)
        normed_ref[r] = normed
        projected = dot(w_ref[...], normed)
        for side in range(2):
            q = projected[2 * side * h : (2 * side + 1) * h]
            s = jax.nn.sigmoid(projected[(2 * side + 1) * h : (2 * side + 2) * h])
            value = s * q
            start = pl.multiple_of(r * 2 * h + side * h, h)
            put_lanes(rows_ref, pl.ds(start, h), value)
            gates_ref[r, pl.ds(2 * side * h, h), :] = s
            gates_ref[r, pl.ds((2 * side + 1) * h, h), :] = value * (1.0 - s)
        return carry

    lax.fori_loop(0, rows, one_row, 0, unroll=4)
    for channel in range(h):
        to, slot = channel // own, (channel % own) * 2
        for side in range(2):
            line = get_lanes(rows_ref, pl.ds(side * h + channel, rows, stride=2 * h))
            out_ref[to, slot + side] = line.astype(BF16)


def triangle_kernel(rows, cols, cot_ref, in_ref, out_ref, g_ref, l_ref, r_ref):
    r, c = in_ref.shape[2:]
    for a in range(rows):
        for b in range(cols):
            at = (pl.ds(a * r, r), pl.ds(b * c, c))
            g_ref[at] = cot_ref[a * cols + b, 0]
            l_ref[at] = in_ref[a * cols + b, 0]
            r_ref[at] = in_ref[a * cols + b, 1]
    for i, (dims, ref) in enumerate(((NN, r_ref), (TN, l_ref))):
        d = dot(g_ref[...], ref[...], dims).astype(BF16)
        for a in range(rows):
            for b in range(cols):
                out_ref[a * cols + b, i] = d[a * r : (a + 1) * r, b * c : (b + 1) * c]


def gates_kernel(own, bit_ref, d_ref, gates_ref, normed_ref, grads_ref, kept_ref, sent_ref, sums_ref, rows_ref):
    rows, h = gates_ref.shape[0], gates_ref.shape[1] // 4

    step = pl.program_id(0) * pl.num_programs(1) + pl.program_id(1)

    @pl.when(step == 0)
    def _():
        sums_ref[...] = jnp.zeros_like(sums_ref)

    for channel in range(h):
        to, slot = channel // own, (channel % own) * 2
        for side in range(2):
            line = d_ref[to, slot + side].astype(F32)
            put_lanes(rows_ref, pl.ds(side * h + channel, rows, stride=2 * h), line)

    def one_row(r, carry):
        parts = []
        for side in range(2):
            d = get_lanes(rows_ref, pl.ds(pl.multiple_of(r * 2 * h + side * h, h), h))
            parts.append(d * gates_ref[r, pl.ds(2 * side * h, h), :])
            parts.append(d * gates_ref[r, pl.ds((2 * side + 1) * h, h), :])
        grads = jnp.concatenate(parts, axis=0).astype(BF16)
        grads_ref[r] = grads
        sums_ref[...] += dot(grads, normed_ref[r], NT)
        return carry

    lax.fori_loop(0, rows, one_row, 0, unroll=4)

    @pl.when(step == pl.num_programs(0) * pl.num_programs(1) - 1)
    def _():
        bit = bit_ref[0]
        kept_ref[...] = sums_ref[pl.ds(pl.multiple_of(bit * 2 * h, 2 * h), 2 * h), :]
        sent_ref[...] = sums_ref[pl.ds(pl.multiple_of((1 - bit) * 2 * h, 2 * h), 2 * h), :]


def input_kernel(pair_ref, grads_ref, wl, wlg, wr, wrg, *refs):
    out_ref, back_ref = refs[-2:]
    h = wl.shape[0]
    for i, ref in enumerate((wl, wlg, wr, wrg)):
        back_ref[:, pl.ds(i * h, h)] = ref[...].T

    def one_row(r, carry):
        standardized, inverse_scale = layer_norm(pair_ref[r])
        d_normed = dot(back_ref[...], grads_ref[r])
        mean = jnp.mean(d_normed, axis=0, keepdims=True)
        input_mean = jnp.mean(d_normed * standardized, axis=0, keepdims=True)
        moved = (d_normed - mean - standardized * input_mean) * inverse_scale
        out_ref[r] = moved.astype(BF16).T
        return carry

    lax.fori_loop(0, pair_ref.shape[0], one_row, 0, unroll=4)


def finish_kernel(scale, bit_ref, mine_ref, other_ref, *out_refs):
    h = out_refs[0].shape[0]
    for i, out_ref in enumerate(out_refs):
        at = pl.ds(i % 2 * h, h)
        mine = bit_ref[0] == i // 2
        out_ref[...] = jnp.where(mine, mine_ref[at, :], other_ref[at, :]) * scale


def channel_shards(sizes, pair, cotangent, *weights):
    rows, cols = sizes
    devices = rows * cols
    hidden, r, c = cotangent.shape
    dim = pair.shape[2]
    own = hidden // devices
    block = 16 if r % 16 == 0 else r
    pieces = 4 if r % 4 == 0 else 1
    weights = [w.T for w in weights]
    whole = pl.BlockSpec((hidden, dim), lambda i: (0, 0))
    tile = pl.BlockSpec((block, c, dim), lambda i: (i, 0, 0))
    exchange = functools.partial(
        lax.all_to_all, axis_name=("row", "col"), split_axis=0, concat_axis=0, tiled=True
    )
    stacked = pltpu.VMEM((4 * hidden, dim), BF16)
    lanes = min(c, 128)
    rows_scratch = pltpu.VMEM((c // lanes, 2 * hidden * block, lanes), F32)

    def cost(flops, *arrays):
        moved = sum(a.size * a.dtype.itemsize for a in arrays)
        return pl.CostEstimate(flops=flops, bytes_accessed=moved, transcendentals=0)

    def memory(mib):
        return pltpu.CompilerParams(vmem_limit_bytes=mib * 2**20)

    columns = r * c
    lr_shape = jax.ShapeDtypeStruct((devices, 2 * own, r, c), BF16)
    gates_shape = jax.ShapeDtypeStruct((r, 4 * hidden, c), F32)
    normed_shape = jax.ShapeDtypeStruct((r, dim, c), BF16)
    by_hidden = pl.BlockSpec((block, 4 * hidden, c), lambda i: (i, 0, 0))
    by_dim = pl.BlockSpec((block, dim, c), lambda i: (i, 0, 0))
    g_all = exchange(cotangent.reshape(devices, own, r, c))
    sent, gates, normed = pl.pallas_call(
        functools.partial(before_kernel, own),
        grid=(r // block,),
        in_specs=[tile] + [whole] * 4,
        out_specs=[
            pl.BlockSpec((devices, 2 * own, block, c), lambda i: (0, 0, i, 0)),
            by_hidden,
            by_dim,
        ],
        out_shape=[lr_shape, gates_shape, normed_shape],
        scratch_shapes=[stacked, rows_scratch],
        compiler_params=memory(60),
        cost_estimate=cost(8 * hidden * dim * columns, pair, lr_shape, gates_shape),
        name="before",
    )(pair, *weights)

    n_i, n_k = rows * r, cols * c
    sent = pl.pallas_call(
        functools.partial(triangle_kernel, rows, cols),
        grid=(own,),
        in_specs=[
            pl.BlockSpec((devices, 1, r, c), lambda i: (0, i, 0, 0)),
            pl.BlockSpec((devices, 2, r, c), lambda i: (0, i, 0, 0)),
        ],
        out_specs=pl.BlockSpec((devices, 2, r, c), lambda i: (0, i, 0, 0)),
        out_shape=lr_shape,
        scratch_shapes=[pltpu.VMEM((n_i, n_k), BF16)] * 3,
        compiler_params=memory(32),
        name="triangle",
    )(g_all, exchange(sent))

    bit = (lax.axis_index("row") % 2).astype(jnp.int32).reshape(1)
    smem = pl.BlockSpec(memory_space=pltpu.SMEM)
    half_shape = jax.ShapeDtypeStruct((2 * hidden, dim), F32)
    half = pl.BlockSpec(half_shape.shape, lambda i, j: (0, 0))
    grads, kept, given = pl.pallas_call(
        functools.partial(gates_kernel, own),
        grid=(r // block, c // lanes),
        in_specs=[
            smem,
            pl.BlockSpec((devices, 2 * own, block, lanes), lambda i, j: (0, 0, i, j)),
            pl.BlockSpec((block, 4 * hidden, lanes), lambda i, j: (i, 0, j)),
            pl.BlockSpec((block, dim, lanes), lambda i, j: (i, 0, j)),
        ],
        out_specs=[pl.BlockSpec((block, 4 * hidden, lanes), lambda i, j: (i, 0, j)), half, half],
        out_shape=[jax.ShapeDtypeStruct((r, 4 * hidden, c), BF16), half_shape, half_shape],
        scratch_shapes=[pltpu.VMEM((4 * hidden, dim), F32), pltpu.VMEM((1, 2 * hidden * block, lanes), F32)],
        compiler_params=memory(60),
        name="gates",
    )(bit, exchange(sent), gates, normed)

    def input_piece(piece, pair_gradient):
        held = [] if pair_gradient is None else [pair_gradient]
        at = pl.BlockSpec((r // pieces, c, dim), lambda i: (piece, 0, 0))
        return pl.pallas_call(
            input_kernel,
            grid=(1,),
            in_specs=[at, pl.BlockSpec((r // pieces, 4 * hidden, c), lambda i: (piece, 0, 0))]
            + [whole] * 4
            + [pl.BlockSpec(memory_space=pl.ANY)] * len(held),
            out_specs=at,
            out_shape=jax.ShapeDtypeStruct(pair.shape, BF16),
            scratch_shapes=[pltpu.VMEM((dim, 4 * hidden), BF16)],
            input_output_aliases={6: 0} if held else {},
            compiler_params=memory(60),
            cost_estimate=cost(8 * hidden * dim * columns // pieces, pair),
            name="input",
        )(pair, grads, *weights, *held)

    steps = [("row", rows, 1 << i) for i in range(1, rows.bit_length() - 1)][::-1]
    steps += [("col", cols, 1 << i) for i in range(cols.bit_length() - 1)]
    neighbours = [(i, i ^ 1) for i in range(rows)]
    pair_gradient = None
    mine = kept + lax.ppermute(given, "row", neighbours)
    for n, (axis, size, step) in enumerate(steps):
        other = lax.ppermute(mine, axis, [(i, i ^ step) for i in range(size)])
        for piece in range(n * pieces // len(steps), (n + 1) * pieces // len(steps)):
            pair_gradient = input_piece(piece, pair_gradient)
        if pair_gradient is not None:
            other, pair_gradient = lax.optimization_barrier((other, pair_gradient))
        mine = mine + other
    weight_grads = pl.pallas_call(
        functools.partial(finish_kernel, 1.0 / n_i),
        in_specs=[smem, pl.BlockSpec(memory_space=pltpu.VMEM), pl.BlockSpec(memory_space=pltpu.VMEM)],
        out_shape=[jax.ShapeDtypeStruct((hidden, dim), F32)] * 4,
        name="finish",
    )(bit, mine, lax.ppermute(mine, "row", neighbours))
    return (pair_gradient, *(g.T for g in weight_grads))


def solution(mesh):
    in_specs = (P("row", "col", None), P(None, "row", "col"), P(), P(), P(), P())
    out_specs = (P("row", "col", None), P(), P(), P(), P())
    sizes = (mesh.shape["row"], mesh.shape["col"])

    def shards(pair, cotangent, *weights):
        plain = all(size > 1 and size & (size - 1) == 0 for size in sizes)
        if plain and cotangent.shape[0] % (sizes[0] * sizes[1]) == 0:
            return channel_shards(sizes, pair, cotangent, *weights)
        return gathered_shards(pair, cotangent, *weights)

    return jax.shard_map(shards, mesh=mesh, in_specs=in_specs, out_specs=out_specs, check_vma=False)
```

```python
import functools

import jax
import jax.numpy as jnp
from jax import lax
from jax.experimental import pallas as pl
from jax.experimental.pallas import tpu as pltpu
from jax.sharding import PartitionSpec as P

BF16, F32 = jnp.bfloat16, jnp.float32


def gathered_shards(pair, cotangent, w_left, w_left_gate, w_right, w_right_gate):
    pair_f = pair.astype(jnp.float32)
    average = jnp.mean(pair_f, axis=-1, keepdims=True)
    centered_input = pair_f - average
    variance = jnp.mean(centered_input * centered_input, axis=-1, keepdims=True)
    inverse_scale = 1.0 / jnp.sqrt(variance + 1e-05)
    standardized_input = centered_input * inverse_scale
    normalized_input = standardized_input.astype(jnp.bfloat16)
    stacked = jnp.concatenate([w_left, w_left_gate, w_right, w_right_gate], axis=1)
    projected = jnp.einsum(
        "rcd,dh->hrc", normalized_input, stacked, preferred_element_type=jnp.float32
    )
    q_left, p_left, q_right, p_right = jnp.split(projected, 4, axis=0)
    s_left = jax.nn.sigmoid(p_left)
    s_right = jax.nn.sigmoid(p_right)
    left = (s_left * q_left).astype(jnp.bfloat16)
    right = (s_right * q_right).astype(jnp.bfloat16)
    g_chan, left_chan, right_chan = (
        lax.all_to_all(cotangent, "col", split_axis=0, concat_axis=2, tiled=True),
        lax.all_to_all(left, "col", split_axis=0, concat_axis=2, tiled=True),
        lax.all_to_all(right, "col", split_axis=0, concat_axis=2, tiled=True),
    )
    residues = g_chan.shape[2]
    g_columns = lax.all_to_all(g_chan, "row", split_axis=2, concat_axis=1, tiled=True)
    d_left = jnp.einsum(
        "hij,hjk->hik",
        g_chan,
        lax.all_gather(right_chan, "row", axis=1, tiled=True),
        preferred_element_type=jnp.float32,
    )
    d_right = jnp.einsum(
        "hij,hik->hjk",
        g_columns,
        lax.all_gather(left_chan, "row", axis=1, tiled=True),
        preferred_element_type=jnp.float32,
    )
    d_left_tile, d_right_tile = (
        lax.all_to_all(d_left.astype(jnp.bfloat16), "col", split_axis=2, concat_axis=0, tiled=True),
        lax.all_to_all(
            d_right.astype(jnp.bfloat16), "col", split_axis=2, concat_axis=0, tiled=True
        ),
    )
    grad_l = d_left_tile.astype(jnp.float32)
    grad_r = d_right_tile.astype(jnp.float32)
    e_left = grad_l * s_left
    f_left = grad_l * q_left * s_left * (1.0 - s_left)
    e_right = grad_r * s_right
    f_right = grad_r * q_right * s_right * (1.0 - s_right)
    grads = jnp.concatenate([e_left, f_left, e_right, f_right], axis=0).astype(jnp.bfloat16)
    local_weights = jnp.einsum(
        "rcd,hrc->dh", normalized_input, grads, preferred_element_type=jnp.float32
    )
    total_weights = lax.psum(local_weights, ("row", "col")) / residues
    normalized_gradient = jnp.einsum(
        "hrc,dh->rcd", grads, stacked, preferred_element_type=jnp.float32
    )
    gradient_mean = jnp.mean(normalized_gradient, axis=-1, keepdims=True)
    gradient_input_mean = jnp.mean(normalized_gradient * standardized_input, axis=-1, keepdims=True)
    pair_gradient = (
        (normalized_gradient - gradient_mean - standardized_input * gradient_input_mean)
        * inverse_scale
    ).astype(jnp.bfloat16)
    pieces_w = jnp.split(total_weights, 4, axis=1)
    return (pair_gradient, pieces_w[0], pieces_w[1], pieces_w[2], pieces_w[3])


NT = (((1,), (1,)), ((), ()))
TN = (((0,), (0,)), ((), ()))
NN = (((1,), (0,)), ((), ()))


def dot(a, b, dims=NN):
    return lax.dot_general(a, b, dims, preferred_element_type=F32)


def stack_weights(w_refs, w_ref):
    h = w_refs[0].shape[0]
    for i, ref in enumerate(w_refs):
        w_ref[pl.ds(i * h, h), :] = ref[...]


def layer_norm(x):
    x = x.T.astype(F32)
    centered = x - jnp.mean(x, axis=0, keepdims=True)
    variance = jnp.mean(centered * centered, axis=0, keepdims=True)
    inverse_scale = lax.rsqrt(variance + 1e-05)
    return centered * inverse_scale, inverse_scale


def project(w_ref, normed):
    projected = dot(w_ref[...], normed)
    h = projected.shape[0] // 4
    q_left, p_left, q_right, p_right = (projected[i * h : (i + 1) * h] for i in range(4))
    return q_left, jax.nn.sigmoid(p_left), q_right, jax.nn.sigmoid(p_right)


def put_lanes(ref, at, value):
    lanes = ref.shape[2]
    for i in range(ref.shape[0]):
        ref[i, at, :] = value[:, i * lanes : (i + 1) * lanes]


def get_lanes(ref, at):
    return jnp.concatenate([ref[i, at, :] for i in range(ref.shape[0])], axis=1)


def before_kernel(own, pair_ref, wl, wlg, wr, wrg, out_ref, gates_ref, normed_ref, w_ref, rows_ref):
    stack_weights((wl, wlg, wr, wrg), w_ref)
    h = wl.shape[0]
    rows = pair_ref.shape[0]

    def one_row(r, carry):
        normed = layer_norm(pair_ref[r])[0].astype(BF16)
        normed_ref[r] = normed
        projected = dot(w_ref[...], normed)
        for side in range(2):
            q = projected[2 * side * h : (2 * side + 1) * h]
            s = jax.nn.sigmoid(projected[(2 * side + 1) * h : (2 * side + 2) * h])
            value = s * q
            start = pl.multiple_of(r * 2 * h + side * h, h)
            put_lanes(rows_ref, pl.ds(start, h), value)
            gates_ref[r, pl.ds(2 * side * h, h), :] = s
            gates_ref[r, pl.ds((2 * side + 1) * h, h), :] = value * (1.0 - s)
        return carry

    lax.fori_loop(0, rows, one_row, 0, unroll=4)
    for channel in range(h):
        to, slot = channel // own, (channel % own) * 2
        for side in range(2):
            line = get_lanes(rows_ref, pl.ds(side * h + channel, rows, stride=2 * h))
            out_ref[to, slot + side] = line.astype(BF16)


def triangle_kernel(rows, cols, cot_ref, in_ref, out_ref, g_ref, l_ref, r_ref):
    r, c = in_ref.shape[2:]
    for a in range(rows):
        for b in range(cols):
            at = (pl.ds(a * r, r), pl.ds(b * c, c))
            g_ref[at] = cot_ref[a * cols + b, 0]
            l_ref[at] = in_ref[a * cols + b, 0]
            r_ref[at] = in_ref[a * cols + b, 1]
    for i, (dims, ref) in enumerate(((NN, r_ref), (TN, l_ref))):
        d = dot(g_ref[...], ref[...], dims).astype(BF16)
        for a in range(rows):
            for b in range(cols):
                out_ref[a * cols + b, i] = d[a * r : (a + 1) * r, b * c : (b + 1) * c]


def gates_kernel(own, bit_ref, d_ref, gates_ref, normed_ref, grads_ref, kept_ref, sent_ref, sums_ref, rows_ref):
    rows, h = gates_ref.shape[0], gates_ref.shape[1] // 4

    @pl.when(pl.program_id(0) == 0)
    def _():
        sums_ref[...] = jnp.zeros_like(sums_ref)

    for channel in range(h):
        to, slot = channel // own, (channel % own) * 2
        for side in range(2):
            line = d_ref[to, slot + side].astype(F32)
            put_lanes(rows_ref, pl.ds(side * h + channel, rows, stride=2 * h), line)

    def one_row(r, carry):
        parts = []
        for side in range(2):
            d = get_lanes(rows_ref, pl.ds(pl.multiple_of(r * 2 * h + side * h, h), h))
            parts.append(d * gates_ref[r, pl.ds(2 * side * h, h), :])
            parts.append(d * gates_ref[r, pl.ds((2 * side + 1) * h, h), :])
        grads = jnp.concatenate(parts, axis=0).astype(BF16)
        grads_ref[r] = grads
        sums_ref[...] += dot(grads, normed_ref[r], NT)
        return carry

    lax.fori_loop(0, rows, one_row, 0, unroll=4)

    @pl.when(pl.program_id(0) == pl.num_programs(0) - 1)
    def _():
        bit = bit_ref[0]
        kept_ref[...] = sums_ref[pl.ds(pl.multiple_of(bit * 2 * h, 2 * h), 2 * h), :]
        sent_ref[...] = sums_ref[pl.ds(pl.multiple_of((1 - bit) * 2 * h, 2 * h), 2 * h), :]


def input_kernel(pair_ref, grads_ref, wl, wlg, wr, wrg, *refs):
    out_ref, back_ref = refs[-2:]
    h = wl.shape[0]
    for i, ref in enumerate((wl, wlg, wr, wrg)):
        back_ref[:, pl.ds(i * h, h)] = ref[...].T

    def one_row(r, carry):
        standardized, inverse_scale = layer_norm(pair_ref[r])
        d_normed = dot(back_ref[...], grads_ref[r])
        mean = jnp.mean(d_normed, axis=0, keepdims=True)
        input_mean = jnp.mean(d_normed * standardized, axis=0, keepdims=True)
        moved = (d_normed - mean - standardized * input_mean) * inverse_scale
        out_ref[r] = moved.astype(BF16).T
        return carry

    lax.fori_loop(0, pair_ref.shape[0], one_row, 0, unroll=4)


def finish_kernel(scale, bit_ref, mine_ref, other_ref, *out_refs):
    h = out_refs[0].shape[0]
    for i, out_ref in enumerate(out_refs):
        at = pl.ds(i % 2 * h, h)
        mine = bit_ref[0] == i // 2
        out_ref[...] = jnp.where(mine, mine_ref[at, :], other_ref[at, :]) * scale


def channel_shards(sizes, pair, cotangent, *weights):
    rows, cols = sizes
    devices = rows * cols
    hidden, r, c = cotangent.shape
    dim = pair.shape[2]
    own = hidden // devices
    block = 16 if r % 16 == 0 else r
    pieces = 4 if r % 4 == 0 else 1
    weights = [w.T for w in weights]
    whole = pl.BlockSpec((hidden, dim), lambda i: (0, 0))
    tile = pl.BlockSpec((block, c, dim), lambda i: (i, 0, 0))
    exchange = functools.partial(
        lax.all_to_all, axis_name=("row", "col"), split_axis=0, concat_axis=0, tiled=True
    )
    stacked = pltpu.VMEM((4 * hidden, dim), BF16)
    lanes = min(c, 128)
    rows_scratch = pltpu.VMEM((c // lanes, 2 * hidden * block, lanes), F32)

    def cost(flops, *arrays):
        moved = sum(a.size * a.dtype.itemsize for a in arrays)
        return pl.CostEstimate(flops=flops, bytes_accessed=moved, transcendentals=0)

    def memory(mib):
        return pltpu.CompilerParams(vmem_limit_bytes=mib * 2**20)

    columns = r * c
    lr_shape = jax.ShapeDtypeStruct((devices, 2 * own, r, c), BF16)
    gates_shape = jax.ShapeDtypeStruct((r, 4 * hidden, c), F32)
    normed_shape = jax.ShapeDtypeStruct((r, dim, c), BF16)
    by_hidden = pl.BlockSpec((block, 4 * hidden, c), lambda i: (i, 0, 0))
    by_dim = pl.BlockSpec((block, dim, c), lambda i: (i, 0, 0))
    g_all = exchange(cotangent.reshape(devices, own, r, c))
    sent, gates, normed = pl.pallas_call(
        functools.partial(before_kernel, own),
        grid=(r // block,),
        in_specs=[tile] + [whole] * 4,
        out_specs=[
            pl.BlockSpec((devices, 2 * own, block, c), lambda i: (0, 0, i, 0)),
            by_hidden,
            by_dim,
        ],
        out_shape=[lr_shape, gates_shape, normed_shape],
        scratch_shapes=[stacked, rows_scratch],
        compiler_params=memory(20),
        cost_estimate=cost(8 * hidden * dim * columns, pair, lr_shape, gates_shape),
        name="before",
    )(pair, *weights)

    n_i, n_k = rows * r, cols * c
    sent = pl.pallas_call(
        functools.partial(triangle_kernel, rows, cols),
        grid=(own,),
        in_specs=[
            pl.BlockSpec((devices, 1, r, c), lambda i: (0, i, 0, 0)),
            pl.BlockSpec((devices, 2, r, c), lambda i: (0, i, 0, 0)),
        ],
        out_specs=pl.BlockSpec((devices, 2, r, c), lambda i: (0, i, 0, 0)),
        out_shape=lr_shape,
        scratch_shapes=[pltpu.VMEM((n_i, n_k), BF16)] * 3,
        compiler_params=memory(32),
        name="triangle",
    )(g_all, exchange(sent))

    bit = (lax.axis_index("row") % 2).astype(jnp.int32).reshape(1)
    smem = pl.BlockSpec(memory_space=pltpu.SMEM)
    half_shape = jax.ShapeDtypeStruct((2 * hidden, dim), F32)
    half = pl.BlockSpec(half_shape.shape, lambda i: (0, 0))
    grads, kept, given = pl.pallas_call(
        functools.partial(gates_kernel, own),
        grid=(r // block,),
        in_specs=[
            smem,
            pl.BlockSpec((devices, 2 * own, block, c), lambda i: (0, 0, i, 0)),
            by_hidden,
            by_dim,
        ],
        out_specs=[by_hidden, half, half],
        out_shape=[jax.ShapeDtypeStruct((r, 4 * hidden, c), BF16), half_shape, half_shape],
        scratch_shapes=[pltpu.VMEM((4 * hidden, dim), F32), rows_scratch],
        compiler_params=memory(22),
        name="gates",
    )(bit, exchange(sent), gates, normed)

    def input_piece(piece, pair_gradient):
        held = [] if pair_gradient is None else [pair_gradient]
        at = pl.BlockSpec((r // pieces, c, dim), lambda i: (piece, 0, 0))
        return pl.pallas_call(
            input_kernel,
            grid=(1,),
            in_specs=[at, pl.BlockSpec((r // pieces, 4 * hidden, c), lambda i: (piece, 0, 0))]
            + [whole] * 4
            + [pl.BlockSpec(memory_space=pl.ANY)] * len(held),
            out_specs=at,
            out_shape=jax.ShapeDtypeStruct(pair.shape, BF16),
            scratch_shapes=[pltpu.VMEM((dim, 4 * hidden), BF16)],
            input_output_aliases={6: 0} if held else {},
            compiler_params=memory(16),
            cost_estimate=cost(8 * hidden * dim * columns // pieces, pair),
            name="input",
        )(pair, grads, *weights, *held)

    steps = [("row", rows, 1 << i) for i in range(1, rows.bit_length() - 1)][::-1]
    steps += [("col", cols, 1 << i) for i in range(cols.bit_length() - 1)]
    neighbours = [(i, i ^ 1) for i in range(rows)]
    pair_gradient = None
    mine = kept + lax.ppermute(given, "row", neighbours)
    for n, (axis, size, step) in enumerate(steps):
        other = lax.ppermute(mine, axis, [(i, i ^ step) for i in range(size)])
        for piece in range(n * pieces // len(steps), (n + 1) * pieces // len(steps)):
            pair_gradient = input_piece(piece, pair_gradient)
        if pair_gradient is not None:
            other, pair_gradient = lax.optimization_barrier((other, pair_gradient))
        mine = mine + other
    weight_grads = pl.pallas_call(
        functools.partial(finish_kernel, 1.0 / n_i),
        in_specs=[smem, pl.BlockSpec(memory_space=pltpu.VMEM), pl.BlockSpec(memory_space=pltpu.VMEM)],
        out_shape=[jax.ShapeDtypeStruct((hidden, dim), F32)] * 4,
        name="finish",
    )(bit, mine, lax.ppermute(mine, "row", neighbours))
    return (pair_gradient, *(g.T for g in weight_grads))


def solution(mesh):
    in_specs = (P("row", "col", None), P(None, "row", "col"), P(), P(), P(), P())
    out_specs = (P("row", "col", None), P(), P(), P(), P())
    sizes = (mesh.shape["row"], mesh.shape["col"])

    def shards(pair, cotangent, *weights):
        plain = all(size > 1 and size & (size - 1) == 0 for size in sizes)
        if plain and cotangent.shape[0] % (sizes[0] * sizes[1]) == 0:
            return channel_shards(sizes, pair, cotangent, *weights)
        return gathered_shards(pair, cotangent, *weights)

    return jax.shard_map(shards, mesh=mesh, in_specs=in_specs, out_specs=out_specs, check_vma=False)
```

```python
import functools

import jax
import jax.numpy as jnp
from jax import lax
from jax.experimental import pallas as pl
from jax.experimental.pallas import tpu as pltpu
from jax.sharding import PartitionSpec as P

BF16, F32 = jnp.bfloat16, jnp.float32


def gathered_shards(pair, cotangent, w_left, w_left_gate, w_right, w_right_gate):
    pair_f = pair.astype(jnp.float32)
    average = jnp.mean(pair_f, axis=-1, keepdims=True)
    centered_input = pair_f - average
    variance = jnp.mean(centered_input * centered_input, axis=-1, keepdims=True)
    inverse_scale = 1.0 / jnp.sqrt(variance + 1e-05)
    standardized_input = centered_input * inverse_scale
    normalized_input = standardized_input.astype(jnp.bfloat16)
    stacked = jnp.concatenate([w_left, w_left_gate, w_right, w_right_gate], axis=1)
    projected = jnp.einsum(
        "rcd,dh->hrc", normalized_input, stacked, preferred_element_type=jnp.float32
    )
    q_left, p_left, q_right, p_right = jnp.split(projected, 4, axis=0)
    s_left = jax.nn.sigmoid(p_left)
    s_right = jax.nn.sigmoid(p_right)
    left = (s_left * q_left).astype(jnp.bfloat16)
    right = (s_right * q_right).astype(jnp.bfloat16)
    g_chan, left_chan, right_chan = (
        lax.all_to_all(cotangent, "col", split_axis=0, concat_axis=2, tiled=True),
        lax.all_to_all(left, "col", split_axis=0, concat_axis=2, tiled=True),
        lax.all_to_all(right, "col", split_axis=0, concat_axis=2, tiled=True),
    )
    residues = g_chan.shape[2]
    g_columns = lax.all_to_all(g_chan, "row", split_axis=2, concat_axis=1, tiled=True)
    d_left = jnp.einsum(
        "hij,hjk->hik",
        g_chan,
        lax.all_gather(right_chan, "row", axis=1, tiled=True),
        preferred_element_type=jnp.float32,
    )
    d_right = jnp.einsum(
        "hij,hik->hjk",
        g_columns,
        lax.all_gather(left_chan, "row", axis=1, tiled=True),
        preferred_element_type=jnp.float32,
    )
    d_left_tile, d_right_tile = (
        lax.all_to_all(d_left.astype(jnp.bfloat16), "col", split_axis=2, concat_axis=0, tiled=True),
        lax.all_to_all(
            d_right.astype(jnp.bfloat16), "col", split_axis=2, concat_axis=0, tiled=True
        ),
    )
    grad_l = d_left_tile.astype(jnp.float32)
    grad_r = d_right_tile.astype(jnp.float32)
    e_left = grad_l * s_left
    f_left = grad_l * q_left * s_left * (1.0 - s_left)
    e_right = grad_r * s_right
    f_right = grad_r * q_right * s_right * (1.0 - s_right)
    grads = jnp.concatenate([e_left, f_left, e_right, f_right], axis=0).astype(jnp.bfloat16)
    local_weights = jnp.einsum(
        "rcd,hrc->dh", normalized_input, grads, preferred_element_type=jnp.float32
    )
    total_weights = lax.psum(local_weights, ("row", "col")) / residues
    normalized_gradient = jnp.einsum(
        "hrc,dh->rcd", grads, stacked, preferred_element_type=jnp.float32
    )
    gradient_mean = jnp.mean(normalized_gradient, axis=-1, keepdims=True)
    gradient_input_mean = jnp.mean(normalized_gradient * standardized_input, axis=-1, keepdims=True)
    pair_gradient = (
        (normalized_gradient - gradient_mean - standardized_input * gradient_input_mean)
        * inverse_scale
    ).astype(jnp.bfloat16)
    pieces_w = jnp.split(total_weights, 4, axis=1)
    return (pair_gradient, pieces_w[0], pieces_w[1], pieces_w[2], pieces_w[3])


NT = (((1,), (1,)), ((), ()))
TN = (((0,), (0,)), ((), ()))
NN = (((1,), (0,)), ((), ()))


def dot(a, b, dims=NN):
    return lax.dot_general(a, b, dims, preferred_element_type=F32)


def stack_weights(w_refs, w_ref):
    h = w_refs[0].shape[0]
    for i, ref in enumerate(w_refs):
        w_ref[pl.ds(i * h, h), :] = ref[...]


def layer_norm(x):
    x = x.T.astype(F32)
    centered = x - jnp.mean(x, axis=0, keepdims=True)
    variance = jnp.mean(centered * centered, axis=0, keepdims=True)
    inverse_scale = lax.rsqrt(variance + 1e-05)
    return centered * inverse_scale, inverse_scale


def project(w_ref, normed):
    projected = dot(w_ref[...], normed)
    h = projected.shape[0] // 4
    q_left, p_left, q_right, p_right = (projected[i * h : (i + 1) * h] for i in range(4))
    return q_left, jax.nn.sigmoid(p_left), q_right, jax.nn.sigmoid(p_right)


def put_lanes(ref, at, value):
    lanes = ref.shape[2]
    for i in range(ref.shape[0]):
        ref[i, at, :] = value[:, i * lanes : (i + 1) * lanes]


def get_lanes(ref, at):
    return jnp.concatenate([ref[i, at, :] for i in range(ref.shape[0])], axis=1)


def before_kernel(own, pair_ref, wl, wlg, wr, wrg, out_ref, w_ref, rows_ref):
    stack_weights((wl, wlg, wr, wrg), w_ref)
    h = wl.shape[0]
    rows = pair_ref.shape[0]
    pitch = rows + 1

    def one_row(r, carry):
        normed = layer_norm(pair_ref[r])[0].astype(BF16)
        q_left, s_left, q_right, s_right = project(w_ref, normed)
        put_lanes(rows_ref, pl.ds(r, h, stride=pitch), s_left * q_left)
        put_lanes(rows_ref, pl.ds(r + h * pitch, h, stride=pitch), s_right * q_right)
        return carry

    lax.fori_loop(0, rows, one_row, 0, unroll=4)
    for channel in range(h):
        to, slot = channel // own, (channel % own) * 2
        for side in range(2):
            line = get_lanes(rows_ref, pl.ds((side * h + channel) * pitch, rows))
            out_ref[to, slot + side] = line.astype(BF16)


def triangle_kernel(rows, cols, cot_ref, in_ref, out_ref, g_ref, l_ref, r_ref):
    r, c = in_ref.shape[2:]
    for a in range(rows):
        for b in range(cols):
            at = (pl.ds(a * r, r), pl.ds(b * c, c))
            g_ref[at] = cot_ref[a * cols + b, 0]
            l_ref[at] = in_ref[a * cols + b, 0]
            r_ref[at] = in_ref[a * cols + b, 1]
    for i, (dims, ref) in enumerate(((NN, r_ref), (TN, l_ref))):
        d = dot(g_ref[...], ref[...], dims).astype(BF16)
        for a in range(rows):
            for b in range(cols):
                out_ref[a * cols + b, i] = d[a * r : (a + 1) * r, b * c : (b + 1) * c]


def gates_kernel(own, bit_ref, pair_ref, d_ref, wl, wlg, wr, wrg, grads_ref, kept_ref, sent_ref, w_ref, sums_ref, rows_ref):
    stack_weights((wl, wlg, wr, wrg), w_ref)
    h = wl.shape[0]
    rows = pair_ref.shape[0]
    pitch = rows + 1

    @pl.when(pl.program_id(0) == 0)
    def _():
        sums_ref[...] = jnp.zeros_like(sums_ref)

    for channel in range(h):
        to, slot = channel // own, (channel % own) * 2
        for side in range(2):
            line = d_ref[to, slot + side].astype(F32)
            put_lanes(rows_ref, pl.ds((side * h + channel) * pitch, rows), line)

    def one_row(r, carry):
        normed = layer_norm(pair_ref[r])[0].astype(BF16)
        q_left, s_left, q_right, s_right = project(w_ref, normed)
        e_left = get_lanes(rows_ref, pl.ds(r, h, stride=pitch)) * s_left
        e_right = get_lanes(rows_ref, pl.ds(r + h * pitch, h, stride=pitch)) * s_right
        f_left = e_left * q_left * (1.0 - s_left)
        f_right = e_right * q_right * (1.0 - s_right)
        grads = jnp.concatenate([e_left, f_left, e_right, f_right], axis=0).astype(BF16)
        grads_ref[r] = grads
        sums_ref[...] += dot(grads, normed, NT)
        return carry

    lax.fori_loop(0, rows, one_row, 0, unroll=4)

    @pl.when(pl.program_id(0) == pl.num_programs(0) - 1)
    def _():
        bit = bit_ref[0]
        kept_ref[...] = sums_ref[pl.ds(pl.multiple_of(bit * 2 * h, 2 * h), 2 * h), :]
        sent_ref[...] = sums_ref[pl.ds(pl.multiple_of((1 - bit) * 2 * h, 2 * h), 2 * h), :]


def input_kernel(pair_ref, grads_ref, wl, wlg, wr, wrg, *refs):
    out_ref, back_ref = refs[-2:]
    h = wl.shape[0]
    for i, ref in enumerate((wl, wlg, wr, wrg)):
        back_ref[:, pl.ds(i * h, h)] = ref[...].T

    def one_row(r, carry):
        standardized, inverse_scale = layer_norm(pair_ref[r])
        d_normed = dot(back_ref[...], grads_ref[r])
        mean = jnp.mean(d_normed, axis=0, keepdims=True)
        input_mean = jnp.mean(d_normed * standardized, axis=0, keepdims=True)
        moved = (d_normed - mean - standardized * input_mean) * inverse_scale
        out_ref[r] = moved.astype(BF16).T
        return carry

    lax.fori_loop(0, pair_ref.shape[0], one_row, 0, unroll=4)


def finish_kernel(scale, bit_ref, mine_ref, other_ref, *out_refs):
    h = out_refs[0].shape[0]
    for i, out_ref in enumerate(out_refs):
        at = pl.ds(i % 2 * h, h)
        mine = bit_ref[0] == i // 2
        out_ref[...] = jnp.where(mine, mine_ref[at, :], other_ref[at, :]) * scale


def channel_shards(sizes, pair, cotangent, *weights):
    rows, cols = sizes
    devices = rows * cols
    hidden, r, c = cotangent.shape
    dim = pair.shape[2]
    own = hidden // devices
    block = 16 if r % 16 == 0 else r
    pieces = 4 if r % 4 == 0 else 1
    weights = [w.T for w in weights]
    whole = pl.BlockSpec((hidden, dim), lambda i: (0, 0))
    tile = pl.BlockSpec((block, c, dim), lambda i: (i, 0, 0))
    exchange = functools.partial(
        lax.all_to_all, axis_name=("row", "col"), split_axis=0, concat_axis=0, tiled=True
    )
    stacked = pltpu.VMEM((4 * hidden, dim), BF16)
    lanes = min(c, 128)
    rows_scratch = pltpu.VMEM((c // lanes, 2 * hidden * (block + 1), lanes), F32)

    def cost(flops, *arrays):
        moved = sum(a.size * a.dtype.itemsize for a in arrays)
        return pl.CostEstimate(flops=flops, bytes_accessed=moved, transcendentals=0)

    def memory(mib):
        return pltpu.CompilerParams(vmem_limit_bytes=mib * 2**20)

    columns = r * c
    lr_shape = jax.ShapeDtypeStruct((devices, 2 * own, r, c), BF16)
    by_hidden = pl.BlockSpec((block, 4 * hidden, c), lambda i: (i, 0, 0))
    g_all = exchange(cotangent.reshape(devices, own, r, c))
    sent = pl.pallas_call(
        functools.partial(before_kernel, own),
        grid=(r // block,),
        in_specs=[tile] + [whole] * 4,
        out_specs=pl.BlockSpec((devices, 2 * own, block, c), lambda i: (0, 0, i, 0)),
        out_shape=lr_shape,
        scratch_shapes=[stacked, rows_scratch],
        compiler_params=memory(60),
        cost_estimate=cost(8 * hidden * dim * columns, pair, lr_shape),
        name="before",
    )(pair, *weights)

    n_i, n_k = rows * r, cols * c
    sent = pl.pallas_call(
        functools.partial(triangle_kernel, rows, cols),
        grid=(own,),
        in_specs=[
            pl.BlockSpec((devices, 1, r, c), lambda i: (0, i, 0, 0)),
            pl.BlockSpec((devices, 2, r, c), lambda i: (0, i, 0, 0)),
        ],
        out_specs=pl.BlockSpec((devices, 2, r, c), lambda i: (0, i, 0, 0)),
        out_shape=lr_shape,
        scratch_shapes=[pltpu.VMEM((n_i, n_k), BF16)] * 3,
        compiler_params=memory(32),
        name="triangle",
    )(g_all, exchange(sent))

    bit = (lax.axis_index("row") % 2).astype(jnp.int32).reshape(1)
    smem = pl.BlockSpec(memory_space=pltpu.SMEM)
    half_shape = jax.ShapeDtypeStruct((2 * hidden, dim), F32)
    half = pl.BlockSpec(half_shape.shape, lambda i: (0, 0))
    grads, kept, given = pl.pallas_call(
        functools.partial(gates_kernel, own),
        grid=(r // block,),
        in_specs=[
            smem,
            tile,
            pl.BlockSpec((devices, 2 * own, block, c), lambda i: (0, 0, i, 0)),
        ]
        + [whole] * 4,
        out_specs=[by_hidden, half, half],
        out_shape=[jax.ShapeDtypeStruct((r, 4 * hidden, c), BF16), half_shape, half_shape],
        scratch_shapes=[stacked, pltpu.VMEM((4 * hidden, dim), F32), rows_scratch],
        compiler_params=memory(28),
        name="gates",
    )(bit, pair, exchange(sent), *weights)

    def input_piece(piece, pair_gradient):
        held = [] if pair_gradient is None else [pair_gradient]
        at = pl.BlockSpec((r // pieces, c, dim), lambda i: (piece, 0, 0))
        return pl.pallas_call(
            input_kernel,
            grid=(1,),
            in_specs=[at, pl.BlockSpec((r // pieces, 4 * hidden, c), lambda i: (piece, 0, 0))]
            + [whole] * 4
            + [pl.BlockSpec(memory_space=pl.ANY)] * len(held),
            out_specs=at,
            out_shape=jax.ShapeDtypeStruct(pair.shape, BF16),
            scratch_shapes=[pltpu.VMEM((dim, 4 * hidden), BF16)],
            input_output_aliases={6: 0} if held else {},
            compiler_params=memory(16),
            cost_estimate=cost(8 * hidden * dim * columns // pieces, pair),
            name="input",
        )(pair, grads, *weights, *held)

    steps = [("row", rows, 1 << i) for i in range(1, rows.bit_length() - 1)][::-1]
    steps += [("col", cols, 1 << i) for i in range(cols.bit_length() - 1)]
    neighbours = [(i, i ^ 1) for i in range(rows)]
    pair_gradient = None
    mine = kept + lax.ppermute(given, "row", neighbours)
    for n, (axis, size, step) in enumerate(steps):
        other = lax.ppermute(mine, axis, [(i, i ^ step) for i in range(size)])
        for piece in range(n * pieces // len(steps), (n + 1) * pieces // len(steps)):
            pair_gradient = input_piece(piece, pair_gradient)
        if pair_gradient is not None:
            other, pair_gradient = lax.optimization_barrier((other, pair_gradient))
        mine = mine + other
    weight_grads = pl.pallas_call(
        functools.partial(finish_kernel, 1.0 / n_i),
        in_specs=[smem, pl.BlockSpec(memory_space=pltpu.VMEM), pl.BlockSpec(memory_space=pltpu.VMEM)],
        out_shape=[jax.ShapeDtypeStruct((hidden, dim), F32)] * 4,
        name="finish",
    )(bit, mine, lax.ppermute(mine, "row", neighbours))
    return (pair_gradient, *(g.T for g in weight_grads))


def solution(mesh):
    in_specs = (P("row", "col", None), P(None, "row", "col"), P(), P(), P(), P())
    out_specs = (P("row", "col", None), P(), P(), P(), P())
    sizes = (mesh.shape["row"], mesh.shape["col"])

    def shards(pair, cotangent, *weights):
        plain = all(size > 1 and size & (size - 1) == 0 for size in sizes)
        if plain and cotangent.shape[0] % (sizes[0] * sizes[1]) == 0:
            return channel_shards(sizes, pair, cotangent, *weights)
        return gathered_shards(pair, cotangent, *weights)

    return jax.shard_map(shards, mesh=mesh, in_specs=in_specs, out_specs=out_specs, check_vma=False)
```

```python
import functools

import jax
import jax.numpy as jnp
from jax import lax
from jax.experimental import pallas as pl
from jax.experimental.pallas import tpu as pltpu
from jax.sharding import PartitionSpec as P

BF16, F32 = jnp.bfloat16, jnp.float32


def gathered_shards(pair, cotangent, w_left, w_left_gate, w_right, w_right_gate):
    pair_f = pair.astype(jnp.float32)
    average = jnp.mean(pair_f, axis=-1, keepdims=True)
    centered_input = pair_f - average
    variance = jnp.mean(centered_input * centered_input, axis=-1, keepdims=True)
    inverse_scale = 1.0 / jnp.sqrt(variance + 1e-05)
    standardized_input = centered_input * inverse_scale
    normalized_input = standardized_input.astype(jnp.bfloat16)
    stacked = jnp.concatenate([w_left, w_left_gate, w_right, w_right_gate], axis=1)
    projected = jnp.einsum(
        "rcd,dh->hrc", normalized_input, stacked, preferred_element_type=jnp.float32
    )
    q_left, p_left, q_right, p_right = jnp.split(projected, 4, axis=0)
    s_left = jax.nn.sigmoid(p_left)
    s_right = jax.nn.sigmoid(p_right)
    left = (s_left * q_left).astype(jnp.bfloat16)
    right = (s_right * q_right).astype(jnp.bfloat16)
    g_chan, left_chan, right_chan = (
        lax.all_to_all(cotangent, "col", split_axis=0, concat_axis=2, tiled=True),
        lax.all_to_all(left, "col", split_axis=0, concat_axis=2, tiled=True),
        lax.all_to_all(right, "col", split_axis=0, concat_axis=2, tiled=True),
    )
    residues = g_chan.shape[2]
    g_columns = lax.all_to_all(g_chan, "row", split_axis=2, concat_axis=1, tiled=True)
    d_left = jnp.einsum(
        "hij,hjk->hik",
        g_chan,
        lax.all_gather(right_chan, "row", axis=1, tiled=True),
        preferred_element_type=jnp.float32,
    )
    d_right = jnp.einsum(
        "hij,hik->hjk",
        g_columns,
        lax.all_gather(left_chan, "row", axis=1, tiled=True),
        preferred_element_type=jnp.float32,
    )
    d_left_tile, d_right_tile = (
        lax.all_to_all(d_left.astype(jnp.bfloat16), "col", split_axis=2, concat_axis=0, tiled=True),
        lax.all_to_all(
            d_right.astype(jnp.bfloat16), "col", split_axis=2, concat_axis=0, tiled=True
        ),
    )
    grad_l = d_left_tile.astype(jnp.float32)
    grad_r = d_right_tile.astype(jnp.float32)
    e_left = grad_l * s_left
    f_left = grad_l * q_left * s_left * (1.0 - s_left)
    e_right = grad_r * s_right
    f_right = grad_r * q_right * s_right * (1.0 - s_right)
    grads = jnp.concatenate([e_left, f_left, e_right, f_right], axis=0).astype(jnp.bfloat16)
    local_weights = jnp.einsum(
        "rcd,hrc->dh", normalized_input, grads, preferred_element_type=jnp.float32
    )
    total_weights = lax.psum(local_weights, ("row", "col")) / residues
    normalized_gradient = jnp.einsum(
        "hrc,dh->rcd", grads, stacked, preferred_element_type=jnp.float32
    )
    gradient_mean = jnp.mean(normalized_gradient, axis=-1, keepdims=True)
    gradient_input_mean = jnp.mean(normalized_gradient * standardized_input, axis=-1, keepdims=True)
    pair_gradient = (
        (normalized_gradient - gradient_mean - standardized_input * gradient_input_mean)
        * inverse_scale
    ).astype(jnp.bfloat16)
    pieces_w = jnp.split(total_weights, 4, axis=1)
    return (pair_gradient, pieces_w[0], pieces_w[1], pieces_w[2], pieces_w[3])


NT = (((1,), (1,)), ((), ()))
TN = (((0,), (0,)), ((), ()))
NN = (((1,), (0,)), ((), ()))


def dot(a, b, dims=NN):
    return lax.dot_general(a, b, dims, preferred_element_type=F32)


def stack_weights(w_refs, w_ref):
    h = w_refs[0].shape[0]
    for i, ref in enumerate(w_refs):
        w_ref[pl.ds(i * h, h), :] = ref[...]


def layer_norm(x):
    x = x.T.astype(F32)
    centered = x - jnp.mean(x, axis=0, keepdims=True)
    variance = jnp.mean(centered * centered, axis=0, keepdims=True)
    inverse_scale = lax.rsqrt(variance + 1e-05)
    return centered * inverse_scale, inverse_scale


def put_lanes(ref, at, value):
    lanes = ref.shape[2]
    for i in range(ref.shape[0]):
        ref[i, at, :] = value[:, i * lanes : (i + 1) * lanes]


def get_lanes(ref, at):
    return jnp.concatenate([ref[i, at, :] for i in range(ref.shape[0])], axis=1)


def before_kernel(own, first, x_ref, wq, wg, *refs):
    if first:
        out_ref, normed_ref, w_ref, rows_ref = refs
    else:
        out_ref, w_ref, rows_ref = refs
    stack_weights((wq, wg), w_ref)
    h = wq.shape[0]
    rows = x_ref.shape[0]
    pitch = rows + 1

    def one_row(r, carry):
        if first:
            normed = layer_norm(x_ref[r])[0].astype(BF16)
            normed_ref[r] = normed
        else:
            normed = x_ref[r]
        projected = dot(w_ref[...], normed)
        value = jax.nn.sigmoid(projected[h:]) * projected[:h]
        put_lanes(rows_ref, pl.ds(r, h, stride=pitch), value)
        return carry

    lax.fori_loop(0, rows, one_row, 0, unroll=4)
    for channel in range(h):
        line = get_lanes(rows_ref, pl.ds(channel * pitch, rows))
        out_ref[channel // own, channel % own] = line.astype(BF16)


def from_blocks(blocks_ref, whole_ref, start, cols):
    n, _, r, c = blocks_ref.shape
    for i in range(n):
        at = pl.ds(pl.multiple_of(start + i // cols * r, r), r)
        whole_ref[at, pl.ds(i % cols * c, c)] = blocks_ref[i, 0]


def left_kernel(cols, half_ref, cot_ref, mine_ref, other_ref, out_ref, g_ref, x_ref):
    n = g_ref.shape[0]
    r, c = out_ref.shape[2:]
    from_blocks(cot_ref, g_ref, 0, cols)
    from_blocks(mine_ref, x_ref, half_ref[0] * n, cols)
    from_blocks(other_ref, x_ref, (1 - half_ref[0]) * n, cols)
    d = dot(g_ref[...], x_ref[...]).astype(BF16)
    for i in range(out_ref.shape[0]):
        a, b = i // cols * r, i % cols * c
        out_ref[i, 0] = d[a : a + r, b : b + c]


def right_kernel(cols, half_ref, cot_ref, in_ref, keep_ref, send_ref, g_ref, x_ref, d_ref):
    n = g_ref.shape[0]
    r, c = in_ref.shape[2:]
    from_blocks(cot_ref, g_ref, 0, cols)
    from_blocks(in_ref, x_ref, 0, cols)
    d_ref[...] = dot(g_ref[...], x_ref[...], TN)
    for half, out_ref in ((half_ref[0], keep_ref), (1 - half_ref[0], send_ref)):
        for i in range(out_ref.shape[0]):
            at = pl.ds(pl.multiple_of(half * n + i // cols * r, r), r)
            out_ref[i, 0] = d_ref[at, pl.ds(i % cols * c, c)].astype(out_ref.dtype)


def gates_kernel(d_count, *refs):
    if len(refs) > d_count + 7:
        bit_ref, left_sums_ref, *refs = refs
        normed_ref, *d_refs, wq, wg, grads_ref, kept_ref, sent_ref, w_ref, rows_ref, sums_ref = refs
    else:
        bit_ref = None
        normed_ref, *d_refs, wq, wg, grads_ref, sums_ref, w_ref, rows_ref = refs
    stack_weights((wq, wg), w_ref)
    h = wq.shape[0]
    rows = normed_ref.shape[0]
    pitch = rows + 1

    @pl.when(pl.program_id(0) == 0)
    def _():
        sums_ref[...] = jnp.zeros_like(sums_ref)

    part = d_refs[0].shape[1]
    for channel in range(h):
        to, slot = channel // (part * d_count), channel % (part * d_count)
        line = d_refs[slot // part][to, slot % part].astype(F32)
        put_lanes(rows_ref, pl.ds(channel * pitch, rows), line)

    def one_row(r, carry):
        normed = normed_ref[r]
        projected = dot(w_ref[...], normed)
        q, s = projected[:h], jax.nn.sigmoid(projected[h:])
        e = get_lanes(rows_ref, pl.ds(r, h, stride=pitch)) * s
        f = e * q * (1.0 - s)
        grads = jnp.concatenate([e, f], axis=0).astype(BF16)
        grads_ref[r] = grads
        sums_ref[...] += dot(grads, normed, NT)
        return carry

    lax.fori_loop(0, rows, one_row, 0, unroll=4)

    if bit_ref is not None:

        @pl.when(pl.program_id(0) == pl.num_programs(0) - 1)
        def _():
            for bit, first, second in ((0, left_sums_ref, sums_ref), (1, sums_ref, left_sums_ref)):

                @pl.when(bit_ref[0] == bit)
                def _(first=first, second=second):
                    kept_ref[...] = first[...]
                    sent_ref[...] = second[...]


def input_kernel(pair_ref, left_ref, right_ref, wl, wlg, wr, wrg, *refs):
    out_ref, back_ref = refs[-2:]
    h = wl.shape[0]
    for i, ref in enumerate((wl, wlg, wr, wrg)):
        back_ref[:, pl.ds(i * h, h)] = ref[...].T

    def one_row(r, carry):
        standardized, inverse_scale = layer_norm(pair_ref[r])
        grads = jnp.concatenate([left_ref[r], right_ref[r]], axis=0)
        d_normed = dot(back_ref[...], grads)
        mean = jnp.mean(d_normed, axis=0, keepdims=True)
        input_mean = jnp.mean(d_normed * standardized, axis=0, keepdims=True)
        moved = (d_normed - mean - standardized * input_mean) * inverse_scale
        out_ref[r] = moved.astype(BF16).T
        return carry

    lax.fori_loop(0, pair_ref.shape[0], one_row, 0, unroll=4)


def finish_kernel(scale, bit_ref, mine_ref, other_ref, *out_refs):
    h = out_refs[0].shape[0]
    for i, out_ref in enumerate(out_refs):
        at = pl.ds(i % 2 * h, h)
        mine = bit_ref[0] == i // 2
        out_ref[...] = jnp.where(mine, mine_ref[at, :], other_ref[at, :]) * scale


def halves_shards(sizes, pair, cotangent, *weights):
    rows, cols = sizes
    half_rows = rows // 2
    members = half_rows * cols
    hidden, r, c = cotangent.shape
    dim = pair.shape[2]
    own = hidden // members
    block = 16 if r % 16 == 0 else r
    lanes = min(c, 128)
    chunks = 2 if own % 2 == 0 else 1
    pieces = 4 if r % 4 == 0 else 1
    n_half, n_k = half_rows * r, cols * c
    columns = r * c
    weights = [w.T for w in weights]
    whole = pl.BlockSpec((hidden, dim), lambda i: (0, 0))
    smem = pl.BlockSpec(memory_space=pltpu.SMEM)
    groups = [[half * members + i for i in range(members)] for half in range(2)]
    exchange = functools.partial(
        lax.all_to_all,
        axis_name=("row", "col"),
        split_axis=0,
        concat_axis=0,
        axis_index_groups=groups,
        tiled=True,
    )
    across = functools.partial(
        lax.ppermute, axis_name="row", perm=[(i, (i + half_rows) % rows) for i in range(rows)]
    )
    row = lax.axis_index("row").astype(jnp.int32)
    half = (row // half_rows).reshape(1)
    bit = (row % 2).reshape(1)

    def cost(flops, *arrays):
        moved = sum(a.size * a.dtype.itemsize for a in arrays)
        return pl.CostEstimate(flops=flops, bytes_accessed=moved, transcendentals=0)

    def memory(mib):
        return pltpu.CompilerParams(vmem_limit_bytes=mib * 2**20)

    blocks_shape = jax.ShapeDtypeStruct((members, own, r, c), BF16)
    normed_shape = jax.ShapeDtypeStruct((r, dim, c), BF16)
    by_rows = pl.BlockSpec((members, own, block, c), lambda i: (0, 0, i, 0))
    by_dim = pl.BlockSpec((block, dim, c), lambda i: (i, 0, 0))
    side_scratch = [
        pltpu.VMEM((2 * hidden, dim), BF16),
        pltpu.VMEM((c // lanes, hidden * (block + 1), lanes), F32),
    ]

    def before(first, x, *w):
        return pl.pallas_call(
            functools.partial(before_kernel, own, first),
            grid=(r // block,),
            in_specs=[
                pl.BlockSpec((block,) + x.shape[1:], lambda i: (i, 0, 0)),
                whole,
                whole,
            ],
            out_specs=[by_rows, by_dim][: 1 + first],
            out_shape=[blocks_shape, normed_shape][: 1 + first],
            scratch_shapes=side_scratch,
            compiler_params=memory(60),
            cost_estimate=cost(4 * hidden * dim * columns, pair, pair),
            name="before",
        )(x, *w)

    right, normed = before(True, pair, *weights[2:])
    (left,) = before(False, normed, *weights[:2])
    right_mine = exchange(right)
    cotangent, right_mine = lax.optimization_barrier((cotangent, right_mine))
    right_other = across(right_mine)
    g_all = exchange(cotangent.reshape(blocks_shape.shape))
    left_all = exchange(left)

    def by_channel(start):
        return pl.BlockSpec((members, 1, r, c), lambda i: (0, start + i, 0, 0))

    chunk = own // chunks
    kept, given = [], []
    for n in range(chunks):
        keep, send = pl.pallas_call(
            functools.partial(right_kernel, cols),
            grid=(chunk,),
            in_specs=[smem] + [by_channel(n * chunk)] * 2,
            out_specs=[by_channel(0)] * 2,
            out_shape=[
                jax.ShapeDtypeStruct((members, chunk, r, c), F32),
                jax.ShapeDtypeStruct((members, chunk, r, c), BF16),
            ],
            scratch_shapes=[pltpu.VMEM((n_half, n_k), BF16)] * 2
            + [pltpu.VMEM((2 * n_half, n_k), F32)],
            compiler_params=memory(24),
            cost_estimate=cost(4 * chunk * n_half * n_half * n_k, pair),
            name="right_sums",
        )(half, g_all, left_all)
        kept.append(keep)
        given.append(across(send))

    d_left = pl.pallas_call(
        functools.partial(left_kernel, cols),
        grid=(own,),
        in_specs=[smem] + [by_channel(0)] * 3,
        out_specs=by_channel(0),
        out_shape=blocks_shape,
        scratch_shapes=[
            pltpu.VMEM((n_half, n_k), BF16),
            pltpu.VMEM((2 * n_half, n_k), BF16),
        ],
        compiler_params=memory(24),
        cost_estimate=cost(4 * own * n_half * n_half * n_k, pair),
        name="left_sums",
    )(half, g_all, right_mine, right_other)
    d_left = exchange(d_left)
    d_right = [exchange((k + g.astype(F32)).astype(BF16)) for k, g in zip(kept, given)]

    sums_shape = jax.ShapeDtypeStruct((2 * hidden, dim), F32)
    sums = pl.BlockSpec(sums_shape.shape, lambda i: (0, 0))
    grads_shape = jax.ShapeDtypeStruct((r, 2 * hidden, c), BF16)
    by_hidden = pl.BlockSpec((block, 2 * hidden, c), lambda i: (i, 0, 0))

    def gates(d, w, *left_sums):
        last = len(left_sums) > 0
        return pl.pallas_call(
            functools.partial(gates_kernel, len(d)),
            grid=(r // block,),
            in_specs=([smem, sums] if last else [])
            + [by_dim]
            + [pl.BlockSpec((members, x.shape[1], block, c), lambda i: (0, 0, i, 0)) for x in d]
            + [whole] * 2,
            out_specs=[by_hidden, sums] + [sums] * last,
            out_shape=[grads_shape, sums_shape] + [sums_shape] * last,
            scratch_shapes=side_scratch + [pltpu.VMEM(sums_shape.shape, F32)] * last,
            compiler_params=memory(20),
            cost_estimate=cost(8 * hidden * dim * columns, pair, pair, pair),
            name="gates",
        )(*((bit,) + left_sums if last else ()), normed, *d, *w)

    grads_left, left_sums = gates([d_left], weights[:2])
    grads_right, kept, given = gates(d_right, weights[2:], left_sums)

    def input_piece(piece, pair_gradient):
        held = [] if pair_gradient is None else [pair_gradient]
        at = pl.BlockSpec((r // pieces, c, dim), lambda i: (piece, 0, 0))
        return pl.pallas_call(
            input_kernel,
            grid=(1,),
            in_specs=[at]
            + [pl.BlockSpec((r // pieces, 2 * hidden, c), lambda i: (piece, 0, 0))] * 2
            + [whole] * 4
            + [pl.BlockSpec(memory_space=pl.ANY)] * len(held),
            out_specs=at,
            out_shape=jax.ShapeDtypeStruct(pair.shape, BF16),
            scratch_shapes=[pltpu.VMEM((dim, 4 * hidden), BF16)],
            input_output_aliases={7: 0} if held else {},
            compiler_params=memory(16),
            cost_estimate=cost(8 * hidden * dim * columns // pieces, pair),
            name="input",
        )(pair, grads_left, grads_right, *weights, *held)

    steps = [("row", rows, 1 << i) for i in range(1, rows.bit_length() - 1)][::-1]
    steps += [("col", cols, 1 << i) for i in range(cols.bit_length() - 1)]
    neighbours = [(i, i ^ 1) for i in range(rows)]
    pair_gradient = None
    mine = kept + lax.ppermute(given, "row", neighbours)
    for n, (axis, size, step) in enumerate(steps):
        other = lax.ppermute(mine, axis, [(i, i ^ step) for i in range(size)])
        for piece in range(n * pieces // len(steps), (n + 1) * pieces // len(steps)):
            pair_gradient = input_piece(piece, pair_gradient)
        if pair_gradient is not None:
            other, pair_gradient = lax.optimization_barrier((other, pair_gradient))
        mine = mine + other
    weight_grads = pl.pallas_call(
        functools.partial(finish_kernel, 1.0 / (rows * r)),
        in_specs=[smem, pl.BlockSpec(memory_space=pltpu.VMEM), pl.BlockSpec(memory_space=pltpu.VMEM)],
        out_shape=[jax.ShapeDtypeStruct((hidden, dim), F32)] * 4,
        name="finish",
    )(bit, mine, lax.ppermute(mine, "row", neighbours))
    return (pair_gradient, *(g.T for g in weight_grads))


def solution(mesh):
    in_specs = (P("row", "col", None), P(None, "row", "col"), P(), P(), P(), P())
    out_specs = (P("row", "col", None), P(), P(), P(), P())
    sizes = (mesh.shape["row"], mesh.shape["col"])

    def shards(pair, cotangent, *weights):
        plain = all(size > 1 and size & (size - 1) == 0 for size in sizes)
        if plain and cotangent.shape[0] % (sizes[0] * sizes[1] // 2) == 0:
            return halves_shards(sizes, pair, cotangent, *weights)
        return gathered_shards(pair, cotangent, *weights)

    return jax.shard_map(shards, mesh=mesh, in_specs=in_specs, out_specs=out_specs, check_vma=False)
```

```python
import functools

import jax
import jax.numpy as jnp
from jax import lax
from jax.experimental import pallas as pl
from jax.experimental.pallas import tpu as pltpu
from jax.sharding import PartitionSpec as P

BF16, F32 = jnp.bfloat16, jnp.float32


def gathered_shards(pair, cotangent, w_left, w_left_gate, w_right, w_right_gate):
    pair_f = pair.astype(jnp.float32)
    average = jnp.mean(pair_f, axis=-1, keepdims=True)
    centered_input = pair_f - average
    variance = jnp.mean(centered_input * centered_input, axis=-1, keepdims=True)
    inverse_scale = 1.0 / jnp.sqrt(variance + 1e-05)
    standardized_input = centered_input * inverse_scale
    normalized_input = standardized_input.astype(jnp.bfloat16)
    stacked = jnp.concatenate([w_left, w_left_gate, w_right, w_right_gate], axis=1)
    projected = jnp.einsum(
        "rcd,dh->hrc", normalized_input, stacked, preferred_element_type=jnp.float32
    )
    q_left, p_left, q_right, p_right = jnp.split(projected, 4, axis=0)
    s_left = jax.nn.sigmoid(p_left)
    s_right = jax.nn.sigmoid(p_right)
    left = (s_left * q_left).astype(jnp.bfloat16)
    right = (s_right * q_right).astype(jnp.bfloat16)
    g_chan, left_chan, right_chan = (
        lax.all_to_all(cotangent, "col", split_axis=0, concat_axis=2, tiled=True),
        lax.all_to_all(left, "col", split_axis=0, concat_axis=2, tiled=True),
        lax.all_to_all(right, "col", split_axis=0, concat_axis=2, tiled=True),
    )
    residues = g_chan.shape[2]
    g_columns = lax.all_to_all(g_chan, "row", split_axis=2, concat_axis=1, tiled=True)
    d_left = jnp.einsum(
        "hij,hjk->hik",
        g_chan,
        lax.all_gather(right_chan, "row", axis=1, tiled=True),
        preferred_element_type=jnp.float32,
    )
    d_right = jnp.einsum(
        "hij,hik->hjk",
        g_columns,
        lax.all_gather(left_chan, "row", axis=1, tiled=True),
        preferred_element_type=jnp.float32,
    )
    d_left_tile, d_right_tile = (
        lax.all_to_all(d_left.astype(jnp.bfloat16), "col", split_axis=2, concat_axis=0, tiled=True),
        lax.all_to_all(
            d_right.astype(jnp.bfloat16), "col", split_axis=2, concat_axis=0, tiled=True
        ),
    )
    grad_l = d_left_tile.astype(jnp.float32)
    grad_r = d_right_tile.astype(jnp.float32)
    e_left = grad_l * s_left
    f_left = grad_l * q_left * s_left * (1.0 - s_left)
    e_right = grad_r * s_right
    f_right = grad_r * q_right * s_right * (1.0 - s_right)
    grads = jnp.concatenate([e_left, f_left, e_right, f_right], axis=0).astype(jnp.bfloat16)
    local_weights = jnp.einsum(
        "rcd,hrc->dh", normalized_input, grads, preferred_element_type=jnp.float32
    )
    total_weights = lax.psum(local_weights, ("row", "col")) / residues
    normalized_gradient = jnp.einsum(
        "hrc,dh->rcd", grads, stacked, preferred_element_type=jnp.float32
    )
    gradient_mean = jnp.mean(normalized_gradient, axis=-1, keepdims=True)
    gradient_input_mean = jnp.mean(normalized_gradient * standardized_input, axis=-1, keepdims=True)
    pair_gradient = (
        (normalized_gradient - gradient_mean - standardized_input * gradient_input_mean)
        * inverse_scale
    ).astype(jnp.bfloat16)
    pieces_w = jnp.split(total_weights, 4, axis=1)
    return (pair_gradient, pieces_w[0], pieces_w[1], pieces_w[2], pieces_w[3])


NT = (((1,), (1,)), ((), ()))
TN = (((0,), (0,)), ((), ()))
NN = (((1,), (0,)), ((), ()))


def dot(a, b, dims=NN):
    return lax.dot_general(a, b, dims, preferred_element_type=F32)


def stack_weights(w_refs, w_ref):
    h = w_refs[0].shape[0]
    for i, ref in enumerate(w_refs):
        w_ref[pl.ds(i * h, h), :] = ref[...]


def layer_norm(x):
    x = x.T.astype(F32)
    centered = x - jnp.mean(x, axis=0, keepdims=True)
    variance = jnp.mean(centered * centered, axis=0, keepdims=True)
    inverse_scale = lax.rsqrt(variance + 1e-05)
    return centered * inverse_scale, inverse_scale


def put_lanes(ref, at, value):
    lanes = ref.shape[2]
    for i in range(ref.shape[0]):
        ref[i, at, :] = value[:, i * lanes : (i + 1) * lanes]


def get_lanes(ref, at):
    return jnp.concatenate([ref[i, at, :] for i in range(ref.shape[0])], axis=1)


def before_kernel(own, first, x_ref, wq, wg, *refs):
    if first:
        out_ref, normed_ref, w_ref, rows_ref = refs
    else:
        out_ref, w_ref, rows_ref = refs
    stack_weights((wq, wg), w_ref)
    h = wq.shape[0]
    rows = x_ref.shape[0]
    pitch = rows + 1

    def one_row(r, carry):
        if first:
            normed = layer_norm(x_ref[r])[0].astype(BF16)
            normed_ref[r] = normed
        else:
            normed = x_ref[r]
        projected = dot(w_ref[...], normed)
        value = jax.nn.sigmoid(projected[h:]) * projected[:h]
        put_lanes(rows_ref, pl.ds(r, h, stride=pitch), value)
        return carry

    lax.fori_loop(0, rows, one_row, 0, unroll=4)
    for channel in range(h):
        line = get_lanes(rows_ref, pl.ds(channel * pitch, rows))
        out_ref[channel // own, channel % own] = line.astype(BF16)


def from_blocks(blocks_ref, whole_ref, start, cols):
    n, _, r, c = blocks_ref.shape
    for i in range(n):
        at = pl.ds(pl.multiple_of(start + i // cols * r, r), r)
        whole_ref[at, pl.ds(i % cols * c, c)] = blocks_ref[i, 0]


def left_kernel(cols, half_ref, cot_ref, mine_ref, other_ref, out_ref, g_ref, x_ref):
    n = g_ref.shape[0]
    r, c = out_ref.shape[2:]
    from_blocks(cot_ref, g_ref, 0, cols)
    from_blocks(mine_ref, x_ref, half_ref[0] * n, cols)
    from_blocks(other_ref, x_ref, (1 - half_ref[0]) * n, cols)
    d = dot(g_ref[...], x_ref[...]).astype(BF16)
    for i in range(out_ref.shape[0]):
        a, b = i // cols * r, i % cols * c
        out_ref[i, 0] = d[a : a + r, b : b + c]


def right_kernel(cols, half_ref, cot_ref, in_ref, keep_ref, send_ref, g_ref, x_ref, d_ref):
    n = g_ref.shape[0]
    r, c = in_ref.shape[2:]
    from_blocks(cot_ref, g_ref, 0, cols)
    from_blocks(in_ref, x_ref, 0, cols)
    d_ref[...] = dot(g_ref[...], x_ref[...], TN)
    for half, out_ref in ((half_ref[0], keep_ref), (1 - half_ref[0], send_ref)):
        for i in range(out_ref.shape[0]):
            at = pl.ds(pl.multiple_of(half * n + i // cols * r, r), r)
            out_ref[i, 0] = d_ref[at, pl.ds(i % cols * c, c)].astype(out_ref.dtype)


def gates_kernel(d_count, *refs):
    if len(refs) > d_count + 7:
        bit_ref, left_sums_ref, *refs = refs
        normed_ref, *d_refs, wq, wg, grads_ref, kept_ref, sent_ref, w_ref, rows_ref, sums_ref = refs
    else:
        bit_ref = None
        normed_ref, *d_refs, wq, wg, grads_ref, sums_ref, w_ref, rows_ref = refs
    stack_weights((wq, wg), w_ref)
    h = wq.shape[0]
    rows = normed_ref.shape[0]
    pitch = rows + 1

    @pl.when(pl.program_id(0) == 0)
    def _():
        sums_ref[...] = jnp.zeros_like(sums_ref)

    part = d_refs[0].shape[1]
    for channel in range(h):
        to, slot = channel // (part * d_count), channel % (part * d_count)
        line = d_refs[slot // part][to, slot % part].astype(F32)
        put_lanes(rows_ref, pl.ds(channel * pitch, rows), line)

    def one_row(r, carry):
        normed = normed_ref[r]
        projected = dot(w_ref[...], normed)
        q, s = projected[:h], jax.nn.sigmoid(projected[h:])
        e = get_lanes(rows_ref, pl.ds(r, h, stride=pitch)) * s
        f = e * q * (1.0 - s)
        grads = jnp.concatenate([e, f], axis=0).astype(BF16)
        grads_ref[r] = grads
        sums_ref[...] += dot(grads, normed, NT)
        return carry

    lax.fori_loop(0, rows, one_row, 0, unroll=4)

    if bit_ref is not None:

        @pl.when(pl.program_id(0) == pl.num_programs(0) - 1)
        def _():
            for bit, first, second in ((0, left_sums_ref, sums_ref), (1, sums_ref, left_sums_ref)):

                @pl.when(bit_ref[0] == bit)
                def _(first=first, second=second):
                    kept_ref[...] = first[...]
                    sent_ref[...] = second[...]


def input_kernel(pair_ref, left_ref, right_ref, wl, wlg, wr, wrg, *refs):
    out_ref, back_ref = refs[-2:]
    h = wl.shape[0]
    for i, ref in enumerate((wl, wlg, wr, wrg)):
        back_ref[:, pl.ds(i * h, h)] = ref[...].T

    def one_row(r, carry):
        standardized, inverse_scale = layer_norm(pair_ref[r])
        grads = jnp.concatenate([left_ref[r], right_ref[r]], axis=0)
        d_normed = dot(back_ref[...], grads)
        mean = jnp.mean(d_normed, axis=0, keepdims=True)
        input_mean = jnp.mean(d_normed * standardized, axis=0, keepdims=True)
        moved = (d_normed - mean - standardized * input_mean) * inverse_scale
        out_ref[r] = moved.astype(BF16).T
        return carry

    lax.fori_loop(0, pair_ref.shape[0], one_row, 0, unroll=4)


def finish_kernel(scale, bit_ref, mine_ref, other_ref, *out_refs):
    h = out_refs[0].shape[0]
    for i, out_ref in enumerate(out_refs):
        at = pl.ds(i % 2 * h, h)
        mine = bit_ref[0] == i // 2
        out_ref[...] = jnp.where(mine, mine_ref[at, :], other_ref[at, :]) * scale


def halves_shards(sizes, pair, cotangent, *weights):
    rows, cols = sizes
    half_rows = rows // 2
    members = half_rows * cols
    hidden, r, c = cotangent.shape
    dim = pair.shape[2]
    own = hidden // members
    block = 16 if r % 16 == 0 else r
    lanes = min(c, 128)
    chunks = 2 if own % 2 == 0 else 1
    pieces = 4 if r % 4 == 0 else 1
    n_half, n_k = half_rows * r, cols * c
    columns = r * c
    weights = [w.T for w in weights]
    whole = pl.BlockSpec((hidden, dim), lambda i: (0, 0))
    smem = pl.BlockSpec(memory_space=pltpu.SMEM)
    groups = [[half * members + i for i in range(members)] for half in range(2)]
    exchange = functools.partial(
        lax.all_to_all,
        axis_name=("row", "col"),
        split_axis=0,
        concat_axis=0,
        axis_index_groups=groups,
        tiled=True,
    )
    across = functools.partial(
        lax.ppermute, axis_name="row", perm=[(i, (i + half_rows) % rows) for i in range(rows)]
    )
    row = lax.axis_index("row").astype(jnp.int32)
    half = (row // half_rows).reshape(1)
    bit = (row % 2).reshape(1)

    def cost(flops, *arrays):
        moved = sum(a.size * a.dtype.itemsize for a in arrays)
        return pl.CostEstimate(flops=flops, bytes_accessed=moved, transcendentals=0)

    def memory(mib):
        return pltpu.CompilerParams(vmem_limit_bytes=mib * 2**20)

    blocks_shape = jax.ShapeDtypeStruct((members, own, r, c), BF16)
    normed_shape = jax.ShapeDtypeStruct((r, dim, c), BF16)
    by_rows = pl.BlockSpec((members, own, block, c), lambda i: (0, 0, i, 0))
    by_dim = pl.BlockSpec((block, dim, c), lambda i: (i, 0, 0))
    side_scratch = [
        pltpu.VMEM((2 * hidden, dim), BF16),
        pltpu.VMEM((c // lanes, hidden * (block + 1), lanes), F32),
    ]

    def before(first, x, *w):
        return pl.pallas_call(
            functools.partial(before_kernel, own, first),
            grid=(r // block,),
            in_specs=[
                pl.BlockSpec((block,) + x.shape[1:], lambda i: (i, 0, 0)),
                whole,
                whole,
            ],
            out_specs=[by_rows, by_dim][: 1 + first],
            out_shape=[blocks_shape, normed_shape][: 1 + first],
            scratch_shapes=side_scratch,
            compiler_params=memory(60),
            cost_estimate=cost(4 * hidden * dim * columns, pair, pair),
            name="before",
        )(x, *w)

    def after(value, *others):
        return lax.optimization_barrier((value,) + others)[0]

    def by_channel(start):
        return pl.BlockSpec((members, 1, r, c), lambda i: (0, start + i, 0, 0))

    chunk = own // chunks

    def right_sums(n, g_all, left_all):
        return pl.pallas_call(
            functools.partial(right_kernel, cols),
            grid=(chunk,),
            in_specs=[smem] + [by_channel(n * chunk)] * 2,
            out_specs=[by_channel(0)] * 2,
            out_shape=[
                jax.ShapeDtypeStruct((members, chunk, r, c), F32),
                jax.ShapeDtypeStruct((members, chunk, r, c), BF16),
            ],
            scratch_shapes=[pltpu.VMEM((n_half, n_k), BF16)] * 2
            + [pltpu.VMEM((2 * n_half, n_k), F32)],
            compiler_params=memory(24),
            cost_estimate=cost(4 * chunk * n_half * n_half * n_k, pair),
            name="right_sums",
        )(half, g_all, left_all)

    def left_sums(g_all, right_mine, right_other):
        return pl.pallas_call(
            functools.partial(left_kernel, cols),
            grid=(own,),
            in_specs=[smem] + [by_channel(0)] * 3,
            out_specs=by_channel(0),
            out_shape=blocks_shape,
            scratch_shapes=[
                pltpu.VMEM((n_half, n_k), BF16),
                pltpu.VMEM((2 * n_half, n_k), BF16),
            ],
            compiler_params=memory(24),
            cost_estimate=cost(4 * own * n_half * n_half * n_k, pair),
            name="left_sums",
        )(half, g_all, right_mine, right_other)

    g_all = exchange(cotangent.reshape(blocks_shape.shape))
    right, normed = before(True, pair, *weights[2:])
    (left,) = before(False, normed, *weights[:2])
    right_parts = [right[:, n * chunk : (n + 1) * chunk] for n in range(chunks)]

    left = after(left, g_all)
    left_all = exchange(left)
    crossed = [across(right_parts[0])]

    right = after(right, left_all, crossed[0])
    right_mine = exchange(right)
    crossed += [across(after(part, left_all, crossed[0])) for part in right_parts[1:]]
    kept, given = zip(*(right_sums(n, g_all, left_all) for n in range(chunks)))

    right_other = after(jnp.concatenate(crossed, axis=1), right_mine, *given)
    right_other = exchange(right_other)
    summed = [across(after(given[0], *crossed))]

    d_left = left_sums(g_all, right_mine, right_other)
    d_left = exchange(after(d_left, *summed))
    summed += [across(after(part, summed[0], right_other)) for part in given[1:]]

    d_right = jnp.concatenate([k + g.astype(F32) for k, g in zip(kept, summed)], axis=1)
    d_right = exchange(after(d_right.astype(BF16), d_left))

    sums_shape = jax.ShapeDtypeStruct((2 * hidden, dim), F32)
    sums = pl.BlockSpec(sums_shape.shape, lambda i: (0, 0))
    grads_shape = jax.ShapeDtypeStruct((r, 2 * hidden, c), BF16)
    by_hidden = pl.BlockSpec((block, 2 * hidden, c), lambda i: (i, 0, 0))

    def gates(d, w, *left_sums):
        last = len(left_sums) > 0
        return pl.pallas_call(
            functools.partial(gates_kernel, len(d)),
            grid=(r // block,),
            in_specs=([smem, sums] if last else [])
            + [by_dim]
            + [pl.BlockSpec((members, x.shape[1], block, c), lambda i: (0, 0, i, 0)) for x in d]
            + [whole] * 2,
            out_specs=[by_hidden, sums] + [sums] * last,
            out_shape=[grads_shape, sums_shape] + [sums_shape] * last,
            scratch_shapes=side_scratch + [pltpu.VMEM(sums_shape.shape, F32)] * last,
            compiler_params=memory(20),
            cost_estimate=cost(8 * hidden * dim * columns, pair, pair, pair),
            name="gates",
        )(*((bit,) + left_sums if last else ()), normed, *d, *w)

    grads_left, sums_left = gates([d_left], weights[:2])
    grads_right, kept, given = gates([d_right], weights[2:], sums_left)

    def input_piece(piece, pair_gradient):
        held = [] if pair_gradient is None else [pair_gradient]
        at = pl.BlockSpec((r // pieces, c, dim), lambda i: (piece, 0, 0))
        return pl.pallas_call(
            input_kernel,
            grid=(1,),
            in_specs=[at]
            + [pl.BlockSpec((r // pieces, 2 * hidden, c), lambda i: (piece, 0, 0))] * 2
            + [whole] * 4
            + [pl.BlockSpec(memory_space=pl.ANY)] * len(held),
            out_specs=at,
            out_shape=jax.ShapeDtypeStruct(pair.shape, BF16),
            scratch_shapes=[pltpu.VMEM((dim, 4 * hidden), BF16)],
            input_output_aliases={7: 0} if held else {},
            compiler_params=memory(16),
            cost_estimate=cost(8 * hidden * dim * columns // pieces, pair),
            name="input",
        )(pair, grads_left, grads_right, *weights, *held)

    steps = [("row", rows, 1 << i) for i in range(1, rows.bit_length() - 1)][::-1]
    steps += [("col", cols, 1 << i) for i in range(cols.bit_length() - 1)]
    neighbours = [(i, i ^ 1) for i in range(rows)]
    pair_gradient = None
    mine = kept + lax.ppermute(given, "row", neighbours)
    for n, (axis, size, step) in enumerate(steps):
        other = lax.ppermute(mine, axis, [(i, i ^ step) for i in range(size)])
        for piece in range(n * pieces // len(steps), (n + 1) * pieces // len(steps)):
            pair_gradient = input_piece(piece, pair_gradient)
        if pair_gradient is not None:
            other, pair_gradient = lax.optimization_barrier((other, pair_gradient))
        mine = mine + other
    weight_grads = pl.pallas_call(
        functools.partial(finish_kernel, 1.0 / (rows * r)),
        in_specs=[smem, pl.BlockSpec(memory_space=pltpu.VMEM), pl.BlockSpec(memory_space=pltpu.VMEM)],
        out_shape=[jax.ShapeDtypeStruct((hidden, dim), F32)] * 4,
        name="finish",
    )(bit, mine, lax.ppermute(mine, "row", neighbours))
    return (pair_gradient, *(g.T for g in weight_grads))


def solution(mesh):
    in_specs = (P("row", "col", None), P(None, "row", "col"), P(), P(), P(), P())
    out_specs = (P("row", "col", None), P(), P(), P(), P())
    sizes = (mesh.shape["row"], mesh.shape["col"])

    def shards(pair, cotangent, *weights):
        plain = all(size > 1 and size & (size - 1) == 0 for size in sizes)
        if plain and cotangent.shape[0] % (sizes[0] * sizes[1] // 2) == 0:
            return halves_shards(sizes, pair, cotangent, *weights)
        return gathered_shards(pair, cotangent, *weights)

    return jax.shard_map(shards, mesh=mesh, in_specs=in_specs, out_specs=out_specs, check_vma=False)
```

```python
import functools

import jax
import jax.numpy as jnp
from jax import lax
from jax.experimental import pallas as pl
from jax.experimental.pallas import tpu as pltpu
from jax.sharding import PartitionSpec as P

BF16, F32 = jnp.bfloat16, jnp.float32


def gathered_shards(pair, cotangent, w_left, w_left_gate, w_right, w_right_gate):
    pair_f = pair.astype(jnp.float32)
    average = jnp.mean(pair_f, axis=-1, keepdims=True)
    centered_input = pair_f - average
    variance = jnp.mean(centered_input * centered_input, axis=-1, keepdims=True)
    inverse_scale = 1.0 / jnp.sqrt(variance + 1e-05)
    standardized_input = centered_input * inverse_scale
    normalized_input = standardized_input.astype(jnp.bfloat16)
    stacked = jnp.concatenate([w_left, w_left_gate, w_right, w_right_gate], axis=1)
    projected = jnp.einsum(
        "rcd,dh->hrc", normalized_input, stacked, preferred_element_type=jnp.float32
    )
    q_left, p_left, q_right, p_right = jnp.split(projected, 4, axis=0)
    s_left = jax.nn.sigmoid(p_left)
    s_right = jax.nn.sigmoid(p_right)
    left = (s_left * q_left).astype(jnp.bfloat16)
    right = (s_right * q_right).astype(jnp.bfloat16)
    g_chan, left_chan, right_chan = (
        lax.all_to_all(cotangent, "col", split_axis=0, concat_axis=2, tiled=True),
        lax.all_to_all(left, "col", split_axis=0, concat_axis=2, tiled=True),
        lax.all_to_all(right, "col", split_axis=0, concat_axis=2, tiled=True),
    )
    residues = g_chan.shape[2]
    g_columns = lax.all_to_all(g_chan, "row", split_axis=2, concat_axis=1, tiled=True)
    d_left = jnp.einsum(
        "hij,hjk->hik",
        g_chan,
        lax.all_gather(right_chan, "row", axis=1, tiled=True),
        preferred_element_type=jnp.float32,
    )
    d_right = jnp.einsum(
        "hij,hik->hjk",
        g_columns,
        lax.all_gather(left_chan, "row", axis=1, tiled=True),
        preferred_element_type=jnp.float32,
    )
    d_left_tile, d_right_tile = (
        lax.all_to_all(d_left.astype(jnp.bfloat16), "col", split_axis=2, concat_axis=0, tiled=True),
        lax.all_to_all(
            d_right.astype(jnp.bfloat16), "col", split_axis=2, concat_axis=0, tiled=True
        ),
    )
    grad_l = d_left_tile.astype(jnp.float32)
    grad_r = d_right_tile.astype(jnp.float32)
    e_left = grad_l * s_left
    f_left = grad_l * q_left * s_left * (1.0 - s_left)
    e_right = grad_r * s_right
    f_right = grad_r * q_right * s_right * (1.0 - s_right)
    grads = jnp.concatenate([e_left, f_left, e_right, f_right], axis=0).astype(jnp.bfloat16)
    local_weights = jnp.einsum(
        "rcd,hrc->dh", normalized_input, grads, preferred_element_type=jnp.float32
    )
    total_weights = lax.psum(local_weights, ("row", "col")) / residues
    normalized_gradient = jnp.einsum(
        "hrc,dh->rcd", grads, stacked, preferred_element_type=jnp.float32
    )
    gradient_mean = jnp.mean(normalized_gradient, axis=-1, keepdims=True)
    gradient_input_mean = jnp.mean(normalized_gradient * standardized_input, axis=-1, keepdims=True)
    pair_gradient = (
        (normalized_gradient - gradient_mean - standardized_input * gradient_input_mean)
        * inverse_scale
    ).astype(jnp.bfloat16)
    pieces_w = jnp.split(total_weights, 4, axis=1)
    return (pair_gradient, pieces_w[0], pieces_w[1], pieces_w[2], pieces_w[3])


NT = (((1,), (1,)), ((), ()))
TN = (((0,), (0,)), ((), ()))
NN = (((1,), (0,)), ((), ()))


def dot(a, b, dims=NN):
    return lax.dot_general(a, b, dims, preferred_element_type=F32)


def stack_weights(w_refs, w_ref):
    h = w_refs[0].shape[0]
    for i, ref in enumerate(w_refs):
        w_ref[pl.ds(i * h, h), :] = ref[...]


def layer_norm(x):
    x = x.T.astype(F32)
    centered = x - jnp.mean(x, axis=0, keepdims=True)
    variance = jnp.mean(centered * centered, axis=0, keepdims=True)
    inverse_scale = lax.rsqrt(variance + 1e-05)
    return centered * inverse_scale, inverse_scale


def project(w_ref, normed):
    projected = dot(w_ref[...], normed)
    h = projected.shape[0] // 4
    q_left, p_left, q_right, p_right = (projected[i * h : (i + 1) * h] for i in range(4))
    return q_left, jax.nn.sigmoid(p_left), q_right, jax.nn.sigmoid(p_right)


def put_lanes(ref, at, value):
    lanes = ref.shape[2]
    for i in range(ref.shape[0]):
        ref[i, at, :] = value[:, i * lanes : (i + 1) * lanes]


def get_lanes(ref, at):
    return jnp.concatenate([ref[i, at, :] for i in range(ref.shape[0])], axis=1)


def before_kernel(own, pair_ref, wl, wlg, wr, wrg, out_ref, normed_ref, w_ref, rows_ref):
    stack_weights((wl, wlg, wr, wrg), w_ref)
    h = wl.shape[0]
    rows = pair_ref.shape[0]
    pitch = rows + 1

    def one_row(r, carry):
        normed = layer_norm(pair_ref[r])[0].astype(BF16)
        normed_ref[r] = normed
        q_left, s_left, q_right, s_right = project(w_ref, normed)
        put_lanes(rows_ref, pl.ds(r, h, stride=pitch), s_left * q_left)
        put_lanes(rows_ref, pl.ds(r + h * pitch, h, stride=pitch), s_right * q_right)
        return carry

    lax.fori_loop(0, rows, one_row, 0, unroll=4)
    for channel in range(h):
        to, slot = channel // own, (channel % own) * 2
        for side in range(2):
            line = get_lanes(rows_ref, pl.ds((side * h + channel) * pitch, rows))
            out_ref[to, slot + side] = line.astype(BF16)


def triangle_kernel(rows, cols, cot_ref, in_ref, out_ref, g_ref, l_ref, r_ref):
    r, c = in_ref.shape[2:]
    for a in range(rows):
        for b in range(cols):
            at = (pl.ds(a * r, r), pl.ds(b * c, c))
            g_ref[at] = cot_ref[a * cols + b, 0]
            l_ref[at] = in_ref[a * cols + b, 0]
            r_ref[at] = in_ref[a * cols + b, 1]
    for i, (dims, ref) in enumerate(((NN, r_ref), (TN, l_ref))):
        d = dot(g_ref[...], ref[...], dims).astype(BF16)
        for a in range(rows):
            for b in range(cols):
                out_ref[a * cols + b, i] = d[a * r : (a + 1) * r, b * c : (b + 1) * c]


def gates_kernel(own, bit_ref, normed_hbm, d_ref, wl, wlg, wr, wrg, grads_ref, kept_ref, sent_ref, *scratch):
    w_ref, sums_ref, rows_ref, normed_ref, sems = scratch
    h = wl.shape[0]
    rows = grads_ref.shape[0]
    pitch = rows + 1
    step = pl.program_id(0)

    def copy(block):
        at = pl.ds(block * rows, rows)
        return pltpu.make_async_copy(normed_hbm.at[at], normed_ref.at[at], sems.at[block])

    @pl.when(step == 0)
    def _():
        for block in range(normed_ref.shape[0] // rows):
            copy(block).start()
        sums_ref[...] = jnp.zeros_like(sums_ref)
        stack_weights((wl, wlg, wr, wrg), w_ref)

    for channel in range(h):
        to, slot = channel // own, (channel % own) * 2
        for side in range(2):
            line = d_ref[to, slot + side].astype(F32)
            put_lanes(rows_ref, pl.ds((side * h + channel) * pitch, rows), line)

    copy(step).wait()

    def one_row(r, carry):
        normed = normed_ref[step * rows + r]
        q_left, s_left, q_right, s_right = project(w_ref, normed)
        e_left = get_lanes(rows_ref, pl.ds(r, h, stride=pitch)) * s_left
        e_right = get_lanes(rows_ref, pl.ds(r + h * pitch, h, stride=pitch)) * s_right
        f_left = e_left * q_left * (1.0 - s_left)
        f_right = e_right * q_right * (1.0 - s_right)
        grads = jnp.concatenate([e_left, f_left, e_right, f_right], axis=0).astype(BF16)
        grads_ref[r] = grads
        sums_ref[...] += dot(grads, normed, NT)
        return carry

    lax.fori_loop(0, rows, one_row, 0, unroll=4)

    @pl.when(step == pl.num_programs(0) - 1)
    def _():
        bit = bit_ref[0]
        kept_ref[...] = sums_ref[pl.ds(pl.multiple_of(bit * 2 * h, 2 * h), 2 * h), :]
        sent_ref[...] = sums_ref[pl.ds(pl.multiple_of((1 - bit) * 2 * h, 2 * h), 2 * h), :]


def input_kernel(start, pair_hbm, grads_ref, wl, wlg, wr, wrg, *refs):
    out_ref, back_ref, pair_ref, sem = refs[-4:]
    copy = pltpu.make_async_copy(pair_hbm.at[pl.ds(start, pair_ref.shape[0])], pair_ref, sem)
    copy.start()
    h = wl.shape[0]
    for i, ref in enumerate((wl, wlg, wr, wrg)):
        back_ref[:, pl.ds(i * h, h)] = ref[...].T

    copy.wait()

    def one_row(r, carry):
        standardized, inverse_scale = layer_norm(pair_ref[r])
        d_normed = dot(back_ref[...], grads_ref[r])
        mean = jnp.mean(d_normed, axis=0, keepdims=True)
        input_mean = jnp.mean(d_normed * standardized, axis=0, keepdims=True)
        moved = (d_normed - mean - standardized * input_mean) * inverse_scale
        out_ref[r] = moved.astype(BF16).T
        return carry

    lax.fori_loop(0, pair_ref.shape[0], one_row, 0, unroll=4)


def finish_kernel(scale, bit_ref, mine_ref, other_ref, *out_refs):
    h = out_refs[0].shape[0]
    for i, out_ref in enumerate(out_refs):
        at = pl.ds(i % 2 * h, h)
        mine = bit_ref[0] == i // 2
        out_ref[...] = jnp.where(mine, mine_ref[at, :], other_ref[at, :]) * scale


def channel_shards(sizes, pair, cotangent, *weights):
    rows, cols = sizes
    devices = rows * cols
    hidden, r, c = cotangent.shape
    dim = pair.shape[2]
    own = hidden // devices
    block = 16 if r % 16 == 0 else r
    pieces = 2 if r % 2 == 0 else 1
    weights = [w.T for w in weights]
    whole = pl.BlockSpec((hidden, dim), lambda i: (0, 0))
    tile = pl.BlockSpec((block, c, dim), lambda i: (i, 0, 0))
    exchange = functools.partial(
        lax.all_to_all, axis_name=("row", "col"), split_axis=0, concat_axis=0, tiled=True
    )
    stacked = pltpu.VMEM((4 * hidden, dim), BF16)
    lanes = min(c, 128)
    rows_scratch = pltpu.VMEM((c // lanes, 2 * hidden * (block + 1), lanes), F32)

    def cost(flops, *arrays):
        moved = sum(a.size * a.dtype.itemsize for a in arrays)
        return pl.CostEstimate(flops=flops, bytes_accessed=moved, transcendentals=0)

    def memory(mib):
        return pltpu.CompilerParams(vmem_limit_bytes=mib * 2**20)

    columns = r * c
    lr_shape = jax.ShapeDtypeStruct((devices, 2 * own, r, c), BF16)
    by_hidden = pl.BlockSpec((block, 4 * hidden, c), lambda i: (i, 0, 0))
    g_all = exchange(cotangent.reshape(devices, own, r, c))
    normed_shape = jax.ShapeDtypeStruct((r, dim, c), BF16)
    sent, normed = pl.pallas_call(
        functools.partial(before_kernel, own),
        grid=(r // block,),
        in_specs=[tile] + [whole] * 4,
        out_specs=[
            pl.BlockSpec((devices, 2 * own, block, c), lambda i: (0, 0, i, 0)),
            pl.BlockSpec((block, dim, c), lambda i: (i, 0, 0)),
        ],
        out_shape=[lr_shape, normed_shape],
        scratch_shapes=[stacked, rows_scratch],
        compiler_params=memory(60),
        cost_estimate=cost(8 * hidden * dim * columns, pair, lr_shape),
        name="before",
    )(pair, *weights)

    n_i, n_k = rows * r, cols * c
    sent = pl.pallas_call(
        functools.partial(triangle_kernel, rows, cols),
        grid=(own,),
        in_specs=[
            pl.BlockSpec((devices, 1, r, c), lambda i: (0, i, 0, 0)),
            pl.BlockSpec((devices, 2, r, c), lambda i: (0, i, 0, 0)),
        ],
        out_specs=pl.BlockSpec((devices, 2, r, c), lambda i: (0, i, 0, 0)),
        out_shape=lr_shape,
        scratch_shapes=[pltpu.VMEM((n_i, n_k), BF16)] * 3,
        compiler_params=memory(32),
        name="triangle",
    )(g_all, exchange(sent))

    bit = (lax.axis_index("row") % 2).astype(jnp.int32).reshape(1)
    smem = pl.BlockSpec(memory_space=pltpu.SMEM)
    half_shape = jax.ShapeDtypeStruct((2 * hidden, dim), F32)
    half = pl.BlockSpec(half_shape.shape, lambda i: (0, 0))
    grads, kept, given = pl.pallas_call(
        functools.partial(gates_kernel, own),
        grid=(r // block,),
        in_specs=[
            smem,
            pl.BlockSpec(memory_space=pltpu.HBM),
            pl.BlockSpec((devices, 2 * own, block, c), lambda i: (0, 0, i, 0)),
        ]
        + [whole] * 4,
        out_specs=[by_hidden, half, half],
        out_shape=[jax.ShapeDtypeStruct((r, 4 * hidden, c), BF16), half_shape, half_shape],
        scratch_shapes=[
            stacked,
            pltpu.VMEM((4 * hidden, dim), F32),
            rows_scratch,
            pltpu.VMEM(normed_shape.shape, BF16),
            pltpu.SemaphoreType.DMA((r // block,)),
        ],
        compiler_params=memory(28),
        name="gates",
    )(bit, pltpu.with_memory_space_constraint(normed, pltpu.HBM), exchange(sent), *weights)

    def input_piece(piece, pair_gradient):
        held = [] if pair_gradient is None else [pair_gradient]
        at = pl.BlockSpec((r // pieces, c, dim), lambda i: (piece, 0, 0))
        return pl.pallas_call(
            functools.partial(input_kernel, piece * r // pieces),
            grid=(1,),
            in_specs=[
                pl.BlockSpec(memory_space=pltpu.HBM),
                pl.BlockSpec((r // pieces, 4 * hidden, c), lambda i: (piece, 0, 0)),
            ]
            + [whole] * 4
            + [pl.BlockSpec(memory_space=pl.ANY)] * len(held),
            out_specs=at,
            out_shape=jax.ShapeDtypeStruct(pair.shape, BF16),
            scratch_shapes=[
                pltpu.VMEM((dim, 4 * hidden), BF16),
                pltpu.VMEM((r // pieces, c, dim), BF16),
                pltpu.SemaphoreType.DMA,
            ],
            input_output_aliases={6: 0} if held else {},
            compiler_params=memory(16),
            cost_estimate=cost(8 * hidden * dim * columns // pieces, pair),
            name="input",
        )(pltpu.with_memory_space_constraint(pair, pltpu.HBM), grads, *weights, *held)

    steps = [("row", rows, 1 << i) for i in range(1, rows.bit_length() - 1)][::-1]
    steps += [("col", cols, 1 << i) for i in range(cols.bit_length() - 1)]
    pieces = min(pieces, len(steps))
    neighbours = [(i, i ^ 1) for i in range(rows)]
    pair_gradient = None
    mine = kept + lax.ppermute(given, "row", neighbours)
    for n, (axis, size, step) in enumerate(steps):
        other = lax.ppermute(mine, axis, [(i, i ^ step) for i in range(size)])
        if n < pieces:
            pair_gradient = input_piece(n, pair_gradient)
            other, pair_gradient = lax.optimization_barrier((other, pair_gradient))
        mine = mine + other
    weight_grads = pl.pallas_call(
        functools.partial(finish_kernel, 1.0 / n_i),
        in_specs=[smem, pl.BlockSpec(memory_space=pltpu.VMEM), pl.BlockSpec(memory_space=pltpu.VMEM)],
        out_shape=[jax.ShapeDtypeStruct((hidden, dim), F32)] * 4,
        name="finish",
    )(bit, mine, lax.ppermute(mine, "row", neighbours))
    return (pair_gradient, *(g.T for g in weight_grads))


def solution(mesh):
    in_specs = (P("row", "col", None), P(None, "row", "col"), P(), P(), P(), P())
    out_specs = (P("row", "col", None), P(), P(), P(), P())
    sizes = (mesh.shape["row"], mesh.shape["col"])

    def shards(pair, cotangent, *weights):
        plain = all(size > 1 and size & (size - 1) == 0 for size in sizes)
        if plain and cotangent.shape[0] % (sizes[0] * sizes[1]) == 0:
            return channel_shards(sizes, pair, cotangent, *weights)
        return gathered_shards(pair, cotangent, *weights)

    return jax.shard_map(shards, mesh=mesh, in_specs=in_specs, out_specs=out_specs, check_vma=False)
```

```python
import functools

import jax
import jax.numpy as jnp
from jax import lax
from jax.experimental import pallas as pl
from jax.experimental.pallas import tpu as pltpu
from jax.sharding import PartitionSpec as P

BF16, F32 = jnp.bfloat16, jnp.float32


def gathered_shards(pair, cotangent, w_left, w_left_gate, w_right, w_right_gate):
    pair_f = pair.astype(jnp.float32)
    average = jnp.mean(pair_f, axis=-1, keepdims=True)
    centered_input = pair_f - average
    variance = jnp.mean(centered_input * centered_input, axis=-1, keepdims=True)
    inverse_scale = 1.0 / jnp.sqrt(variance + 1e-05)
    standardized_input = centered_input * inverse_scale
    normalized_input = standardized_input.astype(jnp.bfloat16)
    stacked = jnp.concatenate([w_left, w_left_gate, w_right, w_right_gate], axis=1)
    projected = jnp.einsum(
        "rcd,dh->hrc", normalized_input, stacked, preferred_element_type=jnp.float32
    )
    q_left, p_left, q_right, p_right = jnp.split(projected, 4, axis=0)
    s_left = jax.nn.sigmoid(p_left)
    s_right = jax.nn.sigmoid(p_right)
    left = (s_left * q_left).astype(jnp.bfloat16)
    right = (s_right * q_right).astype(jnp.bfloat16)
    g_chan, left_chan, right_chan = (
        lax.all_to_all(cotangent, "col", split_axis=0, concat_axis=2, tiled=True),
        lax.all_to_all(left, "col", split_axis=0, concat_axis=2, tiled=True),
        lax.all_to_all(right, "col", split_axis=0, concat_axis=2, tiled=True),
    )
    residues = g_chan.shape[2]
    g_columns = lax.all_to_all(g_chan, "row", split_axis=2, concat_axis=1, tiled=True)
    d_left = jnp.einsum(
        "hij,hjk->hik",
        g_chan,
        lax.all_gather(right_chan, "row", axis=1, tiled=True),
        preferred_element_type=jnp.float32,
    )
    d_right = jnp.einsum(
        "hij,hik->hjk",
        g_columns,
        lax.all_gather(left_chan, "row", axis=1, tiled=True),
        preferred_element_type=jnp.float32,
    )
    d_left_tile, d_right_tile = (
        lax.all_to_all(d_left.astype(jnp.bfloat16), "col", split_axis=2, concat_axis=0, tiled=True),
        lax.all_to_all(
            d_right.astype(jnp.bfloat16), "col", split_axis=2, concat_axis=0, tiled=True
        ),
    )
    grad_l = d_left_tile.astype(jnp.float32)
    grad_r = d_right_tile.astype(jnp.float32)
    e_left = grad_l * s_left
    f_left = grad_l * q_left * s_left * (1.0 - s_left)
    e_right = grad_r * s_right
    f_right = grad_r * q_right * s_right * (1.0 - s_right)
    grads = jnp.concatenate([e_left, f_left, e_right, f_right], axis=0).astype(jnp.bfloat16)
    local_weights = jnp.einsum(
        "rcd,hrc->dh", normalized_input, grads, preferred_element_type=jnp.float32
    )
    total_weights = lax.psum(local_weights, ("row", "col")) / residues
    normalized_gradient = jnp.einsum(
        "hrc,dh->rcd", grads, stacked, preferred_element_type=jnp.float32
    )
    gradient_mean = jnp.mean(normalized_gradient, axis=-1, keepdims=True)
    gradient_input_mean = jnp.mean(normalized_gradient * standardized_input, axis=-1, keepdims=True)
    pair_gradient = (
        (normalized_gradient - gradient_mean - standardized_input * gradient_input_mean)
        * inverse_scale
    ).astype(jnp.bfloat16)
    pieces_w = jnp.split(total_weights, 4, axis=1)
    return (pair_gradient, pieces_w[0], pieces_w[1], pieces_w[2], pieces_w[3])


NT = (((1,), (1,)), ((), ()))
TN = (((0,), (0,)), ((), ()))
NN = (((1,), (0,)), ((), ()))


def dot(a, b, dims=NN):
    return lax.dot_general(a, b, dims, preferred_element_type=F32)


def stack_weights(w_refs, w_ref):
    h = w_refs[0].shape[0]
    for i, ref in enumerate(w_refs):
        w_ref[pl.ds(i * h, h), :] = ref[...]


def layer_norm(x):
    x = x.T.astype(F32)
    centered = x - jnp.mean(x, axis=0, keepdims=True)
    variance = jnp.mean(centered * centered, axis=0, keepdims=True)
    inverse_scale = lax.rsqrt(variance + 1e-05)
    return centered * inverse_scale, inverse_scale


def project(w_ref, normed):
    projected = dot(w_ref[...], normed)
    h = projected.shape[0] // 4
    q_left, p_left, q_right, p_right = (projected[i * h : (i + 1) * h] for i in range(4))
    return q_left, jax.nn.sigmoid(p_left), q_right, jax.nn.sigmoid(p_right)


def put_lanes(ref, at, value):
    lanes = ref.shape[2]
    for i in range(ref.shape[0]):
        ref[i, at, :] = value[:, i * lanes : (i + 1) * lanes]


def get_lanes(ref, at):
    return jnp.concatenate([ref[i, at, :] for i in range(ref.shape[0])], axis=1)


def before_kernel(own, pair_ref, wl, wlg, wr, wrg, out_ref, normed_ref, w_ref, rows_ref):
    stack_weights((wl, wlg, wr, wrg), w_ref)
    h = wl.shape[0]
    rows = pair_ref.shape[0]
    pitch = rows + 1

    def one_row(r, carry):
        normed = layer_norm(pair_ref[r])[0].astype(BF16)
        normed_ref[r] = normed
        q_left, s_left, q_right, s_right = project(w_ref, normed)
        put_lanes(rows_ref, pl.ds(r, h, stride=pitch), s_left * q_left)
        put_lanes(rows_ref, pl.ds(r + h * pitch, h, stride=pitch), s_right * q_right)
        return carry

    lax.fori_loop(0, rows, one_row, 0, unroll=4)
    for channel in range(h):
        to, slot = channel // own, (channel % own) * 2
        for side in range(2):
            line = get_lanes(rows_ref, pl.ds((side * h + channel) * pitch, rows))
            out_ref[to, slot + side] = line.astype(BF16)


def triangle_kernel(rows, cols, cot_ref, in_ref, out_ref, g_ref, l_ref, r_ref):
    r, c = in_ref.shape[2:]
    for a in range(rows):
        for b in range(cols):
            at = (pl.ds(a * r, r), pl.ds(b * c, c))
            g_ref[at] = cot_ref[a * cols + b, 0]
            l_ref[at] = in_ref[a * cols + b, 0]
            r_ref[at] = in_ref[a * cols + b, 1]
    for i, (dims, ref) in enumerate(((NN, r_ref), (TN, l_ref))):
        d = dot(g_ref[...], ref[...], dims).astype(BF16)
        for a in range(rows):
            for b in range(cols):
                out_ref[a * cols + b, i] = d[a * r : (a + 1) * r, b * c : (b + 1) * c]


def gates_kernel(own, bit_ref, normed_hbm, d_ref, wl, wlg, wr, wrg, grads_ref, kept_ref, sent_ref, *scratch):
    w_ref, sums_ref, rows_ref, normed_ref, sems = scratch
    h = wl.shape[0]
    rows = grads_ref.shape[0]
    pitch = rows + 1
    step = pl.program_id(0)

    def copy(block):
        at = pl.ds(block * rows, rows)
        return pltpu.make_async_copy(normed_hbm.at[at], normed_ref.at[at], sems.at[block])

    @pl.when(step == 0)
    def _():
        for block in range(normed_ref.shape[0] // rows):
            copy(block).start()
        sums_ref[...] = jnp.zeros_like(sums_ref)
        stack_weights((wl, wlg, wr, wrg), w_ref)

    for channel in range(h):
        to, slot = channel // own, (channel % own) * 2
        for side in range(2):
            line = d_ref[to, slot + side].astype(F32)
            put_lanes(rows_ref, pl.ds((side * h + channel) * pitch, rows), line)

    copy(step).wait()

    def one_row(r, carry):
        normed = normed_ref[step * rows + r]
        q_left, s_left, q_right, s_right = project(w_ref, normed)
        e_left = get_lanes(rows_ref, pl.ds(r, h, stride=pitch)) * s_left
        e_right = get_lanes(rows_ref, pl.ds(r + h * pitch, h, stride=pitch)) * s_right
        f_left = e_left * q_left * (1.0 - s_left)
        f_right = e_right * q_right * (1.0 - s_right)
        grads = jnp.concatenate([e_left, f_left, e_right, f_right], axis=0).astype(BF16)
        grads_ref[r] = grads
        sums_ref[...] += dot(grads, normed, NT)
        return carry

    lax.fori_loop(0, rows, one_row, 0, unroll=4)

    @pl.when(step == pl.num_programs(0) - 1)
    def _():
        bit = bit_ref[0]
        kept_ref[...] = sums_ref[pl.ds(pl.multiple_of(bit * 2 * h, 2 * h), 2 * h), :]
        sent_ref[...] = sums_ref[pl.ds(pl.multiple_of((1 - bit) * 2 * h, 2 * h), 2 * h), :]


def input_kernel(start, pair_hbm, grads_ref, wl, wlg, wr, wrg, *refs):
    out_ref, back_ref, pair_ref, sem = refs[-4:]
    copy = pltpu.make_async_copy(pair_hbm.at[pl.ds(start, pair_ref.shape[0])], pair_ref, sem)
    copy.start()
    h = wl.shape[0]
    for i, ref in enumerate((wl, wlg, wr, wrg)):
        back_ref[:, pl.ds(i * h, h)] = ref[...].T

    copy.wait()

    def one_row(r, carry):
        standardized, inverse_scale = layer_norm(pair_ref[r])
        d_normed = dot(back_ref[...], grads_ref[r])
        mean = jnp.mean(d_normed, axis=0, keepdims=True)
        input_mean = jnp.mean(d_normed * standardized, axis=0, keepdims=True)
        moved = (d_normed - mean - standardized * input_mean) * inverse_scale
        out_ref[r] = moved.astype(BF16).T
        return carry

    lax.fori_loop(0, pair_ref.shape[0], one_row, 0, unroll=4)


def quarters_kernel(quarter, place_ref, a_ref, b_ref, *out_refs):
    for m, out_ref in enumerate(out_refs):
        at = pl.ds(pl.multiple_of((place_ref[0] ^ m) * quarter, quarter), quarter)
        out_ref[...] = a_ref[at, :] + b_ref[at, :]


def half_kernel(quarter, place_ref, *refs):
    for m, ref in enumerate(refs[:4]):
        at = pl.ds(pl.multiple_of((place_ref[0] ^ m) * quarter, quarter), quarter)
        refs[4][at, :] = ref[...]


def finish_kernel(scale, bit_ref, mine_ref, other_ref, *out_refs):
    h = out_refs[0].shape[0]
    for i, out_ref in enumerate(out_refs):
        at = pl.ds(i % 2 * h, h)
        mine = bit_ref[0] == i // 2
        out_ref[...] = jnp.where(mine, mine_ref[at, :], other_ref[at, :]) * scale


def channel_shards(sizes, pair, cotangent, *weights):
    rows, cols = sizes
    devices = rows * cols
    hidden, r, c = cotangent.shape
    dim = pair.shape[2]
    own = hidden // devices
    block = 16 if r % 16 == 0 else r
    pieces = 2 if r % 2 == 0 else 1
    weights = [w.T for w in weights]
    whole = pl.BlockSpec((hidden, dim), lambda i: (0, 0))
    tile = pl.BlockSpec((block, c, dim), lambda i: (i, 0, 0))
    exchange = functools.partial(
        lax.all_to_all, axis_name=("row", "col"), split_axis=0, concat_axis=0, tiled=True
    )
    stacked = pltpu.VMEM((4 * hidden, dim), BF16)
    lanes = min(c, 128)
    rows_scratch = pltpu.VMEM((c // lanes, 2 * hidden * (block + 1), lanes), F32)

    def cost(flops, *arrays):
        moved = sum(a.size * a.dtype.itemsize for a in arrays)
        return pl.CostEstimate(flops=flops, bytes_accessed=moved, transcendentals=0)

    def memory(mib):
        return pltpu.CompilerParams(vmem_limit_bytes=mib * 2**20)

    columns = r * c
    lr_shape = jax.ShapeDtypeStruct((devices, 2 * own, r, c), BF16)
    by_hidden = pl.BlockSpec((block, 4 * hidden, c), lambda i: (i, 0, 0))
    g_all = exchange(cotangent.reshape(devices, own, r, c))
    normed_shape = jax.ShapeDtypeStruct((r, dim, c), BF16)
    sent, normed = pl.pallas_call(
        functools.partial(before_kernel, own),
        grid=(r // block,),
        in_specs=[tile] + [whole] * 4,
        out_specs=[
            pl.BlockSpec((devices, 2 * own, block, c), lambda i: (0, 0, i, 0)),
            pl.BlockSpec((block, dim, c), lambda i: (i, 0, 0)),
        ],
        out_shape=[lr_shape, normed_shape],
        scratch_shapes=[stacked, rows_scratch],
        compiler_params=memory(60),
        cost_estimate=cost(8 * hidden * dim * columns, pair, lr_shape),
        name="before",
    )(pair, *weights)

    n_i, n_k = rows * r, cols * c
    sent = pl.pallas_call(
        functools.partial(triangle_kernel, rows, cols),
        grid=(own,),
        in_specs=[
            pl.BlockSpec((devices, 1, r, c), lambda i: (0, i, 0, 0)),
            pl.BlockSpec((devices, 2, r, c), lambda i: (0, i, 0, 0)),
        ],
        out_specs=pl.BlockSpec((devices, 2, r, c), lambda i: (0, i, 0, 0)),
        out_shape=pltpu.HBM(lr_shape.shape, BF16),
        scratch_shapes=[pltpu.VMEM((n_i, n_k), BF16)] * 3,
        compiler_params=memory(32),
        name="triangle",
    )(g_all, exchange(sent))

    row, col = (lax.axis_index(axis).astype(jnp.int32) for axis in ("row", "col"))
    bit = (row % 2).reshape(1)
    place = (row // 2 % 2 * 2 + col % 2).reshape(1)
    vmem = pl.BlockSpec(memory_space=pltpu.VMEM)
    smem = pl.BlockSpec(memory_space=pltpu.SMEM)
    half_shape = jax.ShapeDtypeStruct((2 * hidden, dim), F32)
    half = pl.BlockSpec(half_shape.shape, lambda i: (0, 0))
    grads, kept, given = pl.pallas_call(
        functools.partial(gates_kernel, own),
        grid=(r // block,),
        in_specs=[
            smem,
            pl.BlockSpec(memory_space=pltpu.HBM),
            pl.BlockSpec((devices, 2 * own, block, c), lambda i: (0, 0, i, 0)),
        ]
        + [whole] * 4,
        out_specs=[by_hidden, half, half],
        out_shape=[jax.ShapeDtypeStruct((r, 4 * hidden, c), BF16), half_shape, half_shape],
        scratch_shapes=[
            stacked,
            pltpu.VMEM((4 * hidden, dim), F32),
            rows_scratch,
            pltpu.VMEM(normed_shape.shape, BF16),
            pltpu.SemaphoreType.DMA((r // block,)),
        ],
        compiler_params=memory(28),
        name="gates",
    )(bit, pltpu.with_memory_space_constraint(normed, pltpu.HBM), exchange(sent), *weights)

    def input_piece(piece, pair_gradient):
        held = [] if pair_gradient is None else [pair_gradient]
        at = pl.BlockSpec((r // pieces, c, dim), lambda i: (piece, 0, 0))
        return pl.pallas_call(
            functools.partial(input_kernel, piece * r // pieces),
            grid=(1,),
            in_specs=[
                pl.BlockSpec(memory_space=pltpu.HBM),
                pl.BlockSpec((r // pieces, 4 * hidden, c), lambda i: (piece, 0, 0)),
            ]
            + [whole] * 4
            + [pl.BlockSpec(memory_space=pl.ANY)] * len(held),
            out_specs=at,
            out_shape=jax.ShapeDtypeStruct(pair.shape, BF16),
            scratch_shapes=[
                pltpu.VMEM((dim, 4 * hidden), BF16),
                pltpu.VMEM((r // pieces, c, dim), BF16),
                pltpu.SemaphoreType.DMA,
            ],
            input_output_aliases={6: 0} if held else {},
            compiler_params=memory(16),
            cost_estimate=cost(8 * hidden * dim * columns // pieces, pair),
            name="input",
        )(pltpu.with_memory_space_constraint(pair, pltpu.HBM), grads, *weights, *held)

    pair_gradient, piece = None, 0

    def beside(values):
        nonlocal pair_gradient, piece
        if piece < pieces:
            pair_gradient = input_piece(piece, pair_gradient)
            piece += 1
            *values, pair_gradient = lax.optimization_barrier((*values, pair_gradient))
        return values

    def swap(value, axis, size, step):
        return lax.ppermute(value, axis, [(i, i ^ step) for i in range(size)])

    def swap_quarter(value, m):
        size = rows * cols
        far = ((m >> 1) * 2 * cols) ^ (m & 1)
        return lax.ppermute(value, ("row", "col"), [(i, i ^ far) for i in range(size)])

    quarter = 2 * hidden // 4
    quarters = pl.pallas_call(
        functools.partial(quarters_kernel, quarter),
        in_specs=[smem, vmem, vmem],
        out_specs=[vmem] * 4,
        out_shape=[jax.ShapeDtypeStruct((quarter, dim), F32)] * 4,
        compiler_params=memory(8),
        name="quarters",
    )(place, kept, swap(given, "row", rows, 1))
    got = beside([swap_quarter(quarters[m], m) for m in range(1, 4)])
    mine = (quarters[0] + got[0]) + (got[1] + got[2])
    step = 4
    while step < rows:
        if 2 * step < rows:
            got = [swap(mine, "row", rows, m * step) for m in range(1, 4)]
            got = beside(got)
            mine = (mine + got[0]) + (got[1] + got[2])
        else:
            mine = mine + beside([swap(mine, "row", rows, step)])[0]
        step *= 4
    got = beside([swap_quarter(mine, m) for m in range(1, 4)])
    while piece < pieces:
        got = beside(got)
    mine = pl.pallas_call(
        functools.partial(half_kernel, quarter),
        in_specs=[smem] + [vmem] * 4,
        out_specs=vmem,
        out_shape=half_shape,
        compiler_params=memory(8),
        name="half",
    )(place, mine, *got)
    weight_grads = pl.pallas_call(
        functools.partial(finish_kernel, 1.0 / n_i),
        in_specs=[smem, vmem, vmem],
        out_shape=[jax.ShapeDtypeStruct((hidden, dim), F32)] * 4,
        compiler_params=memory(8),
        name="finish",
    )(bit, mine, swap(mine, "row", rows, 1))
    return (pair_gradient, *(g.T for g in weight_grads))


def solution(mesh):
    in_specs = (P("row", "col", None), P(None, "row", "col"), P(), P(), P(), P())
    out_specs = (P("row", "col", None), P(), P(), P(), P())
    sizes = (mesh.shape["row"], mesh.shape["col"])

    def shards(pair, cotangent, *weights):
        plain = sizes[0] >= 4 and sizes[1] == 2 and sizes[0] & (sizes[0] - 1) == 0
        if plain and cotangent.shape[0] % (sizes[0] * sizes[1]) == 0:
            return channel_shards(sizes, pair, cotangent, *weights)
        return gathered_shards(pair, cotangent, *weights)

    return jax.shard_map(shards, mesh=mesh, in_specs=in_specs, out_specs=out_specs, check_vma=False)
```

```python
import functools

import jax
import jax.numpy as jnp
from jax import lax
from jax.experimental import pallas as pl
from jax.experimental.pallas import tpu as pltpu
from jax.sharding import PartitionSpec as P

BF16, F32 = jnp.bfloat16, jnp.float32


def gathered_shards(pair, cotangent, w_left, w_left_gate, w_right, w_right_gate):
    pair_f = pair.astype(jnp.float32)
    average = jnp.mean(pair_f, axis=-1, keepdims=True)
    centered_input = pair_f - average
    variance = jnp.mean(centered_input * centered_input, axis=-1, keepdims=True)
    inverse_scale = 1.0 / jnp.sqrt(variance + 1e-05)
    standardized_input = centered_input * inverse_scale
    normalized_input = standardized_input.astype(jnp.bfloat16)
    stacked = jnp.concatenate([w_left, w_left_gate, w_right, w_right_gate], axis=1)
    projected = jnp.einsum(
        "rcd,dh->hrc", normalized_input, stacked, preferred_element_type=jnp.float32
    )
    q_left, p_left, q_right, p_right = jnp.split(projected, 4, axis=0)
    s_left = jax.nn.sigmoid(p_left)
    s_right = jax.nn.sigmoid(p_right)
    left = (s_left * q_left).astype(jnp.bfloat16)
    right = (s_right * q_right).astype(jnp.bfloat16)
    g_chan, left_chan, right_chan = (
        lax.all_to_all(cotangent, "col", split_axis=0, concat_axis=2, tiled=True),
        lax.all_to_all(left, "col", split_axis=0, concat_axis=2, tiled=True),
        lax.all_to_all(right, "col", split_axis=0, concat_axis=2, tiled=True),
    )
    residues = g_chan.shape[2]
    g_columns = lax.all_to_all(g_chan, "row", split_axis=2, concat_axis=1, tiled=True)
    d_left = jnp.einsum(
        "hij,hjk->hik",
        g_chan,
        lax.all_gather(right_chan, "row", axis=1, tiled=True),
        preferred_element_type=jnp.float32,
    )
    d_right = jnp.einsum(
        "hij,hik->hjk",
        g_columns,
        lax.all_gather(left_chan, "row", axis=1, tiled=True),
        preferred_element_type=jnp.float32,
    )
    d_left_tile, d_right_tile = (
        lax.all_to_all(d_left.astype(jnp.bfloat16), "col", split_axis=2, concat_axis=0, tiled=True),
        lax.all_to_all(
            d_right.astype(jnp.bfloat16), "col", split_axis=2, concat_axis=0, tiled=True
        ),
    )
    grad_l = d_left_tile.astype(jnp.float32)
    grad_r = d_right_tile.astype(jnp.float32)
    e_left = grad_l * s_left
    f_left = grad_l * q_left * s_left * (1.0 - s_left)
    e_right = grad_r * s_right
    f_right = grad_r * q_right * s_right * (1.0 - s_right)
    grads = jnp.concatenate([e_left, f_left, e_right, f_right], axis=0).astype(jnp.bfloat16)
    local_weights = jnp.einsum(
        "rcd,hrc->dh", normalized_input, grads, preferred_element_type=jnp.float32
    )
    total_weights = lax.psum(local_weights, ("row", "col")) / residues
    normalized_gradient = jnp.einsum(
        "hrc,dh->rcd", grads, stacked, preferred_element_type=jnp.float32
    )
    gradient_mean = jnp.mean(normalized_gradient, axis=-1, keepdims=True)
    gradient_input_mean = jnp.mean(normalized_gradient * standardized_input, axis=-1, keepdims=True)
    pair_gradient = (
        (normalized_gradient - gradient_mean - standardized_input * gradient_input_mean)
        * inverse_scale
    ).astype(jnp.bfloat16)
    pieces_w = jnp.split(total_weights, 4, axis=1)
    return (pair_gradient, pieces_w[0], pieces_w[1], pieces_w[2], pieces_w[3])


NT = (((1,), (1,)), ((), ()))
TN = (((0,), (0,)), ((), ()))
NN = (((1,), (0,)), ((), ()))


def dot(a, b, dims=NN):
    return lax.dot_general(a, b, dims, preferred_element_type=F32)


def stack_weights(w_refs, w_ref):
    h = w_refs[0].shape[0]
    for i, ref in enumerate(w_refs):
        w_ref[pl.ds(i * h, h), :] = ref[...]


def layer_norm(x):
    x = x.T.astype(F32)
    centered = x - jnp.mean(x, axis=0, keepdims=True)
    variance = jnp.mean(centered * centered, axis=0, keepdims=True)
    inverse_scale = lax.rsqrt(variance + 1e-05)
    return centered * inverse_scale, inverse_scale


def project(w_ref, normed):
    projected = dot(w_ref[...], normed)
    h = projected.shape[0] // 4
    q_left, p_left, q_right, p_right = (projected[i * h : (i + 1) * h] for i in range(4))
    return q_left, jax.nn.sigmoid(p_left), q_right, jax.nn.sigmoid(p_right)


def put_lanes(ref, at, value):
    lanes = ref.shape[2]
    for i in range(ref.shape[0]):
        ref[i, at, :] = value[:, i * lanes : (i + 1) * lanes]


def get_lanes(ref, at):
    return jnp.concatenate([ref[i, at, :] for i in range(ref.shape[0])], axis=1)


def before_kernel(own, pair_ref, wl, wlg, wr, wrg, out_ref, normed_ref, w_ref, rows_ref):
    stack_weights((wl, wlg, wr, wrg), w_ref)
    h = wl.shape[0]
    rows = pair_ref.shape[0]
    pitch = rows + 1

    def one_row(r, carry):
        normed = layer_norm(pair_ref[r])[0].astype(BF16)
        normed_ref[r] = normed
        q_left, s_left, q_right, s_right = project(w_ref, normed)
        put_lanes(rows_ref, pl.ds(r, h, stride=pitch), s_left * q_left)
        put_lanes(rows_ref, pl.ds(r + h * pitch, h, stride=pitch), s_right * q_right)
        return carry

    lax.fori_loop(0, rows, one_row, 0, unroll=4)
    for channel in range(h):
        to, slot = channel // own, (channel % own) * 2
        for side in range(2):
            line = get_lanes(rows_ref, pl.ds((side * h + channel) * pitch, rows))
            out_ref[to, slot + side] = line.astype(BF16)


def triangle_kernel(rows, cols, cot_ref, in_ref, out_ref, g_ref, l_ref, r_ref):
    r, c = in_ref.shape[2:]
    for a in range(rows):
        for b in range(cols):
            at = (pl.ds(a * r, r), pl.ds(b * c, c))
            g_ref[at] = cot_ref[a * cols + b, 0]
            l_ref[at] = in_ref[a * cols + b, 0]
            r_ref[at] = in_ref[a * cols + b, 1]
    for i, (dims, ref) in enumerate(((NN, r_ref), (TN, l_ref))):
        d = dot(g_ref[...], ref[...], dims).astype(BF16)
        for a in range(rows):
            for b in range(cols):
                out_ref[a * cols + b, i] = d[a * r : (a + 1) * r, b * c : (b + 1) * c]


def gates_kernel(own, bit_ref, normed_hbm, d_ref, wl, wlg, wr, wrg, grads_ref, kept_ref, sent_ref, *scratch):
    w_ref, sums_ref, rows_ref, normed_ref, sems = scratch
    h = wl.shape[0]
    rows = grads_ref.shape[0]
    pitch = rows + 1
    step = pl.program_id(0)

    def copy(block):
        at = pl.ds(block * rows, rows)
        return pltpu.make_async_copy(normed_hbm.at[at], normed_ref.at[at], sems.at[block])

    @pl.when(step == 0)
    def _():
        for block in range(normed_ref.shape[0] // rows):
            copy(block).start()
        sums_ref[...] = jnp.zeros_like(sums_ref)
        stack_weights((wl, wlg, wr, wrg), w_ref)

    for channel in range(h):
        to, slot = channel // own, (channel % own) * 2
        for side in range(2):
            line = d_ref[to, slot + side].astype(F32)
            put_lanes(rows_ref, pl.ds((side * h + channel) * pitch, rows), line)

    copy(step).wait()

    def one_row(r, carry):
        normed = normed_ref[step * rows + r]
        q_left, s_left, q_right, s_right = project(w_ref, normed)
        e_left = get_lanes(rows_ref, pl.ds(r, h, stride=pitch)) * s_left
        e_right = get_lanes(rows_ref, pl.ds(r + h * pitch, h, stride=pitch)) * s_right
        f_left = e_left * q_left * (1.0 - s_left)
        f_right = e_right * q_right * (1.0 - s_right)
        grads = jnp.concatenate([e_left, f_left, e_right, f_right], axis=0).astype(BF16)
        grads_ref[r] = grads
        sums_ref[...] += dot(grads, normed, NT)
        return carry

    lax.fori_loop(0, rows, one_row, 0, unroll=4)

    @pl.when(step == pl.num_programs(0) - 1)
    def _():
        bit = bit_ref[0]
        kept_ref[...] = sums_ref[pl.ds(pl.multiple_of(bit * 2 * h, 2 * h), 2 * h), :]
        sent_ref[...] = sums_ref[pl.ds(pl.multiple_of((1 - bit) * 2 * h, 2 * h), 2 * h), :]


def input_kernel(start, pair_hbm, grads_ref, wl, wlg, wr, wrg, *refs):
    out_ref, back_ref, pair_ref, sem = refs[-4:]
    copy = pltpu.make_async_copy(pair_hbm.at[pl.ds(start, pair_ref.shape[0])], pair_ref, sem)
    copy.start()
    h = wl.shape[0]
    for i, ref in enumerate((wl, wlg, wr, wrg)):
        back_ref[:, pl.ds(i * h, h)] = ref[...].T

    copy.wait()

    def one_row(r, carry):
        standardized, inverse_scale = layer_norm(pair_ref[r])
        d_normed = dot(back_ref[...], grads_ref[r])
        mean = jnp.mean(d_normed, axis=0, keepdims=True)
        input_mean = jnp.mean(d_normed * standardized, axis=0, keepdims=True)
        moved = (d_normed - mean - standardized * input_mean) * inverse_scale
        out_ref[r] = moved.astype(BF16).T
        return carry

    lax.fori_loop(0, pair_ref.shape[0], one_row, 0, unroll=4)


def finish_kernel(scale, bit_ref, mine_ref, other_ref, *out_refs):
    h = out_refs[0].shape[0]
    for i, out_ref in enumerate(out_refs):
        at = pl.ds(i % 2 * h, h)
        mine = bit_ref[0] == i // 2
        out_ref[...] = jnp.where(mine, mine_ref[at, :], other_ref[at, :]) * scale


def channel_shards(sizes, pair, cotangent, *weights):
    rows, cols = sizes
    devices = rows * cols
    hidden, r, c = cotangent.shape
    dim = pair.shape[2]
    own = hidden // devices
    block = 16 if r % 16 == 0 else r
    pieces = 2 if r % 2 == 0 else 1
    weights = [w.T for w in weights]
    whole = pl.BlockSpec((hidden, dim), lambda i: (0, 0))
    tile = pl.BlockSpec((block, c, dim), lambda i: (i, 0, 0))
    exchange = functools.partial(
        lax.all_to_all, axis_name=("row", "col"), split_axis=0, concat_axis=0, tiled=True
    )
    stacked = pltpu.VMEM((4 * hidden, dim), BF16)
    lanes = min(c, 128)
    rows_scratch = pltpu.VMEM((c // lanes, 2 * hidden * (block + 1), lanes), F32)

    def cost(flops, *arrays):
        moved = sum(a.size * a.dtype.itemsize for a in arrays)
        return pl.CostEstimate(flops=flops, bytes_accessed=moved, transcendentals=0)

    def memory(mib):
        return pltpu.CompilerParams(vmem_limit_bytes=mib * 2**20)

    columns = r * c
    lr_shape = jax.ShapeDtypeStruct((devices, 2 * own, r, c), BF16)
    by_hidden = pl.BlockSpec((block, 4 * hidden, c), lambda i: (i, 0, 0))
    g_all = exchange(cotangent.reshape(devices, own, r, c))
    normed_shape = jax.ShapeDtypeStruct((r, dim, c), BF16)
    sent, normed = pl.pallas_call(
        functools.partial(before_kernel, own),
        grid=(r // block,),
        in_specs=[tile] + [whole] * 4,
        out_specs=[
            pl.BlockSpec((devices, 2 * own, block, c), lambda i: (0, 0, i, 0)),
            pl.BlockSpec((block, dim, c), lambda i: (i, 0, 0)),
        ],
        out_shape=[lr_shape, normed_shape],
        scratch_shapes=[stacked, rows_scratch],
        compiler_params=memory(60),
        cost_estimate=cost(8 * hidden * dim * columns, pair, lr_shape),
        name="before",
    )(pair, *weights)

    n_i, n_k = rows * r, cols * c
    sent = pl.pallas_call(
        functools.partial(triangle_kernel, rows, cols),
        grid=(own,),
        in_specs=[
            pl.BlockSpec((devices, 1, r, c), lambda i: (0, i, 0, 0)),
            pl.BlockSpec((devices, 2, r, c), lambda i: (0, i, 0, 0)),
        ],
        out_specs=pl.BlockSpec((devices, 2, r, c), lambda i: (0, i, 0, 0)),
        out_shape=pltpu.HBM(lr_shape.shape, BF16),
        scratch_shapes=[pltpu.VMEM((n_i, n_k), BF16)] * 3,
        compiler_params=memory(32),
        name="triangle",
    )(g_all, exchange(sent))

    bit = (lax.axis_index("row") % 2).astype(jnp.int32).reshape(1)
    smem = pl.BlockSpec(memory_space=pltpu.SMEM)
    half_shape = jax.ShapeDtypeStruct((2 * hidden, dim), F32)
    half = pl.BlockSpec(half_shape.shape, lambda i: (0, 0))
    grads, kept, given = pl.pallas_call(
        functools.partial(gates_kernel, own),
        grid=(r // block,),
        in_specs=[
            smem,
            pl.BlockSpec(memory_space=pltpu.HBM),
            pl.BlockSpec((devices, 2 * own, block, c), lambda i: (0, 0, i, 0)),
        ]
        + [whole] * 4,
        out_specs=[by_hidden, half, half],
        out_shape=[jax.ShapeDtypeStruct((r, 4 * hidden, c), BF16), half_shape, half_shape],
        scratch_shapes=[
            stacked,
            pltpu.VMEM((4 * hidden, dim), F32),
            rows_scratch,
            pltpu.VMEM(normed_shape.shape, BF16),
            pltpu.SemaphoreType.DMA((r // block,)),
        ],
        compiler_params=memory(28),
        name="gates",
    )(bit, pltpu.with_memory_space_constraint(normed, pltpu.HBM), exchange(sent), *weights)

    def input_piece(piece, pair_gradient):
        held = [] if pair_gradient is None else [pair_gradient]
        at = pl.BlockSpec((r // pieces, c, dim), lambda i: (piece, 0, 0))
        return pl.pallas_call(
            functools.partial(input_kernel, piece * r // pieces),
            grid=(1,),
            in_specs=[
                pl.BlockSpec(memory_space=pltpu.HBM),
                pl.BlockSpec((r // pieces, 4 * hidden, c), lambda i: (piece, 0, 0)),
            ]
            + [whole] * 4
            + [pl.BlockSpec(memory_space=pl.ANY)] * len(held),
            out_specs=at,
            out_shape=jax.ShapeDtypeStruct(pair.shape, BF16),
            scratch_shapes=[
                pltpu.VMEM((dim, 4 * hidden), BF16),
                pltpu.VMEM((r // pieces, c, dim), BF16),
                pltpu.SemaphoreType.DMA,
            ],
            input_output_aliases={6: 0} if held else {},
            compiler_params=memory(16),
            cost_estimate=cost(8 * hidden * dim * columns // pieces, pair),
            name="input",
        )(pltpu.with_memory_space_constraint(pair, pltpu.HBM), grads, *weights, *held)

    steps = [("row", rows, 1 << i) for i in range(1, rows.bit_length() - 1)][::-1]
    steps += [("col", cols, 1 << i) for i in range(cols.bit_length() - 1)]
    pieces = min(pieces, len(steps))
    neighbours = [(i, i ^ 1) for i in range(rows)]
    pair_gradient = None
    mine = kept + lax.ppermute(given, "row", neighbours)
    for n, (axis, size, step) in enumerate(steps):
        other = lax.ppermute(mine, axis, [(i, i ^ step) for i in range(size)])
        if n < pieces:
            pair_gradient = input_piece(n, pair_gradient)
            other, pair_gradient = lax.optimization_barrier((other, pair_gradient))
        mine = mine + other
    weight_grads = pl.pallas_call(
        functools.partial(finish_kernel, 1.0 / n_i),
        in_specs=[smem, pl.BlockSpec(memory_space=pltpu.VMEM), pl.BlockSpec(memory_space=pltpu.VMEM)],
        out_shape=[jax.ShapeDtypeStruct((hidden, dim), F32)] * 4,
        compiler_params=memory(8),
        name="finish",
    )(bit, mine, lax.ppermute(mine, "row", neighbours))
    return (pair_gradient, *(g.T for g in weight_grads))


def solution(mesh):
    in_specs = (P("row", "col", None), P(None, "row", "col"), P(), P(), P(), P())
    out_specs = (P("row", "col", None), P(), P(), P(), P())
    sizes = (mesh.shape["row"], mesh.shape["col"])

    def shards(pair, cotangent, *weights):
        plain = all(size > 1 and size & (size - 1) == 0 for size in sizes)
        if plain and cotangent.shape[0] % (sizes[0] * sizes[1]) == 0:
            return channel_shards(sizes, pair, cotangent, *weights)
        return gathered_shards(pair, cotangent, *weights)

    return jax.shard_map(shards, mesh=mesh, in_specs=in_specs, out_specs=out_specs, check_vma=False)
```

```python
import functools

import jax
import jax.numpy as jnp
from jax import lax
from jax.experimental import pallas as pl
from jax.experimental.pallas import tpu as pltpu
from jax.sharding import PartitionSpec as P

BF16, F32 = jnp.bfloat16, jnp.float32


def gathered_shards(pair, cotangent, w_left, w_left_gate, w_right, w_right_gate):
    pair_f = pair.astype(jnp.float32)
    average = jnp.mean(pair_f, axis=-1, keepdims=True)
    centered_input = pair_f - average
    variance = jnp.mean(centered_input * centered_input, axis=-1, keepdims=True)
    inverse_scale = 1.0 / jnp.sqrt(variance + 1e-05)
    standardized_input = centered_input * inverse_scale
    normalized_input = standardized_input.astype(jnp.bfloat16)
    stacked = jnp.concatenate([w_left, w_left_gate, w_right, w_right_gate], axis=1)
    projected = jnp.einsum(
        "rcd,dh->hrc", normalized_input, stacked, preferred_element_type=jnp.float32
    )
    q_left, p_left, q_right, p_right = jnp.split(projected, 4, axis=0)
    s_left = jax.nn.sigmoid(p_left)
    s_right = jax.nn.sigmoid(p_right)
    left = (s_left * q_left).astype(jnp.bfloat16)
    right = (s_right * q_right).astype(jnp.bfloat16)
    g_chan, left_chan, right_chan = (
        lax.all_to_all(cotangent, "col", split_axis=0, concat_axis=2, tiled=True),
        lax.all_to_all(left, "col", split_axis=0, concat_axis=2, tiled=True),
        lax.all_to_all(right, "col", split_axis=0, concat_axis=2, tiled=True),
    )
    residues = g_chan.shape[2]
    g_columns = lax.all_to_all(g_chan, "row", split_axis=2, concat_axis=1, tiled=True)
    d_left = jnp.einsum(
        "hij,hjk->hik",
        g_chan,
        lax.all_gather(right_chan, "row", axis=1, tiled=True),
        preferred_element_type=jnp.float32,
    )
    d_right = jnp.einsum(
        "hij,hik->hjk",
        g_columns,
        lax.all_gather(left_chan, "row", axis=1, tiled=True),
        preferred_element_type=jnp.float32,
    )
    d_left_tile, d_right_tile = (
        lax.all_to_all(d_left.astype(jnp.bfloat16), "col", split_axis=2, concat_axis=0, tiled=True),
        lax.all_to_all(
            d_right.astype(jnp.bfloat16), "col", split_axis=2, concat_axis=0, tiled=True
        ),
    )
    grad_l = d_left_tile.astype(jnp.float32)
    grad_r = d_right_tile.astype(jnp.float32)
    e_left = grad_l * s_left
    f_left = grad_l * q_left * s_left * (1.0 - s_left)
    e_right = grad_r * s_right
    f_right = grad_r * q_right * s_right * (1.0 - s_right)
    grads = jnp.concatenate([e_left, f_left, e_right, f_right], axis=0).astype(jnp.bfloat16)
    local_weights = jnp.einsum(
        "rcd,hrc->dh", normalized_input, grads, preferred_element_type=jnp.float32
    )
    total_weights = lax.psum(local_weights, ("row", "col")) / residues
    normalized_gradient = jnp.einsum(
        "hrc,dh->rcd", grads, stacked, preferred_element_type=jnp.float32
    )
    gradient_mean = jnp.mean(normalized_gradient, axis=-1, keepdims=True)
    gradient_input_mean = jnp.mean(normalized_gradient * standardized_input, axis=-1, keepdims=True)
    pair_gradient = (
        (normalized_gradient - gradient_mean - standardized_input * gradient_input_mean)
        * inverse_scale
    ).astype(jnp.bfloat16)
    pieces_w = jnp.split(total_weights, 4, axis=1)
    return (pair_gradient, pieces_w[0], pieces_w[1], pieces_w[2], pieces_w[3])


NT = (((1,), (1,)), ((), ()))
TN = (((0,), (0,)), ((), ()))
NN = (((1,), (0,)), ((), ()))


def dot(a, b, dims=NN):
    return lax.dot_general(a, b, dims, preferred_element_type=F32)


def stack_weights(w_refs, w_ref):
    h = w_refs[0].shape[0]
    for i, ref in enumerate(w_refs):
        w_ref[pl.ds(i * h, h), :] = ref[...]


def layer_norm(x):
    x = x.T.astype(F32)
    centered = x - jnp.mean(x, axis=0, keepdims=True)
    variance = jnp.mean(centered * centered, axis=0, keepdims=True)
    inverse_scale = lax.rsqrt(variance + 1e-05)
    return centered * inverse_scale, inverse_scale


def project(w_ref, normed):
    projected = dot(w_ref[...], normed)
    h = projected.shape[0] // 4
    q_left, p_left, q_right, p_right = (projected[i * h : (i + 1) * h] for i in range(4))
    return q_left, jax.nn.sigmoid(p_left), q_right, jax.nn.sigmoid(p_right)


def put_lanes(ref, at, value):
    lanes = ref.shape[2]
    for i in range(ref.shape[0]):
        ref[i, at, :] = value[:, i * lanes : (i + 1) * lanes]


def get_lanes(ref, at):
    return jnp.concatenate([ref[i, at, :] for i in range(ref.shape[0])], axis=1)


def before_kernel(own, pair_ref, wl, wlg, wr, wrg, out_ref, normed_ref, w_ref, rows_ref):
    stack_weights((wl, wlg, wr, wrg), w_ref)
    h = wl.shape[0]
    rows = pair_ref.shape[0]
    pitch = rows + 1

    def one_row(r, carry):
        normed = layer_norm(pair_ref[r])[0].astype(BF16)
        normed_ref[r] = normed
        q_left, s_left, q_right, s_right = project(w_ref, normed)
        put_lanes(rows_ref, pl.ds(r, h, stride=pitch), s_left * q_left)
        put_lanes(rows_ref, pl.ds(r + h * pitch, h, stride=pitch), s_right * q_right)
        return carry

    lax.fori_loop(0, rows, one_row, 0, unroll=4)
    for channel in range(h):
        to, slot = channel // own, (channel % own) * 2
        for side in range(2):
            line = get_lanes(rows_ref, pl.ds((side * h + channel) * pitch, rows))
            out_ref[to, slot + side] = line.astype(BF16)


def triangle_kernel(rows, cols, cot_ref, in_ref, out_ref, g_ref, l_ref, r_ref):
    r, c = in_ref.shape[2:]
    for a in range(rows):
        for b in range(cols):
            at = (pl.ds(a * r, r), pl.ds(b * c, c))
            g_ref[at] = cot_ref[a * cols + b, 0]
            l_ref[at] = in_ref[a * cols + b, 0]
            r_ref[at] = in_ref[a * cols + b, 1]
    for i, (dims, ref) in enumerate(((NN, r_ref), (TN, l_ref))):
        d = dot(g_ref[...], ref[...], dims).astype(BF16)
        for a in range(rows):
            for b in range(cols):
                out_ref[a * cols + b, i] = d[a * r : (a + 1) * r, b * c : (b + 1) * c]


def gates_kernel(own, bit_ref, normed_hbm, d_ref, wl, wlg, wr, wrg, grads_ref, kept_ref, sent_ref, *scratch):
    w_ref, sums_ref, rows_ref, normed_ref, sems = scratch
    h = wl.shape[0]
    rows = grads_ref.shape[0]
    pitch = rows + 1
    step = pl.program_id(0)

    def copy(block):
        at = pl.ds(block * rows, rows)
        return pltpu.make_async_copy(normed_hbm.at[at], normed_ref.at[at], sems.at[block])

    @pl.when(step == 0)
    def _():
        for block in range(normed_ref.shape[0] // rows):
            copy(block).start()
        sums_ref[...] = jnp.zeros_like(sums_ref)
        stack_weights((wl, wlg, wr, wrg), w_ref)

    for channel in range(h):
        to, slot = channel // own, (channel % own) * 2
        for side in range(2):
            line = d_ref[to, slot + side].astype(F32)
            put_lanes(rows_ref, pl.ds((side * h + channel) * pitch, rows), line)

    copy(step).wait()

    together = 4 if rows % 4 == 0 else 1

    def some_rows(n, carry):
        all_grads, all_normed = [], []
        for i in range(together):
            r = n * together + i
            normed = normed_ref[step * rows + r]
            q_left, s_left, q_right, s_right = project(w_ref, normed)
            e_left = get_lanes(rows_ref, pl.ds(r, h, stride=pitch)) * s_left
            e_right = get_lanes(rows_ref, pl.ds(r + h * pitch, h, stride=pitch)) * s_right
            f_left = e_left * q_left * (1.0 - s_left)
            f_right = e_right * q_right * (1.0 - s_right)
            grads = jnp.concatenate([e_left, f_left, e_right, f_right], axis=0).astype(BF16)
            grads_ref[r] = grads
            all_grads.append(grads)
            all_normed.append(normed)
        sums_ref[...] += dot(
            jnp.concatenate(all_grads, axis=1), jnp.concatenate(all_normed, axis=1), NT
        )
        return carry

    lax.fori_loop(0, rows // together, some_rows, 0)

    @pl.when(step == pl.num_programs(0) - 1)
    def _():
        bit = bit_ref[0]
        kept_ref[...] = sums_ref[pl.ds(pl.multiple_of(bit * 2 * h, 2 * h), 2 * h), :]
        sent_ref[...] = sums_ref[pl.ds(pl.multiple_of((1 - bit) * 2 * h, 2 * h), 2 * h), :]


def input_kernel(start, pair_hbm, grads_ref, wl, wlg, wr, wrg, *refs):
    out_ref, back_ref, pair_ref, sem = refs[-4:]
    copy = pltpu.make_async_copy(pair_hbm.at[pl.ds(start, pair_ref.shape[0])], pair_ref, sem)
    copy.start()
    h = wl.shape[0]
    for i, ref in enumerate((wl, wlg, wr, wrg)):
        back_ref[:, pl.ds(i * h, h)] = ref[...].T

    copy.wait()

    def one_row(r, carry):
        standardized, inverse_scale = layer_norm(pair_ref[r])
        d_normed = dot(back_ref[...], grads_ref[r])
        mean = jnp.mean(d_normed, axis=0, keepdims=True)
        input_mean = jnp.mean(d_normed * standardized, axis=0, keepdims=True)
        moved = (d_normed - mean - standardized * input_mean) * inverse_scale
        out_ref[r] = moved.astype(BF16).T
        return carry

    lax.fori_loop(0, pair_ref.shape[0], one_row, 0, unroll=4)


def finish_kernel(scale, bit_ref, mine_ref, other_ref, *out_refs):
    h = out_refs[0].shape[0]
    for i, out_ref in enumerate(out_refs):
        at = pl.ds(i % 2 * h, h)
        mine = bit_ref[0] == i // 2
        out_ref[...] = jnp.where(mine, mine_ref[at, :], other_ref[at, :]) * scale


def channel_shards(sizes, pair, cotangent, *weights):
    rows, cols = sizes
    devices = rows * cols
    hidden, r, c = cotangent.shape
    dim = pair.shape[2]
    own = hidden // devices
    block = 16 if r % 16 == 0 else r
    pieces = 2 if r % 2 == 0 else 1
    weights = [w.T for w in weights]
    late_weights = [pltpu.with_memory_space_constraint(w, pltpu.HBM) for w in weights]
    whole = pl.BlockSpec((hidden, dim), lambda i: (0, 0))
    tile = pl.BlockSpec((block, c, dim), lambda i: (i, 0, 0))
    exchange = functools.partial(
        lax.all_to_all, axis_name=("row", "col"), split_axis=0, concat_axis=0, tiled=True
    )
    stacked = pltpu.VMEM((4 * hidden, dim), BF16)
    lanes = min(c, 128)
    rows_scratch = pltpu.VMEM((c // lanes, 2 * hidden * (block + 1), lanes), F32)

    def cost(flops, *arrays):
        moved = sum(a.size * a.dtype.itemsize for a in arrays)
        return pl.CostEstimate(flops=flops, bytes_accessed=moved, transcendentals=0)

    def memory(mib):
        return pltpu.CompilerParams(vmem_limit_bytes=mib * 2**20)

    columns = r * c
    lr_shape = jax.ShapeDtypeStruct((devices, 2 * own, r, c), BF16)
    by_hidden = pl.BlockSpec((block, 4 * hidden, c), lambda i: (i, 0, 0))
    g_all = exchange(cotangent.reshape(devices, own, r, c))
    normed_shape = jax.ShapeDtypeStruct((r, dim, c), BF16)
    sent, normed = pl.pallas_call(
        functools.partial(before_kernel, own),
        grid=(r // block,),
        in_specs=[tile] + [whole] * 4,
        out_specs=[
            pl.BlockSpec((devices, 2 * own, block, c), lambda i: (0, 0, i, 0)),
            pl.BlockSpec((block, dim, c), lambda i: (i, 0, 0)),
        ],
        out_shape=[lr_shape, normed_shape],
        scratch_shapes=[stacked, rows_scratch],
        compiler_params=memory(60),
        cost_estimate=cost(8 * hidden * dim * columns, pair, lr_shape),
        name="before",
    )(pair, *weights)

    n_i, n_k = rows * r, cols * c
    sent = pl.pallas_call(
        functools.partial(triangle_kernel, rows, cols),
        grid=(own,),
        in_specs=[
            pl.BlockSpec((devices, 1, r, c), lambda i: (0, i, 0, 0)),
            pl.BlockSpec((devices, 2, r, c), lambda i: (0, i, 0, 0)),
        ],
        out_specs=pl.BlockSpec((devices, 2, r, c), lambda i: (0, i, 0, 0)),
        out_shape=lr_shape,
        scratch_shapes=[pltpu.VMEM((n_i, n_k), BF16)] * 3,
        compiler_params=memory(32),
        name="triangle",
    )(g_all, exchange(sent))

    bit = (lax.axis_index("row") % 2).astype(jnp.int32).reshape(1)
    smem = pl.BlockSpec(memory_space=pltpu.SMEM)
    half_shape = jax.ShapeDtypeStruct((2 * hidden, dim), F32)
    half = pl.BlockSpec(half_shape.shape, lambda i: (0, 0))
    grads, kept, given = pl.pallas_call(
        functools.partial(gates_kernel, own),
        grid=(r // block,),
        in_specs=[
            smem,
            pl.BlockSpec(memory_space=pltpu.HBM),
            pl.BlockSpec((devices, 2 * own, block, c), lambda i: (0, 0, i, 0)),
        ]
        + [whole] * 4,
        out_specs=[by_hidden, half, half],
        out_shape=[jax.ShapeDtypeStruct((r, 4 * hidden, c), BF16), half_shape, half_shape],
        scratch_shapes=[
            stacked,
            pltpu.VMEM((4 * hidden, dim), F32),
            rows_scratch,
            pltpu.VMEM(normed_shape.shape, BF16),
            pltpu.SemaphoreType.DMA((r // block,)),
        ],
        compiler_params=memory(28),
        name="gates",
    )(bit, pltpu.with_memory_space_constraint(normed, pltpu.HBM), exchange(sent), *late_weights)

    def input_piece(piece, pair_gradient):
        held = [] if pair_gradient is None else [pair_gradient]
        at = pl.BlockSpec((r // pieces, c, dim), lambda i: (piece, 0, 0))
        return pl.pallas_call(
            functools.partial(input_kernel, piece * r // pieces),
            grid=(1,),
            in_specs=[
                pl.BlockSpec(memory_space=pltpu.HBM),
                pl.BlockSpec((r // pieces, 4 * hidden, c), lambda i: (piece, 0, 0)),
            ]
            + [whole] * 4
            + [pl.BlockSpec(memory_space=pl.ANY)] * len(held),
            out_specs=at,
            out_shape=jax.ShapeDtypeStruct(pair.shape, BF16),
            scratch_shapes=[
                pltpu.VMEM((dim, 4 * hidden), BF16),
                pltpu.VMEM((r // pieces, c, dim), BF16),
                pltpu.SemaphoreType.DMA,
            ],
            input_output_aliases={6: 0} if held else {},
            compiler_params=memory(16),
            cost_estimate=cost(8 * hidden * dim * columns // pieces, pair),
            name="input",
        )(pltpu.with_memory_space_constraint(pair, pltpu.HBM), grads, *late_weights, *held)

    steps = [("row", rows, 1 << i) for i in range(1, rows.bit_length() - 1)][::-1]
    steps += [("col", cols, 1 << i) for i in range(cols.bit_length() - 1)]
    pieces = min(pieces, len(steps))
    neighbours = [(i, i ^ 1) for i in range(rows)]
    pair_gradient = None
    mine = kept + lax.ppermute(given, "row", neighbours)
    for n, (axis, size, step) in enumerate(steps):
        other = lax.ppermute(mine, axis, [(i, i ^ step) for i in range(size)])
        if n < pieces:
            pair_gradient = input_piece(n, pair_gradient)
            other, pair_gradient = lax.optimization_barrier((other, pair_gradient))
        mine = mine + other
    weight_grads = pl.pallas_call(
        functools.partial(finish_kernel, 1.0 / n_i),
        in_specs=[smem, pl.BlockSpec(memory_space=pltpu.VMEM), pl.BlockSpec(memory_space=pltpu.VMEM)],
        out_shape=[jax.ShapeDtypeStruct((hidden, dim), F32)] * 4,
        compiler_params=memory(8),
        name="finish",
    )(bit, mine, lax.ppermute(mine, "row", neighbours))
    return (pair_gradient, *(g.T for g in weight_grads))


def solution(mesh):
    in_specs = (P("row", "col", None), P(None, "row", "col"), P(), P(), P(), P())
    out_specs = (P("row", "col", None), P(), P(), P(), P())
    sizes = (mesh.shape["row"], mesh.shape["col"])

    def shards(pair, cotangent, *weights):
        plain = all(size > 1 and size & (size - 1) == 0 for size in sizes)
        if plain and cotangent.shape[0] % (sizes[0] * sizes[1]) == 0:
            return channel_shards(sizes, pair, cotangent, *weights)
        return gathered_shards(pair, cotangent, *weights)

    return jax.shard_map(shards, mesh=mesh, in_specs=in_specs, out_specs=out_specs, check_vma=False)
```

```python
import functools

import jax
import jax.numpy as jnp
from jax import lax
from jax.experimental import pallas as pl
from jax.experimental.pallas import tpu as pltpu
from jax.sharding import PartitionSpec as P

BF16, F32 = jnp.bfloat16, jnp.float32


def gathered_shards(pair, cotangent, w_left, w_left_gate, w_right, w_right_gate):
    pair_f = pair.astype(jnp.float32)
    average = jnp.mean(pair_f, axis=-1, keepdims=True)
    centered_input = pair_f - average
    variance = jnp.mean(centered_input * centered_input, axis=-1, keepdims=True)
    inverse_scale = 1.0 / jnp.sqrt(variance + 1e-05)
    standardized_input = centered_input * inverse_scale
    normalized_input = standardized_input.astype(jnp.bfloat16)
    stacked = jnp.concatenate([w_left, w_left_gate, w_right, w_right_gate], axis=1)
    projected = jnp.einsum(
        "rcd,dh->hrc", normalized_input, stacked, preferred_element_type=jnp.float32
    )
    q_left, p_left, q_right, p_right = jnp.split(projected, 4, axis=0)
    s_left = jax.nn.sigmoid(p_left)
    s_right = jax.nn.sigmoid(p_right)
    left = (s_left * q_left).astype(jnp.bfloat16)
    right = (s_right * q_right).astype(jnp.bfloat16)
    g_chan, left_chan, right_chan = (
        lax.all_to_all(cotangent, "col", split_axis=0, concat_axis=2, tiled=True),
        lax.all_to_all(left, "col", split_axis=0, concat_axis=2, tiled=True),
        lax.all_to_all(right, "col", split_axis=0, concat_axis=2, tiled=True),
    )
    residues = g_chan.shape[2]
    g_columns = lax.all_to_all(g_chan, "row", split_axis=2, concat_axis=1, tiled=True)
    d_left = jnp.einsum(
        "hij,hjk->hik",
        g_chan,
        lax.all_gather(right_chan, "row", axis=1, tiled=True),
        preferred_element_type=jnp.float32,
    )
    d_right = jnp.einsum(
        "hij,hik->hjk",
        g_columns,
        lax.all_gather(left_chan, "row", axis=1, tiled=True),
        preferred_element_type=jnp.float32,
    )
    d_left_tile, d_right_tile = (
        lax.all_to_all(d_left.astype(jnp.bfloat16), "col", split_axis=2, concat_axis=0, tiled=True),
        lax.all_to_all(
            d_right.astype(jnp.bfloat16), "col", split_axis=2, concat_axis=0, tiled=True
        ),
    )
    grad_l = d_left_tile.astype(jnp.float32)
    grad_r = d_right_tile.astype(jnp.float32)
    e_left = grad_l * s_left
    f_left = grad_l * q_left * s_left * (1.0 - s_left)
    e_right = grad_r * s_right
    f_right = grad_r * q_right * s_right * (1.0 - s_right)
    grads = jnp.concatenate([e_left, f_left, e_right, f_right], axis=0).astype(jnp.bfloat16)
    local_weights = jnp.einsum(
        "rcd,hrc->dh", normalized_input, grads, preferred_element_type=jnp.float32
    )
    total_weights = lax.psum(local_weights, ("row", "col")) / residues
    normalized_gradient = jnp.einsum(
        "hrc,dh->rcd", grads, stacked, preferred_element_type=jnp.float32
    )
    gradient_mean = jnp.mean(normalized_gradient, axis=-1, keepdims=True)
    gradient_input_mean = jnp.mean(normalized_gradient * standardized_input, axis=-1, keepdims=True)
    pair_gradient = (
        (normalized_gradient - gradient_mean - standardized_input * gradient_input_mean)
        * inverse_scale
    ).astype(jnp.bfloat16)
    pieces_w = jnp.split(total_weights, 4, axis=1)
    return (pair_gradient, pieces_w[0], pieces_w[1], pieces_w[2], pieces_w[3])


NT = (((1,), (1,)), ((), ()))
TN = (((0,), (0,)), ((), ()))
NN = (((1,), (0,)), ((), ()))


def dot(a, b, dims=NN):
    return lax.dot_general(a, b, dims, preferred_element_type=F32)


def stack_weights(w_refs, w_ref):
    h = w_refs[0].shape[0]
    for i, ref in enumerate(w_refs):
        w_ref[pl.ds(i * h, h), :] = ref[...]


def layer_norm(x):
    x = x.T.astype(F32)
    centered = x - jnp.mean(x, axis=0, keepdims=True)
    variance = jnp.mean(centered * centered, axis=0, keepdims=True)
    inverse_scale = lax.rsqrt(variance + 1e-05)
    return centered * inverse_scale, inverse_scale


def project(w_ref, normed):
    projected = dot(w_ref[...], normed)
    h = projected.shape[0] // 4
    q_left, p_left, q_right, p_right = (projected[i * h : (i + 1) * h] for i in range(4))
    return q_left, jax.nn.sigmoid(p_left), q_right, jax.nn.sigmoid(p_right)


def put_lanes(ref, at, value):
    lanes = ref.shape[2]
    for i in range(ref.shape[0]):
        ref[i, at, :] = value[:, i * lanes : (i + 1) * lanes]


def get_lanes(ref, at):
    return jnp.concatenate([ref[i, at, :] for i in range(ref.shape[0])], axis=1)


def before_kernel(own, pair_ref, wl, wlg, wr, wrg, out_ref, normed_ref, w_ref, rows_ref):
    stack_weights((wl, wlg, wr, wrg), w_ref)
    h = wl.shape[0]
    rows = pair_ref.shape[0]
    pitch = rows + 1

    def one_row(r, carry):
        normed = layer_norm(pair_ref[r])[0].astype(BF16)
        normed_ref[r] = normed
        q_left, s_left, q_right, s_right = project(w_ref, normed)
        put_lanes(rows_ref, pl.ds(r, h, stride=pitch), s_left * q_left)
        put_lanes(rows_ref, pl.ds(r + h * pitch, h, stride=pitch), s_right * q_right)
        return carry

    lax.fori_loop(0, rows, one_row, 0, unroll=4)
    for channel in range(h):
        to, slot = channel // own, (channel % own) * 2
        for side in range(2):
            line = get_lanes(rows_ref, pl.ds((side * h + channel) * pitch, rows))
            out_ref[to, slot + side] = line.astype(BF16)


def triangle_kernel(rows, cols, cot_ref, in_ref, out_ref, g_ref, l_ref, r_ref):
    r, c = in_ref.shape[2:]
    for a in range(rows):
        for b in range(cols):
            at = (pl.ds(a * r, r), pl.ds(b * c, c))
            g_ref[at] = cot_ref[a * cols + b, 0]
            l_ref[at] = in_ref[a * cols + b, 0]
            r_ref[at] = in_ref[a * cols + b, 1]
    for i, (dims, ref) in enumerate(((NN, r_ref), (TN, l_ref))):
        d = dot(g_ref[...], ref[...], dims).astype(BF16)
        for a in range(rows):
            for b in range(cols):
                out_ref[a * cols + b, i] = d[a * r : (a + 1) * r, b * c : (b + 1) * c]


def gates_kernel(own, normed_hbm, d_ref, wl, wlg, wr, wrg, grads_ref, kept_ref, sent_ref, *scratch):
    w_ref, sums_ref, rows_ref, normed_ref, sem = scratch
    copy = pltpu.make_async_copy(normed_hbm, normed_ref, sem)
    copy.start()
    h = wl.shape[0]
    rows = grads_ref.shape[0]
    pitch = rows + 1
    together = 4 if rows % 4 == 0 else 1
    stack_weights((wl, wlg, wr, wrg), w_ref)
    sums_ref[...] = jnp.zeros_like(sums_ref)

    for channel in range(h):
        to, slot = channel // own, (channel % own) * 2
        for side in range(2):
            line = d_ref[to, slot + side].astype(F32)
            put_lanes(rows_ref, pl.ds((side * h + channel) * pitch, rows), line)

    copy.wait()

    def some_rows(n, carry):
        all_grads, all_normed = [], []
        for i in range(together):
            r = n * together + i
            normed = normed_ref[r]
            q_left, s_left, q_right, s_right = project(w_ref, normed)
            e_left = get_lanes(rows_ref, pl.ds(r, h, stride=pitch)) * s_left
            e_right = get_lanes(rows_ref, pl.ds(r + h * pitch, h, stride=pitch)) * s_right
            f_left = e_left * q_left * (1.0 - s_left)
            f_right = e_right * q_right * (1.0 - s_right)
            grads = jnp.concatenate([e_left, f_left, e_right, f_right], axis=0).astype(BF16)
            grads_ref[r] = grads
            all_grads.append(grads)
            all_normed.append(normed)
        sums_ref[...] += dot(
            jnp.concatenate(all_grads, axis=1), jnp.concatenate(all_normed, axis=1), NT
        )
        return carry

    lax.fori_loop(0, rows // together, some_rows, 0)
    bit = lax.rem(lax.axis_index("row"), 2)
    kept_ref[...] = sums_ref[pl.ds(pl.multiple_of(bit * 2 * h, 2 * h), 2 * h), :]
    sent_ref[...] = sums_ref[pl.ds(pl.multiple_of((1 - bit) * 2 * h, 2 * h), 2 * h), :]


def input_kernel(start, pair_hbm, grads_ref, wl, wlg, wr, wrg, *refs):
    out_hbm, back_ref, pair_ref, out_ref, in_sem, out_sems = refs[-6:]
    rows = pair_ref.shape[0]
    come = pltpu.make_async_copy(pair_hbm.at[pl.ds(start, rows)], pair_ref, in_sem)
    come.start()
    h = wl.shape[0]
    for i, ref in enumerate((wl, wlg, wr, wrg)):
        back_ref[:, pl.ds(i * h, h)] = ref[...].T
    come.wait()

    def one_row(r, carry):
        standardized, inverse_scale = layer_norm(pair_ref[r])
        d_normed = dot(back_ref[...], grads_ref[start + r])
        mean = jnp.mean(d_normed, axis=0, keepdims=True)
        input_mean = jnp.mean(d_normed * standardized, axis=0, keepdims=True)
        moved = (d_normed - mean - standardized * input_mean) * inverse_scale
        out_ref[r] = moved.astype(BF16).T
        return carry

    parts = out_sems.shape[0]
    count = rows // parts
    gone = []
    for part in range(parts):
        lax.fori_loop(part * count, (part + 1) * count, one_row, 0, unroll=4)
        at = pl.ds(part * count, count)
        to = out_hbm.at[pl.ds(start + part * count, count)]
        gone.append(pltpu.make_async_copy(out_ref.at[at], to, out_sems.at[part]))
        gone[-1].start()
    for copy in gone:
        copy.wait()


def finish_kernel(scale, mine_ref, other_ref, *out_refs):
    h = out_refs[0].shape[0]
    bit = lax.rem(lax.axis_index("row"), 2)
    for i, out_ref in enumerate(out_refs):
        at = pl.ds(i % 2 * h, h)
        mine = bit == i // 2
        out_ref[...] = jnp.where(mine, mine_ref[at, :], other_ref[at, :]) * scale


def channel_shards(sizes, pair, cotangent, *weights):
    rows, cols = sizes
    devices = rows * cols
    hidden, r, c = cotangent.shape
    dim = pair.shape[2]
    own = hidden // devices
    block = 16 if r % 16 == 0 else r
    pieces = 2 if r % 2 == 0 else 1
    weights = [w.T for w in weights]
    whole = pl.BlockSpec((hidden, dim), lambda i: (0, 0))
    tile = pl.BlockSpec((block, c, dim), lambda i: (i, 0, 0))
    exchange = functools.partial(
        lax.all_to_all, axis_name=("row", "col"), split_axis=0, concat_axis=0, tiled=True
    )
    stacked = pltpu.VMEM((4 * hidden, dim), BF16)
    lanes = min(c, 128)
    rows_scratch = pltpu.VMEM((c // lanes, (2 * hidden + 1) * (block + 1), lanes), F32)

    def cost(flops, *arrays):
        moved = sum(a.size * a.dtype.itemsize for a in arrays)
        return pl.CostEstimate(flops=flops, bytes_accessed=moved, transcendentals=0)

    def memory(mib):
        return pltpu.CompilerParams(vmem_limit_bytes=mib * 2**20)

    columns = r * c
    lr_shape = jax.ShapeDtypeStruct((devices, 2 * own, r, c), BF16)
    g_all = exchange(cotangent.reshape(devices, own, r, c))
    normed_shape = jax.ShapeDtypeStruct((r, dim, c), BF16)
    sent, normed = pl.pallas_call(
        functools.partial(before_kernel, own),
        grid=(r // block,),
        in_specs=[tile] + [whole] * 4,
        out_specs=[
            pl.BlockSpec((devices, 2 * own, block, c), lambda i: (0, 0, i, 0)),
            pl.BlockSpec((block, dim, c), lambda i: (i, 0, 0)),
        ],
        out_shape=[lr_shape, normed_shape],
        scratch_shapes=[stacked, rows_scratch],
        compiler_params=memory(60),
        cost_estimate=cost(8 * hidden * dim * columns, pair, lr_shape),
        name="before",
    )(pair, *weights)

    n_i, n_k = rows * r, cols * c
    sent = pl.pallas_call(
        functools.partial(triangle_kernel, rows, cols),
        grid=(own,),
        in_specs=[
            pl.BlockSpec((devices, 1, r, c), lambda i: (0, i, 0, 0)),
            pl.BlockSpec((devices, 2, r, c), lambda i: (0, i, 0, 0)),
        ],
        out_specs=pl.BlockSpec((devices, 2, r, c), lambda i: (0, i, 0, 0)),
        out_shape=lr_shape,
        scratch_shapes=[pltpu.VMEM((n_i, n_k), BF16)] * 3,
        compiler_params=memory(32),
        name="triangle",
    )(g_all, exchange(sent))

    vmem = pl.BlockSpec(memory_space=pltpu.VMEM)
    hbm = pl.BlockSpec(memory_space=pltpu.HBM)
    half_shape = jax.ShapeDtypeStruct((2 * hidden, dim), F32)
    grads, kept, given = pl.pallas_call(
        functools.partial(gates_kernel, own),
        in_specs=[hbm] + [vmem] * 5,
        out_specs=[vmem] * 3,
        out_shape=[jax.ShapeDtypeStruct((r, 4 * hidden, c), BF16), half_shape, half_shape],
        scratch_shapes=[
            stacked,
            pltpu.VMEM((4 * hidden, dim), F32),
            pltpu.VMEM((c // lanes, (2 * hidden + 1) * (r + 1), lanes), F32),
            pltpu.VMEM(normed_shape.shape, BF16),
            pltpu.SemaphoreType.DMA,
        ],
        compiler_params=memory(28),
        name="gates",
    )(pltpu.with_memory_space_constraint(normed, pltpu.HBM), exchange(sent), *weights)

    def input_piece(piece, pair_gradient):
        held = [] if pair_gradient is None else [pair_gradient]
        count = r // pieces
        return pl.pallas_call(
            functools.partial(input_kernel, piece * count),
            in_specs=[hbm] + [vmem] * 5 + [hbm] * len(held),
            out_specs=hbm,
            out_shape=jax.ShapeDtypeStruct(pair.shape, BF16),
            scratch_shapes=[
                pltpu.VMEM((dim, 4 * hidden), BF16),
                pltpu.VMEM((count, c, dim), BF16),
                pltpu.VMEM((count, c, dim), BF16),
                pltpu.SemaphoreType.DMA,
                pltpu.SemaphoreType.DMA((2 if count % 8 == 0 else 1,)),
            ],
            input_output_aliases={6: 0} if held else {},
            compiler_params=memory(16),
            cost_estimate=cost(8 * hidden * dim * columns // pieces, pair),
            name="input",
        )(pltpu.with_memory_space_constraint(pair, pltpu.HBM), grads, *weights, *held)

    steps = [("row", rows, 1 << i) for i in range(1, rows.bit_length() - 1)][::-1]
    steps += [("col", cols, 1 << i) for i in range(cols.bit_length() - 1)]
    pieces = min(pieces, len(steps))
    neighbours = [(i, i ^ 1) for i in range(rows)]
    pair_gradient = None
    mine = kept + lax.ppermute(given, "row", neighbours)
    for n, (axis, size, step) in enumerate(steps):
        other = lax.ppermute(mine, axis, [(i, i ^ step) for i in range(size)])
        if n < pieces:
            pair_gradient = input_piece(n, pair_gradient)
            other, pair_gradient = lax.optimization_barrier((other, pair_gradient))
        mine = mine + other
    weight_grads = pl.pallas_call(
        functools.partial(finish_kernel, 1.0 / n_i),
        in_specs=[vmem, vmem],
        out_shape=[jax.ShapeDtypeStruct((hidden, dim), F32)] * 4,
        compiler_params=memory(8),
        name="finish",
    )(mine, lax.ppermute(mine, "row", neighbours))
    return (pair_gradient, *(g.T for g in weight_grads))


def solution(mesh):
    in_specs = (P("row", "col", None), P(None, "row", "col"), P(), P(), P(), P())
    out_specs = (P("row", "col", None), P(), P(), P(), P())
    sizes = (mesh.shape["row"], mesh.shape["col"])

    def shards(pair, cotangent, *weights):
        plain = all(size > 1 and size & (size - 1) == 0 for size in sizes)
        if plain and cotangent.shape[0] % (sizes[0] * sizes[1]) == 0:
            return channel_shards(sizes, pair, cotangent, *weights)
        return gathered_shards(pair, cotangent, *weights)

    return jax.shard_map(shards, mesh=mesh, in_specs=in_specs, out_specs=out_specs, check_vma=False)
```

```python
import functools

import jax
import jax.numpy as jnp
from jax import lax
from jax.experimental import pallas as pl
from jax.experimental.pallas import tpu as pltpu
from jax.sharding import PartitionSpec as P

BF16, F32 = jnp.bfloat16, jnp.float32


def gathered_shards(pair, cotangent, w_left, w_left_gate, w_right, w_right_gate):
    pair_f = pair.astype(jnp.float32)
    average = jnp.mean(pair_f, axis=-1, keepdims=True)
    centered_input = pair_f - average
    variance = jnp.mean(centered_input * centered_input, axis=-1, keepdims=True)
    inverse_scale = 1.0 / jnp.sqrt(variance + 1e-05)
    standardized_input = centered_input * inverse_scale
    normalized_input = standardized_input.astype(jnp.bfloat16)
    stacked = jnp.concatenate([w_left, w_left_gate, w_right, w_right_gate], axis=1)
    projected = jnp.einsum(
        "rcd,dh->hrc", normalized_input, stacked, preferred_element_type=jnp.float32
    )
    q_left, p_left, q_right, p_right = jnp.split(projected, 4, axis=0)
    s_left = jax.nn.sigmoid(p_left)
    s_right = jax.nn.sigmoid(p_right)
    left = (s_left * q_left).astype(jnp.bfloat16)
    right = (s_right * q_right).astype(jnp.bfloat16)
    g_chan, left_chan, right_chan = (
        lax.all_to_all(cotangent, "col", split_axis=0, concat_axis=2, tiled=True),
        lax.all_to_all(left, "col", split_axis=0, concat_axis=2, tiled=True),
        lax.all_to_all(right, "col", split_axis=0, concat_axis=2, tiled=True),
    )
    residues = g_chan.shape[2]
    g_columns = lax.all_to_all(g_chan, "row", split_axis=2, concat_axis=1, tiled=True)
    d_left = jnp.einsum(
        "hij,hjk->hik",
        g_chan,
        lax.all_gather(right_chan, "row", axis=1, tiled=True),
        preferred_element_type=jnp.float32,
    )
    d_right = jnp.einsum(
        "hij,hik->hjk",
        g_columns,
        lax.all_gather(left_chan, "row", axis=1, tiled=True),
        preferred_element_type=jnp.float32,
    )
    d_left_tile, d_right_tile = (
        lax.all_to_all(d_left.astype(jnp.bfloat16), "col", split_axis=2, concat_axis=0, tiled=True),
        lax.all_to_all(
            d_right.astype(jnp.bfloat16), "col", split_axis=2, concat_axis=0, tiled=True
        ),
    )
    grad_l = d_left_tile.astype(jnp.float32)
    grad_r = d_right_tile.astype(jnp.float32)
    e_left = grad_l * s_left
    f_left = grad_l * q_left * s_left * (1.0 - s_left)
    e_right = grad_r * s_right
    f_right = grad_r * q_right * s_right * (1.0 - s_right)
    grads = jnp.concatenate([e_left, f_left, e_right, f_right], axis=0).astype(jnp.bfloat16)
    local_weights = jnp.einsum(
        "rcd,hrc->dh", normalized_input, grads, preferred_element_type=jnp.float32
    )
    total_weights = lax.psum(local_weights, ("row", "col")) / residues
    normalized_gradient = jnp.einsum(
        "hrc,dh->rcd", grads, stacked, preferred_element_type=jnp.float32
    )
    gradient_mean = jnp.mean(normalized_gradient, axis=-1, keepdims=True)
    gradient_input_mean = jnp.mean(normalized_gradient * standardized_input, axis=-1, keepdims=True)
    pair_gradient = (
        (normalized_gradient - gradient_mean - standardized_input * gradient_input_mean)
        * inverse_scale
    ).astype(jnp.bfloat16)
    pieces_w = jnp.split(total_weights, 4, axis=1)
    return (pair_gradient, pieces_w[0], pieces_w[1], pieces_w[2], pieces_w[3])


NT = (((1,), (1,)), ((), ()))
TN = (((0,), (0,)), ((), ()))
NN = (((1,), (0,)), ((), ()))


def dot(a, b, dims=NN):
    return lax.dot_general(a, b, dims, preferred_element_type=F32)


def stack_weights(w_refs, w_ref):
    h = w_refs[0].shape[0]
    for i, ref in enumerate(w_refs):
        w_ref[pl.ds(i * h, h), :] = ref[...]


def layer_norm(x):
    x = x.T.astype(F32)
    centered = x - jnp.mean(x, axis=0, keepdims=True)
    variance = jnp.mean(centered * centered, axis=0, keepdims=True)
    inverse_scale = lax.rsqrt(variance + 1e-05)
    return centered * inverse_scale, inverse_scale


def project(w_ref, normed):
    projected = dot(w_ref[...], normed)
    h = projected.shape[0] // 4
    q_left, p_left, q_right, p_right = (projected[i * h : (i + 1) * h] for i in range(4))
    return q_left, jax.nn.sigmoid(p_left), q_right, jax.nn.sigmoid(p_right)


def put_lanes(ref, at, value):
    lanes = ref.shape[2]
    for i in range(ref.shape[0]):
        ref[i, at, :] = value[:, i * lanes : (i + 1) * lanes]


def get_lanes(ref, at):
    return jnp.concatenate([ref[i, at, :] for i in range(ref.shape[0])], axis=1)


def before_kernel(own, pair_ref, wl, wlg, wr, wrg, out_ref, normed_ref, w_ref, rows_ref):
    stack_weights((wl, wlg, wr, wrg), w_ref)
    h = wl.shape[0]
    rows = pair_ref.shape[0]
    pitch = rows + 1

    def one_row(r, carry):
        normed = layer_norm(pair_ref[r])[0].astype(BF16)
        normed_ref[r] = normed
        q_left, s_left, q_right, s_right = project(w_ref, normed)
        put_lanes(rows_ref, pl.ds(r, h, stride=pitch), s_left * q_left)
        put_lanes(rows_ref, pl.ds(r + h * pitch, h, stride=pitch), s_right * q_right)
        return carry

    lax.fori_loop(0, rows, one_row, 0, unroll=4)
    for channel in range(h):
        to, slot = channel // own, (channel % own) * 2
        for side in range(2):
            line = get_lanes(rows_ref, pl.ds((side * h + channel) * pitch, rows))
            out_ref[to, slot + side] = line.astype(BF16)


def triangle_kernel(rows, cols, cot_ref, in_ref, out_ref, g_ref, l_ref, r_ref):
    r, c = in_ref.shape[2:]
    for a in range(rows):
        for b in range(cols):
            at = (pl.ds(a * r, r), pl.ds(b * c, c))
            g_ref[at] = cot_ref[a * cols + b, 0]
            l_ref[at] = in_ref[a * cols + b, 0]
            r_ref[at] = in_ref[a * cols + b, 1]
    for i, (dims, ref) in enumerate(((NN, r_ref), (TN, l_ref))):
        d = dot(g_ref[...], ref[...], dims).astype(BF16)
        for a in range(rows):
            for b in range(cols):
                out_ref[a * cols + b, i] = d[a * r : (a + 1) * r, b * c : (b + 1) * c]


def gates_kernel(own, normed_hbm, d_ref, wl, wlg, wr, wrg, grads_ref, kept_ref, sent_ref, *scratch):
    w_ref, sums_ref, rows_ref, normed_ref, sem = scratch
    copy = pltpu.make_async_copy(normed_hbm, normed_ref, sem)
    copy.start()
    h = wl.shape[0]
    rows = grads_ref.shape[0]
    pitch = rows + 1
    together = 4 if rows % 4 == 0 else 1
    stack_weights((wl, wlg, wr, wrg), w_ref)
    sums_ref[...] = jnp.zeros_like(sums_ref)

    for channel in range(h):
        to, slot = channel // own, (channel % own) * 2
        for side in range(2):
            line = d_ref[to, slot + side].astype(F32)
            put_lanes(rows_ref, pl.ds((side * h + channel) * pitch, rows), line)

    copy.wait()

    def some_rows(n, carry):
        all_grads, all_normed = [], []
        for i in range(together):
            r = n * together + i
            normed = normed_ref[r]
            q_left, s_left, q_right, s_right = project(w_ref, normed)
            e_left = get_lanes(rows_ref, pl.ds(r, h, stride=pitch)) * s_left
            e_right = get_lanes(rows_ref, pl.ds(r + h * pitch, h, stride=pitch)) * s_right
            f_left = e_left * q_left * (1.0 - s_left)
            f_right = e_right * q_right * (1.0 - s_right)
            grads = jnp.concatenate([e_left, f_left, e_right, f_right], axis=0).astype(BF16)
            grads_ref[r] = grads
            all_grads.append(grads)
            all_normed.append(normed)
        sums_ref[...] += dot(
            jnp.concatenate(all_grads, axis=1), jnp.concatenate(all_normed, axis=1), NT
        )
        return carry

    lax.fori_loop(0, rows // together, some_rows, 0)
    bit = lax.rem(lax.axis_index("row"), 2)
    kept_ref[...] = sums_ref[pl.ds(pl.multiple_of(bit * 2 * h, 2 * h), 2 * h), :]
    sent_ref[...] = sums_ref[pl.ds(pl.multiple_of((1 - bit) * 2 * h, 2 * h), 2 * h), :]


def input_kernel(start, pair_hbm, grads_ref, wl, wlg, wr, wrg, *refs):
    out_hbm, back_ref, pair_ref, out_ref, in_sem, out_sems = refs[-6:]
    rows = pair_ref.shape[0]
    come = pltpu.make_async_copy(pair_hbm.at[pl.ds(start, rows)], pair_ref, in_sem)
    come.start()
    h = wl.shape[0]
    for i, ref in enumerate((wl, wlg, wr, wrg)):
        back_ref[:, pl.ds(i * h, h)] = ref[...].T
    come.wait()

    def one_row(r, carry):
        standardized, inverse_scale = layer_norm(pair_ref[r])
        d_normed = dot(back_ref[...], grads_ref[start + r])
        mean = jnp.mean(d_normed, axis=0, keepdims=True)
        input_mean = jnp.mean(d_normed * standardized, axis=0, keepdims=True)
        moved = (d_normed - mean - standardized * input_mean) * inverse_scale
        out_ref[r] = moved.astype(BF16).T
        return carry

    parts = out_sems.shape[0]
    count = rows // parts
    gone = []
    for part in range(parts):
        lax.fori_loop(part * count, (part + 1) * count, one_row, 0, unroll=4)
        at = pl.ds(part * count, count)
        to = out_hbm.at[pl.ds(start + part * count, count)]
        gone.append(pltpu.make_async_copy(out_ref.at[at], to, out_sems.at[part]))
        gone[-1].start()
    for copy in gone:
        copy.wait()


def finish_kernel(scale, mine_ref, other_ref, *out_refs):
    h = out_refs[0].shape[0]
    bit = lax.rem(lax.axis_index("row"), 2)
    for i, out_ref in enumerate(out_refs):
        at = pl.ds(i % 2 * h, h)
        mine = bit == i // 2
        out_ref[...] = jnp.where(mine, mine_ref[at, :], other_ref[at, :]) * scale


def channel_shards(sizes, pair, cotangent, *weights):
    rows, cols = sizes
    devices = rows * cols
    hidden, r, c = cotangent.shape
    dim = pair.shape[2]
    own = hidden // devices
    block = 16 if r % 16 == 0 else r
    pieces = 2 if r % 2 == 0 else 1
    weights = [w.T for w in weights]
    whole = pl.BlockSpec((hidden, dim), lambda i: (0, 0))
    tile = pl.BlockSpec((block, c, dim), lambda i: (i, 0, 0))
    exchange = functools.partial(
        lax.all_to_all, axis_name=("row", "col"), split_axis=0, concat_axis=0, tiled=True
    )
    stacked = pltpu.VMEM((4 * hidden, dim), BF16)
    lanes = min(c, 128)
    rows_scratch = pltpu.VMEM((c // lanes, (2 * hidden + 1) * (block + 1), lanes), F32)

    def cost(flops, *arrays):
        moved = sum(a.size * a.dtype.itemsize for a in arrays)
        return pl.CostEstimate(flops=flops, bytes_accessed=moved, transcendentals=0)

    def memory(mib):
        return pltpu.CompilerParams(vmem_limit_bytes=mib * 2**20)

    columns = r * c
    lr_shape = jax.ShapeDtypeStruct((devices, 2 * own, r, c), BF16)
    g_all = exchange(cotangent.reshape(devices, own, r, c))
    normed_shape = jax.ShapeDtypeStruct((r, dim, c), BF16)
    sent, normed = pl.pallas_call(
        functools.partial(before_kernel, own),
        grid=(r // block,),
        in_specs=[tile] + [whole] * 4,
        out_specs=[
            pl.BlockSpec((devices, 2 * own, block, c), lambda i: (0, 0, i, 0)),
            pl.BlockSpec((block, dim, c), lambda i: (i, 0, 0)),
        ],
        out_shape=[lr_shape, normed_shape],
        scratch_shapes=[stacked, rows_scratch],
        compiler_params=memory(60),
        cost_estimate=cost(8 * hidden * dim * columns, pair, lr_shape),
        name="before",
    )(pair, *weights)

    n_i, n_k = rows * r, cols * c
    sent = pl.pallas_call(
        functools.partial(triangle_kernel, rows, cols),
        grid=(own,),
        in_specs=[
            pl.BlockSpec((devices, 1, r, c), lambda i: (0, i, 0, 0)),
            pl.BlockSpec((devices, 2, r, c), lambda i: (0, i, 0, 0)),
        ],
        out_specs=pl.BlockSpec((devices, 2, r, c), lambda i: (0, i, 0, 0)),
        out_shape=lr_shape,
        scratch_shapes=[pltpu.VMEM((n_i, n_k), BF16)] * 3,
        compiler_params=memory(32),
        name="triangle",
    )(g_all, exchange(sent))

    vmem = pl.BlockSpec(memory_space=pltpu.VMEM)
    hbm = pl.BlockSpec(memory_space=pltpu.HBM)
    half_shape = jax.ShapeDtypeStruct((2 * hidden, dim), F32)
    grads, kept, given = pl.pallas_call(
        functools.partial(gates_kernel, own),
        in_specs=[hbm] + [vmem] * 5,
        out_specs=[vmem] * 3,
        out_shape=[jax.ShapeDtypeStruct((r, 4 * hidden, c), BF16), half_shape, half_shape],
        scratch_shapes=[
            stacked,
            pltpu.VMEM((4 * hidden, dim), F32),
            pltpu.VMEM((c // lanes, (2 * hidden + 1) * (r + 1), lanes), F32),
            pltpu.VMEM(normed_shape.shape, BF16),
            pltpu.SemaphoreType.DMA,
        ],
        compiler_params=memory(28),
        name="gates",
    )(pltpu.with_memory_space_constraint(normed, pltpu.HBM), exchange(sent), *weights)

    def input_piece(piece, pair_gradient):
        held = [] if pair_gradient is None else [pair_gradient]
        count = r // pieces
        return pl.pallas_call(
            functools.partial(input_kernel, piece * count),
            in_specs=[hbm] + [vmem] * 5 + [hbm] * len(held),
            out_specs=hbm,
            out_shape=jax.ShapeDtypeStruct(pair.shape, BF16),
            scratch_shapes=[
                pltpu.VMEM((dim, 4 * hidden), BF16),
                pltpu.VMEM((count, c, dim), BF16),
                pltpu.VMEM((count, c, dim), BF16),
                pltpu.SemaphoreType.DMA,
                pltpu.SemaphoreType.DMA((2 if count % 8 == 0 else 1,)),
            ],
            input_output_aliases={6: 0} if held else {},
            compiler_params=memory(16),
            cost_estimate=cost(8 * hidden * dim * columns // pieces, pair),
            name="input",
        )(pltpu.with_memory_space_constraint(pair, pltpu.HBM), grads, *weights, *held)

    neighbours = [(i, i ^ 1) for i in range(rows)]
    alike = [
        [i * cols + j for i in range(bit, rows, 2) for j in range(cols)] for bit in range(2)
    ]
    pair_gradient, summed = None, []
    mine = kept + lax.ppermute(given, "row", neighbours)
    for piece, part in enumerate(jnp.split(mine, pieces, axis=0)):
        if summed:
            part = lax.optimization_barrier((part, summed[-1]))[0]
        part = lax.psum(part, ("row", "col"), axis_index_groups=alike)
        pair_gradient = input_piece(piece, pair_gradient)
        part, pair_gradient = lax.optimization_barrier((part, pair_gradient))
        summed.append(part)
    mine = jnp.concatenate(summed, axis=0)
    weight_grads = pl.pallas_call(
        functools.partial(finish_kernel, 1.0 / n_i),
        in_specs=[vmem, vmem],
        out_shape=[jax.ShapeDtypeStruct((hidden, dim), F32)] * 4,
        compiler_params=memory(8),
        name="finish",
    )(mine, lax.ppermute(mine, "row", neighbours))
    return (pair_gradient, *(g.T for g in weight_grads))


def solution(mesh):
    in_specs = (P("row", "col", None), P(None, "row", "col"), P(), P(), P(), P())
    out_specs = (P("row", "col", None), P(), P(), P(), P())
    sizes = (mesh.shape["row"], mesh.shape["col"])

    def shards(pair, cotangent, *weights):
        plain = all(size > 1 and size & (size - 1) == 0 for size in sizes)
        if plain and cotangent.shape[0] % (sizes[0] * sizes[1]) == 0:
            return channel_shards(sizes, pair, cotangent, *weights)
        return gathered_shards(pair, cotangent, *weights)

    return jax.shard_map(shards, mesh=mesh, in_specs=in_specs, out_specs=out_specs, check_vma=False)
```

```python
import functools

import jax
import jax.numpy as jnp
from jax import lax
from jax.experimental import pallas as pl
from jax.experimental.pallas import tpu as pltpu
from jax.sharding import PartitionSpec as P

BF16, F32 = jnp.bfloat16, jnp.float32


def gathered_shards(pair, cotangent, w_left, w_left_gate, w_right, w_right_gate):
    pair_f = pair.astype(jnp.float32)
    average = jnp.mean(pair_f, axis=-1, keepdims=True)
    centered_input = pair_f - average
    variance = jnp.mean(centered_input * centered_input, axis=-1, keepdims=True)
    inverse_scale = 1.0 / jnp.sqrt(variance + 1e-05)
    standardized_input = centered_input * inverse_scale
    normalized_input = standardized_input.astype(jnp.bfloat16)
    stacked = jnp.concatenate([w_left, w_left_gate, w_right, w_right_gate], axis=1)
    projected = jnp.einsum(
        "rcd,dh->hrc", normalized_input, stacked, preferred_element_type=jnp.float32
    )
    q_left, p_left, q_right, p_right = jnp.split(projected, 4, axis=0)
    s_left = jax.nn.sigmoid(p_left)
    s_right = jax.nn.sigmoid(p_right)
    left = (s_left * q_left).astype(jnp.bfloat16)
    right = (s_right * q_right).astype(jnp.bfloat16)
    g_chan, left_chan, right_chan = (
        lax.all_to_all(cotangent, "col", split_axis=0, concat_axis=2, tiled=True),
        lax.all_to_all(left, "col", split_axis=0, concat_axis=2, tiled=True),
        lax.all_to_all(right, "col", split_axis=0, concat_axis=2, tiled=True),
    )
    residues = g_chan.shape[2]
    g_columns = lax.all_to_all(g_chan, "row", split_axis=2, concat_axis=1, tiled=True)
    d_left = jnp.einsum(
        "hij,hjk->hik",
        g_chan,
        lax.all_gather(right_chan, "row", axis=1, tiled=True),
        preferred_element_type=jnp.float32,
    )
    d_right = jnp.einsum(
        "hij,hik->hjk",
        g_columns,
        lax.all_gather(left_chan, "row", axis=1, tiled=True),
        preferred_element_type=jnp.float32,
    )
    d_left_tile, d_right_tile = (
        lax.all_to_all(d_left.astype(jnp.bfloat16), "col", split_axis=2, concat_axis=0, tiled=True),
        lax.all_to_all(
            d_right.astype(jnp.bfloat16), "col", split_axis=2, concat_axis=0, tiled=True
        ),
    )
    grad_l = d_left_tile.astype(jnp.float32)
    grad_r = d_right_tile.astype(jnp.float32)
    e_left = grad_l * s_left
    f_left = grad_l * q_left * s_left * (1.0 - s_left)
    e_right = grad_r * s_right
    f_right = grad_r * q_right * s_right * (1.0 - s_right)
    grads = jnp.concatenate([e_left, f_left, e_right, f_right], axis=0).astype(jnp.bfloat16)
    local_weights = jnp.einsum(
        "rcd,hrc->dh", normalized_input, grads, preferred_element_type=jnp.float32
    )
    total_weights = lax.psum(local_weights, ("row", "col")) / residues
    normalized_gradient = jnp.einsum(
        "hrc,dh->rcd", grads, stacked, preferred_element_type=jnp.float32
    )
    gradient_mean = jnp.mean(normalized_gradient, axis=-1, keepdims=True)
    gradient_input_mean = jnp.mean(normalized_gradient * standardized_input, axis=-1, keepdims=True)
    pair_gradient = (
        (normalized_gradient - gradient_mean - standardized_input * gradient_input_mean)
        * inverse_scale
    ).astype(jnp.bfloat16)
    pieces_w = jnp.split(total_weights, 4, axis=1)
    return (pair_gradient, pieces_w[0], pieces_w[1], pieces_w[2], pieces_w[3])


NT = (((1,), (1,)), ((), ()))
TN = (((0,), (0,)), ((), ()))
NN = (((1,), (0,)), ((), ()))


def dot(a, b, dims=NN):
    return lax.dot_general(a, b, dims, preferred_element_type=F32)


def stack_weights(w_refs, w_ref):
    h = w_refs[0].shape[0]
    for i, ref in enumerate(w_refs):
        w_ref[pl.ds(i * h, h), :] = ref[...]


def layer_norm(x):
    x = x.T.astype(F32)
    centered = x - jnp.mean(x, axis=0, keepdims=True)
    variance = jnp.mean(centered * centered, axis=0, keepdims=True)
    inverse_scale = lax.rsqrt(variance + 1e-05)
    return centered * inverse_scale, inverse_scale


def project(w_ref, normed):
    projected = dot(w_ref[...], normed)
    h = projected.shape[0] // 4
    q_left, p_left, q_right, p_right = (projected[i * h : (i + 1) * h] for i in range(4))
    return q_left, jax.nn.sigmoid(p_left), q_right, jax.nn.sigmoid(p_right)


def put_lanes(ref, at, value):
    lanes = ref.shape[2]
    for i in range(ref.shape[0]):
        ref[i, at, :] = value[:, i * lanes : (i + 1) * lanes]


def get_lanes(ref, at):
    return jnp.concatenate([ref[i, at, :] for i in range(ref.shape[0])], axis=1)


def before_kernel(own, pair_hbm, cot_hbm, wl, wlg, wr, wrg, out_ref, normed_hbm, *scratch):
    w_ref, rows_ref, pair_ref, normed_ref, in_sems, out_sems, w_sems, cot_sem = scratch
    h = wl.shape[0]
    rows = pair_ref.shape[0]
    pitch = rows + 1
    parts = in_sems.shape[0]
    count = rows // parts

    def come(part):
        at = pl.ds(part * count, count)
        return pltpu.make_async_copy(pair_hbm.at[at], pair_ref.at[at], in_sems.at[part])

    def leave(part):
        at = pl.ds(part * count, count)
        return pltpu.make_async_copy(normed_ref.at[at], normed_hbm.at[at], out_sems.at[part])

    def weight(i, w):
        return pltpu.make_async_copy(w, w_ref.at[pl.ds(i * h, h)], w_sems.at[i])

    for part in range(parts):
        come(part).start()
    for i, w in enumerate((wl, wlg, wr, wrg)):
        weight(i, w).start()
    cot = pltpu.make_async_copy(cot_hbm, out_ref.at[:, pl.ds(0, own)], cot_sem)
    cot.start()
    for i, w in enumerate((wl, wlg, wr, wrg)):
        weight(i, w).wait()

    def one_row(r, carry):
        normed = layer_norm(pair_ref[r])[0].astype(BF16)
        normed_ref[r] = normed
        q_left, s_left, q_right, s_right = project(w_ref, normed)
        put_lanes(rows_ref, pl.ds(r, h, stride=pitch), s_left * q_left)
        put_lanes(rows_ref, pl.ds(r + h * pitch, h, stride=pitch), s_right * q_right)
        return carry

    for part in range(parts):
        come(part).wait()
        lax.fori_loop(part * count, (part + 1) * count, one_row, 0, unroll=4)
        leave(part).start()
    for channel in range(h):
        for side in range(2):
            line = get_lanes(rows_ref, pl.ds((side * h + channel) * pitch, rows))
            out_ref[channel // own, (1 + side) * own + channel % own] = line.astype(BF16)
    for part in range(parts):
        leave(part).wait()
    cot.wait()


def triangle_kernel(rows, cols, in_ref, out_ref, g_ref, l_ref, r_ref):
    r, c = in_ref.shape[2:]
    own = g_ref.shape[0]
    for n in range(own):
        for i, ref in enumerate((g_ref, l_ref, r_ref)):
            for a in range(rows):
                for b in range(cols):
                    block = in_ref[a * cols + b, i * own + n]
                    ref[n, pl.ds(a * r, r), pl.ds(b * c, c)] = block
        for i, (dims, ref) in enumerate(((NN, r_ref), (TN, l_ref))):
            d = dot(g_ref[n], ref[n], dims).astype(BF16)
            for a in range(rows):
                for b in range(cols):
                    block = d[a * r : (a + 1) * r, b * c : (b + 1) * c]
                    out_ref[a * cols + b, n * 2 + i] = block


def gates_kernel(own, normed_hbm, d_ref, wl, wlg, wr, wrg, grads_ref, kept_ref, sent_ref, *scratch):
    w_ref, sums_ref, rows_ref, normed_ref, sem = scratch
    copy = pltpu.make_async_copy(normed_hbm, normed_ref, sem)
    copy.start()
    h = wl.shape[0]
    rows = grads_ref.shape[0]
    pitch = rows + 1
    together = 4 if rows % 4 == 0 else 1
    stack_weights((wl, wlg, wr, wrg), w_ref)
    sums_ref[...] = jnp.zeros_like(sums_ref)

    for channel in range(h):
        to, slot = channel // own, (channel % own) * 2
        for side in range(2):
            line = d_ref[to, slot + side].astype(F32)
            put_lanes(rows_ref, pl.ds((side * h + channel) * pitch, rows), line)

    copy.wait()

    def some_rows(n, carry):
        all_grads, all_normed = [], []
        for i in range(together):
            r = n * together + i
            normed = normed_ref[r]
            q_left, s_left, q_right, s_right = project(w_ref, normed)
            e_left = get_lanes(rows_ref, pl.ds(r, h, stride=pitch)) * s_left
            e_right = get_lanes(rows_ref, pl.ds(r + h * pitch, h, stride=pitch)) * s_right
            f_left = e_left * q_left * (1.0 - s_left)
            f_right = e_right * q_right * (1.0 - s_right)
            grads = jnp.concatenate([e_left, f_left, e_right, f_right], axis=0).astype(BF16)
            grads_ref[r] = grads
            all_grads.append(grads)
            all_normed.append(normed)
        sums_ref[...] += dot(
            jnp.concatenate(all_grads, axis=1), jnp.concatenate(all_normed, axis=1), NT
        )
        return carry

    lax.fori_loop(0, rows // together, some_rows, 0)
    bit = lax.rem(lax.axis_index("row"), 2)
    kept_ref[...] = sums_ref[pl.ds(pl.multiple_of(bit * 2 * h, 2 * h), 2 * h), :]
    sent_ref[...] = sums_ref[pl.ds(pl.multiple_of((1 - bit) * 2 * h, 2 * h), 2 * h), :]


def input_kernel(start, pair_hbm, grads_ref, wl, wlg, wr, wrg, *refs):
    out_hbm, back_ref, pair_ref, out_ref, in_sem, out_sems = refs[-6:]
    rows = pair_ref.shape[0]
    come = pltpu.make_async_copy(pair_hbm.at[pl.ds(start, rows)], pair_ref, in_sem)
    come.start()
    h = wl.shape[0]
    for i, ref in enumerate((wl, wlg, wr, wrg)):
        back_ref[:, pl.ds(i * h, h)] = ref[...].T
    come.wait()

    def one_row(r, carry):
        standardized, inverse_scale = layer_norm(pair_ref[r])
        d_normed = dot(back_ref[...], grads_ref[start + r])
        mean = jnp.mean(d_normed, axis=0, keepdims=True)
        input_mean = jnp.mean(d_normed * standardized, axis=0, keepdims=True)
        moved = (d_normed - mean - standardized * input_mean) * inverse_scale
        out_ref[r] = moved.astype(BF16).T
        return carry

    parts = out_sems.shape[0]
    count = rows // parts
    gone = []
    for part in range(parts):
        lax.fori_loop(part * count, (part + 1) * count, one_row, 0, unroll=4)
        at = pl.ds(part * count, count)
        to = out_hbm.at[pl.ds(start + part * count, count)]
        gone.append(pltpu.make_async_copy(out_ref.at[at], to, out_sems.at[part]))
        gone[-1].start()
    for copy in gone:
        copy.wait()


def finish_kernel(scale, mine_ref, other_ref, *out_refs):
    h = out_refs[0].shape[0]
    bit = lax.rem(lax.axis_index("row"), 2)
    for i, out_ref in enumerate(out_refs):
        at = pl.ds(i % 2 * h, h)
        mine = bit == i // 2
        out_ref[...] = jnp.where(mine, mine_ref[at, :], other_ref[at, :]) * scale


def channel_shards(sizes, pair, cotangent, *weights):
    rows, cols = sizes
    devices = rows * cols
    hidden, r, c = cotangent.shape
    dim = pair.shape[2]
    own = hidden // devices
    pieces = 2 if r % 2 == 0 else 1
    parts = 4 if r % 16 == 0 else 1
    weights = [w.T for w in weights]
    vmem = pl.BlockSpec(memory_space=pltpu.VMEM)
    hbm = pl.BlockSpec(memory_space=pltpu.HBM)
    exchange = functools.partial(
        lax.all_to_all, axis_name=("row", "col"), split_axis=0, concat_axis=0, tiled=True
    )
    stacked = pltpu.VMEM((4 * hidden, dim), BF16)
    lanes = min(c, 128)
    rows_scratch = pltpu.VMEM((c // lanes, (2 * hidden + 1) * (r + 1), lanes), F32)
    columns = r * c
    n_i, n_k = rows * r, cols * c
    pair = pltpu.with_memory_space_constraint(pair, pltpu.HBM)

    def cost(flops, *arrays):
        moved = sum(a.size * a.dtype.itemsize for a in arrays)
        return pl.CostEstimate(flops=flops, bytes_accessed=moved, transcendentals=0)

    def memory(mib):
        return pltpu.CompilerParams(vmem_limit_bytes=mib * 2**20)

    normed_shape = jax.ShapeDtypeStruct((r, dim, c), BF16)
    sent, normed = pl.pallas_call(
        functools.partial(before_kernel, own),
        in_specs=[hbm] * 6,
        out_specs=[vmem, hbm],
        out_shape=[
            jax.ShapeDtypeStruct((devices, 3 * own, r, c), BF16),
            pltpu.HBM(normed_shape.shape, BF16),
        ],
        scratch_shapes=[
            stacked,
            rows_scratch,
            pltpu.VMEM(pair.shape, BF16),
            pltpu.VMEM(normed_shape.shape, BF16),
            pltpu.SemaphoreType.DMA((parts,)),
            pltpu.SemaphoreType.DMA((parts,)),
            pltpu.SemaphoreType.DMA((4,)),
            pltpu.SemaphoreType.DMA,
        ],
        compiler_params=memory(24),
        name="before",
    )(
        pair,
        pltpu.with_memory_space_constraint(cotangent.reshape(devices, own, r, c), pltpu.HBM),
        *(pltpu.with_memory_space_constraint(w, pltpu.HBM) for w in weights),
    )

    sent = pl.pallas_call(
        functools.partial(triangle_kernel, rows, cols),
        in_specs=[vmem],
        out_specs=vmem,
        out_shape=jax.ShapeDtypeStruct((devices, 2 * own, r, c), BF16),
        scratch_shapes=[pltpu.VMEM((own, n_i, n_k), BF16)] * 3,
        compiler_params=memory(32),
        name="triangle",
    )(exchange(sent))

    half_shape = jax.ShapeDtypeStruct((2 * hidden, dim), F32)
    grads, kept, given = pl.pallas_call(
        functools.partial(gates_kernel, own),
        in_specs=[hbm] + [vmem] * 5,
        out_specs=[vmem] * 3,
        out_shape=[jax.ShapeDtypeStruct((r, 4 * hidden, c), BF16), half_shape, half_shape],
        scratch_shapes=[
            stacked,
            pltpu.VMEM((4 * hidden, dim), F32),
            rows_scratch,
            pltpu.VMEM(normed_shape.shape, BF16),
            pltpu.SemaphoreType.DMA,
        ],
        compiler_params=memory(28),
        name="gates",
    )(pltpu.with_memory_space_constraint(normed, pltpu.HBM), exchange(sent), *weights)

    def input_piece(piece, pair_gradient):
        held = [] if pair_gradient is None else [pair_gradient]
        count = r // pieces
        return pl.pallas_call(
            functools.partial(input_kernel, piece * count),
            in_specs=[hbm] + [vmem] * 5 + [hbm] * len(held),
            out_specs=hbm,
            out_shape=jax.ShapeDtypeStruct(pair.shape, BF16),
            scratch_shapes=[
                pltpu.VMEM((dim, 4 * hidden), BF16),
                pltpu.VMEM((count, c, dim), BF16),
                pltpu.VMEM((count, c, dim), BF16),
                pltpu.SemaphoreType.DMA,
                pltpu.SemaphoreType.DMA((2 if count % 8 == 0 else 1,)),
            ],
            input_output_aliases={6: 0} if held else {},
            compiler_params=memory(16),
            cost_estimate=cost(8 * hidden * dim * columns // pieces, pair),
            name="input",
        )(pair, grads, *weights, *held)

    steps = [("row", rows, 1 << i) for i in range(1, rows.bit_length() - 1)][::-1]
    steps += [("col", cols, 1 << i) for i in range(cols.bit_length() - 1)]
    pieces = min(pieces, len(steps))
    neighbours = [(i, i ^ 1) for i in range(rows)]
    pair_gradient = None
    mine = kept + lax.ppermute(given, "row", neighbours)
    for n, (axis, size, step) in enumerate(steps):
        other = lax.ppermute(mine, axis, [(i, i ^ step) for i in range(size)])
        if n < pieces:
            pair_gradient = input_piece(n, pair_gradient)
            other, pair_gradient = lax.optimization_barrier((other, pair_gradient))
        mine = mine + other
    weight_grads = pl.pallas_call(
        functools.partial(finish_kernel, 1.0 / n_i),
        in_specs=[vmem, vmem],
        out_shape=[jax.ShapeDtypeStruct((hidden, dim), F32)] * 4,
        compiler_params=memory(8),
        name="finish",
    )(mine, lax.ppermute(mine, "row", neighbours))
    return (pair_gradient, *(g.T for g in weight_grads))


def solution(mesh):
    in_specs = (P("row", "col", None), P(None, "row", "col"), P(), P(), P(), P())
    out_specs = (P("row", "col", None), P(), P(), P(), P())
    sizes = (mesh.shape["row"], mesh.shape["col"])

    def shards(pair, cotangent, *weights):
        plain = all(size > 1 and size & (size - 1) == 0 for size in sizes)
        if plain and cotangent.shape[0] % (sizes[0] * sizes[1]) == 0:
            return channel_shards(sizes, pair, cotangent, *weights)
        return gathered_shards(pair, cotangent, *weights)

    return jax.shard_map(shards, mesh=mesh, in_specs=in_specs, out_specs=out_specs, check_vma=False)
```

```python
import functools

import jax
import jax.numpy as jnp
from jax import lax
from jax.experimental import pallas as pl
from jax.experimental.pallas import tpu as pltpu
from jax.sharding import PartitionSpec as P

BF16, F32 = jnp.bfloat16, jnp.float32


def gathered_shards(pair, cotangent, w_left, w_left_gate, w_right, w_right_gate):
    pair_f = pair.astype(jnp.float32)
    average = jnp.mean(pair_f, axis=-1, keepdims=True)
    centered_input = pair_f - average
    variance = jnp.mean(centered_input * centered_input, axis=-1, keepdims=True)
    inverse_scale = 1.0 / jnp.sqrt(variance + 1e-05)
    standardized_input = centered_input * inverse_scale
    normalized_input = standardized_input.astype(jnp.bfloat16)
    stacked = jnp.concatenate([w_left, w_left_gate, w_right, w_right_gate], axis=1)
    projected = jnp.einsum(
        "rcd,dh->hrc", normalized_input, stacked, preferred_element_type=jnp.float32
    )
    q_left, p_left, q_right, p_right = jnp.split(projected, 4, axis=0)
    s_left = jax.nn.sigmoid(p_left)
    s_right = jax.nn.sigmoid(p_right)
    left = (s_left * q_left).astype(jnp.bfloat16)
    right = (s_right * q_right).astype(jnp.bfloat16)
    g_chan, left_chan, right_chan = (
        lax.all_to_all(cotangent, "col", split_axis=0, concat_axis=2, tiled=True),
        lax.all_to_all(left, "col", split_axis=0, concat_axis=2, tiled=True),
        lax.all_to_all(right, "col", split_axis=0, concat_axis=2, tiled=True),
    )
    residues = g_chan.shape[2]
    g_columns = lax.all_to_all(g_chan, "row", split_axis=2, concat_axis=1, tiled=True)
    d_left = jnp.einsum(
        "hij,hjk->hik",
        g_chan,
        lax.all_gather(right_chan, "row", axis=1, tiled=True),
        preferred_element_type=jnp.float32,
    )
    d_right = jnp.einsum(
        "hij,hik->hjk",
        g_columns,
        lax.all_gather(left_chan, "row", axis=1, tiled=True),
        preferred_element_type=jnp.float32,
    )
    d_left_tile, d_right_tile = (
        lax.all_to_all(d_left.astype(jnp.bfloat16), "col", split_axis=2, concat_axis=0, tiled=True),
        lax.all_to_all(
            d_right.astype(jnp.bfloat16), "col", split_axis=2, concat_axis=0, tiled=True
        ),
    )
    grad_l = d_left_tile.astype(jnp.float32)
    grad_r = d_right_tile.astype(jnp.float32)
    e_left = grad_l * s_left
    f_left = grad_l * q_left * s_left * (1.0 - s_left)
    e_right = grad_r * s_right
    f_right = grad_r * q_right * s_right * (1.0 - s_right)
    grads = jnp.concatenate([e_left, f_left, e_right, f_right], axis=0).astype(jnp.bfloat16)
    local_weights = jnp.einsum(
        "rcd,hrc->dh", normalized_input, grads, preferred_element_type=jnp.float32
    )
    total_weights = lax.psum(local_weights, ("row", "col")) / residues
    normalized_gradient = jnp.einsum(
        "hrc,dh->rcd", grads, stacked, preferred_element_type=jnp.float32
    )
    gradient_mean = jnp.mean(normalized_gradient, axis=-1, keepdims=True)
    gradient_input_mean = jnp.mean(normalized_gradient * standardized_input, axis=-1, keepdims=True)
    pair_gradient = (
        (normalized_gradient - gradient_mean - standardized_input * gradient_input_mean)
        * inverse_scale
    ).astype(jnp.bfloat16)
    pieces_w = jnp.split(total_weights, 4, axis=1)
    return (pair_gradient, pieces_w[0], pieces_w[1], pieces_w[2], pieces_w[3])


NT = (((1,), (1,)), ((), ()))
TN = (((0,), (0,)), ((), ()))
NN = (((1,), (0,)), ((), ()))


def dot(a, b, dims=NN):
    return lax.dot_general(a, b, dims, preferred_element_type=F32)


def stack_weights(w_refs, w_ref):
    h = w_refs[0].shape[0]
    for i, ref in enumerate(w_refs):
        w_ref[pl.ds(i * h, h), :] = ref[...]


def identity(n):
    row = lax.broadcasted_iota(jnp.int32, (n, n), 0)
    return (row == lax.broadcasted_iota(jnp.int32, (n, n), 1)).astype(BF16)


def layer_norm(x):
    x = dot(identity(x.shape[1]), x, NT)
    centered = x - jnp.mean(x, axis=0, keepdims=True)
    variance = jnp.mean(centered * centered, axis=0, keepdims=True)
    inverse_scale = lax.rsqrt(variance + 1e-05)
    return centered * inverse_scale, inverse_scale


def project(w_ref, normed):
    projected = dot(w_ref[...], normed)
    h = projected.shape[0] // 4
    q_left, p_left, q_right, p_right = (projected[i * h : (i + 1) * h] for i in range(4))
    return q_left, jax.nn.sigmoid(p_left), q_right, jax.nn.sigmoid(p_right)


def put_lanes(ref, at, value):
    lanes = ref.shape[2]
    for i in range(ref.shape[0]):
        ref[i, at, :] = value[:, i * lanes : (i + 1) * lanes]


def get_lanes(ref, at):
    return jnp.concatenate([ref[i, at, :] for i in range(ref.shape[0])], axis=1)


def before_kernel(own, pair_hbm, cot_hbm, wl, wlg, wr, wrg, out_ref, normed_hbm, *scratch):
    w_ref, rows_ref, pair_ref, normed_ref, in_sems, out_sems, w_sems, cot_sem = scratch
    h = wl.shape[0]
    rows = pair_ref.shape[0]
    pitch = rows + 1
    parts = in_sems.shape[0]
    count = rows // parts

    def come(part):
        at = pl.ds(part * count, count)
        return pltpu.make_async_copy(pair_hbm.at[at], pair_ref.at[at], in_sems.at[part])

    def leave(part):
        at = pl.ds(part * count, count)
        return pltpu.make_async_copy(normed_ref.at[at], normed_hbm.at[at], out_sems.at[part])

    def weight(i, w):
        return pltpu.make_async_copy(w, w_ref.at[pl.ds(i * h, h)], w_sems.at[i])

    for part in range(parts):
        come(part).start()
    for i, w in enumerate((wl, wlg, wr, wrg)):
        weight(i, w).start()
    cot = pltpu.make_async_copy(cot_hbm, out_ref.at[:, pl.ds(0, own)], cot_sem)
    cot.start()
    for i, w in enumerate((wl, wlg, wr, wrg)):
        weight(i, w).wait()

    def one_row(r, carry):
        normed = layer_norm(pair_ref[r])[0].astype(BF16)
        normed_ref[r] = normed
        q_left, s_left, q_right, s_right = project(w_ref, normed)
        put_lanes(rows_ref, pl.ds(r, h, stride=pitch), s_left * q_left)
        put_lanes(rows_ref, pl.ds(r + h * pitch, h, stride=pitch), s_right * q_right)
        return carry

    for part in range(parts):
        come(part).wait()
        lax.fori_loop(part * count, (part + 1) * count, one_row, 0, unroll=4)
        leave(part).start()
    for channel in range(h):
        for side in range(2):
            line = get_lanes(rows_ref, pl.ds((side * h + channel) * pitch, rows))
            out_ref[channel // own, (1 + side) * own + channel % own] = line.astype(BF16)
    for part in range(parts):
        leave(part).wait()
    cot.wait()


def triangle_kernel(rows, cols, in_ref, out_ref, g_ref, l_ref, r_ref):
    r, c = in_ref.shape[2:]
    own = g_ref.shape[0]
    for n in range(own):
        for i, ref in enumerate((g_ref, l_ref, r_ref)):
            for a in range(rows):
                for b in range(cols):
                    block = in_ref[a * cols + b, i * own + n]
                    ref[n, pl.ds(a * r, r), pl.ds(b * c, c)] = block
        for i, (dims, ref) in enumerate(((NN, r_ref), (TN, l_ref))):
            d = dot(g_ref[n], ref[n], dims).astype(BF16)
            for a in range(rows):
                for b in range(cols):
                    block = d[a * r : (a + 1) * r, b * c : (b + 1) * c]
                    out_ref[a * cols + b, n * 2 + i] = block


def gates_kernel(own, normed_hbm, d_ref, wl, wlg, wr, wrg, grads_ref, kept_ref, sent_ref, *scratch):
    w_ref, sums_ref, rows_ref, normed_ref, sem = scratch
    copy = pltpu.make_async_copy(normed_hbm, normed_ref, sem)
    copy.start()
    h = wl.shape[0]
    rows = grads_ref.shape[0]
    pitch = rows + 1
    together = 4 if rows % 4 == 0 else 1
    stack_weights((wl, wlg, wr, wrg), w_ref)
    sums_ref[...] = jnp.zeros_like(sums_ref)

    for channel in range(h):
        to, slot = channel // own, (channel % own) * 2
        for side in range(2):
            line = d_ref[to, slot + side].astype(F32)
            put_lanes(rows_ref, pl.ds((side * h + channel) * pitch, rows), line)

    copy.wait()

    def some_rows(n, carry):
        all_grads, all_normed = [], []
        for i in range(together):
            r = n * together + i
            normed = normed_ref[r]
            q_left, s_left, q_right, s_right = project(w_ref, normed)
            e_left = get_lanes(rows_ref, pl.ds(r, h, stride=pitch)) * s_left
            e_right = get_lanes(rows_ref, pl.ds(r + h * pitch, h, stride=pitch)) * s_right
            f_left = e_left * q_left * (1.0 - s_left)
            f_right = e_right * q_right * (1.0 - s_right)
            grads = jnp.concatenate([e_left, f_left, e_right, f_right], axis=0).astype(BF16)
            grads_ref[r] = grads
            all_grads.append(grads)
            all_normed.append(normed)
        sums_ref[...] += dot(
            jnp.concatenate(all_grads, axis=1), jnp.concatenate(all_normed, axis=1), NT
        )
        return carry

    lax.fori_loop(0, rows // together, some_rows, 0)
    bit = lax.rem(lax.axis_index("row"), 2)
    kept_ref[...] = sums_ref[pl.ds(pl.multiple_of(bit * 2 * h, 2 * h), 2 * h), :]
    sent_ref[...] = sums_ref[pl.ds(pl.multiple_of((1 - bit) * 2 * h, 2 * h), 2 * h), :]


def input_kernel(start, pair_hbm, grads_ref, wl, wlg, wr, wrg, *refs):
    out_hbm, back_ref, pair_ref, out_ref, in_sem, out_sems = refs[-6:]
    rows = pair_ref.shape[0]
    come = pltpu.make_async_copy(pair_hbm.at[pl.ds(start, rows)], pair_ref, in_sem)
    come.start()
    h = wl.shape[0]
    for i, ref in enumerate((wl, wlg, wr, wrg)):
        back_ref[:, pl.ds(i * h, h)] = ref[...].T
    come.wait()

    def one_row(r, carry):
        standardized, inverse_scale = layer_norm(pair_ref[r])
        d_normed = dot(back_ref[...], grads_ref[start + r])
        mean = jnp.mean(d_normed, axis=0, keepdims=True)
        input_mean = jnp.mean(d_normed * standardized, axis=0, keepdims=True)
        moved = (d_normed - mean - standardized * input_mean) * inverse_scale
        out_ref[r] = moved.astype(BF16).T
        return carry

    parts = out_sems.shape[0]
    count = rows // parts
    gone = []
    for part in range(parts):
        lax.fori_loop(part * count, (part + 1) * count, one_row, 0, unroll=4)
        at = pl.ds(part * count, count)
        to = out_hbm.at[pl.ds(start + part * count, count)]
        gone.append(pltpu.make_async_copy(out_ref.at[at], to, out_sems.at[part]))
        gone[-1].start()
    for copy in gone:
        copy.wait()


def finish_kernel(scale, mine_ref, other_ref, *out_refs):
    h = out_refs[0].shape[0]
    bit = lax.rem(lax.axis_index("row"), 2)
    for i, out_ref in enumerate(out_refs):
        at = pl.ds(i % 2 * h, h)
        mine = bit == i // 2
        out_ref[...] = jnp.where(mine, mine_ref[at, :], other_ref[at, :]) * scale


def channel_shards(sizes, pair, cotangent, *weights):
    rows, cols = sizes
    devices = rows * cols
    hidden, r, c = cotangent.shape
    dim = pair.shape[2]
    own = hidden // devices
    pieces = 2 if r % 2 == 0 else 1
    parts = 4 if r % 16 == 0 else 1
    weights = [w.T for w in weights]
    vmem = pl.BlockSpec(memory_space=pltpu.VMEM)
    hbm = pl.BlockSpec(memory_space=pltpu.HBM)
    exchange = functools.partial(
        lax.all_to_all, axis_name=("row", "col"), split_axis=0, concat_axis=0, tiled=True
    )
    stacked = pltpu.VMEM((4 * hidden, dim), BF16)
    lanes = min(c, 128)
    rows_scratch = pltpu.VMEM((c // lanes, (2 * hidden + 1) * (r + 1), lanes), F32)
    columns = r * c
    n_i, n_k = rows * r, cols * c
    pair = pltpu.with_memory_space_constraint(pair, pltpu.HBM)

    def cost(flops, *arrays):
        moved = sum(a.size * a.dtype.itemsize for a in arrays)
        return pl.CostEstimate(flops=flops, bytes_accessed=moved, transcendentals=0)

    def memory(mib):
        return pltpu.CompilerParams(vmem_limit_bytes=mib * 2**20)

    normed_shape = jax.ShapeDtypeStruct((r, dim, c), BF16)
    sent, normed = pl.pallas_call(
        functools.partial(before_kernel, own),
        in_specs=[hbm] * 6,
        out_specs=[vmem, hbm],
        out_shape=[
            jax.ShapeDtypeStruct((devices, 3 * own, r, c), BF16),
            pltpu.HBM(normed_shape.shape, BF16),
        ],
        scratch_shapes=[
            stacked,
            rows_scratch,
            pltpu.VMEM(pair.shape, BF16),
            pltpu.VMEM(normed_shape.shape, BF16),
            pltpu.SemaphoreType.DMA((parts,)),
            pltpu.SemaphoreType.DMA((parts,)),
            pltpu.SemaphoreType.DMA((4,)),
            pltpu.SemaphoreType.DMA,
        ],
        compiler_params=memory(24),
        name="before",
    )(
        pair,
        pltpu.with_memory_space_constraint(cotangent.reshape(devices, own, r, c), pltpu.HBM),
        *(pltpu.with_memory_space_constraint(w, pltpu.HBM) for w in weights),
    )

    sent = pl.pallas_call(
        functools.partial(triangle_kernel, rows, cols),
        in_specs=[vmem],
        out_specs=vmem,
        out_shape=jax.ShapeDtypeStruct((devices, 2 * own, r, c), BF16),
        scratch_shapes=[pltpu.VMEM((own, n_i, n_k), BF16)] * 3,
        compiler_params=memory(32),
        name="triangle",
    )(exchange(sent))

    half_shape = jax.ShapeDtypeStruct((2 * hidden, dim), F32)
    grads, kept, given = pl.pallas_call(
        functools.partial(gates_kernel, own),
        in_specs=[hbm] + [vmem] * 5,
        out_specs=[vmem] * 3,
        out_shape=[jax.ShapeDtypeStruct((r, 4 * hidden, c), BF16), half_shape, half_shape],
        scratch_shapes=[
            stacked,
            pltpu.VMEM((4 * hidden, dim), F32),
            rows_scratch,
            pltpu.VMEM(normed_shape.shape, BF16),
            pltpu.SemaphoreType.DMA,
        ],
        compiler_params=memory(28),
        name="gates",
    )(pltpu.with_memory_space_constraint(normed, pltpu.HBM), exchange(sent), *weights)

    def input_piece(piece, pair_gradient):
        held = [] if pair_gradient is None else [pair_gradient]
        count = r // pieces
        return pl.pallas_call(
            functools.partial(input_kernel, piece * count),
            in_specs=[hbm] + [vmem] * 5 + [hbm] * len(held),
            out_specs=hbm,
            out_shape=jax.ShapeDtypeStruct(pair.shape, BF16),
            scratch_shapes=[
                pltpu.VMEM((dim, 4 * hidden), BF16),
                pltpu.VMEM((count, c, dim), BF16),
                pltpu.VMEM((count, c, dim), BF16),
                pltpu.SemaphoreType.DMA,
                pltpu.SemaphoreType.DMA((2 if count % 8 == 0 else 1,)),
            ],
            input_output_aliases={6: 0} if held else {},
            compiler_params=memory(16),
            cost_estimate=cost(8 * hidden * dim * columns // pieces, pair),
            name="input",
        )(pair, grads, *weights, *held)

    steps = [("row", rows, 1 << i) for i in range(1, rows.bit_length() - 1)][::-1]
    steps += [("col", cols, 1 << i) for i in range(cols.bit_length() - 1)]
    pieces = min(pieces, len(steps))
    neighbours = [(i, i ^ 1) for i in range(rows)]
    pair_gradient = None
    mine = kept + lax.ppermute(given, "row", neighbours)
    for n, (axis, size, step) in enumerate(steps):
        other = lax.ppermute(mine, axis, [(i, i ^ step) for i in range(size)])
        if n < pieces:
            pair_gradient = input_piece(n, pair_gradient)
            other, pair_gradient = lax.optimization_barrier((other, pair_gradient))
        mine = mine + other
    weight_grads = pl.pallas_call(
        functools.partial(finish_kernel, 1.0 / n_i),
        in_specs=[vmem, vmem],
        out_shape=[jax.ShapeDtypeStruct((hidden, dim), F32)] * 4,
        compiler_params=memory(8),
        name="finish",
    )(mine, lax.ppermute(mine, "row", neighbours))
    return (pair_gradient, *(g.T for g in weight_grads))


def solution(mesh):
    in_specs = (P("row", "col", None), P(None, "row", "col"), P(), P(), P(), P())
    out_specs = (P("row", "col", None), P(), P(), P(), P())
    sizes = (mesh.shape["row"], mesh.shape["col"])

    def shards(pair, cotangent, *weights):
        plain = all(size > 1 and size & (size - 1) == 0 for size in sizes)
        if plain and cotangent.shape[0] % (sizes[0] * sizes[1]) == 0:
            return channel_shards(sizes, pair, cotangent, *weights)
        return gathered_shards(pair, cotangent, *weights)

    return jax.shard_map(shards, mesh=mesh, in_specs=in_specs, out_specs=out_specs, check_vma=False)
```

```python
import functools

import jax
import jax.numpy as jnp
from jax import lax
from jax.experimental import pallas as pl
from jax.experimental.pallas import tpu as pltpu
from jax.sharding import PartitionSpec as P

BF16, F32 = jnp.bfloat16, jnp.float32


def gathered_shards(pair, cotangent, w_left, w_left_gate, w_right, w_right_gate):
    pair_f = pair.astype(jnp.float32)
    average = jnp.mean(pair_f, axis=-1, keepdims=True)
    centered_input = pair_f - average
    variance = jnp.mean(centered_input * centered_input, axis=-1, keepdims=True)
    inverse_scale = 1.0 / jnp.sqrt(variance + 1e-05)
    standardized_input = centered_input * inverse_scale
    normalized_input = standardized_input.astype(jnp.bfloat16)
    stacked = jnp.concatenate([w_left, w_left_gate, w_right, w_right_gate], axis=1)
    projected = jnp.einsum(
        "rcd,dh->hrc", normalized_input, stacked, preferred_element_type=jnp.float32
    )
    q_left, p_left, q_right, p_right = jnp.split(projected, 4, axis=0)
    s_left = jax.nn.sigmoid(p_left)
    s_right = jax.nn.sigmoid(p_right)
    left = (s_left * q_left).astype(jnp.bfloat16)
    right = (s_right * q_right).astype(jnp.bfloat16)
    g_chan, left_chan, right_chan = (
        lax.all_to_all(cotangent, "col", split_axis=0, concat_axis=2, tiled=True),
        lax.all_to_all(left, "col", split_axis=0, concat_axis=2, tiled=True),
        lax.all_to_all(right, "col", split_axis=0, concat_axis=2, tiled=True),
    )
    residues = g_chan.shape[2]
    g_columns = lax.all_to_all(g_chan, "row", split_axis=2, concat_axis=1, tiled=True)
    d_left = jnp.einsum(
        "hij,hjk->hik",
        g_chan,
        lax.all_gather(right_chan, "row", axis=1, tiled=True),
        preferred_element_type=jnp.float32,
    )
    d_right = jnp.einsum(
        "hij,hik->hjk",
        g_columns,
        lax.all_gather(left_chan, "row", axis=1, tiled=True),
        preferred_element_type=jnp.float32,
    )
    d_left_tile, d_right_tile = (
        lax.all_to_all(d_left.astype(jnp.bfloat16), "col", split_axis=2, concat_axis=0, tiled=True),
        lax.all_to_all(
            d_right.astype(jnp.bfloat16), "col", split_axis=2, concat_axis=0, tiled=True
        ),
    )
    grad_l = d_left_tile.astype(jnp.float32)
    grad_r = d_right_tile.astype(jnp.float32)
    e_left = grad_l * s_left
    f_left = grad_l * q_left * s_left * (1.0 - s_left)
    e_right = grad_r * s_right
    f_right = grad_r * q_right * s_right * (1.0 - s_right)
    grads = jnp.concatenate([e_left, f_left, e_right, f_right], axis=0).astype(jnp.bfloat16)
    local_weights = jnp.einsum(
        "rcd,hrc->dh", normalized_input, grads, preferred_element_type=jnp.float32
    )
    total_weights = lax.psum(local_weights, ("row", "col")) / residues
    normalized_gradient = jnp.einsum(
        "hrc,dh->rcd", grads, stacked, preferred_element_type=jnp.float32
    )
    gradient_mean = jnp.mean(normalized_gradient, axis=-1, keepdims=True)
    gradient_input_mean = jnp.mean(normalized_gradient * standardized_input, axis=-1, keepdims=True)
    pair_gradient = (
        (normalized_gradient - gradient_mean - standardized_input * gradient_input_mean)
        * inverse_scale
    ).astype(jnp.bfloat16)
    pieces_w = jnp.split(total_weights, 4, axis=1)
    return (pair_gradient, pieces_w[0], pieces_w[1], pieces_w[2], pieces_w[3])


NT = (((1,), (1,)), ((), ()))
TN = (((0,), (0,)), ((), ()))
NN = (((1,), (0,)), ((), ()))


def dot(a, b, dims=NN):
    return lax.dot_general(a, b, dims, preferred_element_type=F32)


def stack_weights(w_refs, w_ref):
    h = w_refs[0].shape[0]
    for i, ref in enumerate(w_refs):
        w_ref[pl.ds(i * h, h), :] = ref[...]


def layer_norm(x):
    x = x.T.astype(F32)
    centered = x - jnp.mean(x, axis=0, keepdims=True)
    variance = jnp.mean(centered * centered, axis=0, keepdims=True)
    inverse_scale = lax.rsqrt(variance + 1e-05)
    return centered * inverse_scale, inverse_scale


def project(w_ref, normed):
    projected = dot(w_ref[...], normed)
    h = projected.shape[0] // 4
    q_left, p_left, q_right, p_right = (projected[i * h : (i + 1) * h] for i in range(4))
    return q_left, jax.nn.sigmoid(p_left), q_right, jax.nn.sigmoid(p_right)


def put_lanes(ref, at, value):
    lanes = ref.shape[2]
    for i in range(ref.shape[0]):
        ref[i, at, :] = value[:, i * lanes : (i + 1) * lanes]


def get_lanes(ref, at):
    return jnp.concatenate([ref[i, at, :] for i in range(ref.shape[0])], axis=1)


def before_kernel(own, pair_hbm, cot_hbm, wl, wlg, wr, wrg, out_ref, normed_hbm, *scratch):
    w_ref, rows_ref, pair_ref, normed_ref, in_sems, out_sems, w_sems, cot_sem = scratch
    h = wl.shape[0]
    rows = pair_ref.shape[0]
    pitch = rows + 1
    parts = in_sems.shape[0]
    count = rows // parts

    def come(part):
        at = pl.ds(part * count, count)
        return pltpu.make_async_copy(pair_hbm.at[at], pair_ref.at[at], in_sems.at[part])

    def leave(part):
        at = pl.ds(part * count, count)
        return pltpu.make_async_copy(normed_ref.at[at], normed_hbm.at[at], out_sems.at[part])

    def weight(i, w):
        return pltpu.make_async_copy(w, w_ref.at[pl.ds(i * h, h)], w_sems.at[i])

    for part in range(parts):
        come(part).start()
    for i, w in enumerate((wl, wlg, wr, wrg)):
        weight(i, w).start()
    cot = pltpu.make_async_copy(cot_hbm, out_ref.at[:, pl.ds(0, own)], cot_sem)
    cot.start()
    for i, w in enumerate((wl, wlg, wr, wrg)):
        weight(i, w).wait()

    def one_row(r, carry):
        normed = layer_norm(pair_ref[r])[0].astype(BF16)
        normed_ref[r] = normed
        q_left, s_left, q_right, s_right = project(w_ref, normed)
        put_lanes(rows_ref, pl.ds(r, h, stride=pitch), s_left * q_left)
        put_lanes(rows_ref, pl.ds(r + h * pitch, h, stride=pitch), s_right * q_right)
        return carry

    for part in range(parts):
        come(part).wait()
        lax.fori_loop(part * count, (part + 1) * count, one_row, 0, unroll=8)
        leave(part).start()
    for channel in range(h):
        for side in range(2):
            line = get_lanes(rows_ref, pl.ds((side * h + channel) * pitch, rows))
            out_ref[channel // own, (1 + side) * own + channel % own] = line.astype(BF16)
    for part in range(parts):
        leave(part).wait()
    cot.wait()


def triangle_kernel(rows, cols, in_ref, out_ref, g_ref, l_ref, r_ref):
    r, c = in_ref.shape[2:]
    own = g_ref.shape[0]
    for n in range(own):
        for i, ref in enumerate((g_ref, l_ref, r_ref)):
            for a in range(rows):
                for b in range(cols):
                    block = in_ref[a * cols + b, i * own + n]
                    ref[n, pl.ds(a * r, r), pl.ds(b * c, c)] = block
        for i, (dims, ref) in enumerate(((NN, r_ref), (TN, l_ref))):
            d = dot(g_ref[n], ref[n], dims).astype(BF16)
            for a in range(rows):
                for b in range(cols):
                    block = d[a * r : (a + 1) * r, b * c : (b + 1) * c]
                    out_ref[a * cols + b, n * 2 + i] = block


def gates_kernel(own, normed_hbm, d_ref, wl, wlg, wr, wrg, grads_ref, kept_ref, sent_ref, *scratch):
    w_ref, sums_ref, rows_ref, normed_ref, sem = scratch
    copy = pltpu.make_async_copy(normed_hbm, normed_ref, sem)
    copy.start()
    h = wl.shape[0]
    rows = grads_ref.shape[0]
    pitch = rows + 1
    together = 8 if rows % 8 == 0 else 1
    stack_weights((wl, wlg, wr, wrg), w_ref)
    sums_ref[...] = jnp.zeros_like(sums_ref)

    for channel in range(h):
        to, slot = channel // own, (channel % own) * 2
        for side in range(2):
            line = d_ref[to, slot + side].astype(F32)
            put_lanes(rows_ref, pl.ds((side * h + channel) * pitch, rows), line)

    copy.wait()

    def some_rows(n, carry):
        all_grads, all_normed = [], []
        for i in range(together):
            r = n * together + i
            normed = normed_ref[r]
            q_left, s_left, q_right, s_right = project(w_ref, normed)
            e_left = get_lanes(rows_ref, pl.ds(r, h, stride=pitch)) * s_left
            e_right = get_lanes(rows_ref, pl.ds(r + h * pitch, h, stride=pitch)) * s_right
            f_left = e_left * q_left * (1.0 - s_left)
            f_right = e_right * q_right * (1.0 - s_right)
            grads = jnp.concatenate([e_left, f_left, e_right, f_right], axis=0).astype(BF16)
            grads_ref[r] = grads
            all_grads.append(grads)
            all_normed.append(normed)
        sums_ref[...] += dot(
            jnp.concatenate(all_grads, axis=1), jnp.concatenate(all_normed, axis=1), NT
        )
        return carry

    lax.fori_loop(0, rows // together, some_rows, 0)
    bit = lax.rem(lax.axis_index("row"), 2)
    kept_ref[...] = sums_ref[pl.ds(pl.multiple_of(bit * 2 * h, 2 * h), 2 * h), :]
    sent_ref[...] = sums_ref[pl.ds(pl.multiple_of((1 - bit) * 2 * h, 2 * h), 2 * h), :]


def input_kernel(start, pair_hbm, grads_ref, wl, wlg, wr, wrg, *refs):
    out_hbm, back_ref, pair_ref, out_ref, in_sem, out_sems = refs[-6:]
    rows = pair_ref.shape[0]
    come = pltpu.make_async_copy(pair_hbm.at[pl.ds(start, rows)], pair_ref, in_sem)
    come.start()
    h = wl.shape[0]
    for i, ref in enumerate((wl, wlg, wr, wrg)):
        back_ref[:, pl.ds(i * h, h)] = ref[...].T
    come.wait()

    def one_row(r, carry):
        standardized, inverse_scale = layer_norm(pair_ref[r])
        d_normed = dot(back_ref[...], grads_ref[start + r])
        mean = jnp.mean(d_normed, axis=0, keepdims=True)
        input_mean = jnp.mean(d_normed * standardized, axis=0, keepdims=True)
        moved = (d_normed - mean - standardized * input_mean) * inverse_scale
        out_ref[r] = moved.astype(BF16).T
        return carry

    parts = out_sems.shape[0]
    count = rows // parts
    gone = []
    for part in range(parts):
        lax.fori_loop(part * count, (part + 1) * count, one_row, 0, unroll=4)
        at = pl.ds(part * count, count)
        to = out_hbm.at[pl.ds(start + part * count, count)]
        gone.append(pltpu.make_async_copy(out_ref.at[at], to, out_sems.at[part]))
        gone[-1].start()
    for copy in gone:
        copy.wait()


def finish_kernel(scale, mine_ref, other_ref, *out_refs):
    h = out_refs[0].shape[0]
    bit = lax.rem(lax.axis_index("row"), 2)
    for i, out_ref in enumerate(out_refs):
        at = pl.ds(i % 2 * h, h)
        mine = bit == i // 2
        out_ref[...] = jnp.where(mine, mine_ref[at, :], other_ref[at, :]) * scale


def channel_shards(sizes, pair, cotangent, *weights):
    rows, cols = sizes
    devices = rows * cols
    hidden, r, c = cotangent.shape
    dim = pair.shape[2]
    own = hidden // devices
    pieces = 2 if r % 2 == 0 else 1
    parts = 4 if r % 16 == 0 else 1
    weights = [w.T for w in weights]
    vmem = pl.BlockSpec(memory_space=pltpu.VMEM)
    hbm = pl.BlockSpec(memory_space=pltpu.HBM)
    exchange = functools.partial(
        lax.all_to_all, axis_name=("row", "col"), split_axis=0, concat_axis=0, tiled=True
    )
    stacked = pltpu.VMEM((4 * hidden, dim), BF16)
    lanes = min(c, 128)
    rows_scratch = pltpu.VMEM((c // lanes, (2 * hidden + 1) * (r + 1), lanes), F32)
    columns = r * c
    n_i, n_k = rows * r, cols * c
    pair = pltpu.with_memory_space_constraint(pair, pltpu.HBM)

    def cost(flops, *arrays):
        moved = sum(a.size * a.dtype.itemsize for a in arrays)
        return pl.CostEstimate(flops=flops, bytes_accessed=moved, transcendentals=0)

    def memory(mib):
        return pltpu.CompilerParams(vmem_limit_bytes=mib * 2**20)

    normed_shape = jax.ShapeDtypeStruct((r, dim, c), BF16)
    sent, normed = pl.pallas_call(
        functools.partial(before_kernel, own),
        in_specs=[hbm] * 6,
        out_specs=[vmem, hbm],
        out_shape=[
            jax.ShapeDtypeStruct((devices, 3 * own, r, c), BF16),
            pltpu.HBM(normed_shape.shape, BF16),
        ],
        scratch_shapes=[
            stacked,
            rows_scratch,
            pltpu.VMEM(pair.shape, BF16),
            pltpu.VMEM(normed_shape.shape, BF16),
            pltpu.SemaphoreType.DMA((parts,)),
            pltpu.SemaphoreType.DMA((parts,)),
            pltpu.SemaphoreType.DMA((4,)),
            pltpu.SemaphoreType.DMA,
        ],
        compiler_params=memory(24),
        name="before",
    )(
        pair,
        pltpu.with_memory_space_constraint(cotangent.reshape(devices, own, r, c), pltpu.HBM),
        *(pltpu.with_memory_space_constraint(w, pltpu.HBM) for w in weights),
    )

    sent = pl.pallas_call(
        functools.partial(triangle_kernel, rows, cols),
        in_specs=[vmem],
        out_specs=vmem,
        out_shape=jax.ShapeDtypeStruct((devices, 2 * own, r, c), BF16),
        scratch_shapes=[pltpu.VMEM((own, n_i, n_k), BF16)] * 3,
        compiler_params=memory(32),
        name="triangle",
    )(exchange(sent))

    half_shape = jax.ShapeDtypeStruct((2 * hidden, dim), F32)
    grads, kept, given = pl.pallas_call(
        functools.partial(gates_kernel, own),
        in_specs=[hbm] + [vmem] * 5,
        out_specs=[vmem] * 3,
        out_shape=[jax.ShapeDtypeStruct((r, 4 * hidden, c), BF16), half_shape, half_shape],
        scratch_shapes=[
            stacked,
            pltpu.VMEM((4 * hidden, dim), F32),
            rows_scratch,
            pltpu.VMEM(normed_shape.shape, BF16),
            pltpu.SemaphoreType.DMA,
        ],
        compiler_params=memory(28),
        name="gates",
    )(pltpu.with_memory_space_constraint(normed, pltpu.HBM), exchange(sent), *weights)

    def input_piece(piece, pair_gradient):
        held = [] if pair_gradient is None else [pair_gradient]
        count = r // pieces
        return pl.pallas_call(
            functools.partial(input_kernel, piece * count),
            in_specs=[hbm] + [vmem] * 5 + [hbm] * len(held),
            out_specs=hbm,
            out_shape=jax.ShapeDtypeStruct(pair.shape, BF16),
            scratch_shapes=[
                pltpu.VMEM((dim, 4 * hidden), BF16),
                pltpu.VMEM((count, c, dim), BF16),
                pltpu.VMEM((count, c, dim), BF16),
                pltpu.SemaphoreType.DMA,
                pltpu.SemaphoreType.DMA((2 if count % 8 == 0 else 1,)),
            ],
            input_output_aliases={6: 0} if held else {},
            compiler_params=memory(16),
            cost_estimate=cost(8 * hidden * dim * columns // pieces, pair),
            name="input",
        )(pair, grads, *weights, *held)

    steps = [("row", rows, 1 << i) for i in range(1, rows.bit_length() - 1)][::-1]
    steps += [("col", cols, 1 << i) for i in range(cols.bit_length() - 1)]
    pieces = min(pieces, len(steps))
    neighbours = [(i, i ^ 1) for i in range(rows)]
    pair_gradient = None
    mine = kept + lax.ppermute(given, "row", neighbours)
    for n, (axis, size, step) in enumerate(steps):
        other = lax.ppermute(mine, axis, [(i, i ^ step) for i in range(size)])
        if n < pieces:
            pair_gradient = input_piece(n, pair_gradient)
            other, pair_gradient = lax.optimization_barrier((other, pair_gradient))
        mine = mine + other
    weight_grads = pl.pallas_call(
        functools.partial(finish_kernel, 1.0 / n_i),
        in_specs=[vmem, vmem],
        out_shape=[jax.ShapeDtypeStruct((hidden, dim), F32)] * 4,
        compiler_params=memory(8),
        name="finish",
    )(mine, lax.ppermute(mine, "row", neighbours))
    return (pair_gradient, *(g.T for g in weight_grads))


def solution(mesh):
    in_specs = (P("row", "col", None), P(None, "row", "col"), P(), P(), P(), P())
    out_specs = (P("row", "col", None), P(), P(), P(), P())
    sizes = (mesh.shape["row"], mesh.shape["col"])

    def shards(pair, cotangent, *weights):
        plain = all(size > 1 and size & (size - 1) == 0 for size in sizes)
        if plain and cotangent.shape[0] % (sizes[0] * sizes[1]) == 0:
            return channel_shards(sizes, pair, cotangent, *weights)
        return gathered_shards(pair, cotangent, *weights)

    return jax.shard_map(shards, mesh=mesh, in_specs=in_specs, out_specs=out_specs, check_vma=False)
```

```python
import functools

import jax
import jax.numpy as jnp
from jax import lax
from jax.experimental import pallas as pl
from jax.experimental.pallas import tpu as pltpu
from jax.sharding import PartitionSpec as P

BF16, F32 = jnp.bfloat16, jnp.float32


def gathered_shards(pair, cotangent, w_left, w_left_gate, w_right, w_right_gate):
    pair_f = pair.astype(jnp.float32)
    average = jnp.mean(pair_f, axis=-1, keepdims=True)
    centered_input = pair_f - average
    variance = jnp.mean(centered_input * centered_input, axis=-1, keepdims=True)
    inverse_scale = 1.0 / jnp.sqrt(variance + 1e-05)
    standardized_input = centered_input * inverse_scale
    normalized_input = standardized_input.astype(jnp.bfloat16)
    stacked = jnp.concatenate([w_left, w_left_gate, w_right, w_right_gate], axis=1)
    projected = jnp.einsum(
        "rcd,dh->hrc", normalized_input, stacked, preferred_element_type=jnp.float32
    )
    q_left, p_left, q_right, p_right = jnp.split(projected, 4, axis=0)
    s_left = jax.nn.sigmoid(p_left)
    s_right = jax.nn.sigmoid(p_right)
    left = (s_left * q_left).astype(jnp.bfloat16)
    right = (s_right * q_right).astype(jnp.bfloat16)
    g_chan, left_chan, right_chan = (
        lax.all_to_all(cotangent, "col", split_axis=0, concat_axis=2, tiled=True),
        lax.all_to_all(left, "col", split_axis=0, concat_axis=2, tiled=True),
        lax.all_to_all(right, "col", split_axis=0, concat_axis=2, tiled=True),
    )
    residues = g_chan.shape[2]
    g_columns = lax.all_to_all(g_chan, "row", split_axis=2, concat_axis=1, tiled=True)
    d_left = jnp.einsum(
        "hij,hjk->hik",
        g_chan,
        lax.all_gather(right_chan, "row", axis=1, tiled=True),
        preferred_element_type=jnp.float32,
    )
    d_right = jnp.einsum(
        "hij,hik->hjk",
        g_columns,
        lax.all_gather(left_chan, "row", axis=1, tiled=True),
        preferred_element_type=jnp.float32,
    )
    d_left_tile, d_right_tile = (
        lax.all_to_all(d_left.astype(jnp.bfloat16), "col", split_axis=2, concat_axis=0, tiled=True),
        lax.all_to_all(
            d_right.astype(jnp.bfloat16), "col", split_axis=2, concat_axis=0, tiled=True
        ),
    )
    grad_l = d_left_tile.astype(jnp.float32)
    grad_r = d_right_tile.astype(jnp.float32)
    e_left = grad_l * s_left
    f_left = grad_l * q_left * s_left * (1.0 - s_left)
    e_right = grad_r * s_right
    f_right = grad_r * q_right * s_right * (1.0 - s_right)
    grads = jnp.concatenate([e_left, f_left, e_right, f_right], axis=0).astype(jnp.bfloat16)
    local_weights = jnp.einsum(
        "rcd,hrc->dh", normalized_input, grads, preferred_element_type=jnp.float32
    )
    total_weights = lax.psum(local_weights, ("row", "col")) / residues
    normalized_gradient = jnp.einsum(
        "hrc,dh->rcd", grads, stacked, preferred_element_type=jnp.float32
    )
    gradient_mean = jnp.mean(normalized_gradient, axis=-1, keepdims=True)
    gradient_input_mean = jnp.mean(normalized_gradient * standardized_input, axis=-1, keepdims=True)
    pair_gradient = (
        (normalized_gradient - gradient_mean - standardized_input * gradient_input_mean)
        * inverse_scale
    ).astype(jnp.bfloat16)
    pieces_w = jnp.split(total_weights, 4, axis=1)
    return (pair_gradient, pieces_w[0], pieces_w[1], pieces_w[2], pieces_w[3])


NT = (((1,), (1,)), ((), ()))
TN = (((0,), (0,)), ((), ()))
NN = (((1,), (0,)), ((), ()))


def dot(a, b, dims=NN):
    return lax.dot_general(a, b, dims, preferred_element_type=F32)


def stack_weights(w_refs, w_ref):
    h = w_refs[0].shape[0]
    for i, ref in enumerate(w_refs):
        w_ref[pl.ds(i * h, h), :] = ref[...]


def layer_norm(x):
    x = x.T.astype(F32)
    centered = x - jnp.mean(x, axis=0, keepdims=True)
    variance = jnp.mean(centered * centered, axis=0, keepdims=True)
    inverse_scale = lax.rsqrt(variance + 1e-05)
    return centered * inverse_scale, inverse_scale


def project(w_ref, normed):
    projected = dot(w_ref[...], normed)
    h = projected.shape[0] // 4
    q_left, p_left, q_right, p_right = (projected[i * h : (i + 1) * h] for i in range(4))
    return q_left, jax.nn.sigmoid(p_left), q_right, jax.nn.sigmoid(p_right)


def put_lanes(ref, at, value):
    lanes = ref.shape[2]
    for i in range(ref.shape[0]):
        ref[i, at, :] = value[:, i * lanes : (i + 1) * lanes]


def get_lanes(ref, at):
    return jnp.concatenate([ref[i, at, :] for i in range(ref.shape[0])], axis=1)


def before_kernel(own, pair_hbm, cot_hbm, wl, wlg, wr, wrg, out_ref, normed_hbm, *scratch):
    w_ref, rows_ref, pair_ref, normed_ref, in_sems, out_sems, w_sems, cot_sem = scratch
    h = wl.shape[0]
    rows = pair_ref.shape[0]
    pitch = rows + 1
    parts = in_sems.shape[0]
    count = rows // parts

    def come(part):
        at = pl.ds(part * count, count)
        return pltpu.make_async_copy(pair_hbm.at[at], pair_ref.at[at], in_sems.at[part])

    def leave(part):
        at = pl.ds(part * count, count)
        return pltpu.make_async_copy(normed_ref.at[at], normed_hbm.at[at], out_sems.at[part])

    def weight(i, w):
        return pltpu.make_async_copy(w, w_ref.at[pl.ds(i * h, h)], w_sems.at[i])

    for part in range(parts):
        come(part).start()
    for i, w in enumerate((wl, wlg, wr, wrg)):
        weight(i, w).start()
    cot = pltpu.make_async_copy(cot_hbm, out_ref.at[:, pl.ds(0, own)], cot_sem)
    cot.start()
    for i, w in enumerate((wl, wlg, wr, wrg)):
        weight(i, w).wait()

    def one_row(r, carry):
        normed = layer_norm(pair_ref[r])[0].astype(BF16)
        normed_ref[r] = normed
        q_left, s_left, q_right, s_right = project(w_ref, normed)
        put_lanes(rows_ref, pl.ds(r, h, stride=pitch), s_left * q_left)
        put_lanes(rows_ref, pl.ds(r + h * pitch, h, stride=pitch), s_right * q_right)
        return carry

    for part in range(parts):
        come(part).wait()
        lax.fori_loop(part * count, (part + 1) * count, one_row, 0, unroll=16)
        leave(part).start()
    for channel in range(h):
        for side in range(2):
            line = get_lanes(rows_ref, pl.ds((side * h + channel) * pitch, rows))
            out_ref[channel // own, (1 + side) * own + channel % own] = line.astype(BF16)
    for part in range(parts):
        leave(part).wait()
    cot.wait()


def triangle_kernel(rows, cols, in_ref, out_ref, g_ref, l_ref, r_ref):
    r, c = in_ref.shape[2:]
    own = g_ref.shape[0]
    for n in range(own):
        for i, ref in enumerate((g_ref, l_ref, r_ref)):
            for a in range(rows):
                for b in range(cols):
                    block = in_ref[a * cols + b, i * own + n]
                    ref[n, pl.ds(a * r, r), pl.ds(b * c, c)] = block
        for i, (dims, ref) in enumerate(((NN, r_ref), (TN, l_ref))):
            d = dot(g_ref[n], ref[n], dims).astype(BF16)
            for a in range(rows):
                for b in range(cols):
                    block = d[a * r : (a + 1) * r, b * c : (b + 1) * c]
                    out_ref[a * cols + b, n * 2 + i] = block


def gates_kernel(own, normed_hbm, d_ref, wl, wlg, wr, wrg, grads_ref, kept_ref, sent_ref, *scratch):
    w_ref, sums_ref, rows_ref, normed_ref, sem = scratch
    copy = pltpu.make_async_copy(normed_hbm, normed_ref, sem)
    copy.start()
    h = wl.shape[0]
    rows = grads_ref.shape[0]
    pitch = rows + 1
    together = 16 if rows % 16 == 0 else 1
    stack_weights((wl, wlg, wr, wrg), w_ref)
    sums_ref[...] = jnp.zeros_like(sums_ref)

    for channel in range(h):
        to, slot = channel // own, (channel % own) * 2
        for side in range(2):
            line = d_ref[to, slot + side].astype(F32)
            put_lanes(rows_ref, pl.ds((side * h + channel) * pitch, rows), line)

    copy.wait()

    def some_rows(n, carry):
        all_grads, all_normed = [], []
        for i in range(together):
            r = n * together + i
            normed = normed_ref[r]
            q_left, s_left, q_right, s_right = project(w_ref, normed)
            e_left = get_lanes(rows_ref, pl.ds(r, h, stride=pitch)) * s_left
            e_right = get_lanes(rows_ref, pl.ds(r + h * pitch, h, stride=pitch)) * s_right
            f_left = e_left * q_left * (1.0 - s_left)
            f_right = e_right * q_right * (1.0 - s_right)
            grads = jnp.concatenate([e_left, f_left, e_right, f_right], axis=0).astype(BF16)
            grads_ref[r] = grads
            all_grads.append(grads)
            all_normed.append(normed)
        sums_ref[...] += dot(
            jnp.concatenate(all_grads, axis=1), jnp.concatenate(all_normed, axis=1), NT
        )
        return carry

    lax.fori_loop(0, rows // together, some_rows, 0)
    bit = lax.rem(lax.axis_index("row"), 2)
    kept_ref[...] = sums_ref[pl.ds(pl.multiple_of(bit * 2 * h, 2 * h), 2 * h), :]
    sent_ref[...] = sums_ref[pl.ds(pl.multiple_of((1 - bit) * 2 * h, 2 * h), 2 * h), :]


def input_kernel(start, pair_hbm, grads_ref, wl, wlg, wr, wrg, *refs):
    out_hbm, back_ref, pair_ref, out_ref, in_sem, out_sems = refs[-6:]
    rows = pair_ref.shape[0]
    come = pltpu.make_async_copy(pair_hbm.at[pl.ds(start, rows)], pair_ref, in_sem)
    come.start()
    h = wl.shape[0]
    for i, ref in enumerate((wl, wlg, wr, wrg)):
        back_ref[:, pl.ds(i * h, h)] = ref[...].T
    come.wait()

    def one_row(r, carry):
        standardized, inverse_scale = layer_norm(pair_ref[r])
        d_normed = dot(back_ref[...], grads_ref[start + r])
        mean = jnp.mean(d_normed, axis=0, keepdims=True)
        input_mean = jnp.mean(d_normed * standardized, axis=0, keepdims=True)
        moved = (d_normed - mean - standardized * input_mean) * inverse_scale
        out_ref[r] = moved.astype(BF16).T
        return carry

    parts = out_sems.shape[0]
    count = rows // parts
    gone = []
    for part in range(parts):
        lax.fori_loop(part * count, (part + 1) * count, one_row, 0, unroll=8)
        at = pl.ds(part * count, count)
        to = out_hbm.at[pl.ds(start + part * count, count)]
        gone.append(pltpu.make_async_copy(out_ref.at[at], to, out_sems.at[part]))
        gone[-1].start()
    for copy in gone:
        copy.wait()


def finish_kernel(scale, mine_ref, other_ref, *out_refs):
    h = out_refs[0].shape[0]
    bit = lax.rem(lax.axis_index("row"), 2)
    for i, out_ref in enumerate(out_refs):
        at = pl.ds(i % 2 * h, h)
        mine = bit == i // 2
        out_ref[...] = jnp.where(mine, mine_ref[at, :], other_ref[at, :]) * scale


def channel_shards(sizes, pair, cotangent, *weights):
    rows, cols = sizes
    devices = rows * cols
    hidden, r, c = cotangent.shape
    dim = pair.shape[2]
    own = hidden // devices
    pieces = 2 if r % 2 == 0 else 1
    parts = 2 if r % 16 == 0 else 1
    weights = [w.T for w in weights]
    vmem = pl.BlockSpec(memory_space=pltpu.VMEM)
    hbm = pl.BlockSpec(memory_space=pltpu.HBM)
    exchange = functools.partial(
        lax.all_to_all, axis_name=("row", "col"), split_axis=0, concat_axis=0, tiled=True
    )
    stacked = pltpu.VMEM((4 * hidden, dim), BF16)
    lanes = min(c, 128)
    rows_scratch = pltpu.VMEM((c // lanes, (2 * hidden + 1) * (r + 1), lanes), F32)
    columns = r * c
    n_i, n_k = rows * r, cols * c
    pair = pltpu.with_memory_space_constraint(pair, pltpu.HBM)

    def cost(flops, *arrays):
        moved = sum(a.size * a.dtype.itemsize for a in arrays)
        return pl.CostEstimate(flops=flops, bytes_accessed=moved, transcendentals=0)

    def memory(mib):
        return pltpu.CompilerParams(vmem_limit_bytes=mib * 2**20)

    normed_shape = jax.ShapeDtypeStruct((r, dim, c), BF16)
    sent, normed = pl.pallas_call(
        functools.partial(before_kernel, own),
        in_specs=[hbm] * 6,
        out_specs=[vmem, hbm],
        out_shape=[
            jax.ShapeDtypeStruct((devices, 3 * own, r, c), BF16),
            pltpu.HBM(normed_shape.shape, BF16),
        ],
        scratch_shapes=[
            stacked,
            rows_scratch,
            pltpu.VMEM(pair.shape, BF16),
            pltpu.VMEM(normed_shape.shape, BF16),
            pltpu.SemaphoreType.DMA((parts,)),
            pltpu.SemaphoreType.DMA((parts,)),
            pltpu.SemaphoreType.DMA((4,)),
            pltpu.SemaphoreType.DMA,
        ],
        compiler_params=memory(24),
        name="before",
    )(
        pair,
        pltpu.with_memory_space_constraint(cotangent.reshape(devices, own, r, c), pltpu.HBM),
        *(pltpu.with_memory_space_constraint(w, pltpu.HBM) for w in weights),
    )

    sent = pl.pallas_call(
        functools.partial(triangle_kernel, rows, cols),
        in_specs=[vmem],
        out_specs=vmem,
        out_shape=jax.ShapeDtypeStruct((devices, 2 * own, r, c), BF16),
        scratch_shapes=[pltpu.VMEM((own, n_i, n_k), BF16)] * 3,
        compiler_params=memory(32),
        name="triangle",
    )(exchange(sent))

    half_shape = jax.ShapeDtypeStruct((2 * hidden, dim), F32)
    grads, kept, given = pl.pallas_call(
        functools.partial(gates_kernel, own),
        in_specs=[hbm] + [vmem] * 5,
        out_specs=[vmem] * 3,
        out_shape=[jax.ShapeDtypeStruct((r, 4 * hidden, c), BF16), half_shape, half_shape],
        scratch_shapes=[
            stacked,
            pltpu.VMEM((4 * hidden, dim), F32),
            rows_scratch,
            pltpu.VMEM(normed_shape.shape, BF16),
            pltpu.SemaphoreType.DMA,
        ],
        compiler_params=memory(28),
        name="gates",
    )(pltpu.with_memory_space_constraint(normed, pltpu.HBM), exchange(sent), *weights)

    def input_piece(piece, pair_gradient):
        held = [] if pair_gradient is None else [pair_gradient]
        count = r // pieces
        return pl.pallas_call(
            functools.partial(input_kernel, piece * count),
            in_specs=[hbm] + [vmem] * 5 + [hbm] * len(held),
            out_specs=hbm,
            out_shape=jax.ShapeDtypeStruct(pair.shape, BF16),
            scratch_shapes=[
                pltpu.VMEM((dim, 4 * hidden), BF16),
                pltpu.VMEM((count, c, dim), BF16),
                pltpu.VMEM((count, c, dim), BF16),
                pltpu.SemaphoreType.DMA,
                pltpu.SemaphoreType.DMA((2 if count % 8 == 0 else 1,)),
            ],
            input_output_aliases={6: 0} if held else {},
            compiler_params=memory(16),
            cost_estimate=cost(8 * hidden * dim * columns // pieces, pair),
            name="input",
        )(pair, grads, *weights, *held)

    steps = [("row", rows, 1 << i) for i in range(1, rows.bit_length() - 1)][::-1]
    steps += [("col", cols, 1 << i) for i in range(cols.bit_length() - 1)]
    pieces = min(pieces, len(steps))
    neighbours = [(i, i ^ 1) for i in range(rows)]
    pair_gradient = None
    mine = kept + lax.ppermute(given, "row", neighbours)
    for n, (axis, size, step) in enumerate(steps):
        other = lax.ppermute(mine, axis, [(i, i ^ step) for i in range(size)])
        if n < pieces:
            pair_gradient = input_piece(n, pair_gradient)
            other, pair_gradient = lax.optimization_barrier((other, pair_gradient))
        mine = mine + other
    weight_grads = pl.pallas_call(
        functools.partial(finish_kernel, 1.0 / n_i),
        in_specs=[vmem, vmem],
        out_shape=[jax.ShapeDtypeStruct((hidden, dim), F32)] * 4,
        compiler_params=memory(8),
        name="finish",
    )(mine, lax.ppermute(mine, "row", neighbours))
    return (pair_gradient, *(g.T for g in weight_grads))


def solution(mesh):
    in_specs = (P("row", "col", None), P(None, "row", "col"), P(), P(), P(), P())
    out_specs = (P("row", "col", None), P(), P(), P(), P())
    sizes = (mesh.shape["row"], mesh.shape["col"])

    def shards(pair, cotangent, *weights):
        plain = all(size > 1 and size & (size - 1) == 0 for size in sizes)
        if plain and cotangent.shape[0] % (sizes[0] * sizes[1]) == 0:
            return channel_shards(sizes, pair, cotangent, *weights)
        return gathered_shards(pair, cotangent, *weights)

    return jax.shard_map(shards, mesh=mesh, in_specs=in_specs, out_specs=out_specs, check_vma=False)
```

```python
import functools

import jax
import jax.numpy as jnp
from jax import lax
from jax.experimental import pallas as pl
from jax.experimental.pallas import tpu as pltpu
from jax.sharding import PartitionSpec as P

BF16, F32 = jnp.bfloat16, jnp.float32


def gathered_shards(pair, cotangent, w_left, w_left_gate, w_right, w_right_gate):
    pair_f = pair.astype(jnp.float32)
    average = jnp.mean(pair_f, axis=-1, keepdims=True)
    centered_input = pair_f - average
    variance = jnp.mean(centered_input * centered_input, axis=-1, keepdims=True)
    inverse_scale = 1.0 / jnp.sqrt(variance + 1e-05)
    standardized_input = centered_input * inverse_scale
    normalized_input = standardized_input.astype(jnp.bfloat16)
    stacked = jnp.concatenate([w_left, w_left_gate, w_right, w_right_gate], axis=1)
    projected = jnp.einsum(
        "rcd,dh->hrc", normalized_input, stacked, preferred_element_type=jnp.float32
    )
    q_left, p_left, q_right, p_right = jnp.split(projected, 4, axis=0)
    s_left = jax.nn.sigmoid(p_left)
    s_right = jax.nn.sigmoid(p_right)
    left = (s_left * q_left).astype(jnp.bfloat16)
    right = (s_right * q_right).astype(jnp.bfloat16)
    g_chan, left_chan, right_chan = (
        lax.all_to_all(cotangent, "col", split_axis=0, concat_axis=2, tiled=True),
        lax.all_to_all(left, "col", split_axis=0, concat_axis=2, tiled=True),
        lax.all_to_all(right, "col", split_axis=0, concat_axis=2, tiled=True),
    )
    residues = g_chan.shape[2]
    g_columns = lax.all_to_all(g_chan, "row", split_axis=2, concat_axis=1, tiled=True)
    d_left = jnp.einsum(
        "hij,hjk->hik",
        g_chan,
        lax.all_gather(right_chan, "row", axis=1, tiled=True),
        preferred_element_type=jnp.float32,
    )
    d_right = jnp.einsum(
        "hij,hik->hjk",
        g_columns,
        lax.all_gather(left_chan, "row", axis=1, tiled=True),
        preferred_element_type=jnp.float32,
    )
    d_left_tile, d_right_tile = (
        lax.all_to_all(d_left.astype(jnp.bfloat16), "col", split_axis=2, concat_axis=0, tiled=True),
        lax.all_to_all(
            d_right.astype(jnp.bfloat16), "col", split_axis=2, concat_axis=0, tiled=True
        ),
    )
    grad_l = d_left_tile.astype(jnp.float32)
    grad_r = d_right_tile.astype(jnp.float32)
    e_left = grad_l * s_left
    f_left = grad_l * q_left * s_left * (1.0 - s_left)
    e_right = grad_r * s_right
    f_right = grad_r * q_right * s_right * (1.0 - s_right)
    grads = jnp.concatenate([e_left, f_left, e_right, f_right], axis=0).astype(jnp.bfloat16)
    local_weights = jnp.einsum(
        "rcd,hrc->dh", normalized_input, grads, preferred_element_type=jnp.float32
    )
    total_weights = lax.psum(local_weights, ("row", "col")) / residues
    normalized_gradient = jnp.einsum(
        "hrc,dh->rcd", grads, stacked, preferred_element_type=jnp.float32
    )
    gradient_mean = jnp.mean(normalized_gradient, axis=-1, keepdims=True)
    gradient_input_mean = jnp.mean(normalized_gradient * standardized_input, axis=-1, keepdims=True)
    pair_gradient = (
        (normalized_gradient - gradient_mean - standardized_input * gradient_input_mean)
        * inverse_scale
    ).astype(jnp.bfloat16)
    pieces_w = jnp.split(total_weights, 4, axis=1)
    return (pair_gradient, pieces_w[0], pieces_w[1], pieces_w[2], pieces_w[3])


NT = (((1,), (1,)), ((), ()))
TN = (((0,), (0,)), ((), ()))
NN = (((1,), (0,)), ((), ()))


def dot(a, b, dims=NN):
    return lax.dot_general(a, b, dims, preferred_element_type=F32)


def stack_weights(w_refs, w_ref):
    h = w_refs[0].shape[0]
    for i, ref in enumerate(w_refs):
        w_ref[pl.ds(i * h, h), :] = ref[...]


def layer_norm(x):
    x = x.T.astype(F32)
    centered = x - jnp.mean(x, axis=0, keepdims=True)
    variance = jnp.mean(centered * centered, axis=0, keepdims=True)
    inverse_scale = lax.rsqrt(variance + 1e-05)
    return centered * inverse_scale, inverse_scale


def project(w_ref, normed):
    projected = dot(w_ref[...], normed)
    h = projected.shape[0] // 4
    q_left, p_left, q_right, p_right = (projected[i * h : (i + 1) * h] for i in range(4))
    return q_left, jax.nn.sigmoid(p_left), q_right, jax.nn.sigmoid(p_right)


def put_lanes(ref, at, value):
    lanes = ref.shape[2]
    for i in range(ref.shape[0]):
        ref[i, at, :] = value[:, i * lanes : (i + 1) * lanes]


def get_lanes(ref, at):
    return jnp.concatenate([ref[i, at, :] for i in range(ref.shape[0])], axis=1)


def before_kernel(own, pair_hbm, cot_hbm, wl, wlg, wr, wrg, out_ref, normed_hbm, *scratch):
    w_ref, *rows_refs, pair_ref, normed_ref, in_sems, out_sems, w_sems, cot_sem = scratch
    h = wl.shape[0]
    rows = pair_ref.shape[0]
    parts = in_sems.shape[0]
    count = rows // parts
    pitch = count + 1

    def come(part):
        at = pl.ds(part * count, count)
        return pltpu.make_async_copy(pair_hbm.at[at], pair_ref.at[at], in_sems.at[part])

    def leave(part):
        at = pl.ds(part * count, count)
        return pltpu.make_async_copy(normed_ref.at[at], normed_hbm.at[at], out_sems.at[part])

    def weight(i, w):
        return pltpu.make_async_copy(w, w_ref.at[pl.ds(i * h, h)], w_sems.at[i])

    for part in range(parts):
        come(part).start()
    for i, w in enumerate((wl, wlg, wr, wrg)):
        weight(i, w).start()
    cot = pltpu.make_async_copy(cot_hbm, out_ref.at[:, pl.ds(0, own)], cot_sem)
    cot.start()
    for i, w in enumerate((wl, wlg, wr, wrg)):
        weight(i, w).wait()

    def one_row(part, i):
        r = part * count + i
        normed = layer_norm(pair_ref[r])[0].astype(BF16)
        normed_ref[r] = normed
        q_left, s_left, q_right, s_right = project(w_ref, normed)
        put_lanes(rows_refs[part], pl.ds(i, h, stride=pitch), s_left * q_left)
        put_lanes(rows_refs[part], pl.ds(i + h * pitch, h, stride=pitch), s_right * q_right)

    def some_channels(part, i):
        for channel in range(i * h // count, (i + 1) * h // count):
            for side in range(2):
                at = pl.ds((side * h + channel) * pitch, count)
                line = get_lanes(rows_refs[part], at).astype(BF16)
                slot = (1 + side) * own + channel % own
                out_ref[channel // own, slot, pl.ds(part * count, count), :] = line

    for part in range(parts + 1):
        if part < parts:
            come(part).wait()
        for i in range(count):
            if part < parts:
                one_row(part, i)
            if part > 0:
                some_channels(part - 1, i)
        if part < parts:
            leave(part).start()
    for part in range(parts):
        leave(part).wait()
    cot.wait()


def triangle_kernel(rows, cols, in_ref, out_ref, g_ref, l_ref, r_ref):
    r, c = in_ref.shape[2:]
    own = g_ref.shape[0]
    for n in range(own):
        for i, ref in enumerate((g_ref, l_ref, r_ref)):
            for a in range(rows):
                for b in range(cols):
                    block = in_ref[a * cols + b, i * own + n]
                    ref[n, pl.ds(a * r, r), pl.ds(b * c, c)] = block
        for i, (dims, ref) in enumerate(((NN, r_ref), (TN, l_ref))):
            d = dot(g_ref[n], ref[n], dims).astype(BF16)
            for a in range(rows):
                for b in range(cols):
                    block = d[a * r : (a + 1) * r, b * c : (b + 1) * c]
                    out_ref[a * cols + b, n * 2 + i] = block


def gates_kernel(own, normed_hbm, d_ref, wl, wlg, wr, wrg, grads_ref, kept_ref, sent_ref, *scratch):
    w_ref, sums_ref, *rows_refs, normed_ref, sem = scratch
    copy = pltpu.make_async_copy(normed_hbm, normed_ref, sem)
    copy.start()
    h = wl.shape[0]
    rows = grads_ref.shape[0]
    parts = len(rows_refs)
    count = rows // parts
    pitch = count + 1
    stack_weights((wl, wlg, wr, wrg), w_ref)

    def some_channels(part, i):
        for channel in range(i * h // count, (i + 1) * h // count):
            to, slot = channel // own, (channel % own) * 2
            for side in range(2):
                line = d_ref[to, slot + side, pl.ds(part * count, count), :].astype(F32)
                put_lanes(rows_refs[part], pl.ds((side * h + channel) * pitch, count), line)

    def one_row(part, i):
        normed = normed_ref[part * count + i]
        q_left, s_left, q_right, s_right = project(w_ref, normed)
        e_left = get_lanes(rows_refs[part], pl.ds(i, h, stride=pitch)) * s_left
        e_right = get_lanes(rows_refs[part], pl.ds(i + h * pitch, h, stride=pitch)) * s_right
        f_left = e_left * q_left * (1.0 - s_left)
        f_right = e_right * q_right * (1.0 - s_right)
        grads = jnp.concatenate([e_left, f_left, e_right, f_right], axis=0).astype(BF16)
        grads_ref[part * count + i] = grads
        return grads, normed

    for part in range(parts + 1):
        if part == 1:
            copy.wait()
        done = []
        for i in range(count):
            if part > 0:
                done.append(one_row(part - 1, i))
            if part < parts:
                some_channels(part, i)
        if part > 0:
            all_grads, all_normed = (jnp.concatenate(x, axis=1) for x in zip(*done))
            total = dot(all_grads, all_normed, NT)
            sums_ref[...] = total if part == 1 else sums_ref[...] + total
    bit = lax.rem(lax.axis_index("row"), 2)
    kept_ref[...] = sums_ref[pl.ds(pl.multiple_of(bit * 2 * h, 2 * h), 2 * h), :]
    sent_ref[...] = sums_ref[pl.ds(pl.multiple_of((1 - bit) * 2 * h, 2 * h), 2 * h), :]


def input_kernel(start, pair_hbm, grads_ref, wl, wlg, wr, wrg, *refs):
    out_hbm, back_ref, pair_ref, out_ref, in_sem, out_sems = refs[-6:]
    rows = pair_ref.shape[0]
    come = pltpu.make_async_copy(pair_hbm.at[pl.ds(start, rows)], pair_ref, in_sem)
    come.start()
    h = wl.shape[0]
    for i, ref in enumerate((wl, wlg, wr, wrg)):
        back_ref[:, pl.ds(i * h, h)] = ref[...].T
    come.wait()

    def one_row(r, carry):
        standardized, inverse_scale = layer_norm(pair_ref[r])
        d_normed = dot(back_ref[...], grads_ref[start + r])
        mean = jnp.mean(d_normed, axis=0, keepdims=True)
        input_mean = jnp.mean(d_normed * standardized, axis=0, keepdims=True)
        moved = (d_normed - mean - standardized * input_mean) * inverse_scale
        out_ref[r] = moved.astype(BF16).T
        return carry

    parts = out_sems.shape[0]
    count = rows // parts
    gone = []
    for part in range(parts):
        lax.fori_loop(part * count, (part + 1) * count, one_row, 0, unroll=8)
        at = pl.ds(part * count, count)
        to = out_hbm.at[pl.ds(start + part * count, count)]
        gone.append(pltpu.make_async_copy(out_ref.at[at], to, out_sems.at[part]))
        gone[-1].start()
    for copy in gone:
        copy.wait()


def finish_kernel(scale, mine_ref, other_ref, *out_refs):
    h = out_refs[0].shape[0]
    bit = lax.rem(lax.axis_index("row"), 2)
    for i, out_ref in enumerate(out_refs):
        at = pl.ds(i % 2 * h, h)
        mine = bit == i // 2
        out_ref[...] = jnp.where(mine, mine_ref[at, :], other_ref[at, :]) * scale


def channel_shards(sizes, pair, cotangent, *weights):
    rows, cols = sizes
    devices = rows * cols
    hidden, r, c = cotangent.shape
    dim = pair.shape[2]
    own = hidden // devices
    pieces = 2 if r % 2 == 0 else 1
    parts = 2 if r % 32 == 0 else 1
    weights = [w.T for w in weights]
    vmem = pl.BlockSpec(memory_space=pltpu.VMEM)
    hbm = pl.BlockSpec(memory_space=pltpu.HBM)
    exchange = functools.partial(
        lax.all_to_all, axis_name=("row", "col"), split_axis=0, concat_axis=0, tiled=True
    )
    stacked = pltpu.VMEM((4 * hidden, dim), BF16)
    lanes = min(c, 128)
    rows_scratch = pltpu.VMEM((c // lanes, (2 * hidden + 1) * (r // parts + 1), lanes), F32)
    columns = r * c
    n_i, n_k = rows * r, cols * c
    pair = pltpu.with_memory_space_constraint(pair, pltpu.HBM)

    def cost(flops, *arrays):
        moved = sum(a.size * a.dtype.itemsize for a in arrays)
        return pl.CostEstimate(flops=flops, bytes_accessed=moved, transcendentals=0)

    def memory(mib):
        return pltpu.CompilerParams(vmem_limit_bytes=mib * 2**20)

    normed_shape = jax.ShapeDtypeStruct((r, dim, c), BF16)
    sent, normed = pl.pallas_call(
        functools.partial(before_kernel, own),
        in_specs=[hbm] * 6,
        out_specs=[vmem, hbm],
        out_shape=[
            jax.ShapeDtypeStruct((devices, 3 * own, r, c), BF16),
            pltpu.HBM(normed_shape.shape, BF16),
        ],
        scratch_shapes=[
            stacked,
            *[rows_scratch] * parts,
            pltpu.VMEM(pair.shape, BF16),
            pltpu.VMEM(normed_shape.shape, BF16),
            pltpu.SemaphoreType.DMA((parts,)),
            pltpu.SemaphoreType.DMA((parts,)),
            pltpu.SemaphoreType.DMA((4,)),
            pltpu.SemaphoreType.DMA,
        ],
        compiler_params=memory(24),
        name="before",
    )(
        pair,
        pltpu.with_memory_space_constraint(cotangent.reshape(devices, own, r, c), pltpu.HBM),
        *(pltpu.with_memory_space_constraint(w, pltpu.HBM) for w in weights),
    )

    sent = pl.pallas_call(
        functools.partial(triangle_kernel, rows, cols),
        in_specs=[vmem],
        out_specs=vmem,
        out_shape=jax.ShapeDtypeStruct((devices, 2 * own, r, c), BF16),
        scratch_shapes=[pltpu.VMEM((own, n_i, n_k), BF16)] * 3,
        compiler_params=memory(32),
        name="triangle",
    )(exchange(sent))

    half_shape = jax.ShapeDtypeStruct((2 * hidden, dim), F32)
    grads, kept, given = pl.pallas_call(
        functools.partial(gates_kernel, own),
        in_specs=[hbm] + [vmem] * 5,
        out_specs=[vmem] * 3,
        out_shape=[jax.ShapeDtypeStruct((r, 4 * hidden, c), BF16), half_shape, half_shape],
        scratch_shapes=[
            stacked,
            pltpu.VMEM((4 * hidden, dim), F32),
            *[rows_scratch] * parts,
            pltpu.VMEM(normed_shape.shape, BF16),
            pltpu.SemaphoreType.DMA,
        ],
        compiler_params=memory(28),
        name="gates",
    )(pltpu.with_memory_space_constraint(normed, pltpu.HBM), exchange(sent), *weights)

    def input_piece(piece, pair_gradient):
        held = [] if pair_gradient is None else [pair_gradient]
        count = r // pieces
        return pl.pallas_call(
            functools.partial(input_kernel, piece * count),
            in_specs=[hbm] + [vmem] * 5 + [hbm] * len(held),
            out_specs=hbm,
            out_shape=jax.ShapeDtypeStruct(pair.shape, BF16),
            scratch_shapes=[
                pltpu.VMEM((dim, 4 * hidden), BF16),
                pltpu.VMEM((count, c, dim), BF16),
                pltpu.VMEM((count, c, dim), BF16),
                pltpu.SemaphoreType.DMA,
                pltpu.SemaphoreType.DMA((2 if count % 8 == 0 else 1,)),
            ],
            input_output_aliases={6: 0} if held else {},
            compiler_params=memory(16),
            cost_estimate=cost(8 * hidden * dim * columns // pieces, pair),
            name="input",
        )(pair, grads, *weights, *held)

    steps = [("row", rows, 1 << i) for i in range(1, rows.bit_length() - 1)][::-1]
    steps += [("col", cols, 1 << i) for i in range(cols.bit_length() - 1)]
    pieces = min(pieces, len(steps))
    neighbours = [(i, i ^ 1) for i in range(rows)]
    pair_gradient = None
    mine = kept + lax.ppermute(given, "row", neighbours)
    for n, (axis, size, step) in enumerate(steps):
        other = lax.ppermute(mine, axis, [(i, i ^ step) for i in range(size)])
        if n < pieces:
            pair_gradient = input_piece(n, pair_gradient)
            other, pair_gradient = lax.optimization_barrier((other, pair_gradient))
        mine = mine + other
    weight_grads = pl.pallas_call(
        functools.partial(finish_kernel, 1.0 / n_i),
        in_specs=[vmem, vmem],
        out_shape=[jax.ShapeDtypeStruct((hidden, dim), F32)] * 4,
        compiler_params=memory(8),
        name="finish",
    )(mine, lax.ppermute(mine, "row", neighbours))
    return (pair_gradient, *(g.T for g in weight_grads))


def solution(mesh):
    in_specs = (P("row", "col", None), P(None, "row", "col"), P(), P(), P(), P())
    out_specs = (P("row", "col", None), P(), P(), P(), P())
    sizes = (mesh.shape["row"], mesh.shape["col"])

    def shards(pair, cotangent, *weights):
        plain = all(size > 1 and size & (size - 1) == 0 for size in sizes)
        if plain and cotangent.shape[0] % (sizes[0] * sizes[1]) == 0:
            return channel_shards(sizes, pair, cotangent, *weights)
        return gathered_shards(pair, cotangent, *weights)

    return jax.shard_map(shards, mesh=mesh, in_specs=in_specs, out_specs=out_specs, check_vma=False)
```

```python
import functools

import jax
import jax.numpy as jnp
from jax import lax
from jax.experimental import pallas as pl
from jax.experimental.pallas import tpu as pltpu
from jax.sharding import PartitionSpec as P

BF16, F32 = jnp.bfloat16, jnp.float32


def gathered_shards(pair, cotangent, w_left, w_left_gate, w_right, w_right_gate):
    pair_f = pair.astype(jnp.float32)
    average = jnp.mean(pair_f, axis=-1, keepdims=True)
    centered_input = pair_f - average
    variance = jnp.mean(centered_input * centered_input, axis=-1, keepdims=True)
    inverse_scale = 1.0 / jnp.sqrt(variance + 1e-05)
    standardized_input = centered_input * inverse_scale
    normalized_input = standardized_input.astype(jnp.bfloat16)
    stacked = jnp.concatenate([w_left, w_left_gate, w_right, w_right_gate], axis=1)
    projected = jnp.einsum(
        "rcd,dh->hrc", normalized_input, stacked, preferred_element_type=jnp.float32
    )
    q_left, p_left, q_right, p_right = jnp.split(projected, 4, axis=0)
    s_left = jax.nn.sigmoid(p_left)
    s_right = jax.nn.sigmoid(p_right)
    left = (s_left * q_left).astype(jnp.bfloat16)
    right = (s_right * q_right).astype(jnp.bfloat16)
    g_chan, left_chan, right_chan = (
        lax.all_to_all(cotangent, "col", split_axis=0, concat_axis=2, tiled=True),
        lax.all_to_all(left, "col", split_axis=0, concat_axis=2, tiled=True),
        lax.all_to_all(right, "col", split_axis=0, concat_axis=2, tiled=True),
    )
    residues = g_chan.shape[2]
    g_columns = lax.all_to_all(g_chan, "row", split_axis=2, concat_axis=1, tiled=True)
    d_left = jnp.einsum(
        "hij,hjk->hik",
        g_chan,
        lax.all_gather(right_chan, "row", axis=1, tiled=True),
        preferred_element_type=jnp.float32,
    )
    d_right = jnp.einsum(
        "hij,hik->hjk",
        g_columns,
        lax.all_gather(left_chan, "row", axis=1, tiled=True),
        preferred_element_type=jnp.float32,
    )
    d_left_tile, d_right_tile = (
        lax.all_to_all(d_left.astype(jnp.bfloat16), "col", split_axis=2, concat_axis=0, tiled=True),
        lax.all_to_all(
            d_right.astype(jnp.bfloat16), "col", split_axis=2, concat_axis=0, tiled=True
        ),
    )
    grad_l = d_left_tile.astype(jnp.float32)
    grad_r = d_right_tile.astype(jnp.float32)
    e_left = grad_l * s_left
    f_left = grad_l * q_left * s_left * (1.0 - s_left)
    e_right = grad_r * s_right
    f_right = grad_r * q_right * s_right * (1.0 - s_right)
    grads = jnp.concatenate([e_left, f_left, e_right, f_right], axis=0).astype(jnp.bfloat16)
    local_weights = jnp.einsum(
        "rcd,hrc->dh", normalized_input, grads, preferred_element_type=jnp.float32
    )
    total_weights = lax.psum(local_weights, ("row", "col")) / residues
    normalized_gradient = jnp.einsum(
        "hrc,dh->rcd", grads, stacked, preferred_element_type=jnp.float32
    )
    gradient_mean = jnp.mean(normalized_gradient, axis=-1, keepdims=True)
    gradient_input_mean = jnp.mean(normalized_gradient * standardized_input, axis=-1, keepdims=True)
    pair_gradient = (
        (normalized_gradient - gradient_mean - standardized_input * gradient_input_mean)
        * inverse_scale
    ).astype(jnp.bfloat16)
    pieces_w = jnp.split(total_weights, 4, axis=1)
    return (pair_gradient, pieces_w[0], pieces_w[1], pieces_w[2], pieces_w[3])


NT = (((1,), (1,)), ((), ()))
TN = (((0,), (0,)), ((), ()))
NN = (((1,), (0,)), ((), ()))


def dot(a, b, dims=NN):
    return lax.dot_general(a, b, dims, preferred_element_type=F32)


def stack_weights(w_refs, w_ref):
    h = w_refs[0].shape[0]
    for i, ref in enumerate(w_refs):
        w_ref[pl.ds(i * h, h), :] = ref[...]


def layer_norm(x):
    x = x.T.astype(F32)
    centered = x - jnp.mean(x, axis=0, keepdims=True)
    variance = jnp.mean(centered * centered, axis=0, keepdims=True)
    inverse_scale = lax.rsqrt(variance + 1e-05)
    return centered * inverse_scale, inverse_scale


def project(w_ref, normed):
    projected = dot(w_ref[...], normed)
    h = projected.shape[0] // 4
    q_left, p_left, q_right, p_right = (projected[i * h : (i + 1) * h] for i in range(4))
    return q_left, jax.nn.sigmoid(p_left), q_right, jax.nn.sigmoid(p_right)


def put_lanes(ref, at, value):
    lanes = ref.shape[2]
    for i in range(ref.shape[0]):
        ref[i, at, :] = value[:, i * lanes : (i + 1) * lanes]


def get_lanes(ref, at):
    return jnp.concatenate([ref[i, at, :] for i in range(ref.shape[0])], axis=1)


def before_kernel(own, pair_hbm, cot_hbm, wl, wlg, wr, wrg, out_ref, normed_hbm, *scratch):
    w_ref, *rows_refs, pair_ref, normed_ref, in_sems, out_sems, w_sems, cot_sem = scratch
    h = wl.shape[0]
    rows = pair_ref.shape[0]
    parts = in_sems.shape[0]
    count = rows // parts
    pitch = count + 1

    def come(part):
        at = pl.ds(part * count, count)
        return pltpu.make_async_copy(pair_hbm.at[at], pair_ref.at[at], in_sems.at[part])

    def leave(part):
        at = pl.ds(part * count, count)
        return pltpu.make_async_copy(normed_ref.at[at], normed_hbm.at[at], out_sems.at[part])

    def weight(i, w):
        return pltpu.make_async_copy(w, w_ref.at[pl.ds(i * h, h)], w_sems.at[i])

    for part in range(parts):
        come(part).start()
    for i, w in enumerate((wl, wlg, wr, wrg)):
        weight(i, w).start()
    cot = pltpu.make_async_copy(cot_hbm, out_ref.at[:, pl.ds(0, own)], cot_sem)
    cot.start()
    for i, w in enumerate((wl, wlg, wr, wrg)):
        weight(i, w).wait()

    def one_row(part, i):
        r = part * count + i
        normed = layer_norm(pair_ref[r])[0].astype(BF16)
        normed_ref[r] = normed
        q_left, s_left, q_right, s_right = project(w_ref, normed)
        put_lanes(rows_refs[part], pl.ds(i, h, stride=pitch), s_left * q_left)
        put_lanes(rows_refs[part], pl.ds(i + h * pitch, h, stride=pitch), s_right * q_right)

    def some_channels(part, i):
        for channel in range(i * h // count, (i + 1) * h // count):
            for side in range(2):
                at = pl.ds((side * h + channel) * pitch, count)
                line = get_lanes(rows_refs[part], at).astype(BF16)
                slot = (1 + side) * own + channel % own
                out_ref[channel // own, slot, pl.ds(part * count, count), :] = line

    for part in range(parts + 1):
        if part < parts:
            come(part).wait()
        for i in range(count):
            if part < parts:
                one_row(part, i)
            if part > 0:
                some_channels(part - 1, i)
        if part < parts:
            leave(part).start()
    for part in range(parts):
        leave(part).wait()
    cot.wait()


def triangle_kernel(rows, cols, in_ref, out_ref, g_ref, l_ref, r_ref):
    r, c = in_ref.shape[2:]
    own = g_ref.shape[0]
    for n in range(own):
        for i, ref in enumerate((g_ref, l_ref, r_ref)):
            for a in range(rows):
                for b in range(cols):
                    block = in_ref[a * cols + b, i * own + n]
                    ref[n, pl.ds(a * r, r), pl.ds(b * c, c)] = block
        for i, (dims, ref) in enumerate(((NN, r_ref), (TN, l_ref))):
            d = dot(g_ref[n], ref[n], dims).astype(BF16)
            for a in range(rows):
                for b in range(cols):
                    block = d[a * r : (a + 1) * r, b * c : (b + 1) * c]
                    out_ref[a * cols + b, n * 2 + i] = block


def gates_kernel(own, normed_hbm, d_ref, wl, wlg, wr, wrg, grads_ref, kept_ref, sent_ref, *scratch):
    w_ref, sums_ref, *rows_refs, normed_ref, sem = scratch
    copy = pltpu.make_async_copy(normed_hbm, normed_ref, sem)
    copy.start()
    h = wl.shape[0]
    rows = grads_ref.shape[0]
    parts = len(rows_refs)
    count = rows // parts
    pitch = count + 1
    stack_weights((wl, wlg, wr, wrg), w_ref)

    def some_channels(part, i):
        for channel in range(i * h // count, (i + 1) * h // count):
            to, slot = channel // own, (channel % own) * 2
            for side in range(2):
                line = d_ref[to, slot + side, pl.ds(part * count, count), :].astype(F32)
                put_lanes(rows_refs[part], pl.ds((side * h + channel) * pitch, count), line)

    def one_row(part, i):
        normed = normed_ref[part * count + i]
        q_left, s_left, q_right, s_right = project(w_ref, normed)
        e_left = get_lanes(rows_refs[part], pl.ds(i, h, stride=pitch)) * s_left
        e_right = get_lanes(rows_refs[part], pl.ds(i + h * pitch, h, stride=pitch)) * s_right
        f_left = e_left * q_left * (1.0 - s_left)
        f_right = e_right * q_right * (1.0 - s_right)
        grads = jnp.concatenate([e_left, f_left, e_right, f_right], axis=0).astype(BF16)
        grads_ref[part * count + i] = grads
        return grads, normed

    for part in range(parts + 1):
        if part == 1:
            copy.wait()
        done = []
        for i in range(count):
            if part > 0:
                done.append(one_row(part - 1, i))
            if part < parts:
                some_channels(part, i)
        if part > 0:
            all_grads, all_normed = (jnp.concatenate(x, axis=1) for x in zip(*done))
            total = dot(all_grads, all_normed, NT)
            sums_ref[...] = total if part == 1 else sums_ref[...] + total
    bit = lax.rem(lax.axis_index("row"), 2)
    kept_ref[...] = sums_ref[pl.ds(pl.multiple_of(bit * 2 * h, 2 * h), 2 * h), :]
    sent_ref[...] = sums_ref[pl.ds(pl.multiple_of((1 - bit) * 2 * h, 2 * h), 2 * h), :]


def input_kernel(start, pair_hbm, grads_ref, wl, wlg, wr, wrg, *refs):
    out_hbm, back_ref, pair_ref, out_ref, in_sem, out_sems = refs[-6:]
    rows = pair_ref.shape[0]
    come = pltpu.make_async_copy(pair_hbm.at[pl.ds(start, rows)], pair_ref, in_sem)
    come.start()
    h = wl.shape[0]
    for i, ref in enumerate((wl, wlg, wr, wrg)):
        back_ref[:, pl.ds(i * h, h)] = ref[...].T
    come.wait()

    def one_row(r, carry):
        standardized, inverse_scale = layer_norm(pair_ref[r])
        d_normed = dot(back_ref[...], grads_ref[start + r])
        mean = jnp.mean(d_normed, axis=0, keepdims=True)
        input_mean = jnp.mean(d_normed * standardized, axis=0, keepdims=True)
        moved = (d_normed - mean - standardized * input_mean) * inverse_scale
        out_ref[r] = moved.astype(BF16).T
        return carry

    parts = out_sems.shape[0]
    count = rows // parts
    gone = []
    for part in range(parts):
        lax.fori_loop(part * count, (part + 1) * count, one_row, 0, unroll=8)
        at = pl.ds(part * count, count)
        to = out_hbm.at[pl.ds(start + part * count, count)]
        gone.append(pltpu.make_async_copy(out_ref.at[at], to, out_sems.at[part]))
        gone[-1].start()
    for copy in gone:
        copy.wait()


def finish_kernel(scale, mine_ref, other_ref, *out_refs):
    h = out_refs[0].shape[0]
    bit = lax.rem(lax.axis_index("row"), 2)
    for i, out_ref in enumerate(out_refs):
        at = pl.ds(i % 2 * h, h)
        mine = bit == i // 2
        out_ref[...] = jnp.where(mine, mine_ref[at, :], other_ref[at, :]) * scale


def channel_shards(sizes, pair, cotangent, *weights):
    rows, cols = sizes
    devices = rows * cols
    hidden, r, c = cotangent.shape
    dim = pair.shape[2]
    own = hidden // devices
    pieces = 2 if r % 2 == 0 else 1
    parts = 2 if r % 32 == 0 else 1
    weights = [w.T for w in weights]
    vmem = pl.BlockSpec(memory_space=pltpu.VMEM)
    hbm = pl.BlockSpec(memory_space=pltpu.HBM)
    exchange = functools.partial(
        lax.all_to_all, axis_name=("row", "col"), split_axis=0, concat_axis=0, tiled=True
    )
    stacked = pltpu.VMEM((4 * hidden, dim), BF16)
    lanes = min(c, 128)
    rows_scratch = pltpu.VMEM((c // lanes, (2 * hidden + 1) * (r // parts + 1), lanes), F32)
    columns = r * c
    n_i, n_k = rows * r, cols * c
    pair = pltpu.with_memory_space_constraint(pair, pltpu.HBM)

    def cost(flops, *arrays):
        moved = sum(a.size * a.dtype.itemsize for a in arrays)
        return pl.CostEstimate(flops=flops, bytes_accessed=moved, transcendentals=0)

    def memory(mib):
        return pltpu.CompilerParams(vmem_limit_bytes=mib * 2**20)

    normed_shape = jax.ShapeDtypeStruct((r, dim, c), BF16)
    sent, normed = pl.pallas_call(
        functools.partial(before_kernel, own),
        in_specs=[hbm] * 6,
        out_specs=[vmem, hbm],
        out_shape=[
            jax.ShapeDtypeStruct((devices, 3 * own, r, c), BF16),
            pltpu.HBM(normed_shape.shape, BF16),
        ],
        scratch_shapes=[
            stacked,
            *[rows_scratch] * parts,
            pltpu.VMEM(pair.shape, BF16),
            pltpu.VMEM(normed_shape.shape, BF16),
            pltpu.SemaphoreType.DMA((parts,)),
            pltpu.SemaphoreType.DMA((parts,)),
            pltpu.SemaphoreType.DMA((4,)),
            pltpu.SemaphoreType.DMA,
        ],
        compiler_params=memory(24),
        name="before",
    )(
        pair,
        pltpu.with_memory_space_constraint(cotangent.reshape(devices, own, r, c), pltpu.HBM),
        *(pltpu.with_memory_space_constraint(w, pltpu.HBM) for w in weights),
    )

    sent = pl.pallas_call(
        functools.partial(triangle_kernel, rows, cols),
        in_specs=[vmem],
        out_specs=vmem,
        out_shape=jax.ShapeDtypeStruct((devices, 2 * own, r, c), BF16),
        scratch_shapes=[pltpu.VMEM((own, n_i, n_k), BF16)] * 3,
        compiler_params=memory(32),
        name="triangle",
    )(exchange(sent))

    half_shape = jax.ShapeDtypeStruct((2 * hidden, dim), F32)
    grads, kept, given = pl.pallas_call(
        functools.partial(gates_kernel, own),
        in_specs=[hbm] + [vmem] * 5,
        out_specs=[vmem] * 3,
        out_shape=[jax.ShapeDtypeStruct((r, 4 * hidden, c), BF16), half_shape, half_shape],
        scratch_shapes=[
            stacked,
            pltpu.VMEM((4 * hidden, dim), F32),
            *[rows_scratch] * parts,
            pltpu.VMEM(normed_shape.shape, BF16),
            pltpu.SemaphoreType.DMA,
        ],
        compiler_params=memory(28),
        name="gates",
    )(pltpu.with_memory_space_constraint(normed, pltpu.HBM), exchange(sent), *weights)

    def input_piece(piece, pair_gradient):
        held = [] if pair_gradient is None else [pair_gradient]
        count = r // pieces
        return pl.pallas_call(
            functools.partial(input_kernel, piece * count),
            in_specs=[hbm] + [vmem] * 5 + [hbm] * len(held),
            out_specs=hbm,
            out_shape=jax.ShapeDtypeStruct(pair.shape, BF16),
            scratch_shapes=[
                pltpu.VMEM((dim, 4 * hidden), BF16),
                pltpu.VMEM((count, c, dim), BF16),
                pltpu.VMEM((count, c, dim), BF16),
                pltpu.SemaphoreType.DMA,
                pltpu.SemaphoreType.DMA((2 if count % 8 == 0 else 1,)),
            ],
            input_output_aliases={6: 0} if held else {},
            compiler_params=memory(16),
            cost_estimate=cost(8 * hidden * dim * columns // pieces, pair),
            name="input",
        )(pair, grads, *weights, *held)

    neighbours = [(i, i ^ 1) for i in range(rows)]
    alike = [
        [i * cols + j for i in range(bit, rows, 2) for j in range(cols)] for bit in range(2)
    ]
    share = functools.partial(exchange, axis_index_groups=alike)
    mine = kept + lax.ppermute(given, "row", neighbours)
    blocks = mine.reshape(devices // 2, -1, dim)
    pair_gradient = None
    for piece in range(pieces):
        if piece == 1:
            blocks = jnp.broadcast_to(jnp.sum(blocks, axis=0, keepdims=True), blocks.shape)
        blocks = share(blocks)
        pair_gradient = input_piece(piece, pair_gradient)
        blocks, pair_gradient = lax.optimization_barrier((blocks, pair_gradient))
    mine = blocks.reshape(mine.shape)
    weight_grads = pl.pallas_call(
        functools.partial(finish_kernel, 1.0 / n_i),
        in_specs=[vmem, vmem],
        out_shape=[jax.ShapeDtypeStruct((hidden, dim), F32)] * 4,
        compiler_params=memory(8),
        name="finish",
    )(mine, lax.ppermute(mine, "row", neighbours))
    return (pair_gradient, *(g.T for g in weight_grads))


def solution(mesh):
    in_specs = (P("row", "col", None), P(None, "row", "col"), P(), P(), P(), P())
    out_specs = (P("row", "col", None), P(), P(), P(), P())
    sizes = (mesh.shape["row"], mesh.shape["col"])

    def shards(pair, cotangent, *weights):
        plain = all(size > 1 and size & (size - 1) == 0 for size in sizes)
        if plain and cotangent.shape[0] % (sizes[0] * sizes[1]) == 0:
            return channel_shards(sizes, pair, cotangent, *weights)
        return gathered_shards(pair, cotangent, *weights)

    return jax.shard_map(shards, mesh=mesh, in_specs=in_specs, out_specs=out_specs, check_vma=False)
```

```python
import functools

import jax
import jax.numpy as jnp
from jax import lax
from jax.experimental import pallas as pl
from jax.experimental.pallas import tpu as pltpu
from jax.sharding import PartitionSpec as P

BF16, F32 = jnp.bfloat16, jnp.float32


def gathered_shards(pair, cotangent, w_left, w_left_gate, w_right, w_right_gate):
    pair_f = pair.astype(jnp.float32)
    average = jnp.mean(pair_f, axis=-1, keepdims=True)
    centered_input = pair_f - average
    variance = jnp.mean(centered_input * centered_input, axis=-1, keepdims=True)
    inverse_scale = 1.0 / jnp.sqrt(variance + 1e-05)
    standardized_input = centered_input * inverse_scale
    normalized_input = standardized_input.astype(jnp.bfloat16)
    stacked = jnp.concatenate([w_left, w_left_gate, w_right, w_right_gate], axis=1)
    projected = jnp.einsum(
        "rcd,dh->hrc", normalized_input, stacked, preferred_element_type=jnp.float32
    )
    q_left, p_left, q_right, p_right = jnp.split(projected, 4, axis=0)
    s_left = jax.nn.sigmoid(p_left)
    s_right = jax.nn.sigmoid(p_right)
    left = (s_left * q_left).astype(jnp.bfloat16)
    right = (s_right * q_right).astype(jnp.bfloat16)
    g_chan, left_chan, right_chan = (
        lax.all_to_all(cotangent, "col", split_axis=0, concat_axis=2, tiled=True),
        lax.all_to_all(left, "col", split_axis=0, concat_axis=2, tiled=True),
        lax.all_to_all(right, "col", split_axis=0, concat_axis=2, tiled=True),
    )
    residues = g_chan.shape[2]
    g_columns = lax.all_to_all(g_chan, "row", split_axis=2, concat_axis=1, tiled=True)
    d_left = jnp.einsum(
        "hij,hjk->hik",
        g_chan,
        lax.all_gather(right_chan, "row", axis=1, tiled=True),
        preferred_element_type=jnp.float32,
    )
    d_right = jnp.einsum(
        "hij,hik->hjk",
        g_columns,
        lax.all_gather(left_chan, "row", axis=1, tiled=True),
        preferred_element_type=jnp.float32,
    )
    d_left_tile, d_right_tile = (
        lax.all_to_all(d_left.astype(jnp.bfloat16), "col", split_axis=2, concat_axis=0, tiled=True),
        lax.all_to_all(
            d_right.astype(jnp.bfloat16), "col", split_axis=2, concat_axis=0, tiled=True
        ),
    )
    grad_l = d_left_tile.astype(jnp.float32)
    grad_r = d_right_tile.astype(jnp.float32)
    e_left = grad_l * s_left
    f_left = grad_l * q_left * s_left * (1.0 - s_left)
    e_right = grad_r * s_right
    f_right = grad_r * q_right * s_right * (1.0 - s_right)
    grads = jnp.concatenate([e_left, f_left, e_right, f_right], axis=0).astype(jnp.bfloat16)
    local_weights = jnp.einsum(
        "rcd,hrc->dh", normalized_input, grads, preferred_element_type=jnp.float32
    )
    total_weights = lax.psum(local_weights, ("row", "col")) / residues
    normalized_gradient = jnp.einsum(
        "hrc,dh->rcd", grads, stacked, preferred_element_type=jnp.float32
    )
    gradient_mean = jnp.mean(normalized_gradient, axis=-1, keepdims=True)
    gradient_input_mean = jnp.mean(normalized_gradient * standardized_input, axis=-1, keepdims=True)
    pair_gradient = (
        (normalized_gradient - gradient_mean - standardized_input * gradient_input_mean)
        * inverse_scale
    ).astype(jnp.bfloat16)
    pieces_w = jnp.split(total_weights, 4, axis=1)
    return (pair_gradient, pieces_w[0], pieces_w[1], pieces_w[2], pieces_w[3])


NT = (((1,), (1,)), ((), ()))
TN = (((0,), (0,)), ((), ()))
NN = (((1,), (0,)), ((), ()))


def dot(a, b, dims=NN):
    return lax.dot_general(a, b, dims, preferred_element_type=F32)


def stack_weights(w_refs, w_ref):
    h = w_refs[0].shape[0]
    for i, ref in enumerate(w_refs):
        w_ref[pl.ds(i * h, h), :] = ref[...]


def layer_norm(x):
    x = x.T.astype(F32)
    centered = x - jnp.mean(x, axis=0, keepdims=True)
    variance = jnp.mean(centered * centered, axis=0, keepdims=True)
    inverse_scale = lax.rsqrt(variance + 1e-05)
    return centered * inverse_scale, inverse_scale


def project(w_ref, normed):
    projected = dot(w_ref[...], normed)
    h = projected.shape[0] // 4
    q_left, p_left, q_right, p_right = (projected[i * h : (i + 1) * h] for i in range(4))
    return q_left, jax.nn.sigmoid(p_left), q_right, jax.nn.sigmoid(p_right)


def put_lanes(ref, at, value):
    lanes = ref.shape[2]
    for i in range(ref.shape[0]):
        ref[i, at, :] = value[:, i * lanes : (i + 1) * lanes]


def get_lanes(ref, at):
    return jnp.concatenate([ref[i, at, :] for i in range(ref.shape[0])], axis=1)


def before_kernel(own, pair_hbm, cot_hbm, wl, wlg, wr, wrg, out_ref, normed_hbm, *scratch):
    w_ref, *rows_refs, pair_ref, normed_ref, in_sems, out_sems, w_sems, cot_sem = scratch
    h = wl.shape[0]
    rows = pair_ref.shape[0]
    parts = in_sems.shape[0]
    count = rows // parts
    pitch = count + 1

    def come(part):
        at = pl.ds(part * count, count)
        return pltpu.make_async_copy(pair_hbm.at[at], pair_ref.at[at], in_sems.at[part])

    def leave(part):
        at = pl.ds(part * count, count)
        return pltpu.make_async_copy(normed_ref.at[at], normed_hbm.at[at], out_sems.at[part])

    def weight(i, w):
        return pltpu.make_async_copy(w, w_ref.at[pl.ds(i * h, h)], w_sems.at[i])

    for i, w in enumerate((wl, wlg, wr, wrg)):
        weight(i, w).start()
    for part in range(parts):
        come(part).start()
    cot = pltpu.make_async_copy(cot_hbm, out_ref.at[:, pl.ds(0, own)], cot_sem)
    cot.start()
    for i, w in enumerate((wl, wlg, wr, wrg)):
        weight(i, w).wait()

    def one_row(part, i):
        r = part * count + i
        normed = layer_norm(pair_ref[r])[0].astype(BF16)
        normed_ref[r] = normed
        q_left, s_left, q_right, s_right = project(w_ref, normed)
        put_lanes(rows_refs[part], pl.ds(i, h, stride=pitch), s_left * q_left)
        put_lanes(rows_refs[part], pl.ds(i + h * pitch, h, stride=pitch), s_right * q_right)

    def some_channels(part, i):
        for channel in range(i * h // count, (i + 1) * h // count):
            for side in range(2):
                at = pl.ds((side * h + channel) * pitch, count)
                line = get_lanes(rows_refs[part], at).astype(BF16)
                slot = (1 + side) * own + channel % own
                out_ref[channel // own, slot, pl.ds(part * count, count), :] = line

    for part in range(parts + 1):
        if part < parts:
            come(part).wait()
        for i in range(count):
            if part < parts:
                one_row(part, i)
            if part > 0:
                some_channels(part - 1, i)
        if part < parts:
            leave(part).start()
    for part in range(parts):
        leave(part).wait()
    cot.wait()


def triangle_kernel(rows, cols, in_ref, out_ref, g_ref, l_ref, r_ref):
    r, c = in_ref.shape[2:]
    own = g_ref.shape[0]
    for n in range(own):
        for i, ref in enumerate((g_ref, l_ref, r_ref)):
            for a in range(rows):
                for b in range(cols):
                    block = in_ref[a * cols + b, i * own + n]
                    ref[n, pl.ds(a * r, r), pl.ds(b * c, c)] = block
        for i, (dims, ref) in enumerate(((NN, r_ref), (TN, l_ref))):
            d = dot(g_ref[n], ref[n], dims).astype(BF16)
            for a in range(rows):
                for b in range(cols):
                    block = d[a * r : (a + 1) * r, b * c : (b + 1) * c]
                    out_ref[a * cols + b, n * 2 + i] = block


def gates_kernel(own, normed_hbm, d_ref, wl, wlg, wr, wrg, grads_ref, kept_ref, sent_ref, *scratch):
    w_ref, sums_ref, *rows_refs, normed_ref, sem = scratch
    copy = pltpu.make_async_copy(normed_hbm, normed_ref, sem)
    copy.start()
    h = wl.shape[0]
    rows = grads_ref.shape[0]
    parts = len(rows_refs)
    count = rows // parts
    pitch = count + 1
    stack_weights((wl, wlg, wr, wrg), w_ref)

    def some_channels(part, i):
        for channel in range(i * h // count, (i + 1) * h // count):
            to, slot = channel // own, (channel % own) * 2
            for side in range(2):
                line = d_ref[to, slot + side, pl.ds(part * count, count), :].astype(F32)
                put_lanes(rows_refs[part], pl.ds((side * h + channel) * pitch, count), line)

    def one_row(part, i):
        normed = normed_ref[part * count + i]
        q_left, s_left, q_right, s_right = project(w_ref, normed)
        e_left = get_lanes(rows_refs[part], pl.ds(i, h, stride=pitch)) * s_left
        e_right = get_lanes(rows_refs[part], pl.ds(i + h * pitch, h, stride=pitch)) * s_right
        f_left = e_left * q_left * (1.0 - s_left)
        f_right = e_right * q_right * (1.0 - s_right)
        grads = jnp.concatenate([e_left, f_left, e_right, f_right], axis=0).astype(BF16)
        grads_ref[part * count + i] = grads
        return grads, normed

    together = 8 if count % 8 == 0 else count
    sums_ref[...] = jnp.zeros_like(sums_ref)
    for part in range(parts + 1):
        if part == 1:
            copy.wait()
        done = []
        for i in range(count):
            if part > 0:
                done.append(one_row(part - 1, i))
            if part < parts:
                some_channels(part, i)
            if len(done) == together:
                all_grads, all_normed = (jnp.concatenate(x, axis=1) for x in zip(*done))
                sums_ref[...] += dot(all_grads, all_normed, NT)
                done = []
    bit = lax.rem(lax.axis_index("row"), 2)
    kept_ref[...] = sums_ref[pl.ds(pl.multiple_of(bit * 2 * h, 2 * h), 2 * h), :]
    sent_ref[...] = sums_ref[pl.ds(pl.multiple_of((1 - bit) * 2 * h, 2 * h), 2 * h), :]


def input_kernel(start, pair_hbm, grads_ref, wl, wlg, wr, wrg, *refs):
    out_hbm, back_ref, pair_ref, out_ref, in_sem, out_sems = refs[-6:]
    rows = pair_ref.shape[0]
    come = pltpu.make_async_copy(pair_hbm.at[pl.ds(start, rows)], pair_ref, in_sem)
    come.start()
    h = wl.shape[0]
    for i, ref in enumerate((wl, wlg, wr, wrg)):
        back_ref[:, pl.ds(i * h, h)] = ref[...].T
    come.wait()

    def one_row(r, carry):
        standardized, inverse_scale = layer_norm(pair_ref[r])
        d_normed = dot(back_ref[...], grads_ref[start + r])
        mean = jnp.mean(d_normed, axis=0, keepdims=True)
        input_mean = jnp.mean(d_normed * standardized, axis=0, keepdims=True)
        moved = (d_normed - mean - standardized * input_mean) * inverse_scale
        out_ref[r] = moved.astype(BF16).T
        return carry

    parts = out_sems.shape[0]
    count = rows // parts
    gone = []
    for part in range(parts):
        lax.fori_loop(part * count, (part + 1) * count, one_row, 0, unroll=8)
        at = pl.ds(part * count, count)
        to = out_hbm.at[pl.ds(start + part * count, count)]
        gone.append(pltpu.make_async_copy(out_ref.at[at], to, out_sems.at[part]))
        gone[-1].start()
    for copy in gone:
        copy.wait()


def finish_kernel(scale, mine_ref, other_ref, *out_refs):
    h = out_refs[0].shape[0]
    bit = lax.rem(lax.axis_index("row"), 2)
    for i, out_ref in enumerate(out_refs):
        at = pl.ds(i % 2 * h, h)
        mine = bit == i // 2
        out_ref[...] = jnp.where(mine, mine_ref[at, :], other_ref[at, :]) * scale


def channel_shards(sizes, pair, cotangent, *weights):
    rows, cols = sizes
    devices = rows * cols
    hidden, r, c = cotangent.shape
    dim = pair.shape[2]
    own = hidden // devices
    pieces = 2 if r % 2 == 0 else 1
    parts = 2 if r % 32 == 0 else 1
    weights = [w.T for w in weights]
    vmem = pl.BlockSpec(memory_space=pltpu.VMEM)
    hbm = pl.BlockSpec(memory_space=pltpu.HBM)
    exchange = functools.partial(
        lax.all_to_all, axis_name=("row", "col"), split_axis=0, concat_axis=0, tiled=True
    )
    stacked = pltpu.VMEM((4 * hidden, dim), BF16)
    lanes = min(c, 128)
    rows_scratch = pltpu.VMEM((c // lanes, (2 * hidden + 1) * (r // parts + 1), lanes), F32)
    columns = r * c
    n_i, n_k = rows * r, cols * c
    pair = pltpu.with_memory_space_constraint(pair, pltpu.HBM)

    def cost(flops, *arrays):
        moved = sum(a.size * a.dtype.itemsize for a in arrays)
        return pl.CostEstimate(flops=flops, bytes_accessed=moved, transcendentals=0)

    def memory(mib):
        return pltpu.CompilerParams(vmem_limit_bytes=mib * 2**20)

    normed_shape = jax.ShapeDtypeStruct((r, dim, c), BF16)
    sent, normed = pl.pallas_call(
        functools.partial(before_kernel, own),
        in_specs=[hbm] * 6,
        out_specs=[vmem, hbm],
        out_shape=[
            jax.ShapeDtypeStruct((devices, 3 * own, r, c), BF16),
            pltpu.HBM(normed_shape.shape, BF16),
        ],
        scratch_shapes=[
            stacked,
            *[rows_scratch] * parts,
            pltpu.VMEM(pair.shape, BF16),
            pltpu.VMEM(normed_shape.shape, BF16),
            pltpu.SemaphoreType.DMA((parts,)),
            pltpu.SemaphoreType.DMA((parts,)),
            pltpu.SemaphoreType.DMA((4,)),
            pltpu.SemaphoreType.DMA,
        ],
        compiler_params=memory(24),
        name="before",
    )(
        pair,
        pltpu.with_memory_space_constraint(cotangent.reshape(devices, own, r, c), pltpu.HBM),
        *(pltpu.with_memory_space_constraint(w, pltpu.HBM) for w in weights),
    )

    sent = pl.pallas_call(
        functools.partial(triangle_kernel, rows, cols),
        in_specs=[vmem],
        out_specs=vmem,
        out_shape=jax.ShapeDtypeStruct((devices, 2 * own, r, c), BF16),
        scratch_shapes=[pltpu.VMEM((own, n_i, n_k), BF16)] * 3,
        compiler_params=memory(32),
        name="triangle",
    )(exchange(sent))

    half_shape = jax.ShapeDtypeStruct((2 * hidden, dim), F32)
    grads, kept, given = pl.pallas_call(
        functools.partial(gates_kernel, own),
        in_specs=[hbm] + [vmem] * 5,
        out_specs=[vmem] * 3,
        out_shape=[jax.ShapeDtypeStruct((r, 4 * hidden, c), BF16), half_shape, half_shape],
        scratch_shapes=[
            stacked,
            pltpu.VMEM((4 * hidden, dim), F32),
            *[rows_scratch] * parts,
            pltpu.VMEM(normed_shape.shape, BF16),
            pltpu.SemaphoreType.DMA,
        ],
        compiler_params=memory(28),
        name="gates",
    )(pltpu.with_memory_space_constraint(normed, pltpu.HBM), exchange(sent), *weights)

    def input_piece(piece, pair_gradient):
        held = [] if pair_gradient is None else [pair_gradient]
        count = r // pieces
        return pl.pallas_call(
            functools.partial(input_kernel, piece * count),
            in_specs=[hbm] + [vmem] * 5 + [hbm] * len(held),
            out_specs=hbm,
            out_shape=jax.ShapeDtypeStruct(pair.shape, BF16),
            scratch_shapes=[
                pltpu.VMEM((dim, 4 * hidden), BF16),
                pltpu.VMEM((count, c, dim), BF16),
                pltpu.VMEM((count, c, dim), BF16),
                pltpu.SemaphoreType.DMA,
                pltpu.SemaphoreType.DMA((2 if count % 8 == 0 else 1,)),
            ],
            input_output_aliases={6: 0} if held else {},
            compiler_params=memory(16),
            cost_estimate=cost(8 * hidden * dim * columns // pieces, pair),
            name="input",
        )(pair, grads, *weights, *held)

    steps = [("row", rows, 1 << i) for i in range(1, rows.bit_length() - 1)][::-1]
    steps += [("col", cols, 1 << i) for i in range(cols.bit_length() - 1)]
    pieces = min(pieces, len(steps))
    neighbours = [(i, i ^ 1) for i in range(rows)]
    pair_gradient = None
    mine = kept + lax.ppermute(given, "row", neighbours)
    for n, (axis, size, step) in enumerate(steps):
        other = lax.ppermute(mine, axis, [(i, i ^ step) for i in range(size)])
        if n < pieces:
            pair_gradient = input_piece(n, pair_gradient)
            other, pair_gradient = lax.optimization_barrier((other, pair_gradient))
        mine = mine + other
    weight_grads = pl.pallas_call(
        functools.partial(finish_kernel, 1.0 / n_i),
        in_specs=[vmem, vmem],
        out_shape=[jax.ShapeDtypeStruct((hidden, dim), F32)] * 4,
        compiler_params=memory(8),
        name="finish",
    )(mine, lax.ppermute(mine, "row", neighbours))
    return (pair_gradient, *(g.T for g in weight_grads))


def solution(mesh):
    in_specs = (P("row", "col", None), P(None, "row", "col"), P(), P(), P(), P())
    out_specs = (P("row", "col", None), P(), P(), P(), P())
    sizes = (mesh.shape["row"], mesh.shape["col"])

    def shards(pair, cotangent, *weights):
        plain = all(size > 1 and size & (size - 1) == 0 for size in sizes)
        if plain and cotangent.shape[0] % (sizes[0] * sizes[1]) == 0:
            return channel_shards(sizes, pair, cotangent, *weights)
        return gathered_shards(pair, cotangent, *weights)

    return jax.shard_map(shards, mesh=mesh, in_specs=in_specs, out_specs=out_specs, check_vma=False)
```

```python
import functools

import jax
import jax.numpy as jnp
from jax import lax
from jax.experimental import pallas as pl
from jax.experimental.pallas import tpu as pltpu
from jax.sharding import PartitionSpec as P

BF16, F32 = jnp.bfloat16, jnp.float32


def gathered_shards(pair, cotangent, w_left, w_left_gate, w_right, w_right_gate):
    pair_f = pair.astype(jnp.float32)
    average = jnp.mean(pair_f, axis=-1, keepdims=True)
    centered_input = pair_f - average
    variance = jnp.mean(centered_input * centered_input, axis=-1, keepdims=True)
    inverse_scale = 1.0 / jnp.sqrt(variance + 1e-05)
    standardized_input = centered_input * inverse_scale
    normalized_input = standardized_input.astype(jnp.bfloat16)
    stacked = jnp.concatenate([w_left, w_left_gate, w_right, w_right_gate], axis=1)
    projected = jnp.einsum(
        "rcd,dh->hrc", normalized_input, stacked, preferred_element_type=jnp.float32
    )
    q_left, p_left, q_right, p_right = jnp.split(projected, 4, axis=0)
    s_left = jax.nn.sigmoid(p_left)
    s_right = jax.nn.sigmoid(p_right)
    left = (s_left * q_left).astype(jnp.bfloat16)
    right = (s_right * q_right).astype(jnp.bfloat16)
    g_chan, left_chan, right_chan = (
        lax.all_to_all(cotangent, "col", split_axis=0, concat_axis=2, tiled=True),
        lax.all_to_all(left, "col", split_axis=0, concat_axis=2, tiled=True),
        lax.all_to_all(right, "col", split_axis=0, concat_axis=2, tiled=True),
    )
    residues = g_chan.shape[2]
    g_columns = lax.all_to_all(g_chan, "row", split_axis=2, concat_axis=1, tiled=True)
    d_left = jnp.einsum(
        "hij,hjk->hik",
        g_chan,
        lax.all_gather(right_chan, "row", axis=1, tiled=True),
        preferred_element_type=jnp.float32,
    )
    d_right = jnp.einsum(
        "hij,hik->hjk",
        g_columns,
        lax.all_gather(left_chan, "row", axis=1, tiled=True),
        preferred_element_type=jnp.float32,
    )
    d_left_tile, d_right_tile = (
        lax.all_to_all(d_left.astype(jnp.bfloat16), "col", split_axis=2, concat_axis=0, tiled=True),
        lax.all_to_all(
            d_right.astype(jnp.bfloat16), "col", split_axis=2, concat_axis=0, tiled=True
        ),
    )
    grad_l = d_left_tile.astype(jnp.float32)
    grad_r = d_right_tile.astype(jnp.float32)
    e_left = grad_l * s_left
    f_left = grad_l * q_left * s_left * (1.0 - s_left)
    e_right = grad_r * s_right
    f_right = grad_r * q_right * s_right * (1.0 - s_right)
    grads = jnp.concatenate([e_left, f_left, e_right, f_right], axis=0).astype(jnp.bfloat16)
    local_weights = jnp.einsum(
        "rcd,hrc->dh", normalized_input, grads, preferred_element_type=jnp.float32
    )
    total_weights = lax.psum(local_weights, ("row", "col")) / residues
    normalized_gradient = jnp.einsum(
        "hrc,dh->rcd", grads, stacked, preferred_element_type=jnp.float32
    )
    gradient_mean = jnp.mean(normalized_gradient, axis=-1, keepdims=True)
    gradient_input_mean = jnp.mean(normalized_gradient * standardized_input, axis=-1, keepdims=True)
    pair_gradient = (
        (normalized_gradient - gradient_mean - standardized_input * gradient_input_mean)
        * inverse_scale
    ).astype(jnp.bfloat16)
    pieces_w = jnp.split(total_weights, 4, axis=1)
    return (pair_gradient, pieces_w[0], pieces_w[1], pieces_w[2], pieces_w[3])


NT = (((1,), (1,)), ((), ()))
TN = (((0,), (0,)), ((), ()))
NN = (((1,), (0,)), ((), ()))


def dot(a, b, dims=NN):
    return lax.dot_general(a, b, dims, preferred_element_type=F32)


def stack_weights(w_refs, w_ref):
    h = w_refs[0].shape[0]
    for i, ref in enumerate(w_refs):
        w_ref[pl.ds(i * h, h), :] = ref[...]


def layer_norm(x):
    x = x.astype(F32).T
    centered = x - jnp.mean(x, axis=0, keepdims=True)
    variance = jnp.mean(centered * centered, axis=0, keepdims=True)
    inverse_scale = lax.rsqrt(variance + 1e-05)
    return centered * inverse_scale, inverse_scale


def project(w_ref, normed):
    projected = dot(w_ref[...], normed)
    h = projected.shape[0] // 4
    q_left, p_left, q_right, p_right = (projected[i * h : (i + 1) * h] for i in range(4))
    return q_left, jax.nn.sigmoid(p_left), q_right, jax.nn.sigmoid(p_right)


def put_lanes(ref, at, value):
    lanes = ref.shape[2]
    for i in range(ref.shape[0]):
        ref[i, at, :] = value[:, i * lanes : (i + 1) * lanes]


def get_lanes(ref, at):
    return jnp.concatenate([ref[i, at, :] for i in range(ref.shape[0])], axis=1)


def before_kernel(own, pair_hbm, cot_hbm, wl, wlg, wr, wrg, out_ref, normed_hbm, *scratch):
    w_ref, *rows_refs, pair_ref, normed_ref, in_sems, out_sems, w_sems, cot_sem = scratch
    h = wl.shape[0]
    rows = pair_ref.shape[0]
    parts = in_sems.shape[0]
    count = rows // parts
    pitch = count + 1

    def come(part):
        at = pl.ds(part * count, count)
        return pltpu.make_async_copy(pair_hbm.at[at], pair_ref.at[at], in_sems.at[part])

    def leave(part):
        at = pl.ds(part * count, count)
        return pltpu.make_async_copy(normed_ref.at[at], normed_hbm.at[at], out_sems.at[part])

    def weight(i, w):
        return pltpu.make_async_copy(w, w_ref.at[pl.ds(i * h, h)], w_sems.at[i])

    for i, w in enumerate((wl, wlg, wr, wrg)):
        weight(i, w).start()
    for part in range(parts):
        come(part).start()
    cot = pltpu.make_async_copy(cot_hbm, out_ref.at[:, pl.ds(0, own)], cot_sem)
    cot.start()
    for i, w in enumerate((wl, wlg, wr, wrg)):
        weight(i, w).wait()

    def one_row(part, i):
        r = part * count + i
        normed = layer_norm(pair_ref[r])[0].astype(BF16)
        normed_ref[r] = normed
        q_left, s_left, q_right, s_right = project(w_ref, normed)
        put_lanes(rows_refs[part], pl.ds(i, h, stride=pitch), s_left * q_left)
        put_lanes(rows_refs[part], pl.ds(i + h * pitch, h, stride=pitch), s_right * q_right)

    def some_channels(part, i):
        for channel in range(i * h // count, (i + 1) * h // count):
            for side in range(2):
                at = pl.ds((side * h + channel) * pitch, count)
                line = get_lanes(rows_refs[part], at).astype(BF16)
                slot = (1 + side) * own + channel % own
                out_ref[channel // own, slot, pl.ds(part * count, count), :] = line

    for part in range(parts + 1):
        if part < parts:
            come(part).wait()
        for i in range(count):
            if part < parts:
                one_row(part, i)
            if part > 0:
                some_channels(part - 1, i)
        if part < parts:
            leave(part).start()
    for part in range(parts):
        leave(part).wait()
    cot.wait()


def triangle_kernel(rows, cols, in_ref, out_ref, g_ref, l_ref, r_ref):
    r, c = in_ref.shape[2:]
    own = g_ref.shape[0]
    for n in range(own):
        for i, ref in enumerate((g_ref, l_ref, r_ref)):
            for a in range(rows):
                for b in range(cols):
                    block = in_ref[a * cols + b, i * own + n]
                    ref[n, pl.ds(a * r, r), pl.ds(b * c, c)] = block
        for i, (dims, ref) in enumerate(((NN, r_ref), (TN, l_ref))):
            d = dot(g_ref[n], ref[n], dims).astype(BF16)
            for a in range(rows):
                for b in range(cols):
                    block = d[a * r : (a + 1) * r, b * c : (b + 1) * c]
                    out_ref[a * cols + b, n * 2 + i] = block


def gates_kernel(own, normed_hbm, d_ref, wl, wlg, wr, wrg, grads_ref, kept_ref, sent_ref, *scratch):
    w_ref, sums_ref, *rows_refs, normed_ref, sem = scratch
    copy = pltpu.make_async_copy(normed_hbm, normed_ref, sem)
    copy.start()
    h = wl.shape[0]
    rows = grads_ref.shape[0]
    parts = len(rows_refs)
    count = rows // parts
    pitch = count + 1
    stack_weights((wl, wlg, wr, wrg), w_ref)

    def some_channels(part, i):
        for channel in range(i * h // count, (i + 1) * h // count):
            to, slot = channel // own, (channel % own) * 2
            for side in range(2):
                line = d_ref[to, slot + side, pl.ds(part * count, count), :].astype(F32)
                put_lanes(rows_refs[part], pl.ds((side * h + channel) * pitch, count), line)

    def one_row(part, i):
        normed = normed_ref[part * count + i]
        q_left, s_left, q_right, s_right = project(w_ref, normed)
        e_left = get_lanes(rows_refs[part], pl.ds(i, h, stride=pitch)) * s_left
        e_right = get_lanes(rows_refs[part], pl.ds(i + h * pitch, h, stride=pitch)) * s_right
        f_left = e_left * q_left * (1.0 - s_left)
        f_right = e_right * q_right * (1.0 - s_right)
        grads = jnp.concatenate([e_left, f_left, e_right, f_right], axis=0).astype(BF16)
        grads_ref[part * count + i] = grads
        return grads, normed

    together = 8 if count % 8 == 0 else count
    sums_ref[...] = jnp.zeros_like(sums_ref)
    for part in range(parts + 1):
        if part == 1:
            copy.wait()
        done = []
        for i in range(count):
            if part > 0:
                done.append(one_row(part - 1, i))
            if part < parts:
                some_channels(part, i)
            if len(done) == together:
                all_grads, all_normed = (jnp.concatenate(x, axis=1) for x in zip(*done))
                sums_ref[...] += dot(all_grads, all_normed, NT)
                done = []
    bit = lax.rem(lax.axis_index("row"), 2)
    kept_ref[...] = sums_ref[pl.ds(pl.multiple_of(bit * 2 * h, 2 * h), 2 * h), :]
    sent_ref[...] = sums_ref[pl.ds(pl.multiple_of((1 - bit) * 2 * h, 2 * h), 2 * h), :]


def input_kernel(start, pair_hbm, grads_ref, wl, wlg, wr, wrg, *refs):
    out_hbm, back_ref, pair_ref, out_ref, in_sem, out_sems = refs[-6:]
    rows = pair_ref.shape[0]
    come = pltpu.make_async_copy(pair_hbm.at[pl.ds(start, rows)], pair_ref, in_sem)
    come.start()
    h = wl.shape[0]
    for i, ref in enumerate((wl, wlg, wr, wrg)):
        back_ref[:, pl.ds(i * h, h)] = ref[...].T
    come.wait()

    def one_row(r, carry):
        standardized, inverse_scale = layer_norm(pair_ref[r])
        d_normed = dot(back_ref[...], grads_ref[start + r])
        mean = jnp.mean(d_normed, axis=0, keepdims=True)
        input_mean = jnp.mean(d_normed * standardized, axis=0, keepdims=True)
        moved = (d_normed - mean - standardized * input_mean) * inverse_scale
        out_ref[r] = moved.astype(BF16).T
        return carry

    parts = out_sems.shape[0]
    count = rows // parts
    gone = []
    for part in range(parts):
        lax.fori_loop(part * count, (part + 1) * count, one_row, 0, unroll=8)
        at = pl.ds(part * count, count)
        to = out_hbm.at[pl.ds(start + part * count, count)]
        gone.append(pltpu.make_async_copy(out_ref.at[at], to, out_sems.at[part]))
        gone[-1].start()
    for copy in gone:
        copy.wait()


def finish_kernel(scale, mine_ref, other_ref, *out_refs):
    h = out_refs[0].shape[0]
    bit = lax.rem(lax.axis_index("row"), 2)
    for i, out_ref in enumerate(out_refs):
        at = pl.ds(i % 2 * h, h)
        mine = bit == i // 2
        out_ref[...] = jnp.where(mine, mine_ref[at, :], other_ref[at, :]) * scale


def channel_shards(sizes, pair, cotangent, *weights):
    rows, cols = sizes
    devices = rows * cols
    hidden, r, c = cotangent.shape
    dim = pair.shape[2]
    own = hidden // devices
    pieces = 2 if r % 2 == 0 else 1
    parts = 2 if r % 32 == 0 else 1
    weights = [w.T for w in weights]
    vmem = pl.BlockSpec(memory_space=pltpu.VMEM)
    hbm = pl.BlockSpec(memory_space=pltpu.HBM)
    exchange = functools.partial(
        lax.all_to_all, axis_name=("row", "col"), split_axis=0, concat_axis=0, tiled=True
    )
    stacked = pltpu.VMEM((4 * hidden, dim), BF16)
    lanes = min(c, 128)
    rows_scratch = pltpu.VMEM((c // lanes, (2 * hidden + 1) * (r // parts + 1), lanes), F32)
    columns = r * c
    n_i, n_k = rows * r, cols * c
    pair = pltpu.with_memory_space_constraint(pair, pltpu.HBM)

    def cost(flops, *arrays):
        moved = sum(a.size * a.dtype.itemsize for a in arrays)
        return pl.CostEstimate(flops=flops, bytes_accessed=moved, transcendentals=0)

    def memory(mib):
        return pltpu.CompilerParams(vmem_limit_bytes=mib * 2**20)

    normed_shape = jax.ShapeDtypeStruct((r, dim, c), BF16)
    sent, normed = pl.pallas_call(
        functools.partial(before_kernel, own),
        in_specs=[hbm] * 6,
        out_specs=[vmem, hbm],
        out_shape=[
            jax.ShapeDtypeStruct((devices, 3 * own, r, c), BF16),
            pltpu.HBM(normed_shape.shape, BF16),
        ],
        scratch_shapes=[
            stacked,
            *[rows_scratch] * parts,
            pltpu.VMEM(pair.shape, BF16),
            pltpu.VMEM(normed_shape.shape, BF16),
            pltpu.SemaphoreType.DMA((parts,)),
            pltpu.SemaphoreType.DMA((parts,)),
            pltpu.SemaphoreType.DMA((4,)),
            pltpu.SemaphoreType.DMA,
        ],
        compiler_params=memory(24),
        name="before",
    )(
        pair,
        pltpu.with_memory_space_constraint(cotangent.reshape(devices, own, r, c), pltpu.HBM),
        *(pltpu.with_memory_space_constraint(w, pltpu.HBM) for w in weights),
    )

    sent = pl.pallas_call(
        functools.partial(triangle_kernel, rows, cols),
        in_specs=[vmem],
        out_specs=vmem,
        out_shape=jax.ShapeDtypeStruct((devices, 2 * own, r, c), BF16),
        scratch_shapes=[pltpu.VMEM((own, n_i, n_k), BF16)] * 3,
        compiler_params=memory(32),
        name="triangle",
    )(exchange(sent))

    half_shape = jax.ShapeDtypeStruct((2 * hidden, dim), F32)
    grads, kept, given = pl.pallas_call(
        functools.partial(gates_kernel, own),
        in_specs=[hbm] + [vmem] * 5,
        out_specs=[vmem] * 3,
        out_shape=[jax.ShapeDtypeStruct((r, 4 * hidden, c), BF16), half_shape, half_shape],
        scratch_shapes=[
            stacked,
            pltpu.VMEM((4 * hidden, dim), F32),
            *[rows_scratch] * parts,
            pltpu.VMEM(normed_shape.shape, BF16),
            pltpu.SemaphoreType.DMA,
        ],
        compiler_params=memory(28),
        name="gates",
    )(pltpu.with_memory_space_constraint(normed, pltpu.HBM), exchange(sent), *weights)

    def input_piece(piece, pair_gradient):
        held = [] if pair_gradient is None else [pair_gradient]
        count = r // pieces
        return pl.pallas_call(
            functools.partial(input_kernel, piece * count),
            in_specs=[hbm] + [vmem] * 5 + [hbm] * len(held),
            out_specs=hbm,
            out_shape=jax.ShapeDtypeStruct(pair.shape, BF16),
            scratch_shapes=[
                pltpu.VMEM((dim, 4 * hidden), BF16),
                pltpu.VMEM((count, c, dim), BF16),
                pltpu.VMEM((count, c, dim), BF16),
                pltpu.SemaphoreType.DMA,
                pltpu.SemaphoreType.DMA((2 if count % 8 == 0 else 1,)),
            ],
            input_output_aliases={6: 0} if held else {},
            compiler_params=memory(16),
            cost_estimate=cost(8 * hidden * dim * columns // pieces, pair),
            name="input",
        )(pair, grads, *weights, *held)

    steps = [("row", rows, 1 << i) for i in range(1, rows.bit_length() - 1)][::-1]
    steps += [("col", cols, 1 << i) for i in range(cols.bit_length() - 1)]
    pieces = min(pieces, len(steps))
    neighbours = [(i, i ^ 1) for i in range(rows)]
    pair_gradient = None
    mine = kept + lax.ppermute(given, "row", neighbours)
    for n, (axis, size, step) in enumerate(steps):
        other = lax.ppermute(mine, axis, [(i, i ^ step) for i in range(size)])
        if n < pieces:
            pair_gradient = input_piece(n, pair_gradient)
            other, pair_gradient = lax.optimization_barrier((other, pair_gradient))
        mine = mine + other
    weight_grads = pl.pallas_call(
        functools.partial(finish_kernel, 1.0 / n_i),
        in_specs=[vmem, vmem],
        out_shape=[jax.ShapeDtypeStruct((hidden, dim), F32)] * 4,
        compiler_params=memory(8),
        name="finish",
    )(mine, lax.ppermute(mine, "row", neighbours))
    return (pair_gradient, *(g.T for g in weight_grads))


def solution(mesh):
    in_specs = (P("row", "col", None), P(None, "row", "col"), P(), P(), P(), P())
    out_specs = (P("row", "col", None), P(), P(), P(), P())
    sizes = (mesh.shape["row"], mesh.shape["col"])

    def shards(pair, cotangent, *weights):
        plain = all(size > 1 and size & (size - 1) == 0 for size in sizes)
        if plain and cotangent.shape[0] % (sizes[0] * sizes[1]) == 0:
            return channel_shards(sizes, pair, cotangent, *weights)
        return gathered_shards(pair, cotangent, *weights)

    return jax.shard_map(shards, mesh=mesh, in_specs=in_specs, out_specs=out_specs, check_vma=False)
```

```python
import functools

import jax
import jax.numpy as jnp
from jax import lax
from jax.experimental import pallas as pl
from jax.experimental.pallas import tpu as pltpu
from jax.sharding import PartitionSpec as P

BF16, F32 = jnp.bfloat16, jnp.float32


def gathered_shards(pair, cotangent, w_left, w_left_gate, w_right, w_right_gate):
    pair_f = pair.astype(jnp.float32)
    average = jnp.mean(pair_f, axis=-1, keepdims=True)
    centered_input = pair_f - average
    variance = jnp.mean(centered_input * centered_input, axis=-1, keepdims=True)
    inverse_scale = 1.0 / jnp.sqrt(variance + 1e-05)
    standardized_input = centered_input * inverse_scale
    normalized_input = standardized_input.astype(jnp.bfloat16)
    stacked = jnp.concatenate([w_left, w_left_gate, w_right, w_right_gate], axis=1)
    projected = jnp.einsum(
        "rcd,dh->hrc", normalized_input, stacked, preferred_element_type=jnp.float32
    )
    q_left, p_left, q_right, p_right = jnp.split(projected, 4, axis=0)
    s_left = jax.nn.sigmoid(p_left)
    s_right = jax.nn.sigmoid(p_right)
    left = (s_left * q_left).astype(jnp.bfloat16)
    right = (s_right * q_right).astype(jnp.bfloat16)
    g_chan, left_chan, right_chan = (
        lax.all_to_all(cotangent, "col", split_axis=0, concat_axis=2, tiled=True),
        lax.all_to_all(left, "col", split_axis=0, concat_axis=2, tiled=True),
        lax.all_to_all(right, "col", split_axis=0, concat_axis=2, tiled=True),
    )
    residues = g_chan.shape[2]
    g_columns = lax.all_to_all(g_chan, "row", split_axis=2, concat_axis=1, tiled=True)
    d_left = jnp.einsum(
        "hij,hjk->hik",
        g_chan,
        lax.all_gather(right_chan, "row", axis=1, tiled=True),
        preferred_element_type=jnp.float32,
    )
    d_right = jnp.einsum(
        "hij,hik->hjk",
        g_columns,
        lax.all_gather(left_chan, "row", axis=1, tiled=True),
        preferred_element_type=jnp.float32,
    )
    d_left_tile, d_right_tile = (
        lax.all_to_all(d_left.astype(jnp.bfloat16), "col", split_axis=2, concat_axis=0, tiled=True),
        lax.all_to_all(
            d_right.astype(jnp.bfloat16), "col", split_axis=2, concat_axis=0, tiled=True
        ),
    )
    grad_l = d_left_tile.astype(jnp.float32)
    grad_r = d_right_tile.astype(jnp.float32)
    e_left = grad_l * s_left
    f_left = grad_l * q_left * s_left * (1.0 - s_left)
    e_right = grad_r * s_right
    f_right = grad_r * q_right * s_right * (1.0 - s_right)
    grads = jnp.concatenate([e_left, f_left, e_right, f_right], axis=0).astype(jnp.bfloat16)
    local_weights = jnp.einsum(
        "rcd,hrc->dh", normalized_input, grads, preferred_element_type=jnp.float32
    )
    total_weights = lax.psum(local_weights, ("row", "col")) / residues
    normalized_gradient = jnp.einsum(
        "hrc,dh->rcd", grads, stacked, preferred_element_type=jnp.float32
    )
    gradient_mean = jnp.mean(normalized_gradient, axis=-1, keepdims=True)
    gradient_input_mean = jnp.mean(normalized_gradient * standardized_input, axis=-1, keepdims=True)
    pair_gradient = (
        (normalized_gradient - gradient_mean - standardized_input * gradient_input_mean)
        * inverse_scale
    ).astype(jnp.bfloat16)
    pieces_w = jnp.split(total_weights, 4, axis=1)
    return (pair_gradient, pieces_w[0], pieces_w[1], pieces_w[2], pieces_w[3])


NT = (((1,), (1,)), ((), ()))
TN = (((0,), (0,)), ((), ()))
NN = (((1,), (0,)), ((), ()))


def dot(a, b, dims=NN):
    return lax.dot_general(a, b, dims, preferred_element_type=F32)


def stack_weights(w_refs, w_ref):
    h = w_refs[0].shape[0]
    for i, ref in enumerate(w_refs):
        w_ref[pl.ds(i * h, h), :] = ref[...]


def layer_norm(x):
    x = x.T.astype(F32)
    centered = x - jnp.mean(x, axis=0, keepdims=True)
    variance = jnp.mean(centered * centered, axis=0, keepdims=True)
    inverse_scale = lax.rsqrt(variance + 1e-05)
    return centered * inverse_scale, inverse_scale


def sigmoid(p):
    y = 1.0 + jnp.exp(-p)
    r = pl.reciprocal(y, approx=True)
    return r * (2.0 - y * r)


def project(w_ref, normed):
    projected = dot(w_ref[...], normed)
    h = projected.shape[0] // 4
    q_left, p_left, q_right, p_right = (projected[i * h : (i + 1) * h] for i in range(4))
    return q_left, sigmoid(p_left), q_right, sigmoid(p_right)


def put_lanes(ref, at, value):
    lanes = ref.shape[2]
    for i in range(ref.shape[0]):
        ref[i, at, :] = value[:, i * lanes : (i + 1) * lanes]


def get_lanes(ref, at):
    return jnp.concatenate([ref[i, at, :] for i in range(ref.shape[0])], axis=1)


def before_kernel(own, pair_hbm, cot_hbm, wl, wlg, wr, wrg, out_ref, normed_hbm, *scratch):
    w_ref, *rows_refs, pair_ref, normed_ref, in_sems, out_sems, w_sems, cot_sem = scratch
    h = wl.shape[0]
    rows = pair_ref.shape[0]
    parts = in_sems.shape[0]
    count = rows // parts
    pitch = count + 1

    def come(part):
        at = pl.ds(part * count, count)
        return pltpu.make_async_copy(pair_hbm.at[at], pair_ref.at[at], in_sems.at[part])

    def leave(part):
        at = pl.ds(part * count, count)
        return pltpu.make_async_copy(normed_ref.at[at], normed_hbm.at[at], out_sems.at[part])

    def weight(i, w):
        return pltpu.make_async_copy(w, w_ref.at[pl.ds(i * h, h)], w_sems.at[i])

    for i, w in enumerate((wl, wlg, wr, wrg)):
        weight(i, w).start()
    for part in range(parts):
        come(part).start()
    cot = pltpu.make_async_copy(cot_hbm, out_ref.at[:, pl.ds(0, own)], cot_sem)
    cot.start()
    for i, w in enumerate((wl, wlg, wr, wrg)):
        weight(i, w).wait()

    def one_row(part, i):
        r = part * count + i
        normed = layer_norm(pair_ref[r])[0].astype(BF16)
        normed_ref[r] = normed
        q_left, s_left, q_right, s_right = project(w_ref, normed)
        put_lanes(rows_refs[part], pl.ds(i, h, stride=pitch), s_left * q_left)
        put_lanes(rows_refs[part], pl.ds(i + h * pitch, h, stride=pitch), s_right * q_right)

    def some_channels(part, i):
        for channel in range(i * h // count, (i + 1) * h // count):
            for side in range(2):
                at = pl.ds((side * h + channel) * pitch, count)
                line = get_lanes(rows_refs[part], at).astype(BF16)
                slot = (1 + side) * own + channel % own
                out_ref[channel // own, slot, pl.ds(part * count, count), :] = line

    for part in range(parts + 1):
        if part < parts:
            come(part).wait()
        for i in range(count):
            if part < parts:
                one_row(part, i)
            if part > 0:
                some_channels(part - 1, i)
        if part < parts:
            leave(part).start()
    for part in range(parts):
        leave(part).wait()
    cot.wait()


def triangle_kernel(rows, cols, in_ref, out_ref, g_ref, l_ref, r_ref):
    r, c = in_ref.shape[2:]
    own = g_ref.shape[0]
    for n in range(own):
        for i, ref in enumerate((g_ref, l_ref, r_ref)):
            for a in range(rows):
                for b in range(cols):
                    block = in_ref[a * cols + b, i * own + n]
                    ref[n, pl.ds(a * r, r), pl.ds(b * c, c)] = block
        for i, (dims, ref) in enumerate(((NN, r_ref), (TN, l_ref))):
            d = dot(g_ref[n], ref[n], dims).astype(BF16)
            for a in range(rows):
                for b in range(cols):
                    block = d[a * r : (a + 1) * r, b * c : (b + 1) * c]
                    out_ref[a * cols + b, n * 2 + i] = block


def gates_kernel(own, normed_hbm, d_ref, wl, wlg, wr, wrg, grads_ref, kept_ref, sent_ref, *scratch):
    w_ref, sums_ref, *rows_refs, normed_ref, sem = scratch
    copy = pltpu.make_async_copy(normed_hbm, normed_ref, sem)
    copy.start()
    h = wl.shape[0]
    rows = grads_ref.shape[0]
    parts = len(rows_refs)
    count = rows // parts
    pitch = count + 1
    stack_weights((wl, wlg, wr, wrg), w_ref)

    def some_channels(part, i):
        for channel in range(i * h // count, (i + 1) * h // count):
            to, slot = channel // own, (channel % own) * 2
            for side in range(2):
                line = d_ref[to, slot + side, pl.ds(part * count, count), :].astype(F32)
                put_lanes(rows_refs[part], pl.ds((side * h + channel) * pitch, count), line)

    def one_row(part, i):
        normed = normed_ref[part * count + i]
        q_left, s_left, q_right, s_right = project(w_ref, normed)
        e_left = get_lanes(rows_refs[part], pl.ds(i, h, stride=pitch)) * s_left
        e_right = get_lanes(rows_refs[part], pl.ds(i + h * pitch, h, stride=pitch)) * s_right
        f_left = e_left * q_left * (1.0 - s_left)
        f_right = e_right * q_right * (1.0 - s_right)
        grads = jnp.concatenate([e_left, f_left, e_right, f_right], axis=0).astype(BF16)
        grads_ref[part * count + i] = grads
        return grads, normed

    together = 8 if count % 8 == 0 else count
    sums_ref[...] = jnp.zeros_like(sums_ref)
    for part in range(parts + 1):
        if part == 1:
            copy.wait()
        done = []
        for i in range(count):
            if part > 0:
                done.append(one_row(part - 1, i))
            if part < parts:
                some_channels(part, i)
            if len(done) == together:
                all_grads, all_normed = (jnp.concatenate(x, axis=1) for x in zip(*done))
                sums_ref[...] += dot(all_grads, all_normed, NT)
                done = []
    bit = lax.rem(lax.axis_index("row"), 2)
    kept_ref[...] = sums_ref[pl.ds(pl.multiple_of(bit * 2 * h, 2 * h), 2 * h), :]
    sent_ref[...] = sums_ref[pl.ds(pl.multiple_of((1 - bit) * 2 * h, 2 * h), 2 * h), :]


def input_kernel(start, pair_hbm, grads_ref, wl, wlg, wr, wrg, *refs):
    out_hbm, back_ref, pair_ref, out_ref, in_sem, out_sems = refs[-6:]
    rows = pair_ref.shape[0]
    come = pltpu.make_async_copy(pair_hbm.at[pl.ds(start, rows)], pair_ref, in_sem)
    come.start()
    h = wl.shape[0]
    for i, ref in enumerate((wl, wlg, wr, wrg)):
        back_ref[:, pl.ds(i * h, h)] = ref[...].T
    come.wait()

    def one_row(r, carry):
        standardized, inverse_scale = layer_norm(pair_ref[r])
        d_normed = dot(back_ref[...], grads_ref[start + r])
        mean = jnp.mean(d_normed, axis=0, keepdims=True)
        input_mean = jnp.mean(d_normed * standardized, axis=0, keepdims=True)
        moved = (d_normed - mean - standardized * input_mean) * inverse_scale
        out_ref[r] = moved.astype(BF16).T
        return carry

    parts = out_sems.shape[0]
    count = rows // parts
    gone = []
    for part in range(parts):
        lax.fori_loop(part * count, (part + 1) * count, one_row, 0, unroll=8)
        at = pl.ds(part * count, count)
        to = out_hbm.at[pl.ds(start + part * count, count)]
        gone.append(pltpu.make_async_copy(out_ref.at[at], to, out_sems.at[part]))
        gone[-1].start()
    for copy in gone:
        copy.wait()


def finish_kernel(scale, mine_ref, other_ref, *out_refs):
    h = out_refs[0].shape[0]
    bit = lax.rem(lax.axis_index("row"), 2)
    for i, out_ref in enumerate(out_refs):
        at = pl.ds(i % 2 * h, h)
        mine = bit == i // 2
        out_ref[...] = jnp.where(mine, mine_ref[at, :], other_ref[at, :]) * scale


def channel_shards(sizes, pair, cotangent, *weights):
    rows, cols = sizes
    devices = rows * cols
    hidden, r, c = cotangent.shape
    dim = pair.shape[2]
    own = hidden // devices
    pieces = 2 if r % 2 == 0 else 1
    parts = 2 if r % 32 == 0 else 1
    weights = [w.T for w in weights]
    vmem = pl.BlockSpec(memory_space=pltpu.VMEM)
    hbm = pl.BlockSpec(memory_space=pltpu.HBM)
    exchange = functools.partial(
        lax.all_to_all, axis_name=("row", "col"), split_axis=0, concat_axis=0, tiled=True
    )
    stacked = pltpu.VMEM((4 * hidden, dim), BF16)
    lanes = min(c, 128)
    rows_scratch = pltpu.VMEM((c // lanes, (2 * hidden + 1) * (r // parts + 1), lanes), F32)
    columns = r * c
    n_i, n_k = rows * r, cols * c
    pair = pltpu.with_memory_space_constraint(pair, pltpu.HBM)

    def cost(flops, *arrays):
        moved = sum(a.size * a.dtype.itemsize for a in arrays)
        return pl.CostEstimate(flops=flops, bytes_accessed=moved, transcendentals=0)

    def memory(mib):
        return pltpu.CompilerParams(vmem_limit_bytes=mib * 2**20)

    normed_shape = jax.ShapeDtypeStruct((r, dim, c), BF16)
    sent, normed = pl.pallas_call(
        functools.partial(before_kernel, own),
        in_specs=[hbm] * 6,
        out_specs=[vmem, hbm],
        out_shape=[
            jax.ShapeDtypeStruct((devices, 3 * own, r, c), BF16),
            pltpu.HBM(normed_shape.shape, BF16),
        ],
        scratch_shapes=[
            stacked,
            *[rows_scratch] * parts,
            pltpu.VMEM(pair.shape, BF16),
            pltpu.VMEM(normed_shape.shape, BF16),
            pltpu.SemaphoreType.DMA((parts,)),
            pltpu.SemaphoreType.DMA((parts,)),
            pltpu.SemaphoreType.DMA((4,)),
            pltpu.SemaphoreType.DMA,
        ],
        compiler_params=memory(24),
        name="before",
    )(
        pair,
        pltpu.with_memory_space_constraint(cotangent.reshape(devices, own, r, c), pltpu.HBM),
        *(pltpu.with_memory_space_constraint(w, pltpu.HBM) for w in weights),
    )

    sent = pl.pallas_call(
        functools.partial(triangle_kernel, rows, cols),
        in_specs=[vmem],
        out_specs=vmem,
        out_shape=jax.ShapeDtypeStruct((devices, 2 * own, r, c), BF16),
        scratch_shapes=[pltpu.VMEM((own, n_i, n_k), BF16)] * 3,
        compiler_params=memory(32),
        name="triangle",
    )(exchange(sent))

    half_shape = jax.ShapeDtypeStruct((2 * hidden, dim), F32)
    grads, kept, given = pl.pallas_call(
        functools.partial(gates_kernel, own),
        in_specs=[hbm] + [vmem] * 5,
        out_specs=[vmem] * 3,
        out_shape=[jax.ShapeDtypeStruct((r, 4 * hidden, c), BF16), half_shape, half_shape],
        scratch_shapes=[
            stacked,
            pltpu.VMEM((4 * hidden, dim), F32),
            *[rows_scratch] * parts,
            pltpu.VMEM(normed_shape.shape, BF16),
            pltpu.SemaphoreType.DMA,
        ],
        compiler_params=memory(28),
        name="gates",
    )(pltpu.with_memory_space_constraint(normed, pltpu.HBM), exchange(sent), *weights)

    def input_piece(piece, pair_gradient):
        held = [] if pair_gradient is None else [pair_gradient]
        count = r // pieces
        return pl.pallas_call(
            functools.partial(input_kernel, piece * count),
            in_specs=[hbm] + [vmem] * 5 + [hbm] * len(held),
            out_specs=hbm,
            out_shape=jax.ShapeDtypeStruct(pair.shape, BF16),
            scratch_shapes=[
                pltpu.VMEM((dim, 4 * hidden), BF16),
                pltpu.VMEM((count, c, dim), BF16),
                pltpu.VMEM((count, c, dim), BF16),
                pltpu.SemaphoreType.DMA,
                pltpu.SemaphoreType.DMA((2 if count % 8 == 0 else 1,)),
            ],
            input_output_aliases={6: 0} if held else {},
            compiler_params=memory(16),
            cost_estimate=cost(8 * hidden * dim * columns // pieces, pair),
            name="input",
        )(pair, grads, *weights, *held)

    steps = [("row", rows, 1 << i) for i in range(1, rows.bit_length() - 1)][::-1]
    steps += [("col", cols, 1 << i) for i in range(cols.bit_length() - 1)]
    pieces = min(pieces, len(steps))
    neighbours = [(i, i ^ 1) for i in range(rows)]
    pair_gradient = None
    mine = kept + lax.ppermute(given, "row", neighbours)
    for n, (axis, size, step) in enumerate(steps):
        other = lax.ppermute(mine, axis, [(i, i ^ step) for i in range(size)])
        if n < pieces:
            pair_gradient = input_piece(n, pair_gradient)
            other, pair_gradient = lax.optimization_barrier((other, pair_gradient))
        mine = mine + other
    weight_grads = pl.pallas_call(
        functools.partial(finish_kernel, 1.0 / n_i),
        in_specs=[vmem, vmem],
        out_shape=[jax.ShapeDtypeStruct((hidden, dim), F32)] * 4,
        compiler_params=memory(8),
        name="finish",
    )(mine, lax.ppermute(mine, "row", neighbours))
    return (pair_gradient, *(g.T for g in weight_grads))


def solution(mesh):
    in_specs = (P("row", "col", None), P(None, "row", "col"), P(), P(), P(), P())
    out_specs = (P("row", "col", None), P(), P(), P(), P())
    sizes = (mesh.shape["row"], mesh.shape["col"])

    def shards(pair, cotangent, *weights):
        plain = all(size > 1 and size & (size - 1) == 0 for size in sizes)
        if plain and cotangent.shape[0] % (sizes[0] * sizes[1]) == 0:
            return channel_shards(sizes, pair, cotangent, *weights)
        return gathered_shards(pair, cotangent, *weights)

    return jax.shard_map(shards, mesh=mesh, in_specs=in_specs, out_specs=out_specs, check_vma=False)
```

```python
import functools

import jax
import jax.numpy as jnp
from jax import lax
from jax.experimental import pallas as pl
from jax.experimental.pallas import tpu as pltpu
from jax.sharding import PartitionSpec as P

BF16, F32 = jnp.bfloat16, jnp.float32


def gathered_shards(pair, cotangent, w_left, w_left_gate, w_right, w_right_gate):
    pair_f = pair.astype(jnp.float32)
    average = jnp.mean(pair_f, axis=-1, keepdims=True)
    centered_input = pair_f - average
    variance = jnp.mean(centered_input * centered_input, axis=-1, keepdims=True)
    inverse_scale = 1.0 / jnp.sqrt(variance + 1e-05)
    standardized_input = centered_input * inverse_scale
    normalized_input = standardized_input.astype(jnp.bfloat16)
    stacked = jnp.concatenate([w_left, w_left_gate, w_right, w_right_gate], axis=1)
    projected = jnp.einsum(
        "rcd,dh->hrc", normalized_input, stacked, preferred_element_type=jnp.float32
    )
    q_left, p_left, q_right, p_right = jnp.split(projected, 4, axis=0)
    s_left = jax.nn.sigmoid(p_left)
    s_right = jax.nn.sigmoid(p_right)
    left = (s_left * q_left).astype(jnp.bfloat16)
    right = (s_right * q_right).astype(jnp.bfloat16)
    g_chan, left_chan, right_chan = (
        lax.all_to_all(cotangent, "col", split_axis=0, concat_axis=2, tiled=True),
        lax.all_to_all(left, "col", split_axis=0, concat_axis=2, tiled=True),
        lax.all_to_all(right, "col", split_axis=0, concat_axis=2, tiled=True),
    )
    residues = g_chan.shape[2]
    g_columns = lax.all_to_all(g_chan, "row", split_axis=2, concat_axis=1, tiled=True)
    d_left = jnp.einsum(
        "hij,hjk->hik",
        g_chan,
        lax.all_gather(right_chan, "row", axis=1, tiled=True),
        preferred_element_type=jnp.float32,
    )
    d_right = jnp.einsum(
        "hij,hik->hjk",
        g_columns,
        lax.all_gather(left_chan, "row", axis=1, tiled=True),
        preferred_element_type=jnp.float32,
    )
    d_left_tile, d_right_tile = (
        lax.all_to_all(d_left.astype(jnp.bfloat16), "col", split_axis=2, concat_axis=0, tiled=True),
        lax.all_to_all(
            d_right.astype(jnp.bfloat16), "col", split_axis=2, concat_axis=0, tiled=True
        ),
    )
    grad_l = d_left_tile.astype(jnp.float32)
    grad_r = d_right_tile.astype(jnp.float32)
    e_left = grad_l * s_left
    f_left = grad_l * q_left * s_left * (1.0 - s_left)
    e_right = grad_r * s_right
    f_right = grad_r * q_right * s_right * (1.0 - s_right)
    grads = jnp.concatenate([e_left, f_left, e_right, f_right], axis=0).astype(jnp.bfloat16)
    local_weights = jnp.einsum(
        "rcd,hrc->dh", normalized_input, grads, preferred_element_type=jnp.float32
    )
    total_weights = lax.psum(local_weights, ("row", "col")) / residues
    normalized_gradient = jnp.einsum(
        "hrc,dh->rcd", grads, stacked, preferred_element_type=jnp.float32
    )
    gradient_mean = jnp.mean(normalized_gradient, axis=-1, keepdims=True)
    gradient_input_mean = jnp.mean(normalized_gradient * standardized_input, axis=-1, keepdims=True)
    pair_gradient = (
        (normalized_gradient - gradient_mean - standardized_input * gradient_input_mean)
        * inverse_scale
    ).astype(jnp.bfloat16)
    pieces_w = jnp.split(total_weights, 4, axis=1)
    return (pair_gradient, pieces_w[0], pieces_w[1], pieces_w[2], pieces_w[3])


NT = (((1,), (1,)), ((), ()))
TN = (((0,), (0,)), ((), ()))
NN = (((1,), (0,)), ((), ()))


def dot(a, b, dims=NN):
    return lax.dot_general(a, b, dims, preferred_element_type=F32)


def stack_weights(w_refs, w_ref):
    h = w_refs[0].shape[0]
    for i, ref in enumerate(w_refs):
        w_ref[pl.ds(i * h, h), :] = ref[...]


def layer_norm(x):
    x = x.T.astype(F32)
    centered = x - jnp.mean(x, axis=0, keepdims=True)
    variance = jnp.mean(centered * centered, axis=0, keepdims=True)
    inverse_scale = lax.rsqrt(variance + 1e-05)
    return centered * inverse_scale, inverse_scale


def project(w_ref, normed):
    projected = dot(w_ref[...], normed)
    h = projected.shape[0] // 4
    q_left, p_left, q_right, p_right = (projected[i * h : (i + 1) * h] for i in range(4))
    return q_left, jax.nn.sigmoid(p_left), q_right, jax.nn.sigmoid(p_right)


def put_lanes(ref, at, value):
    lanes = ref.shape[2]
    for i in range(ref.shape[0]):
        ref[i, at, :] = value[:, i * lanes : (i + 1) * lanes]


def get_lanes(ref, at):
    return jnp.concatenate([ref[i, at, :] for i in range(ref.shape[0])], axis=1)


def before_kernel(own, pair_hbm, cot_hbm, wl, wlg, wr, wrg, out_ref, normed_hbm, *scratch):
    w_ref, *rows_refs, pair_ref, normed_ref, in_sems, out_sems, w_sems, cot_sem = scratch
    h = wl.shape[0]
    rows = pair_ref.shape[0]
    parts = in_sems.shape[0]
    count = rows // parts
    pitch = count + 1

    def come(part):
        at = pl.ds(part * count, count)
        return pltpu.make_async_copy(pair_hbm.at[at], pair_ref.at[at], in_sems.at[part])

    def leave(part):
        at = pl.ds(part * count, count)
        return pltpu.make_async_copy(normed_ref.at[at], normed_hbm.at[at], out_sems.at[part])

    def weight(i, w):
        return pltpu.make_async_copy(w, w_ref.at[pl.ds(i * h, h)], w_sems.at[i])

    for i, w in enumerate((wl, wlg, wr, wrg)):
        weight(i, w).start()
    come(0).start()
    cot = pltpu.make_async_copy(cot_hbm, out_ref.at[:, pl.ds(0, own)], cot_sem)
    for i, w in enumerate((wl, wlg, wr, wrg)):
        weight(i, w).wait()

    def one_row(part, i):
        r = part * count + i
        normed = layer_norm(pair_ref[r])[0].astype(BF16)
        normed_ref[r] = normed
        q_left, s_left, q_right, s_right = project(w_ref, normed)
        put_lanes(rows_refs[part], pl.ds(i, h, stride=pitch), s_left * q_left)
        put_lanes(rows_refs[part], pl.ds(i + h * pitch, h, stride=pitch), s_right * q_right)

    def some_channels(part, i):
        for channel in range(i * h // count, (i + 1) * h // count):
            for side in range(2):
                at = pl.ds((side * h + channel) * pitch, count)
                line = get_lanes(rows_refs[part], at).astype(BF16)
                slot = (1 + side) * own + channel % own
                out_ref[channel // own, slot, pl.ds(part * count, count), :] = line

    for part in range(parts + 1):
        if part < parts:
            come(part).wait()
        if part == 0:
            for later in range(1, parts):
                come(later).start()
            cot.start()
        for i in range(count):
            if part < parts:
                one_row(part, i)
            if part > 0:
                some_channels(part - 1, i)
        if part < parts:
            leave(part).start()
    for part in range(parts):
        leave(part).wait()
    cot.wait()


def triangle_kernel(rows, cols, in_ref, out_ref, g_ref, l_ref, r_ref):
    r, c = in_ref.shape[2:]
    own = g_ref.shape[0]
    for n in range(own):
        for i, ref in enumerate((g_ref, l_ref, r_ref)):
            for a in range(rows):
                for b in range(cols):
                    block = in_ref[a * cols + b, i * own + n]
                    ref[n, pl.ds(a * r, r), pl.ds(b * c, c)] = block
        for i, (dims, ref) in enumerate(((NN, r_ref), (TN, l_ref))):
            d = dot(g_ref[n], ref[n], dims).astype(BF16)
            for a in range(rows):
                for b in range(cols):
                    block = d[a * r : (a + 1) * r, b * c : (b + 1) * c]
                    out_ref[a * cols + b, n * 2 + i] = block


def gates_kernel(own, normed_hbm, d_ref, wl, wlg, wr, wrg, grads_ref, kept_ref, sent_ref, *scratch):
    w_ref, sums_ref, *rows_refs, normed_ref, sem = scratch
    copy = pltpu.make_async_copy(normed_hbm, normed_ref, sem)
    copy.start()
    h = wl.shape[0]
    rows = grads_ref.shape[0]
    parts = len(rows_refs)
    count = rows // parts
    pitch = count + 1
    stack_weights((wl, wlg, wr, wrg), w_ref)

    def some_channels(part, i):
        for channel in range(i * h // count, (i + 1) * h // count):
            to, slot = channel // own, (channel % own) * 2
            for side in range(2):
                line = d_ref[to, slot + side, pl.ds(part * count, count), :].astype(F32)
                put_lanes(rows_refs[part], pl.ds((side * h + channel) * pitch, count), line)

    def one_row(part, i):
        normed = normed_ref[part * count + i]
        q_left, s_left, q_right, s_right = project(w_ref, normed)
        e_left = get_lanes(rows_refs[part], pl.ds(i, h, stride=pitch)) * s_left
        e_right = get_lanes(rows_refs[part], pl.ds(i + h * pitch, h, stride=pitch)) * s_right
        f_left = e_left * q_left * (1.0 - s_left)
        f_right = e_right * q_right * (1.0 - s_right)
        grads = jnp.concatenate([e_left, f_left, e_right, f_right], axis=0).astype(BF16)
        grads_ref[part * count + i] = grads
        return grads, normed

    together = 8 if count % 8 == 0 else count
    sums_ref[...] = jnp.zeros_like(sums_ref)
    for part in range(parts + 1):
        if part == 1:
            copy.wait()
        done = []
        for i in range(count):
            if part > 0:
                done.append(one_row(part - 1, i))
            if part < parts:
                some_channels(part, i)
            if len(done) == together:
                all_grads, all_normed = (jnp.concatenate(x, axis=1) for x in zip(*done))
                sums_ref[...] += dot(all_grads, all_normed, NT)
                done = []
    bit = lax.rem(lax.axis_index("row"), 2)
    kept_ref[...] = sums_ref[pl.ds(pl.multiple_of(bit * 2 * h, 2 * h), 2 * h), :]
    sent_ref[...] = sums_ref[pl.ds(pl.multiple_of((1 - bit) * 2 * h, 2 * h), 2 * h), :]


def input_kernel(start, pair_hbm, grads_ref, wl, wlg, wr, wrg, *refs):
    out_hbm, back_ref, pair_ref, out_ref, in_sem, out_sems = refs[-6:]
    rows = pair_ref.shape[0]
    come = pltpu.make_async_copy(pair_hbm.at[pl.ds(start, rows)], pair_ref, in_sem)
    come.start()
    h = wl.shape[0]
    for i, ref in enumerate((wl, wlg, wr, wrg)):
        back_ref[:, pl.ds(i * h, h)] = ref[...].T
    come.wait()

    def one_row(r, carry):
        standardized, inverse_scale = layer_norm(pair_ref[r])
        d_normed = dot(back_ref[...], grads_ref[start + r])
        mean = jnp.mean(d_normed, axis=0, keepdims=True)
        input_mean = jnp.mean(d_normed * standardized, axis=0, keepdims=True)
        moved = (d_normed - mean - standardized * input_mean) * inverse_scale
        out_ref[r] = moved.astype(BF16).T
        return carry

    parts = out_sems.shape[0]
    count = rows // parts
    gone = []
    for part in range(parts):
        lax.fori_loop(part * count, (part + 1) * count, one_row, 0, unroll=8)
        at = pl.ds(part * count, count)
        to = out_hbm.at[pl.ds(start + part * count, count)]
        gone.append(pltpu.make_async_copy(out_ref.at[at], to, out_sems.at[part]))
        gone[-1].start()
    for copy in gone:
        copy.wait()


def finish_kernel(scale, mine_ref, other_ref, *out_refs):
    h = out_refs[0].shape[0]
    bit = lax.rem(lax.axis_index("row"), 2)
    for i, out_ref in enumerate(out_refs):
        at = pl.ds(i % 2 * h, h)
        mine = bit == i // 2
        out_ref[...] = jnp.where(mine, mine_ref[at, :], other_ref[at, :]) * scale


def channel_shards(sizes, pair, cotangent, *weights):
    rows, cols = sizes
    devices = rows * cols
    hidden, r, c = cotangent.shape
    dim = pair.shape[2]
    own = hidden // devices
    pieces = 2 if r % 2 == 0 else 1
    parts = 2 if r % 32 == 0 else 1
    weights = [w.T for w in weights]
    vmem = pl.BlockSpec(memory_space=pltpu.VMEM)
    hbm = pl.BlockSpec(memory_space=pltpu.HBM)
    exchange = functools.partial(
        lax.all_to_all, axis_name=("row", "col"), split_axis=0, concat_axis=0, tiled=True
    )
    stacked = pltpu.VMEM((4 * hidden, dim), BF16)
    lanes = min(c, 128)
    rows_scratch = pltpu.VMEM((c // lanes, (2 * hidden + 1) * (r // parts + 1), lanes), F32)
    columns = r * c
    n_i, n_k = rows * r, cols * c
    pair = pltpu.with_memory_space_constraint(pair, pltpu.HBM)

    def cost(flops, *arrays):
        moved = sum(a.size * a.dtype.itemsize for a in arrays)
        return pl.CostEstimate(flops=flops, bytes_accessed=moved, transcendentals=0)

    def memory(mib):
        return pltpu.CompilerParams(vmem_limit_bytes=mib * 2**20)

    normed_shape = jax.ShapeDtypeStruct((r, dim, c), BF16)
    sent, normed = pl.pallas_call(
        functools.partial(before_kernel, own),
        in_specs=[hbm] * 6,
        out_specs=[vmem, hbm],
        out_shape=[
            jax.ShapeDtypeStruct((devices, 3 * own, r, c), BF16),
            pltpu.HBM(normed_shape.shape, BF16),
        ],
        scratch_shapes=[
            stacked,
            *[rows_scratch] * parts,
            pltpu.VMEM(pair.shape, BF16),
            pltpu.VMEM(normed_shape.shape, BF16),
            pltpu.SemaphoreType.DMA((parts,)),
            pltpu.SemaphoreType.DMA((parts,)),
            pltpu.SemaphoreType.DMA((4,)),
            pltpu.SemaphoreType.DMA,
        ],
        compiler_params=memory(24),
        name="before",
    )(
        pair,
        pltpu.with_memory_space_constraint(cotangent.reshape(devices, own, r, c), pltpu.HBM),
        *(pltpu.with_memory_space_constraint(w, pltpu.HBM) for w in weights),
    )

    sent = pl.pallas_call(
        functools.partial(triangle_kernel, rows, cols),
        in_specs=[vmem],
        out_specs=vmem,
        out_shape=jax.ShapeDtypeStruct((devices, 2 * own, r, c), BF16),
        scratch_shapes=[pltpu.VMEM((own, n_i, n_k), BF16)] * 3,
        compiler_params=memory(32),
        name="triangle",
    )(exchange(sent))

    half_shape = jax.ShapeDtypeStruct((2 * hidden, dim), F32)
    grads, kept, given = pl.pallas_call(
        functools.partial(gates_kernel, own),
        in_specs=[hbm] + [vmem] * 5,
        out_specs=[vmem] * 3,
        out_shape=[jax.ShapeDtypeStruct((r, 4 * hidden, c), BF16), half_shape, half_shape],
        scratch_shapes=[
            stacked,
            pltpu.VMEM((4 * hidden, dim), F32),
            *[rows_scratch] * parts,
            pltpu.VMEM(normed_shape.shape, BF16),
            pltpu.SemaphoreType.DMA,
        ],
        compiler_params=memory(28),
        name="gates",
    )(pltpu.with_memory_space_constraint(normed, pltpu.HBM), exchange(sent), *weights)

    def input_piece(piece, pair_gradient):
        held = [] if pair_gradient is None else [pair_gradient]
        count = r // pieces
        return pl.pallas_call(
            functools.partial(input_kernel, piece * count),
            in_specs=[hbm] + [vmem] * 5 + [hbm] * len(held),
            out_specs=hbm,
            out_shape=jax.ShapeDtypeStruct(pair.shape, BF16),
            scratch_shapes=[
                pltpu.VMEM((dim, 4 * hidden), BF16),
                pltpu.VMEM((count, c, dim), BF16),
                pltpu.VMEM((count, c, dim), BF16),
                pltpu.SemaphoreType.DMA,
                pltpu.SemaphoreType.DMA((2 if count % 8 == 0 else 1,)),
            ],
            input_output_aliases={6: 0} if held else {},
            compiler_params=memory(16),
            cost_estimate=cost(8 * hidden * dim * columns // pieces, pair),
            name="input",
        )(pair, grads, *weights, *held)

    steps = [("row", rows, 1 << i) for i in range(1, rows.bit_length() - 1)][::-1]
    steps += [("col", cols, 1 << i) for i in range(cols.bit_length() - 1)]
    pieces = min(pieces, len(steps))
    neighbours = [(i, i ^ 1) for i in range(rows)]
    pair_gradient = None
    mine = kept + lax.ppermute(given, "row", neighbours)
    for n, (axis, size, step) in enumerate(steps):
        other = lax.ppermute(mine, axis, [(i, i ^ step) for i in range(size)])
        if n < pieces:
            pair_gradient = input_piece(n, pair_gradient)
            other, pair_gradient = lax.optimization_barrier((other, pair_gradient))
        mine = mine + other
    weight_grads = pl.pallas_call(
        functools.partial(finish_kernel, 1.0 / n_i),
        in_specs=[vmem, vmem],
        out_shape=[jax.ShapeDtypeStruct((hidden, dim), F32)] * 4,
        compiler_params=memory(8),
        name="finish",
    )(mine, lax.ppermute(mine, "row", neighbours))
    return (pair_gradient, *(g.T for g in weight_grads))


def solution(mesh):
    in_specs = (P("row", "col", None), P(None, "row", "col"), P(), P(), P(), P())
    out_specs = (P("row", "col", None), P(), P(), P(), P())
    sizes = (mesh.shape["row"], mesh.shape["col"])

    def shards(pair, cotangent, *weights):
        plain = all(size > 1 and size & (size - 1) == 0 for size in sizes)
        if plain and cotangent.shape[0] % (sizes[0] * sizes[1]) == 0:
            return channel_shards(sizes, pair, cotangent, *weights)
        return gathered_shards(pair, cotangent, *weights)

    return jax.shard_map(shards, mesh=mesh, in_specs=in_specs, out_specs=out_specs, check_vma=False)
```

```python
import functools

import jax
import jax.numpy as jnp
from jax import lax
from jax.experimental import pallas as pl
from jax.experimental.pallas import tpu as pltpu
from jax.sharding import PartitionSpec as P

BF16, F32 = jnp.bfloat16, jnp.float32


def gathered_shards(pair, cotangent, w_left, w_left_gate, w_right, w_right_gate):
    pair_f = pair.astype(jnp.float32)
    average = jnp.mean(pair_f, axis=-1, keepdims=True)
    centered_input = pair_f - average
    variance = jnp.mean(centered_input * centered_input, axis=-1, keepdims=True)
    inverse_scale = 1.0 / jnp.sqrt(variance + 1e-05)
    standardized_input = centered_input * inverse_scale
    normalized_input = standardized_input.astype(jnp.bfloat16)
    stacked = jnp.concatenate([w_left, w_left_gate, w_right, w_right_gate], axis=1)
    projected = jnp.einsum(
        "rcd,dh->hrc", normalized_input, stacked, preferred_element_type=jnp.float32
    )
    q_left, p_left, q_right, p_right = jnp.split(projected, 4, axis=0)
    s_left = jax.nn.sigmoid(p_left)
    s_right = jax.nn.sigmoid(p_right)
    left = (s_left * q_left).astype(jnp.bfloat16)
    right = (s_right * q_right).astype(jnp.bfloat16)
    g_chan, left_chan, right_chan = (
        lax.all_to_all(cotangent, "col", split_axis=0, concat_axis=2, tiled=True),
        lax.all_to_all(left, "col", split_axis=0, concat_axis=2, tiled=True),
        lax.all_to_all(right, "col", split_axis=0, concat_axis=2, tiled=True),
    )
    residues = g_chan.shape[2]
    g_columns = lax.all_to_all(g_chan, "row", split_axis=2, concat_axis=1, tiled=True)
    d_left = jnp.einsum(
        "hij,hjk->hik",
        g_chan,
        lax.all_gather(right_chan, "row", axis=1, tiled=True),
        preferred_element_type=jnp.float32,
    )
    d_right = jnp.einsum(
        "hij,hik->hjk",
        g_columns,
        lax.all_gather(left_chan, "row", axis=1, tiled=True),
        preferred_element_type=jnp.float32,
    )
    d_left_tile, d_right_tile = (
        lax.all_to_all(d_left.astype(jnp.bfloat16), "col", split_axis=2, concat_axis=0, tiled=True),
        lax.all_to_all(
            d_right.astype(jnp.bfloat16), "col", split_axis=2, concat_axis=0, tiled=True
        ),
    )
    grad_l = d_left_tile.astype(jnp.float32)
    grad_r = d_right_tile.astype(jnp.float32)
    e_left = grad_l * s_left
    f_left = grad_l * q_left * s_left * (1.0 - s_left)
    e_right = grad_r * s_right
    f_right = grad_r * q_right * s_right * (1.0 - s_right)
    grads = jnp.concatenate([e_left, f_left, e_right, f_right], axis=0).astype(jnp.bfloat16)
    local_weights = jnp.einsum(
        "rcd,hrc->dh", normalized_input, grads, preferred_element_type=jnp.float32
    )
    total_weights = lax.psum(local_weights, ("row", "col")) / residues
    normalized_gradient = jnp.einsum(
        "hrc,dh->rcd", grads, stacked, preferred_element_type=jnp.float32
    )
    gradient_mean = jnp.mean(normalized_gradient, axis=-1, keepdims=True)
    gradient_input_mean = jnp.mean(normalized_gradient * standardized_input, axis=-1, keepdims=True)
    pair_gradient = (
        (normalized_gradient - gradient_mean - standardized_input * gradient_input_mean)
        * inverse_scale
    ).astype(jnp.bfloat16)
    pieces_w = jnp.split(total_weights, 4, axis=1)
    return (pair_gradient, pieces_w[0], pieces_w[1], pieces_w[2], pieces_w[3])


NT = (((1,), (1,)), ((), ()))
TN = (((0,), (0,)), ((), ()))
NN = (((1,), (0,)), ((), ()))


def dot(a, b, dims=NN):
    return lax.dot_general(a, b, dims, preferred_element_type=F32)


def stack_weights(w_refs, w_ref):
    h = w_refs[0].shape[0]
    for i, ref in enumerate(w_refs):
        w_ref[pl.ds(i * h, h), :] = ref[...]


def layer_norm(x):
    x = x.T.astype(F32)
    centered = x - jnp.mean(x, axis=0, keepdims=True)
    variance = jnp.mean(centered * centered, axis=0, keepdims=True)
    inverse_scale = lax.rsqrt(variance + 1e-05)
    return centered * inverse_scale, inverse_scale


def project(w_ref, normed):
    projected = dot(w_ref[...], normed)
    h = projected.shape[0] // 4
    q_left, p_left, q_right, p_right = (projected[i * h : (i + 1) * h] for i in range(4))
    return q_left, jax.nn.sigmoid(p_left), q_right, jax.nn.sigmoid(p_right)


def put_lanes(ref, at, value):
    lanes = ref.shape[2]
    for i in range(ref.shape[0]):
        ref[i, at, :] = value[:, i * lanes : (i + 1) * lanes]


def get_lanes(ref, at):
    return jnp.concatenate([ref[i, at, :] for i in range(ref.shape[0])], axis=1)


def before_kernel(own, pair_hbm, cot_hbm, wl, wlg, wr, wrg, out_ref, normed_hbm, *scratch):
    w_ref, *rows_refs, pair_ref, normed_ref, in_sems, out_sems, w_sems, cot_sem = scratch
    h = wl.shape[0]
    rows = pair_ref.shape[0]
    parts = in_sems.shape[0]
    count = rows // parts
    pitch = count + 1

    def come(part):
        at = pl.ds(part * count, count)
        return pltpu.make_async_copy(pair_hbm.at[at], pair_ref.at[at], in_sems.at[part])

    def leave(part):
        at = pl.ds(part * count, count)
        return pltpu.make_async_copy(normed_ref.at[at], normed_hbm.at[at], out_sems.at[part])

    def weight(i, w):
        return pltpu.make_async_copy(w, w_ref.at[pl.ds(i * h, h)], w_sems.at[i])

    for i, w in enumerate((wl, wlg, wr, wrg)):
        weight(i, w).start()
    for part in range(parts):
        come(part).start()
    cot = pltpu.make_async_copy(cot_hbm, out_ref.at[:, pl.ds(0, own)], cot_sem)
    cot.start()
    for i, w in enumerate((wl, wlg, wr, wrg)):
        weight(i, w).wait()

    def one_row(part, i):
        r = part * count + i
        normed = layer_norm(pair_ref[r])[0].astype(BF16)
        normed_ref[r] = normed
        q_left, s_left, q_right, s_right = project(w_ref, normed)
        put_lanes(rows_refs[part], pl.ds(i, h, stride=pitch), s_left * q_left)
        put_lanes(rows_refs[part], pl.ds(i + h * pitch, h, stride=pitch), s_right * q_right)

    def some_channels(part, i):
        for channel in range(i * h // count, (i + 1) * h // count):
            for side in range(2):
                at = pl.ds((side * h + channel) * pitch, count)
                line = get_lanes(rows_refs[part], at).astype(BF16)
                slot = (1 + side) * own + channel % own
                out_ref[channel // own, slot, pl.ds(part * count, count), :] = line

    for part in range(parts + 1):
        if part < parts:
            come(part).wait()
        for i in range(count):
            if part < parts:
                one_row(part, i)
            if part > 0:
                some_channels(part - 1, i)
        if part < parts:
            leave(part).start()
    for part in range(parts):
        leave(part).wait()
    cot.wait()


def triangle_kernel(rows, cols, in_ref, out_ref, g_ref, l_ref, r_ref):
    r, c = in_ref.shape[2:]
    own = g_ref.shape[0]
    for n in range(own):
        for i, ref in enumerate((g_ref, l_ref, r_ref)):
            for a in range(rows):
                for b in range(cols):
                    block = in_ref[a * cols + b, i * own + n]
                    ref[n, pl.ds(a * r, r), pl.ds(b * c, c)] = block
        for i, (dims, ref) in enumerate(((NN, r_ref), (TN, l_ref))):
            d = dot(g_ref[n], ref[n], dims).astype(BF16)
            for a in range(rows):
                for b in range(cols):
                    block = d[a * r : (a + 1) * r, b * c : (b + 1) * c]
                    out_ref[a * cols + b, n * 2 + i] = block


def gates_kernel(own, normed_hbm, d_ref, wl, wlg, wr, wrg, grads_ref, kept_ref, sent_ref, *scratch):
    w_ref, sums_ref, *rows_refs, normed_ref, sem = scratch
    copy = pltpu.make_async_copy(normed_hbm, normed_ref, sem)
    copy.start()
    h = wl.shape[0]
    rows = grads_ref.shape[0]
    parts = len(rows_refs)
    count = rows // parts
    pitch = count + 1
    stack_weights((wl, wlg, wr, wrg), w_ref)

    def some_channels(part, i):
        for channel in range(i * h // count, (i + 1) * h // count):
            to, slot = channel // own, (channel % own) * 2
            for side in range(2):
                line = d_ref[to, slot + side, pl.ds(part * count, count), :].astype(F32)
                put_lanes(rows_refs[part], pl.ds((side * h + channel) * pitch, count), line)

    def one_row(part, i):
        normed = normed_ref[part * count + i]
        q_left, s_left, q_right, s_right = project(w_ref, normed)
        e_left = get_lanes(rows_refs[part], pl.ds(i, h, stride=pitch)) * s_left
        e_right = get_lanes(rows_refs[part], pl.ds(i + h * pitch, h, stride=pitch)) * s_right
        f_left = e_left * q_left * (1.0 - s_left)
        f_right = e_right * q_right * (1.0 - s_right)
        grads = jnp.concatenate([e_left, f_left, e_right, f_right], axis=0).astype(BF16)
        grads_ref[part * count + i] = grads
        return grads, normed

    together = 8 if count % 8 == 0 else count
    sums_ref[...] = jnp.zeros_like(sums_ref)
    for part in range(parts + 1):
        if part == 1:
            copy.wait()
        done = []
        for i in range(count):
            if part > 0:
                done.append(one_row(part - 1, i))
            if part < parts:
                some_channels(part, i)
            if len(done) == together:
                all_grads, all_normed = (jnp.concatenate(x, axis=1) for x in zip(*done))
                sums_ref[...] += dot(all_grads, all_normed, NT)
                done = []
    bit = lax.rem(lax.axis_index("row"), 2)
    kept_ref[...] = sums_ref[pl.ds(pl.multiple_of(bit * 2 * h, 2 * h), 2 * h), :]
    sent_ref[...] = sums_ref[pl.ds(pl.multiple_of((1 - bit) * 2 * h, 2 * h), 2 * h), :]


def input_kernel(start, pair_hbm, grads_ref, wl, wlg, wr, wrg, *refs):
    out_hbm, back_ref, pair_ref, out_ref, in_sem, out_sems = refs[-6:]
    rows = pair_ref.shape[0]
    come = pltpu.make_async_copy(pair_hbm.at[pl.ds(start, rows)], pair_ref, in_sem)
    come.start()
    h = wl.shape[0]
    for i, ref in enumerate((wl, wlg, wr, wrg)):
        back_ref[:, pl.ds(i * h, h)] = ref[...].T
    come.wait()

    def one_row(r, carry):
        standardized, inverse_scale = layer_norm(pair_ref[r])
        d_normed = dot(back_ref[...], grads_ref[start + r])
        mean = jnp.mean(d_normed, axis=0, keepdims=True)
        input_mean = jnp.mean(d_normed * standardized, axis=0, keepdims=True)
        moved = (d_normed - mean - standardized * input_mean) * inverse_scale
        out_ref[r] = moved.astype(BF16).T
        return carry

    parts = out_sems.shape[0]
    count = rows // parts
    gone = []
    for part in range(parts):
        lax.fori_loop(part * count, (part + 1) * count, one_row, 0, unroll=8)
        at = pl.ds(part * count, count)
        to = out_hbm.at[pl.ds(start + part * count, count)]
        gone.append(pltpu.make_async_copy(out_ref.at[at], to, out_sems.at[part]))
        gone[-1].start()
    for copy in gone:
        copy.wait()


def finish_kernel(scale, mine_ref, other_ref, *out_refs):
    h = out_refs[0].shape[0]
    bit = lax.rem(lax.axis_index("row"), 2)
    for i, out_ref in enumerate(out_refs):
        at = pl.ds(i % 2 * h, h)
        mine = bit == i // 2
        out_ref[...] = jnp.where(mine, mine_ref[at, :], other_ref[at, :]) * scale


def channel_shards(sizes, pair, cotangent, *weights):
    rows, cols = sizes
    devices = rows * cols
    hidden, r, c = cotangent.shape
    dim = pair.shape[2]
    own = hidden // devices
    pieces = 2 if r % 2 == 0 else 1
    parts = 2 if r % 32 == 0 else 1
    weights = [w.T for w in weights]
    vmem = pl.BlockSpec(memory_space=pltpu.VMEM)
    hbm = pl.BlockSpec(memory_space=pltpu.HBM)
    exchange = functools.partial(
        lax.all_to_all, axis_name=("row", "col"), split_axis=0, concat_axis=0, tiled=True
    )
    stacked = pltpu.VMEM((4 * hidden, dim), BF16)
    lanes = min(c, 128)
    rows_scratch = pltpu.VMEM((c // lanes, (2 * hidden + 1) * (r // parts + 1), lanes), F32)
    columns = r * c
    n_i, n_k = rows * r, cols * c
    pair = pltpu.with_memory_space_constraint(pair, pltpu.HBM)

    def cost(flops, *arrays):
        moved = sum(a.size * a.dtype.itemsize for a in arrays)
        return pl.CostEstimate(flops=flops, bytes_accessed=moved, transcendentals=0)

    def memory(mib):
        return pltpu.CompilerParams(vmem_limit_bytes=mib * 2**20)

    normed_shape = jax.ShapeDtypeStruct((r, dim, c), BF16)
    sent, normed = pl.pallas_call(
        functools.partial(before_kernel, own),
        in_specs=[hbm] * 6,
        out_specs=[vmem, hbm],
        out_shape=[
            jax.ShapeDtypeStruct((devices, 3 * own, r, c), BF16),
            pltpu.HBM(normed_shape.shape, BF16),
        ],
        scratch_shapes=[
            stacked,
            *[rows_scratch] * parts,
            pltpu.VMEM(pair.shape, BF16),
            pltpu.VMEM(normed_shape.shape, BF16),
            pltpu.SemaphoreType.DMA((parts,)),
            pltpu.SemaphoreType.DMA((parts,)),
            pltpu.SemaphoreType.DMA((4,)),
            pltpu.SemaphoreType.DMA,
        ],
        compiler_params=memory(24),
        name="before",
    )(
        pair,
        pltpu.with_memory_space_constraint(cotangent.reshape(devices, own, r, c), pltpu.HBM),
        *(pltpu.with_memory_space_constraint(w, pltpu.HBM) for w in weights),
    )

    sent = pl.pallas_call(
        functools.partial(triangle_kernel, rows, cols),
        in_specs=[vmem],
        out_specs=vmem,
        out_shape=jax.ShapeDtypeStruct((devices, 2 * own, r, c), BF16),
        scratch_shapes=[pltpu.VMEM((own, n_i, n_k), BF16)] * 3,
        compiler_params=memory(32),
        name="triangle",
    )(exchange(sent))

    half_shape = jax.ShapeDtypeStruct((2 * hidden, dim), F32)
    grads, kept, given = pl.pallas_call(
        functools.partial(gates_kernel, own),
        in_specs=[hbm] + [vmem] * 5,
        out_specs=[vmem] * 3,
        out_shape=[jax.ShapeDtypeStruct((r, 4 * hidden, c), BF16), half_shape, half_shape],
        scratch_shapes=[
            stacked,
            pltpu.VMEM((4 * hidden, dim), F32),
            *[rows_scratch] * parts,
            pltpu.VMEM(normed_shape.shape, BF16),
            pltpu.SemaphoreType.DMA,
        ],
        compiler_params=memory(28),
        name="gates",
    )(pltpu.with_memory_space_constraint(normed, pltpu.HBM), exchange(sent), *weights)

    def input_piece(piece, pair_gradient):
        held = [] if pair_gradient is None else [pair_gradient]
        count = r // pieces
        return pl.pallas_call(
            functools.partial(input_kernel, piece * count),
            in_specs=[hbm] + [vmem] * 5 + [hbm] * len(held),
            out_specs=hbm,
            out_shape=jax.ShapeDtypeStruct(pair.shape, BF16),
            scratch_shapes=[
                pltpu.VMEM((dim, 4 * hidden), BF16),
                pltpu.VMEM((count, c, dim), BF16),
                pltpu.VMEM((count, c, dim), BF16),
                pltpu.SemaphoreType.DMA,
                pltpu.SemaphoreType.DMA((2 if count % 8 == 0 else 1,)),
            ],
            input_output_aliases={6: 0} if held else {},
            compiler_params=memory(16),
            cost_estimate=cost(8 * hidden * dim * columns // pieces, pair),
            name="input",
        )(pair, grads, *weights, *held)

    steps = [("row", rows, 1 << i) for i in range(1, rows.bit_length() - 1)]
    steps = steps[1:] + steps[:1]
    steps += [("col", cols, 1 << i) for i in range(cols.bit_length() - 1)]
    pieces = min(pieces, len(steps))
    neighbours = [(i, i ^ 1) for i in range(rows)]
    pair_gradient = None
    mine = kept + lax.ppermute(given, "row", neighbours)
    for n, (axis, size, step) in enumerate(steps):
        other = lax.ppermute(mine, axis, [(i, i ^ step) for i in range(size)])
        if n < pieces:
            pair_gradient = input_piece(n, pair_gradient)
            other, pair_gradient = lax.optimization_barrier((other, pair_gradient))
        mine = mine + other
    weight_grads = pl.pallas_call(
        functools.partial(finish_kernel, 1.0 / n_i),
        in_specs=[vmem, vmem],
        out_shape=[jax.ShapeDtypeStruct((hidden, dim), F32)] * 4,
        compiler_params=memory(8),
        name="finish",
    )(mine, lax.ppermute(mine, "row", neighbours))
    return (pair_gradient, *(g.T for g in weight_grads))


def solution(mesh):
    in_specs = (P("row", "col", None), P(None, "row", "col"), P(), P(), P(), P())
    out_specs = (P("row", "col", None), P(), P(), P(), P())
    sizes = (mesh.shape["row"], mesh.shape["col"])

    def shards(pair, cotangent, *weights):
        plain = all(size > 1 and size & (size - 1) == 0 for size in sizes)
        if plain and cotangent.shape[0] % (sizes[0] * sizes[1]) == 0:
            return channel_shards(sizes, pair, cotangent, *weights)
        return gathered_shards(pair, cotangent, *weights)

    return jax.shard_map(shards, mesh=mesh, in_specs=in_specs, out_specs=out_specs, check_vma=False)
```

```python
import functools

import jax
import jax.numpy as jnp
from jax import lax
from jax.experimental import pallas as pl
from jax.experimental.pallas import tpu as pltpu
from jax.sharding import PartitionSpec as P

BF16, F32 = jnp.bfloat16, jnp.float32


def gathered_shards(pair, cotangent, w_left, w_left_gate, w_right, w_right_gate):
    pair_f = pair.astype(jnp.float32)
    average = jnp.mean(pair_f, axis=-1, keepdims=True)
    centered_input = pair_f - average
    variance = jnp.mean(centered_input * centered_input, axis=-1, keepdims=True)
    inverse_scale = 1.0 / jnp.sqrt(variance + 1e-05)
    standardized_input = centered_input * inverse_scale
    normalized_input = standardized_input.astype(jnp.bfloat16)
    stacked = jnp.concatenate([w_left, w_left_gate, w_right, w_right_gate], axis=1)
    projected = jnp.einsum(
        "rcd,dh->hrc", normalized_input, stacked, preferred_element_type=jnp.float32
    )
    q_left, p_left, q_right, p_right = jnp.split(projected, 4, axis=0)
    s_left = jax.nn.sigmoid(p_left)
    s_right = jax.nn.sigmoid(p_right)
    left = (s_left * q_left).astype(jnp.bfloat16)
    right = (s_right * q_right).astype(jnp.bfloat16)
    g_chan, left_chan, right_chan = (
        lax.all_to_all(cotangent, "col", split_axis=0, concat_axis=2, tiled=True),
        lax.all_to_all(left, "col", split_axis=0, concat_axis=2, tiled=True),
        lax.all_to_all(right, "col", split_axis=0, concat_axis=2, tiled=True),
    )
    residues = g_chan.shape[2]
    g_columns = lax.all_to_all(g_chan, "row", split_axis=2, concat_axis=1, tiled=True)
    d_left = jnp.einsum(
        "hij,hjk->hik",
        g_chan,
        lax.all_gather(right_chan, "row", axis=1, tiled=True),
        preferred_element_type=jnp.float32,
    )
    d_right = jnp.einsum(
        "hij,hik->hjk",
        g_columns,
        lax.all_gather(left_chan, "row", axis=1, tiled=True),
        preferred_element_type=jnp.float32,
    )
    d_left_tile, d_right_tile = (
        lax.all_to_all(d_left.astype(jnp.bfloat16), "col", split_axis=2, concat_axis=0, tiled=True),
        lax.all_to_all(
            d_right.astype(jnp.bfloat16), "col", split_axis=2, concat_axis=0, tiled=True
        ),
    )
    grad_l = d_left_tile.astype(jnp.float32)
    grad_r = d_right_tile.astype(jnp.float32)
    e_left = grad_l * s_left
    f_left = grad_l * q_left * s_left * (1.0 - s_left)
    e_right = grad_r * s_right
    f_right = grad_r * q_right * s_right * (1.0 - s_right)
    grads = jnp.concatenate([e_left, f_left, e_right, f_right], axis=0).astype(jnp.bfloat16)
    local_weights = jnp.einsum(
        "rcd,hrc->dh", normalized_input, grads, preferred_element_type=jnp.float32
    )
    total_weights = lax.psum(local_weights, ("row", "col")) / residues
    normalized_gradient = jnp.einsum(
        "hrc,dh->rcd", grads, stacked, preferred_element_type=jnp.float32
    )
    gradient_mean = jnp.mean(normalized_gradient, axis=-1, keepdims=True)
    gradient_input_mean = jnp.mean(normalized_gradient * standardized_input, axis=-1, keepdims=True)
    pair_gradient = (
        (normalized_gradient - gradient_mean - standardized_input * gradient_input_mean)
        * inverse_scale
    ).astype(jnp.bfloat16)
    pieces_w = jnp.split(total_weights, 4, axis=1)
    return (pair_gradient, pieces_w[0], pieces_w[1], pieces_w[2], pieces_w[3])


NT = (((1,), (1,)), ((), ()))
TN = (((0,), (0,)), ((), ()))
NN = (((1,), (0,)), ((), ()))


def dot(a, b, dims=NN):
    return lax.dot_general(a, b, dims, preferred_element_type=F32)


def stack_weights(w_refs, w_ref):
    h = w_refs[0].shape[0]
    for i, ref in enumerate(w_refs):
        w_ref[pl.ds(i * h, h), :] = ref[...]


def layer_norm(x):
    x = x.T.astype(F32)
    centered = x - jnp.mean(x, axis=0, keepdims=True)
    variance = jnp.mean(centered * centered, axis=0, keepdims=True)
    inverse_scale = lax.rsqrt(variance + 1e-05)
    return centered * inverse_scale, inverse_scale


def project(w_ref, normed):
    projected = dot(w_ref[...], normed)
    h = projected.shape[0] // 4
    q_left, p_left, q_right, p_right = (projected[i * h : (i + 1) * h] for i in range(4))
    return q_left, jax.nn.sigmoid(p_left), q_right, jax.nn.sigmoid(p_right)


def put_lanes(ref, at, value):
    lanes = ref.shape[2]
    for i in range(ref.shape[0]):
        ref[i, at, :] = value[:, i * lanes : (i + 1) * lanes]


def get_lanes(ref, at):
    return jnp.concatenate([ref[i, at, :] for i in range(ref.shape[0])], axis=1)


def before_kernel(own, pair_hbm, cot_hbm, wl, wlg, wr, wrg, out_ref, normed_hbm, *scratch):
    w_ref, *rows_refs, pair_ref, normed_ref, in_sems, out_sems, w_sems, cot_sem = scratch
    h = wl.shape[0]
    rows = pair_ref.shape[0]
    parts = in_sems.shape[0]
    count = rows // parts
    pitch = count + 1
    rows_each = count
    pair_of = 2 if count % 2 == 0 else 1

    def come(part):
        at = pl.ds(part * count, count)
        return pltpu.make_async_copy(pair_hbm.at[at], pair_ref.at[at], in_sems.at[part])

    def leave(part):
        at = pl.ds(part * count, count)
        return pltpu.make_async_copy(normed_ref.at[at], normed_hbm.at[at], out_sems.at[part])

    def weight(i, w):
        return pltpu.make_async_copy(w, w_ref.at[pl.ds(i * h, h)], w_sems.at[i])

    for i, w in enumerate((wl, wlg, wr, wrg)):
        weight(i, w).start()
    for part in range(parts):
        come(part).start()
    cot = pltpu.make_async_copy(cot_hbm, out_ref.at[:, pl.ds(0, own)], cot_sem)
    cot.start()
    for i, w in enumerate((wl, wlg, wr, wrg)):
        weight(i, w).wait()

    def some_rows(part, first, count):
        all_normed = []
        for i in range(first, first + count):
            all_normed.append(layer_norm(pair_ref[part * rows_each + i])[0].astype(BF16))
            normed_ref[part * rows_each + i] = all_normed[-1]
        columns = all_normed[0].shape[1]
        q_left, s_left, q_right, s_right = project(w_ref, jnp.concatenate(all_normed, axis=1))
        left, right = s_left * q_left, s_right * q_right
        for n in range(count):
            i, at = first + n, slice(n * columns, (n + 1) * columns)
            put_lanes(rows_refs[part], pl.ds(i, h, stride=pitch), left[:, at])
            put_lanes(rows_refs[part], pl.ds(i + h * pitch, h, stride=pitch), right[:, at])

    def some_channels(part, i):
        for channel in range(i * h // count, (i + 1) * h // count):
            for side in range(2):
                at = pl.ds((side * h + channel) * pitch, count)
                line = get_lanes(rows_refs[part], at).astype(BF16)
                slot = (1 + side) * own + channel % own
                out_ref[channel // own, slot, pl.ds(part * count, count), :] = line

    for part in range(parts + 1):
        if part < parts:
            come(part).wait()
        for i in range(count):
            if part < parts and i % pair_of == 0:
                some_rows(part, i, pair_of)
            if part > 0:
                some_channels(part - 1, i)
        if part < parts:
            leave(part).start()
    for part in range(parts):
        leave(part).wait()
    cot.wait()


def triangle_kernel(rows, cols, in_ref, out_ref, g_ref, l_ref, r_ref):
    r, c = in_ref.shape[2:]
    own = g_ref.shape[0]
    for n in range(own):
        for i, ref in enumerate((g_ref, l_ref, r_ref)):
            for a in range(rows):
                for b in range(cols):
                    block = in_ref[a * cols + b, i * own + n]
                    ref[n, pl.ds(a * r, r), pl.ds(b * c, c)] = block
        for i, (dims, ref) in enumerate(((NN, r_ref), (TN, l_ref))):
            d = dot(g_ref[n], ref[n], dims).astype(BF16)
            for a in range(rows):
                for b in range(cols):
                    block = d[a * r : (a + 1) * r, b * c : (b + 1) * c]
                    out_ref[a * cols + b, n * 2 + i] = block


def gates_kernel(own, normed_hbm, d_ref, wl, wlg, wr, wrg, grads_ref, kept_ref, sent_ref, *scratch):
    w_ref, sums_ref, *rows_refs, normed_ref, sem = scratch
    copy = pltpu.make_async_copy(normed_hbm, normed_ref, sem)
    copy.start()
    h = wl.shape[0]
    rows = grads_ref.shape[0]
    parts = len(rows_refs)
    count = rows // parts
    pitch = count + 1
    rows_each = count
    pair_of = 2 if count % 2 == 0 else 1
    stack_weights((wl, wlg, wr, wrg), w_ref)

    def some_channels(part, i):
        for channel in range(i * h // count, (i + 1) * h // count):
            to, slot = channel // own, (channel % own) * 2
            for side in range(2):
                line = d_ref[to, slot + side, pl.ds(part * count, count), :].astype(F32)
                put_lanes(rows_refs[part], pl.ds((side * h + channel) * pitch, count), line)

    def some_rows(part, first, count):
        at = [part * rows_each + first + n for n in range(count)]
        normed = jnp.concatenate([normed_ref[r] for r in at], axis=1)
        q_left, s_left, q_right, s_right = project(w_ref, normed)

        def lines(start):
            starts = [start + first + n for n in range(count)]
            each = [get_lanes(rows_refs[part], pl.ds(n, h, stride=pitch)) for n in starts]
            return jnp.concatenate(each, axis=1)

        e_left = lines(0) * s_left
        e_right = lines(h * pitch) * s_right
        f_left = e_left * q_left * (1.0 - s_left)
        f_right = e_right * q_right * (1.0 - s_right)
        grads = jnp.concatenate([e_left, f_left, e_right, f_right], axis=0).astype(BF16)
        columns = grads_ref.shape[2]
        for n, r in enumerate(at):
            grads_ref[r] = grads[:, n * columns : (n + 1) * columns]
        return grads, normed

    together = 8 if count % 8 == 0 else count
    sums_ref[...] = jnp.zeros_like(sums_ref)
    for part in range(parts + 1):
        if part == 1:
            copy.wait()
        done = []
        for i in range(count):
            if part > 0 and i % pair_of == 0:
                done.append(some_rows(part - 1, i, pair_of))
            if part < parts:
                some_channels(part, i)
            if len(done) * pair_of == together:
                all_grads, all_normed = (jnp.concatenate(x, axis=1) for x in zip(*done))
                sums_ref[...] += dot(all_grads, all_normed, NT)
                done = []
    bit = lax.rem(lax.axis_index("row"), 2)
    kept_ref[...] = sums_ref[pl.ds(pl.multiple_of(bit * 2 * h, 2 * h), 2 * h), :]
    sent_ref[...] = sums_ref[pl.ds(pl.multiple_of((1 - bit) * 2 * h, 2 * h), 2 * h), :]


def input_kernel(start, pair_hbm, grads_ref, wl, wlg, wr, wrg, *refs):
    out_hbm, back_ref, pair_ref, out_ref, in_sem, out_sems = refs[-6:]
    rows = pair_ref.shape[0]
    come = pltpu.make_async_copy(pair_hbm.at[pl.ds(start, rows)], pair_ref, in_sem)
    come.start()
    h = wl.shape[0]
    for i, ref in enumerate((wl, wlg, wr, wrg)):
        back_ref[:, pl.ds(i * h, h)] = ref[...].T
    come.wait()

    def one_row(r, carry):
        standardized, inverse_scale = layer_norm(pair_ref[r])
        d_normed = dot(back_ref[...], grads_ref[start + r])
        mean = jnp.mean(d_normed, axis=0, keepdims=True)
        input_mean = jnp.mean(d_normed * standardized, axis=0, keepdims=True)
        moved = (d_normed - mean - standardized * input_mean) * inverse_scale
        out_ref[r] = moved.astype(BF16).T
        return carry

    parts = out_sems.shape[0]
    count = rows // parts
    gone = []
    for part in range(parts):
        lax.fori_loop(part * count, (part + 1) * count, one_row, 0, unroll=8)
        at = pl.ds(part * count, count)
        to = out_hbm.at[pl.ds(start + part * count, count)]
        gone.append(pltpu.make_async_copy(out_ref.at[at], to, out_sems.at[part]))
        gone[-1].start()
    for copy in gone:
        copy.wait()


def finish_kernel(scale, mine_ref, other_ref, *out_refs):
    h = out_refs[0].shape[0]
    bit = lax.rem(lax.axis_index("row"), 2)
    for i, out_ref in enumerate(out_refs):
        at = pl.ds(i % 2 * h, h)
        mine = bit == i // 2
        out_ref[...] = jnp.where(mine, mine_ref[at, :], other_ref[at, :]) * scale


def channel_shards(sizes, pair, cotangent, *weights):
    rows, cols = sizes
    devices = rows * cols
    hidden, r, c = cotangent.shape
    dim = pair.shape[2]
    own = hidden // devices
    pieces = 2 if r % 2 == 0 else 1
    parts = 2 if r % 32 == 0 else 1
    weights = [w.T for w in weights]
    vmem = pl.BlockSpec(memory_space=pltpu.VMEM)
    hbm = pl.BlockSpec(memory_space=pltpu.HBM)
    exchange = functools.partial(
        lax.all_to_all, axis_name=("row", "col"), split_axis=0, concat_axis=0, tiled=True
    )
    stacked = pltpu.VMEM((4 * hidden, dim), BF16)
    lanes = min(c, 128)
    rows_scratch = pltpu.VMEM((c // lanes, (2 * hidden + 1) * (r // parts + 1), lanes), F32)
    columns = r * c
    n_i, n_k = rows * r, cols * c
    pair = pltpu.with_memory_space_constraint(pair, pltpu.HBM)

    def cost(flops, *arrays):
        moved = sum(a.size * a.dtype.itemsize for a in arrays)
        return pl.CostEstimate(flops=flops, bytes_accessed=moved, transcendentals=0)

    def memory(mib):
        return pltpu.CompilerParams(vmem_limit_bytes=mib * 2**20)

    normed_shape = jax.ShapeDtypeStruct((r, dim, c), BF16)
    sent, normed = pl.pallas_call(
        functools.partial(before_kernel, own),
        in_specs=[hbm] * 6,
        out_specs=[vmem, hbm],
        out_shape=[
            jax.ShapeDtypeStruct((devices, 3 * own, r, c), BF16),
            pltpu.HBM(normed_shape.shape, BF16),
        ],
        scratch_shapes=[
            stacked,
            *[rows_scratch] * parts,
            pltpu.VMEM(pair.shape, BF16),
            pltpu.VMEM(normed_shape.shape, BF16),
            pltpu.SemaphoreType.DMA((parts,)),
            pltpu.SemaphoreType.DMA((parts,)),
            pltpu.SemaphoreType.DMA((4,)),
            pltpu.SemaphoreType.DMA,
        ],
        compiler_params=memory(24),
        name="before",
    )(
        pair,
        pltpu.with_memory_space_constraint(cotangent.reshape(devices, own, r, c), pltpu.HBM),
        *(pltpu.with_memory_space_constraint(w, pltpu.HBM) for w in weights),
    )

    sent = pl.pallas_call(
        functools.partial(triangle_kernel, rows, cols),
        in_specs=[vmem],
        out_specs=vmem,
        out_shape=jax.ShapeDtypeStruct((devices, 2 * own, r, c), BF16),
        scratch_shapes=[pltpu.VMEM((own, n_i, n_k), BF16)] * 3,
        compiler_params=memory(32),
        name="triangle",
    )(exchange(sent))

    half_shape = jax.ShapeDtypeStruct((2 * hidden, dim), F32)
    grads, kept, given = pl.pallas_call(
        functools.partial(gates_kernel, own),
        in_specs=[hbm] + [vmem] * 5,
        out_specs=[vmem] * 3,
        out_shape=[jax.ShapeDtypeStruct((r, 4 * hidden, c), BF16), half_shape, half_shape],
        scratch_shapes=[
            stacked,
            pltpu.VMEM((4 * hidden, dim), F32),
            *[rows_scratch] * parts,
            pltpu.VMEM(normed_shape.shape, BF16),
            pltpu.SemaphoreType.DMA,
        ],
        compiler_params=memory(28),
        name="gates",
    )(pltpu.with_memory_space_constraint(normed, pltpu.HBM), exchange(sent), *weights)

    def input_piece(piece, pair_gradient):
        held = [] if pair_gradient is None else [pair_gradient]
        count = r // pieces
        return pl.pallas_call(
            functools.partial(input_kernel, piece * count),
            in_specs=[hbm] + [vmem] * 5 + [hbm] * len(held),
            out_specs=hbm,
            out_shape=jax.ShapeDtypeStruct(pair.shape, BF16),
            scratch_shapes=[
                pltpu.VMEM((dim, 4 * hidden), BF16),
                pltpu.VMEM((count, c, dim), BF16),
                pltpu.VMEM((count, c, dim), BF16),
                pltpu.SemaphoreType.DMA,
                pltpu.SemaphoreType.DMA((2 if count % 8 == 0 else 1,)),
            ],
            input_output_aliases={6: 0} if held else {},
            compiler_params=memory(16),
            cost_estimate=cost(8 * hidden * dim * columns // pieces, pair),
            name="input",
        )(pair, grads, *weights, *held)

    steps = [("row", rows, 1 << i) for i in range(1, rows.bit_length() - 1)][::-1]
    steps += [("col", cols, 1 << i) for i in range(cols.bit_length() - 1)]
    pieces = min(pieces, len(steps))
    neighbours = [(i, i ^ 1) for i in range(rows)]
    pair_gradient = None
    mine = kept + lax.ppermute(given, "row", neighbours)
    for n, (axis, size, step) in enumerate(steps):
        other = lax.ppermute(mine, axis, [(i, i ^ step) for i in range(size)])
        if n < pieces:
            pair_gradient = input_piece(n, pair_gradient)
            other, pair_gradient = lax.optimization_barrier((other, pair_gradient))
        mine = mine + other
    weight_grads = pl.pallas_call(
        functools.partial(finish_kernel, 1.0 / n_i),
        in_specs=[vmem, vmem],
        out_shape=[jax.ShapeDtypeStruct((hidden, dim), F32)] * 4,
        compiler_params=memory(8),
        name="finish",
    )(mine, lax.ppermute(mine, "row", neighbours))
    return (pair_gradient, *(g.T for g in weight_grads))


def solution(mesh):
    in_specs = (P("row", "col", None), P(None, "row", "col"), P(), P(), P(), P())
    out_specs = (P("row", "col", None), P(), P(), P(), P())
    sizes = (mesh.shape["row"], mesh.shape["col"])

    def shards(pair, cotangent, *weights):
        plain = all(size > 1 and size & (size - 1) == 0 for size in sizes)
        if plain and cotangent.shape[0] % (sizes[0] * sizes[1]) == 0:
            return channel_shards(sizes, pair, cotangent, *weights)
        return gathered_shards(pair, cotangent, *weights)

    return jax.shard_map(shards, mesh=mesh, in_specs=in_specs, out_specs=out_specs, check_vma=False)
```

```python
import functools

import jax
import jax.numpy as jnp
from jax import lax
from jax.experimental import pallas as pl
from jax.experimental.pallas import tpu as pltpu
from jax.sharding import PartitionSpec as P

BF16, F32 = jnp.bfloat16, jnp.float32


def gathered_shards(pair, cotangent, w_left, w_left_gate, w_right, w_right_gate):
    pair_f = pair.astype(jnp.float32)
    average = jnp.mean(pair_f, axis=-1, keepdims=True)
    centered_input = pair_f - average
    variance = jnp.mean(centered_input * centered_input, axis=-1, keepdims=True)
    inverse_scale = 1.0 / jnp.sqrt(variance + 1e-05)
    standardized_input = centered_input * inverse_scale
    normalized_input = standardized_input.astype(jnp.bfloat16)
    stacked = jnp.concatenate([w_left, w_left_gate, w_right, w_right_gate], axis=1)
    projected = jnp.einsum(
        "rcd,dh->hrc", normalized_input, stacked, preferred_element_type=jnp.float32
    )
    q_left, p_left, q_right, p_right = jnp.split(projected, 4, axis=0)
    s_left = jax.nn.sigmoid(p_left)
    s_right = jax.nn.sigmoid(p_right)
    left = (s_left * q_left).astype(jnp.bfloat16)
    right = (s_right * q_right).astype(jnp.bfloat16)
    g_chan, left_chan, right_chan = (
        lax.all_to_all(cotangent, "col", split_axis=0, concat_axis=2, tiled=True),
        lax.all_to_all(left, "col", split_axis=0, concat_axis=2, tiled=True),
        lax.all_to_all(right, "col", split_axis=0, concat_axis=2, tiled=True),
    )
    residues = g_chan.shape[2]
    g_columns = lax.all_to_all(g_chan, "row", split_axis=2, concat_axis=1, tiled=True)
    d_left = jnp.einsum(
        "hij,hjk->hik",
        g_chan,
        lax.all_gather(right_chan, "row", axis=1, tiled=True),
        preferred_element_type=jnp.float32,
    )
    d_right = jnp.einsum(
        "hij,hik->hjk",
        g_columns,
        lax.all_gather(left_chan, "row", axis=1, tiled=True),
        preferred_element_type=jnp.float32,
    )
    d_left_tile, d_right_tile = (
        lax.all_to_all(d_left.astype(jnp.bfloat16), "col", split_axis=2, concat_axis=0, tiled=True),
        lax.all_to_all(
            d_right.astype(jnp.bfloat16), "col", split_axis=2, concat_axis=0, tiled=True
        ),
    )
    grad_l = d_left_tile.astype(jnp.float32)
    grad_r = d_right_tile.astype(jnp.float32)
    e_left = grad_l * s_left
    f_left = grad_l * q_left * s_left * (1.0 - s_left)
    e_right = grad_r * s_right
    f_right = grad_r * q_right * s_right * (1.0 - s_right)
    grads = jnp.concatenate([e_left, f_left, e_right, f_right], axis=0).astype(jnp.bfloat16)
    local_weights = jnp.einsum(
        "rcd,hrc->dh", normalized_input, grads, preferred_element_type=jnp.float32
    )
    total_weights = lax.psum(local_weights, ("row", "col")) / residues
    normalized_gradient = jnp.einsum(
        "hrc,dh->rcd", grads, stacked, preferred_element_type=jnp.float32
    )
    gradient_mean = jnp.mean(normalized_gradient, axis=-1, keepdims=True)
    gradient_input_mean = jnp.mean(normalized_gradient * standardized_input, axis=-1, keepdims=True)
    pair_gradient = (
        (normalized_gradient - gradient_mean - standardized_input * gradient_input_mean)
        * inverse_scale
    ).astype(jnp.bfloat16)
    pieces_w = jnp.split(total_weights, 4, axis=1)
    return (pair_gradient, pieces_w[0], pieces_w[1], pieces_w[2], pieces_w[3])


NT = (((1,), (1,)), ((), ()))
TN = (((0,), (0,)), ((), ()))
NN = (((1,), (0,)), ((), ()))


def dot(a, b, dims=NN):
    return lax.dot_general(a, b, dims, preferred_element_type=F32)


def stack_weights(w_refs, w_ref):
    h = w_refs[0].shape[0]
    for i, ref in enumerate(w_refs):
        w_ref[pl.ds(i * h, h), :] = ref[...]


def layer_norm(x):
    x = x.T.astype(F32)
    centered = x - jnp.mean(x, axis=0, keepdims=True)
    variance = jnp.mean(centered * centered, axis=0, keepdims=True)
    inverse_scale = lax.rsqrt(variance + 1e-05)
    return centered * inverse_scale, inverse_scale


def project(w_ref, normed):
    projected = dot(w_ref[...], normed)
    h = projected.shape[0] // 4
    q_left, p_left, q_right, p_right = (projected[i * h : (i + 1) * h] for i in range(4))
    return q_left, jax.nn.sigmoid(p_left), q_right, jax.nn.sigmoid(p_right)


def put_lanes(ref, at, value):
    lanes = ref.shape[2]
    for i in range(ref.shape[0]):
        ref[i, at, :] = value[:, i * lanes : (i + 1) * lanes]


def get_lanes(ref, at):
    return jnp.concatenate([ref[i, at, :] for i in range(ref.shape[0])], axis=1)


def before_kernel(own, pair_hbm, cot_hbm, wl, wlg, wr, wrg, out_ref, normed_hbm, *scratch):
    w_ref, *rows_refs, pair_ref, normed_ref, in_sems, out_sems, w_sems, cot_sem = scratch
    h = wl.shape[0]
    rows = pair_ref.shape[0]
    parts = in_sems.shape[0]
    count = rows // parts
    pitch = count + 1

    def come(part):
        at = pl.ds(part * count, count)
        return pltpu.make_async_copy(pair_hbm.at[at], pair_ref.at[at], in_sems.at[part])

    def leave(part):
        at = pl.ds(part * count, count)
        return pltpu.make_async_copy(normed_ref.at[at], normed_hbm.at[at], out_sems.at[part])

    def weight(i, w):
        return pltpu.make_async_copy(w, w_ref.at[pl.ds(i * h, h)], w_sems.at[i])

    for i, w in enumerate((wl, wlg, wr, wrg)):
        weight(i, w).start()
    for part in range(parts):
        come(part).start()
    cot = pltpu.make_async_copy(cot_hbm, out_ref.at[:, pl.ds(0, own)], cot_sem)
    cot.start()
    for i, w in enumerate((wl, wlg, wr, wrg)):
        weight(i, w).wait()

    def one_row(part, i):
        r = part * count + i
        normed = layer_norm(pair_ref[r])[0].astype(BF16)
        normed_ref[r] = normed
        q_left, s_left, q_right, s_right = project(w_ref, normed)
        put_lanes(rows_refs[part], pl.ds(i, h, stride=pitch), s_left * q_left)
        put_lanes(rows_refs[part], pl.ds(i + h * pitch, h, stride=pitch), s_right * q_right)

    def some_channels(part, i):
        for channel in range(i * h // count, (i + 1) * h // count):
            for side in range(2):
                at = pl.ds((side * h + channel) * pitch, count)
                line = get_lanes(rows_refs[part], at).astype(BF16)
                slot = (1 + side) * own + channel % own
                out_ref[channel // own, slot, pl.ds(part * count, count), :] = line

    for part in range(parts + 1):
        if part < parts:
            come(part).wait()
        for i in range(count):
            if part < parts:
                one_row(part, i)
            if part > 0:
                some_channels(part - 1, i)
        if part < parts:
            leave(part).start()
    for part in range(parts):
        leave(part).wait()
    cot.wait()


def triangle_kernel(rows, cols, in_ref, out_ref, g_ref, l_ref, r_ref):
    r, c = in_ref.shape[2:]
    own = g_ref.shape[0]
    for n in range(own):
        for i, ref in enumerate((g_ref, l_ref, r_ref)):
            for a in range(rows):
                for b in range(cols):
                    block = in_ref[a * cols + b, i * own + n]
                    ref[n, pl.ds(a * r, r), pl.ds(b * c, c)] = block
        for i, (dims, ref) in enumerate(((NN, r_ref), (TN, l_ref))):
            d = dot(g_ref[n], ref[n], dims).astype(BF16)
            for a in range(rows):
                for b in range(cols):
                    block = d[a * r : (a + 1) * r, b * c : (b + 1) * c]
                    out_ref[a * cols + b, n * 2 + i] = block


def gates_kernel(own, normed_hbm, d_ref, wl, wlg, wr, wrg, grads_ref, kept_ref, sent_ref, *scratch):
    w_ref, sums_ref, *rows_refs, normed_ref, sems = scratch
    h = wl.shape[0]
    rows = grads_ref.shape[0]
    parts = len(rows_refs)
    count = rows // parts
    pitch = count + 1

    def come(part):
        at = pl.ds(part * count, count)
        return pltpu.make_async_copy(normed_hbm.at[at], normed_ref.at[at], sems.at[part])

    for part in range(parts):
        come(part).start()
    stack_weights((wl, wlg, wr, wrg), w_ref)

    def some_channels(part, i):
        for channel in range(i * h // count, (i + 1) * h // count):
            to, slot = channel // own, (channel % own) * 2
            for side in range(2):
                line = d_ref[to, slot + side, pl.ds(part * count, count), :].astype(F32)
                put_lanes(rows_refs[part], pl.ds((side * h + channel) * pitch, count), line)

    def one_row(part, i):
        normed = normed_ref[part * count + i]
        q_left, s_left, q_right, s_right = project(w_ref, normed)
        e_left = get_lanes(rows_refs[part], pl.ds(i, h, stride=pitch)) * s_left
        e_right = get_lanes(rows_refs[part], pl.ds(i + h * pitch, h, stride=pitch)) * s_right
        f_left = e_left * q_left * (1.0 - s_left)
        f_right = e_right * q_right * (1.0 - s_right)
        grads = jnp.concatenate([e_left, f_left, e_right, f_right], axis=0).astype(BF16)
        grads_ref[part * count + i] = grads
        return grads, normed

    together = 8 if count % 8 == 0 else count
    sums_ref[...] = jnp.zeros_like(sums_ref)
    for part in range(parts + 1):
        if part > 0:
            come(part - 1).wait()
        done = []
        for i in range(count):
            if part > 0:
                done.append(one_row(part - 1, i))
            if part < parts:
                some_channels(part, i)
            if len(done) == together:
                all_grads, all_normed = (jnp.concatenate(x, axis=1) for x in zip(*done))
                sums_ref[...] += dot(all_grads, all_normed, NT)
                done = []
    bit = lax.rem(lax.axis_index("row"), 2)
    kept_ref[...] = sums_ref[pl.ds(pl.multiple_of(bit * 2 * h, 2 * h), 2 * h), :]
    sent_ref[...] = sums_ref[pl.ds(pl.multiple_of((1 - bit) * 2 * h, 2 * h), 2 * h), :]


def input_kernel(start, pair_hbm, grads_ref, wl, wlg, wr, wrg, *refs):
    out_hbm, back_ref, pair_ref, out_ref, in_sem, out_sems = refs[-6:]
    rows = pair_ref.shape[0]
    come = pltpu.make_async_copy(pair_hbm.at[pl.ds(start, rows)], pair_ref, in_sem)
    come.start()
    h = wl.shape[0]
    for i, ref in enumerate((wl, wlg, wr, wrg)):
        back_ref[:, pl.ds(i * h, h)] = ref[...].T
    come.wait()

    def one_row(r, carry):
        standardized, inverse_scale = layer_norm(pair_ref[r])
        d_normed = dot(back_ref[...], grads_ref[start + r])
        mean = jnp.mean(d_normed, axis=0, keepdims=True)
        input_mean = jnp.mean(d_normed * standardized, axis=0, keepdims=True)
        moved = (d_normed - mean - standardized * input_mean) * inverse_scale
        out_ref[r] = moved.astype(BF16).T
        return carry

    parts = out_sems.shape[0]
    count = rows // parts
    gone = []
    for part in range(parts):
        lax.fori_loop(part * count, (part + 1) * count, one_row, 0, unroll=8)
        at = pl.ds(part * count, count)
        to = out_hbm.at[pl.ds(start + part * count, count)]
        gone.append(pltpu.make_async_copy(out_ref.at[at], to, out_sems.at[part]))
        gone[-1].start()
    for copy in gone:
        copy.wait()


def finish_kernel(scale, mine_ref, other_ref, *out_refs):
    h = out_refs[0].shape[0]
    bit = lax.rem(lax.axis_index("row"), 2)
    for i, out_ref in enumerate(out_refs):
        at = pl.ds(i % 2 * h, h)
        mine = bit == i // 2
        out_ref[...] = jnp.where(mine, mine_ref[at, :], other_ref[at, :]) * scale


def channel_shards(sizes, pair, cotangent, *weights):
    rows, cols = sizes
    devices = rows * cols
    hidden, r, c = cotangent.shape
    dim = pair.shape[2]
    own = hidden // devices
    pieces = 2 if r % 2 == 0 else 1
    parts = 2 if r % 32 == 0 else 1
    weights = [w.T for w in weights]
    vmem = pl.BlockSpec(memory_space=pltpu.VMEM)
    hbm = pl.BlockSpec(memory_space=pltpu.HBM)
    exchange = functools.partial(
        lax.all_to_all, axis_name=("row", "col"), split_axis=0, concat_axis=0, tiled=True
    )
    stacked = pltpu.VMEM((4 * hidden, dim), BF16)
    lanes = min(c, 128)
    rows_scratch = pltpu.VMEM((c // lanes, (2 * hidden + 1) * (r // parts + 1), lanes), F32)
    columns = r * c
    n_i, n_k = rows * r, cols * c
    pair = pltpu.with_memory_space_constraint(pair, pltpu.HBM)

    def cost(flops, *arrays):
        moved = sum(a.size * a.dtype.itemsize for a in arrays)
        return pl.CostEstimate(flops=flops, bytes_accessed=moved, transcendentals=0)

    def memory(mib):
        return pltpu.CompilerParams(vmem_limit_bytes=mib * 2**20)

    normed_shape = jax.ShapeDtypeStruct((r, dim, c), BF16)
    sent, normed = pl.pallas_call(
        functools.partial(before_kernel, own),
        in_specs=[hbm] * 6,
        out_specs=[vmem, hbm],
        out_shape=[
            jax.ShapeDtypeStruct((devices, 3 * own, r, c), BF16),
            pltpu.HBM(normed_shape.shape, BF16),
        ],
        scratch_shapes=[
            stacked,
            *[rows_scratch] * parts,
            pltpu.VMEM(pair.shape, BF16),
            pltpu.VMEM(normed_shape.shape, BF16),
            pltpu.SemaphoreType.DMA((parts,)),
            pltpu.SemaphoreType.DMA((parts,)),
            pltpu.SemaphoreType.DMA((4,)),
            pltpu.SemaphoreType.DMA,
        ],
        compiler_params=memory(24),
        name="before",
    )(
        pair,
        pltpu.with_memory_space_constraint(cotangent.reshape(devices, own, r, c), pltpu.HBM),
        *(pltpu.with_memory_space_constraint(w, pltpu.HBM) for w in weights),
    )

    sent = pl.pallas_call(
        functools.partial(triangle_kernel, rows, cols),
        in_specs=[vmem],
        out_specs=vmem,
        out_shape=jax.ShapeDtypeStruct((devices, 2 * own, r, c), BF16),
        scratch_shapes=[pltpu.VMEM((own, n_i, n_k), BF16)] * 3,
        compiler_params=memory(32),
        name="triangle",
    )(exchange(sent))

    half_shape = jax.ShapeDtypeStruct((2 * hidden, dim), F32)
    grads, kept, given = pl.pallas_call(
        functools.partial(gates_kernel, own),
        in_specs=[hbm] + [vmem] * 5,
        out_specs=[vmem] * 3,
        out_shape=[jax.ShapeDtypeStruct((r, 4 * hidden, c), BF16), half_shape, half_shape],
        scratch_shapes=[
            stacked,
            pltpu.VMEM((4 * hidden, dim), F32),
            *[rows_scratch] * parts,
            pltpu.VMEM(normed_shape.shape, BF16),
            pltpu.SemaphoreType.DMA((parts,)),
        ],
        compiler_params=memory(28),
        name="gates",
    )(pltpu.with_memory_space_constraint(normed, pltpu.HBM), exchange(sent), *weights)

    def input_piece(piece, pair_gradient):
        held = [] if pair_gradient is None else [pair_gradient]
        count = r // pieces
        return pl.pallas_call(
            functools.partial(input_kernel, piece * count),
            in_specs=[hbm] + [vmem] * 5 + [hbm] * len(held),
            out_specs=hbm,
            out_shape=jax.ShapeDtypeStruct(pair.shape, BF16),
            scratch_shapes=[
                pltpu.VMEM((dim, 4 * hidden), BF16),
                pltpu.VMEM((count, c, dim), BF16),
                pltpu.VMEM((count, c, dim), BF16),
                pltpu.SemaphoreType.DMA,
                pltpu.SemaphoreType.DMA((2 if count % 8 == 0 else 1,)),
            ],
            input_output_aliases={6: 0} if held else {},
            compiler_params=memory(16),
            cost_estimate=cost(8 * hidden * dim * columns // pieces, pair),
            name="input",
        )(pair, grads, *weights, *held)

    steps = [("row", rows, 1 << i) for i in range(1, rows.bit_length() - 1)][::-1]
    steps += [("col", cols, 1 << i) for i in range(cols.bit_length() - 1)]
    pieces = min(pieces, len(steps))
    neighbours = [(i, i ^ 1) for i in range(rows)]
    pair_gradient = None
    mine = kept + lax.ppermute(given, "row", neighbours)
    for n, (axis, size, step) in enumerate(steps):
        other = lax.ppermute(mine, axis, [(i, i ^ step) for i in range(size)])
        if n < pieces:
            pair_gradient = input_piece(n, pair_gradient)
            other, pair_gradient = lax.optimization_barrier((other, pair_gradient))
        mine = mine + other
    weight_grads = pl.pallas_call(
        functools.partial(finish_kernel, 1.0 / n_i),
        in_specs=[vmem, vmem],
        out_shape=[jax.ShapeDtypeStruct((hidden, dim), F32)] * 4,
        compiler_params=memory(8),
        name="finish",
    )(mine, lax.ppermute(mine, "row", neighbours))
    return (pair_gradient, *(g.T for g in weight_grads))


def solution(mesh):
    in_specs = (P("row", "col", None), P(None, "row", "col"), P(), P(), P(), P())
    out_specs = (P("row", "col", None), P(), P(), P(), P())
    sizes = (mesh.shape["row"], mesh.shape["col"])

    def shards(pair, cotangent, *weights):
        plain = all(size > 1 and size & (size - 1) == 0 for size in sizes)
        if plain and cotangent.shape[0] % (sizes[0] * sizes[1]) == 0:
            return channel_shards(sizes, pair, cotangent, *weights)
        return gathered_shards(pair, cotangent, *weights)

    return jax.shard_map(shards, mesh=mesh, in_specs=in_specs, out_specs=out_specs, check_vma=False)
```
